32 devices in a mesh: dp: 8 (over z, x), blk: 4 (over y, core).
Axes of the slice: x: 2, y: 2, z: 4, core: 2. Of those that a mesh axis runs over, the one named last changes fastest.
Arguments:
- encoder_input: bfloat16 [24, 4, 256, 768], P('dp', 'blk'), may hold values from -6 to 6
- decoder_input: bfloat16 [24, 20, 768], P('dp'), may hold values from -6 to 6
- encoder_cotangent: bfloat16 [24, 4, 256, 768], P('dp', 'blk'), may hold values from -6 to 6
- decoder_cotangent: bfloat16 [24, 20, 768], P('dp'), may hold values from -6 to 6
- segment_ids: int32 [24, 4, 256], P('dp', 'blk'), may hold values from 0 to 3, never falling along the last dimension, each value on 1 to 128 neighbouring positions
- padding_mask: int32 [24, 4, 256], P('dp', 'blk'), may hold values from 0 to 1, as said below
- answer_length: int32 [24], P('dp'), may hold values from 1 to 20, as said below
- encoder_attn_gain: bfloat16 [768], replicated, may hold values from 0.25 to 1.75
- encoder_query: bfloat16 [768, 768], replicated, may hold values from -0.02734375 to 0.02734375
- encoder_key: bfloat16 [768, 768], replicated, may hold values from -0.21875 to 0.21875
- encoder_value: bfloat16 [768, 768], replicated, may hold values from -0.21875 to 0.21875
- encoder_mix: bfloat16 [768, 768], replicated, may hold values from -0.875 to 0.875
- encoder_bias_table: bfloat16 [32, 12], replicated, may hold values from -4 to 4
- encoder_ffn_gain: bfloat16 [768], replicated, may hold values from 0.25 to 1.75
- encoder_ffn_in: bfloat16 [768, 3072], replicated, may hold values from -0.21875 to 0.21875
- encoder_ffn_out: bfloat16 [3072, 768], replicated, may hold values from -0.109375 to 0.109375
- final_gain: bfloat16 [768], replicated, may hold values from 0.25 to 1.75
- cross_key: bfloat16 [768, 768], replicated, may hold values from -0.21875 to 0.21875
- cross_value: bfloat16 [768, 768], replicated, may hold values from -0.21875 to 0.21875
- decoder_self_gain: bfloat16 [768], replicated, may hold values from 0.25 to 1.75
- decoder_query: bfloat16 [768, 768], replicated, may hold values from -0.02734375 to 0.02734375
- decoder_key: bfloat16 [768, 768], replicated, may hold values from -0.21875 to 0.21875
- decoder_value: bfloat16 [768, 768], replicated, may hold values from -0.21875 to 0.21875
- decoder_mix: bfloat16 [768, 768], replicated, may hold values from -0.4375 to 0.4375
- decoder_bias_table: bfloat16 [32, 12], replicated, may hold values from -4 to 4
- decoder_cross_gain: bfloat16 [768], replicated, may hold values from 0.25 to 1.75
- cross_query: bfloat16 [768, 768], replicated, may hold values from -0.0546875 to 0.0546875
- cross_mix: bfloat16 [768, 768], replicated, may hold values from -1.25 to 1.25
- decoder_ffn_gain: bfloat16 [768], replicated, may hold values from 0.25 to 1.75
- decoder_ffn_in: bfloat16 [768, 3072], replicated, may hold values from -0.21875 to 0.21875
- decoder_ffn_out: bfloat16 [3072, 768], replicated, may hold values from -0.109375 to 0.109375
Outputs:
- encoder_result: bfloat16 [24, 4, 256, 768], P('dp', 'blk')
- decoder_result: bfloat16 [24, 20, 768], P('dp')
- gradient_encoder_input: float32 [24, 4, 256, 768], P('dp', 'blk')
- gradient_decoder_input: float32 [24, 20, 768], P('dp')
- gradient_encoder_attn_gain: float32 [768], P('dp')
- gradient_encoder_query: float32 [768, 768], P('dp')
- gradient_encoder_key: float32 [768, 768], P('dp')
- gradient_encoder_value: float32 [768, 768], P('dp')
- gradient_encoder_mix: float32 [768, 768], P('dp')
- gradient_encoder_bias_table: float32 [32, 12], P('dp')
- gradient_encoder_ffn_gain: float32 [768], P('dp')
- gradient_encoder_ffn_in: float32 [768, 3072], P('dp')
- gradient_encoder_ffn_out: float32 [3072, 768], P('dp')
- gradient_final_gain: float32 [768], P('dp')
- gradient_cross_key: float32 [768, 768], P('dp')
- gradient_cross_value: float32 [768, 768], P('dp')
- gradient_decoder_self_gain: float32 [768], P('dp')
- gradient_decoder_query: float32 [768, 768], P('dp')
- gradient_decoder_key: float32 [768, 768], P('dp')
- gradient_decoder_value: float32 [768, 768], P('dp')
- gradient_decoder_mix: float32 [768, 768], P('dp')
- gradient_decoder_bias_table: float32 [32, 12], P('dp')
- gradient_decoder_cross_gain: float32 [768], P('dp')
- gradient_cross_query: float32 [768, 768], P('dp')
- gradient_cross_mix: float32 [768, 768], P('dp')
- gradient_decoder_ffn_gain: float32 [768], P('dp')
- gradient_decoder_ffn_in: float32 [768, 3072], P('dp')
- gradient_decoder_ffn_out: float32 [3072, 768], P('dp')
The draws below stay inside these ranges and needn't reach their ends.
Inputs may be any that keep to these rules, and one draw needn't show every extreme that they name: `segment_ids`: within a row segment numbers never fall; a segment covers 1 to 128 positions. `padding_mask`: in each packed row the ones come first and there are 128 or more of them; in each question some row has no padding. `answer_length`: some question has every slot filled.
All inputs are finite; a program needn't handle non-finite values.
Results may differ from the reference program's by a relative error of at most 0.028.
Values may be sent and summed in bfloat16 or wider, within the bound.
No kernel may reach another device: no remote copies, remote signals or barrier semaphores. Data moves between devices by JAX's collectives and lax.ppermute only.
A program may use at most 256 MiB of HBM per device.

```python
import math
import jax
import jax.numpy as jnp
import numpy as np
from jax import lax

D = 768
H = 12
HD = 64
FF = 3072
NB = 32
MAXD = 128
ROW = 256
ANS = 20
QUEST = 24
ROWS_Q = 4


def draw_padding_mask(key, part):
    key = jax.random.fold_in(key, 7)
    first, second = jax.random.split(key)
    lengths = jax.random.randint(first, (QUEST, ROWS_Q), ROW // 2, ROW + 1)
    chosen = jax.random.randint(second, (QUEST, 1), 0, ROWS_Q)
    lengths = jnp.where(jnp.arange(ROWS_Q)[None, :] == chosen, ROW, lengths)
    places = jnp.arange(ROW)[None, None, :]
    return (places < lengths[:, :, None]).astype(jnp.int32)


def draw_answer_length(key, part):
    key = jax.random.fold_in(key, 11)
    first, second = jax.random.split(key)
    lengths = jax.random.randint(first, (QUEST,), 1, ANS + 1)
    chosen = jax.random.randint(second, (), 0, QUEST)
    return jnp.where(jnp.arange(QUEST) == chosen, ANS, lengths).astype(jnp.int32)


def block_levels(rng, dims, pieces, low, top_value):
    def one(axis_at, parts):
        steps = jax.random.uniform(jax.random.fold_in(jax.random.fold_in(rng, 6), axis_at), (parts,), jnp.float32, low / len(pieces), top_value / len(pieces))
        return jnp.repeat(jnp.exp(steps), dims[axis_at] // parts).reshape((-1,) + (1,) * (len(dims) - axis_at - 1))

    loudness = one(*pieces[0])
    for cut in pieces[1:]:
        loudness = loudness * one(*cut)
    return loudness


def length_profile(number_of, total, reach, slope):
    weights = [(1 << 20) // math.isqrt(standing ** slope) + 1 for standing in range(2, number_of + 1)]
    surplus, counts = total - reach - (number_of - 1), [1] * (number_of - 1)
    while surplus > 0:
        candidates = [i for i in range(number_of - 1) if counts[i] < reach]
        pool, left = sum([weights[i] for i in candidates]), surplus
        for i in candidates:
            extra = min(reach - counts[i], max(1, left * weights[i] // pool), surplus)
            counts[i] = counts[i] + extra
            surplus = surplus - extra
    return np.array([reach] + counts)


def ragged_sizes(rng, amount, total, most, slope):
    if amount == 2:
        one = jax.random.randint(rng, (), max(1, total - most), min(most, total - 1) + 1)
        return jnp.stack([one, total - one])
    sizes = jnp.asarray(length_profile(amount, total, most, slope), jnp.int32)
    twos = (amount - 1) // 2
    donor, receiver = sizes[1:1 + 2 * twos:2], sizes[2:2 + 2 * twos:2]
    margin = jnp.minimum(donor - 1, most - receiver)
    shifted = jax.random.randint(jax.random.fold_in(rng, 1), (twos,), 0, 1 << 20) % (margin + 1)
    sizes = sizes.at[1:1 + 2 * twos:2].set(donor - shifted).at[2:2 + 2 * twos:2].set(receiver + shifted)
    return sizes[jax.random.permutation(jax.random.fold_in(rng, 2), amount)]


def scatter_about(own_key, dims, deviation, reach, cuts=(), held_as=jnp.bfloat16):
    array = jax.random.normal(own_key, dims, jnp.float32) * deviation
    if len(cuts) > 0:
        array = block_levels(own_key, dims, cuts, -0.22, 0.18) * array
    return jnp.clip(array, min=-reach, max=reach).astype(held_as)


def setup_inputs(seed: int = 0) -> dict:
    key_of = jax.random.split(jax.random.key(seed), 32)
    encoder_input = scatter_about(key_of[0], (QUEST, ROWS_Q, ROW, D), 1.0, 6.0, ((0, 8), (1, 4)))
    decoder_input = scatter_about(key_of[1], (QUEST, ANS, D), 1.0, 6.0, ((0, 8),))
    encoder_cotangent = scatter_about(key_of[2], (QUEST, ROWS_Q, ROW, D), 1.0, 6.0, ((0, 8), (1, 4)))
    decoder_cotangent = scatter_about(key_of[3], (QUEST, ANS, D), 1.0, 6.0, ((0, 8),))
    segment_ids = jax.vmap(lambda own: jnp.searchsorted(jnp.cumsum(ragged_sizes(own, 4, ROW, ROW // 2, 0)), jnp.arange(ROW), side="right"))(jax.random.split(key_of[4], QUEST * ROWS_Q)).reshape((QUEST, ROWS_Q, ROW)).astype(jnp.int32)
    padding_mask = draw_padding_mask(jax.random.fold_in(key_of[31], 71), 0)
    answer_length = draw_answer_length(jax.random.fold_in(key_of[31], 71), 0)
    encoder_attn_gain = jnp.clip(1.0 + 0.15 * jax.random.normal(key_of[7], (D,), jnp.float32), 0.25, 1.75).astype(jnp.bfloat16)
    encoder_query = scatter_about(key_of[8], (D, D), (D * HD) ** -0.5, 0.02734375)
    encoder_key = scatter_about(key_of[9], (D, D), D ** -0.5, 0.21875)
    encoder_value = scatter_about(key_of[10], (D, D), D ** -0.5, 0.21875)
    encoder_mix = scatter_about(key_of[11], (D, D), (D // 16) ** -0.5, 0.875)
    encoder_bias_table = scatter_about(key_of[12], (NB, H), 1.0, 4.0)
    encoder_ffn_gain = jnp.clip(1.0 + 0.15 * jax.random.normal(key_of[13], (D,), jnp.float32), 0.25, 1.75).astype(jnp.bfloat16)
    encoder_ffn_in = scatter_about(key_of[14], (D, FF), D ** -0.5, 0.21875)
    encoder_ffn_out = scatter_about(key_of[15], (FF, D), FF ** -0.5, 0.109375)
    final_gain = jnp.clip(1.0 + 0.15 * jax.random.normal(key_of[16], (D,), jnp.float32), 0.25, 1.75).astype(jnp.bfloat16)
    cross_key = scatter_about(key_of[17], (D, D), D ** -0.5, 0.21875)
    cross_value = scatter_about(key_of[18], (D, D), D ** -0.5, 0.21875)
    decoder_self_gain = jnp.clip(1.0 + 0.15 * jax.random.normal(key_of[19], (D,), jnp.float32), 0.25, 1.75).astype(jnp.bfloat16)
    decoder_query = scatter_about(key_of[20], (D, D), (D * HD) ** -0.5, 0.02734375)
    decoder_key = scatter_about(key_of[21], (D, D), D ** -0.5, 0.21875)
    decoder_value = scatter_about(key_of[22], (D, D), D ** -0.5, 0.21875)
    decoder_mix = scatter_about(key_of[23], (D, D), (D // 4) ** -0.5, 0.4375)
    decoder_bias_table = scatter_about(key_of[24], (NB, H), 1.0, 4.0)
    decoder_cross_gain = jnp.clip(1.0 + 0.15 * jax.random.normal(key_of[25], (D,), jnp.float32), 0.25, 1.75).astype(jnp.bfloat16)
    cross_query = scatter_about(key_of[26], (D, D), (D * HD // 4) ** -0.5, 0.0546875)
    cross_mix = scatter_about(key_of[27], (D, D), (D // 32) ** -0.5, 1.25)
    decoder_ffn_gain = jnp.clip(1.0 + 0.15 * jax.random.normal(key_of[28], (D,), jnp.float32), 0.25, 1.75).astype(jnp.bfloat16)
    decoder_ffn_in = scatter_about(key_of[29], (D, FF), D ** -0.5, 0.21875)
    decoder_ffn_out = scatter_about(key_of[30], (FF, D), FF ** -0.5, 0.109375)
    return {"encoder_input": encoder_input, "decoder_input": decoder_input, "encoder_cotangent": encoder_cotangent, "decoder_cotangent": decoder_cotangent, "segment_ids": segment_ids, "padding_mask": padding_mask, "answer_length": answer_length, "encoder_attn_gain": encoder_attn_gain, "encoder_query": encoder_query, "encoder_key": encoder_key, "encoder_value": encoder_value, "encoder_mix": encoder_mix, "encoder_bias_table": encoder_bias_table, "encoder_ffn_gain": encoder_ffn_gain, "encoder_ffn_in": encoder_ffn_in, "encoder_ffn_out": encoder_ffn_out, "final_gain": final_gain, "cross_key": cross_key, "cross_value": cross_value, "decoder_self_gain": decoder_self_gain, "decoder_query": decoder_query, "decoder_key": decoder_key, "decoder_value": decoder_value, "decoder_mix": decoder_mix, "decoder_bias_table": decoder_bias_table, "decoder_cross_gain": decoder_cross_gain, "cross_query": cross_query, "cross_mix": cross_mix, "decoder_ffn_gain": decoder_ffn_gain, "decoder_ffn_in": decoder_ffn_in, "decoder_ffn_out": decoder_ffn_out}


@jax.custom_vjp
def low(v):
    return lax.optimization_barrier(v.astype(jnp.bfloat16)).astype(jnp.float32)

@jax.custom_vjp
def low_back(v):
    return v

def low_keep(v):
    return (low(v), None)

def low_pass(kept, grad):
    return (grad,)

def back_keep(v):
    return (v, None)

def back_low(kept, grad):
    return (low(grad),)
low.defvjp(low_keep, low_pass)
low_back.defvjp(back_keep, back_low)
EPSILON = 1e-06
WEIGHT_NAMES = ('encoder_attn_gain', 'encoder_query', 'encoder_key', 'encoder_value', 'encoder_mix', 'encoder_bias_table', 'encoder_ffn_gain', 'encoder_ffn_in', 'encoder_ffn_out', 'final_gain', 'cross_key', 'cross_value', 'decoder_self_gain', 'decoder_query', 'decoder_key', 'decoder_value', 'decoder_mix', 'decoder_bias_table', 'decoder_cross_gain', 'cross_query', 'cross_mix', 'decoder_ffn_gain', 'decoder_ffn_in', 'decoder_ffn_out')

def bucket_onehot(length, both_ways):
    places = jnp.arange(length, dtype=jnp.int32)
    offsets = places[None, :] - places[:, None]
    if both_ways:
        buckets = NB // 2
        index = jnp.where(offsets > 0, buckets, 0)
        distance = jnp.abs(offsets)
    else:
        buckets = NB
        index = jnp.zeros_like(offsets)
        distance = jnp.maximum(-offsets, 0)
    exact = buckets // 2
    index = index + jnp.minimum(distance, exact)
    for step in range(1, buckets - exact):
        border = math.ceil(exact * (MAXD / exact) ** (step / (buckets - exact)) - 1e-09)
        index = index + jnp.where(distance >= border, 1, 0)
    matches = index[:, :, None] == jnp.arange(NB, dtype=jnp.int32)[None, None, :]
    return matches.reshape(length * length, NB)

def relative_bias(table, length, both_ways):
    onehot = bucket_onehot(length, both_ways).astype(jnp.float32)
    return jnp.dot(onehot, table, precision=lax.Precision.HIGHEST).reshape(length, length, H).transpose(2, 0, 1)[None]

def rms_norm(values, gain):
    return values * lax.rsqrt(lax.optimization_barrier(jnp.mean(values * values, axis=-1, keepdims=True)) + EPSILON) * gain

def product(left, right):
    return jnp.dot(left, right, precision=lax.Precision.HIGHEST)

def attend(query, key, value, bias, allowed):
    scores = low_back(jnp.einsum('blhe,bmhe->bhlm', query, key, precision=lax.Precision.HIGHEST) + bias)
    scores = jnp.where(allowed, scores, -1e+30)
    scores = scores - lax.optimization_barrier(jnp.max(scores, axis=-1, keepdims=True))
    weights = jnp.exp(scores)
    weights = weights / lax.optimization_barrier(jnp.sum(weights, axis=-1, keepdims=True))
    return jnp.einsum('bhlm,bmhe->blhe', low(weights), value, precision=lax.Precision.HIGHEST)

def block(passage, answer, params, segments, padding, length):
    rows = passage.shape[0]
    heads = (rows, ROW, H, HD)
    normed = low(rms_norm(passage, params['encoder_attn_gain']))
    query = low_back(low(product(normed, params['encoder_query']))).reshape(heads)
    key = low_back(low(product(normed, params['encoder_key']))).reshape(heads)
    value = low_back(low(product(normed, params['encoder_value']))).reshape(heads)
    places = jnp.arange(ROW)
    diagonal = places[:, None] == places[None, :]
    allowed = ((segments[:, :, None] == segments[:, None, :]) & ((padding[:, None, :] == 1) | diagonal[None]))[:, None]
    attended = attend(query, key, value, relative_bias(params['encoder_bias_table'], ROW, True), allowed)
    attended = low_back(low(attended.reshape(rows, ROW, D)))
    hidden = passage + low_back(product(attended, params['encoder_mix']))
    normed = low(rms_norm(hidden, params['encoder_ffn_gain']))
    before = low_back(product(normed, params['encoder_ffn_in']))
    active = low(jax.nn.gelu(before, approximate=True))
    encoded = hidden + low_back(product(active, params['encoder_ffn_out']))
    final = low(rms_norm(encoded, params['final_gain']))
    memory = (1, rows * ROW, H, HD)
    memory_key = low_back(low(product(final, params['cross_key']))).reshape(memory)
    memory_value = low_back(low(product(final, params['cross_value']))).reshape(memory)
    visible = (padding.reshape(1, rows * ROW) == 1)[:, None, None, :]
    shape = (1, ANS, H, HD)
    normed = low(rms_norm(answer, params['decoder_self_gain']))
    query = low_back(low(product(normed, params['decoder_query']))).reshape(shape)
    key = low_back(low(product(normed, params['decoder_key']))).reshape(shape)
    value = low_back(low(product(normed, params['decoder_value']))).reshape(shape)
    steps = jnp.arange(ANS)
    allowed = ((steps[None, :] <= steps[:, None]) & (steps[None, :] < length))[None, None]
    attended = attend(query, key, value, relative_bias(params['decoder_bias_table'], ANS, False), allowed)
    attended = low_back(low(attended.reshape(ANS, D)))
    hidden = answer + low_back(product(attended, params['decoder_mix']))
    normed = low(rms_norm(hidden, params['decoder_cross_gain']))
    asking = low_back(low(product(normed, params['cross_query']))).reshape(shape)
    reading = low_back(low(attend(asking, memory_key, memory_value, 0.0, visible).reshape(ANS, D)))
    middle = hidden + low_back(product(reading, params['cross_mix']))
    normed = low(rms_norm(middle, params['decoder_ffn_gain']))
    before = low_back(product(normed, params['decoder_ffn_in']))
    active = low(jax.nn.gelu(before, approximate=True))
    decoded = middle + low_back(product(active, params['decoder_ffn_out']))
    return (encoded, decoded)

def reference(encoder_input, decoder_input, encoder_cotangent, decoder_cotangent, segment_ids, padding_mask, answer_length, encoder_attn_gain, encoder_query, encoder_key, encoder_value, encoder_mix, encoder_bias_table, encoder_ffn_gain, encoder_ffn_in, encoder_ffn_out, final_gain, cross_key, cross_value, decoder_self_gain, decoder_query, decoder_key, decoder_value, decoder_mix, decoder_bias_table, decoder_cross_gain, cross_query, cross_mix, decoder_ffn_gain, decoder_ffn_in, decoder_ffn_out):
    weights = (encoder_attn_gain, encoder_query, encoder_key, encoder_value, encoder_mix, encoder_bias_table, encoder_ffn_gain, encoder_ffn_in, encoder_ffn_out, final_gain, cross_key, cross_value, decoder_self_gain, decoder_query, decoder_key, decoder_value, decoder_mix, decoder_bias_table, decoder_cross_gain, cross_query, cross_mix, decoder_ffn_gain, decoder_ffn_in, decoder_ffn_out)
    params = {name: value.astype(jnp.float32) for name, value in zip(WEIGHT_NAMES, weights)}

    def one_question(totals, items):
        passage, answer, passage_cotangent, answer_cotangent, segments, padding, length = items

        def forward(inputs, values):
            return block(inputs[0], inputs[1], values, segments, padding, length)
        results, pullback = jax.vjp(forward, (passage.astype(jnp.float32), answer.astype(jnp.float32)), params)
        input_deltas, weight_deltas = pullback((passage_cotangent.astype(jnp.float32), answer_cotangent.astype(jnp.float32)))
        totals = jax.tree.map(jnp.add, totals, weight_deltas)
        return (totals, (results[0].astype(jnp.bfloat16), results[1].astype(jnp.bfloat16), input_deltas[0], input_deltas[1]))
    start = jax.tree.map(jnp.zeros_like, params)
    totals, outputs = lax.scan(one_question, start, (encoder_input, decoder_input, encoder_cotangent, decoder_cotangent, segment_ids, padding_mask, answer_length))
    return (outputs[0], outputs[1], outputs[2], outputs[3], totals['encoder_attn_gain'], totals['encoder_query'], totals['encoder_key'], totals['encoder_value'], totals['encoder_mix'], totals['encoder_bias_table'], totals['encoder_ffn_gain'], totals['encoder_ffn_in'], totals['encoder_ffn_out'], totals['final_gain'], totals['cross_key'], totals['cross_value'], totals['decoder_self_gain'], totals['decoder_query'], totals['decoder_key'], totals['decoder_value'], totals['decoder_mix'], totals['decoder_bias_table'], totals['decoder_cross_gain'], totals['cross_query'], totals['cross_mix'], totals['decoder_ffn_gain'], totals['decoder_ffn_in'], totals['decoder_ffn_out'])
```

```python
import functools
import math

import jax
import jax.numpy as jnp
from jax import lax
from jax.sharding import PartitionSpec as P

D = 768
H = 12
HD = 64
NB = 32
MAXD = 128
ROW = 256
ANS = 20


EPSILON = 1e-06
NEGATIVE = -1e30


def bucket_onehot(length, both_ways):
    places = jnp.arange(length, dtype=jnp.int32)
    offsets = places[None, :] - places[:, None]
    if both_ways:
        buckets = NB // 2
        index = jnp.where(offsets > 0, buckets, 0)
        distance = jnp.abs(offsets)
    else:
        buckets = NB
        index = jnp.zeros_like(offsets)
        distance = jnp.maximum(-offsets, 0)
    exact = buckets // 2
    index = index + jnp.minimum(distance, exact)
    for step in range(1, buckets - exact):
        border = math.ceil(exact * (MAXD / exact) ** (step / (buckets - exact)) - 1e-09)
        index = index + jnp.where(distance >= border, 1, 0)
    matches = index[:, :, None] == jnp.arange(NB, dtype=jnp.int32)[None, None, :]
    return matches.reshape(length * length, NB)


def rms_forward(values, gain):
    scale = lax.rsqrt(jnp.mean(values * values, axis=-1, keepdims=True) + EPSILON)
    return (values * scale * gain, scale)


def rms_backward(values, scale, gain, upstream):
    scaled = upstream * gain
    inner = jnp.mean(scaled * values, axis=-1, keepdims=True)
    delta_values = scaled * scale - values * (scale * scale * scale) * inner
    delta_gain = jnp.sum((upstream * values * scale).reshape(-1, values.shape[-1]), axis=0)
    return (delta_values, delta_gain)


def project(inputs, weight):
    return jnp.dot(inputs, weight, preferred_element_type=jnp.float32)


def project_back(inputs, upstream, weight):
    flat_inputs = inputs.reshape(-1, inputs.shape[-1])
    flat_upstream = upstream.reshape(-1, upstream.shape[-1])
    delta_weight = jnp.einsum(
        "nd,ne->de", flat_inputs, flat_upstream, preferred_element_type=jnp.float32
    )
    delta_inputs = jnp.einsum("...e,de->...d", upstream, weight, preferred_element_type=jnp.float32)
    return (delta_inputs, delta_weight)


def smooth(values):
    return jax.nn.gelu(values, approximate=True)


def gelu_delta(before, upstream):
    ignored, pullback = jax.vjp(smooth, before)
    return pullback(upstream)[0]


def score_block(query, key, bias, allowed):
    scores = jnp.einsum("blhe,bmhe->bhlm", query, key, preferred_element_type=jnp.float32) + bias
    return jnp.where(allowed, scores, NEGATIVE)


def log_totals(scores):
    top = jnp.max(scores, axis=-1, keepdims=True)
    return top + jnp.log(jnp.sum(jnp.exp(scores - top), axis=-1, keepdims=True))


def weigh_values(chances, value):
    return jnp.einsum("bhlm,bmhe->blhe", chances, value, preferred_element_type=jnp.float32)


def score_deltas(value, chances, upstream, inner):
    delta_chances = jnp.einsum(
        "blhe,bmhe->bhlm", upstream, value, preferred_element_type=jnp.float32
    )
    if inner is None:
        inner = jnp.sum(delta_chances * chances, axis=-1, keepdims=True)
    return (chances * (delta_chances - inner)).astype(jnp.bfloat16)


def query_from_scores(delta_scores, key):
    return jnp.einsum("bhlm,bmhe->blhe", delta_scores, key, preferred_element_type=jnp.float32)


def key_value_deltas(delta_scores, rounded, query, upstream):
    delta_key = jnp.einsum(
        "bhlm,blhe->bmhe", delta_scores, query, preferred_element_type=jnp.float32
    )
    delta_value = jnp.einsum(
        "bhlm,blhe->bmhe", rounded, upstream, preferred_element_type=jnp.float32
    )
    return (delta_key, delta_value)


def bias_delta(delta_scores, onehot):
    count = delta_scores.shape[0]
    width = delta_scores.shape[1]
    flat_scores = delta_scores.reshape(count, width, -1)
    return jnp.einsum("bhx,xn->nh", flat_scores, onehot, preferred_element_type=jnp.float32)


def attend_forward(normed, query_weight, key_weight, value_weight, bias, allowed, shape):
    query = project(normed, query_weight).astype(jnp.bfloat16).reshape(shape)
    key = project(normed, key_weight).astype(jnp.bfloat16).reshape(shape)
    value = project(normed, value_weight).astype(jnp.bfloat16).reshape(shape)
    scores = score_block(query, key, bias, allowed)
    log_total = log_totals(scores)
    attended = weigh_values(jnp.exp(scores - log_total).astype(jnp.bfloat16), value)
    return ((query, key, value), log_total, attended.reshape(normed.shape).astype(jnp.bfloat16))


def attend_backward(
    normed,
    heads,
    log_total,
    bias,
    allowed,
    upstream,
    query_weight,
    key_weight,
    value_weight,
    onehot,
):
    query, key, value = heads
    chances = jnp.exp(score_block(query, key, bias, allowed) - log_total)
    upstream = upstream.reshape(query.shape)
    delta_scores = score_deltas(value, chances, upstream, None)
    delta_query = query_from_scores(delta_scores, key)
    delta_key, delta_value = key_value_deltas(
        delta_scores, chances.astype(jnp.bfloat16), query, upstream
    )
    flat = normed.shape
    from_query, weight_query = project_back(
        normed, delta_query.astype(jnp.bfloat16).reshape(flat), query_weight
    )
    from_key, weight_key = project_back(
        normed, delta_key.astype(jnp.bfloat16).reshape(flat), key_weight
    )
    from_value, weight_value = project_back(
        normed, delta_value.astype(jnp.bfloat16).reshape(flat), value_weight
    )
    return (
        from_query + from_key + from_value,
        weight_query,
        weight_key,
        weight_value,
        bias_delta(delta_scores, onehot),
    )


class Ring:
    def __init__(self, dp, blk):
        depth = 4 if dp % 4 == 0 else dp
        pair = 2 if blk % 2 == 0 else 1
        self.dp = dp
        self.blk = blk
        self.sizes = {"z": depth, "x": dp // depth, "y": blk // pair, "c": pair}

    def place(self, name):
        across = lax.axis_index("dp")
        along = lax.axis_index("blk")
        return {
            "z": across // self.sizes["x"],
            "x": across % self.sizes["x"],
            "y": along // self.sizes["c"],
            "c": along % self.sizes["c"],
        }[name]

    def shift(self, values, name):
        sizes = self.sizes
        moves = []
        for z in range(sizes["z"]):
            for x in range(sizes["x"]):
                for y in range(sizes["y"]):
                    for c in range(sizes["c"]):
                        here = {"z": z, "x": x, "y": y, "c": c}
                        there = dict(here)
                        there[name] = (there[name] + 1) % sizes[name]
                        moves.append((self.number(here), self.number(there)))
        return lax.ppermute(values, ("dp", "blk"), moves)

    def number(self, at):
        sizes = self.sizes
        across = at["z"] * sizes["x"] + at["x"]
        along = at["y"] * sizes["c"] + at["c"]
        return across * self.blk + along

    def scatter(self, values, axis, name):
        size = self.sizes[name]
        here = self.place(name)

        def part(index):
            return lax.dynamic_index_in_dim(values, index % size, axis, keepdims=False)

        total = part(here + size - 1)
        for step in range(1, size):
            got = self.shift(total, name)
            own = part(here + 2 * size - 1 - step)
            total = (got.astype(jnp.float32) + own.astype(jnp.float32)).astype(values.dtype)
        return total

    def scatter_all(self, values, names, order):
        names = list(names)
        for name in order:
            axis = names.index(name)
            values = self.scatter(values, axis, name)
            names.pop(axis)
        return values

    def gather(self, values, name):
        size = self.sizes[name]
        here = self.place(name)
        if size == 2:
            got = self.shift(values, name)
            first = here == 0
            return jnp.stack([jnp.where(first, values, got), jnp.where(first, got, values)])
        whole = jnp.zeros((size,) + values.shape, values.dtype)
        for step in range(size):
            whole = lax.dynamic_update_index_in_dim(whole, values, (here + size - step) % size, 0)
            if step < size - 1:
                values = self.shift(values, name)
        return whole

    def total(self, values):
        count = self.dp * self.blk
        if count & (count - 1):
            return lax.psum(values, ("dp", "blk"))
        bit = 1
        while bit < count:
            moves = [(index, index ^ bit) for index in range(count)]
            values = values + lax.ppermute(values, ("dp", "blk"), moves)
            bit *= 2
        return values


def unit_parts(units, ring):
    sizes = ring.sizes
    count = len(units)
    split = ring.blk // count
    rows = D // ring.dp // split
    stacked = jnp.stack([unit.astype(jnp.bfloat16).reshape(ring.dp, split, rows, D) for unit in units])
    if split > 1:
        stacked = stacked.transpose(0, 2, 1, 3, 4)
    return stacked.reshape(sizes["c"], sizes["y"], sizes["z"], sizes["x"], rows, D)


def units_back(whole, count):
    return whole.astype(jnp.float32).reshape(count, -1, D)


def weight_delta(inputs, upstream):
    return jnp.einsum(
        "nd,ne->de",
        inputs.reshape(-1, inputs.shape[-1]),
        upstream.reshape(-1, upstream.shape[-1]),
        preferred_element_type=jnp.float32,
    )


def input_delta(upstream, weight):
    return jnp.einsum("...e,de->...d", upstream, weight, preferred_element_type=jnp.float32)


def on_device(
    ring,
    encoder_input,
    decoder_input,
    encoder_cotangent,
    decoder_cotangent,
    segment_ids,
    padding_mask,
    answer_length,
    encoder_attn_gain,
    encoder_query,
    encoder_key,
    encoder_value,
    encoder_mix,
    encoder_bias_table,
    encoder_ffn_gain,
    encoder_ffn_in,
    encoder_ffn_out,
    final_gain,
    cross_key,
    cross_value,
    decoder_self_gain,
    decoder_query,
    decoder_key,
    decoder_value,
    decoder_mix,
    decoder_bias_table,
    decoder_cross_gain,
    cross_query,
    cross_mix,
    decoder_ffn_gain,
    decoder_ffn_in,
    decoder_ffn_out,
):
    questions = encoder_input.shape[0]
    batch = questions * encoder_input.shape[1]
    local = encoder_input.shape[1] * ROW
    flat_rows = (batch, ROW, D)
    passage_rows = encoder_input.reshape(flat_rows).astype(jnp.float32)
    segments = segment_ids.reshape(batch, ROW)
    padding = padding_mask.reshape(batch, ROW)
    places = jnp.arange(ROW)
    diagonal = places[:, None] == places[None, :]
    passage_allowed = (
        (segments[:, :, None] == segments[:, None, :])
        & ((padding[:, None, :] == 1) | diagonal[None])
    )[:, None]
    passage_onehot = bucket_onehot(ROW, True).astype(jnp.bfloat16)
    passage_bias = (
        jnp.dot(passage_onehot, encoder_bias_table, preferred_element_type=jnp.float32)
        .reshape(ROW, ROW, H)
        .transpose(2, 0, 1)[None]
    )
    normed_one, scale_one = rms_forward(passage_rows, encoder_attn_gain.astype(jnp.float32))
    normed_one = normed_one.astype(jnp.bfloat16)
    passage_heads, passage_total, passage_attended = attend_forward(
        normed_one,
        encoder_query,
        encoder_key,
        encoder_value,
        passage_bias,
        passage_allowed,
        (batch, ROW, H, HD),
    )
    passage_hidden = passage_rows + project(passage_attended, encoder_mix)
    normed_two, scale_two = rms_forward(passage_hidden, encoder_ffn_gain.astype(jnp.float32))
    normed_two = normed_two.astype(jnp.bfloat16)
    passage_before = project(normed_two, encoder_ffn_in)
    passage_active = smooth(passage_before).astype(jnp.bfloat16)
    passage_output = passage_hidden + project(passage_active, encoder_ffn_out)
    normed_final, scale_final = rms_forward(passage_output, final_gain.astype(jnp.float32))
    normed_final = normed_final.astype(jnp.bfloat16)
    memory_shape = (questions, local, H, HD)
    memory_key = project(normed_final, cross_key).astype(jnp.bfloat16).reshape(memory_shape)
    memory_value = project(normed_final, cross_value).astype(jnp.bfloat16).reshape(memory_shape)
    key_valid = padding_mask.reshape(questions, local) == 1
    answer_rows = decoder_input.astype(jnp.float32)
    answer_places = jnp.arange(ANS)
    causal = answer_places[None, :] <= answer_places[:, None]
    within = answer_places[None, None, :] < answer_length[:, None, None]
    answer_allowed = (causal[None] & within)[:, None]
    answer_onehot = bucket_onehot(ANS, False).astype(jnp.bfloat16)
    answer_bias = (
        jnp.dot(answer_onehot, decoder_bias_table, preferred_element_type=jnp.float32)
        .reshape(ANS, ANS, H)
        .transpose(2, 0, 1)[None]
    )
    answer_shape = (questions, ANS, H, HD)
    normed_three, scale_three = rms_forward(answer_rows, decoder_self_gain.astype(jnp.float32))
    normed_three = normed_three.astype(jnp.bfloat16)
    answer_heads, answer_total, answer_attended = attend_forward(
        normed_three,
        decoder_query,
        decoder_key,
        decoder_value,
        answer_bias,
        answer_allowed,
        answer_shape,
    )
    answer_hidden = answer_rows + project(answer_attended, decoder_mix)
    normed_four, scale_four = rms_forward(answer_hidden, decoder_cross_gain.astype(jnp.float32))
    normed_four = normed_four.astype(jnp.bfloat16)
    asking = project(normed_four, cross_query).astype(jnp.bfloat16).reshape(answer_shape)
    cross_allowed = key_valid[:, None, None, :]
    cross_scores = score_block(asking, memory_key, 0.0, cross_allowed)
    local_total = log_totals(cross_scores)
    local_reading = weigh_values(
        jnp.exp(cross_scores - local_total).astype(jnp.bfloat16), memory_value
    ).reshape(questions, ANS, D)
    local_total = local_total[..., 0].transpose(0, 2, 1)
    total_high = local_total.astype(jnp.bfloat16)
    total_rest = local_total - total_high.astype(jnp.float32)
    total_low = total_rest.astype(jnp.bfloat16)
    total_rest = total_rest - total_low.astype(jnp.float32)
    spare = jnp.zeros((questions, ANS, 128 - 3 * H), jnp.bfloat16)
    packed = jnp.concatenate(
        [local_reading.astype(jnp.bfloat16), total_high, total_low, total_rest.astype(jnp.bfloat16), spare],
        axis=-1,
    )
    every = lax.all_gather(packed, "blk", axis=0)
    every_total = (
        every[..., D : D + H].astype(jnp.float32)
        + every[..., D + H : D + 2 * H].astype(jnp.float32)
        + every[..., D + 2 * H : D + 3 * H].astype(jnp.float32)
    )
    top = jnp.max(every_total, axis=0)
    cross_total = top + jnp.log(jnp.sum(jnp.exp(every_total - top), axis=0))
    share = jnp.exp(every_total - cross_total)
    reading = jnp.sum(
        every[..., :D].astype(jnp.float32).reshape(-1, questions, ANS, H, HD) * share[..., None],
        axis=0,
    )
    cross_total = cross_total.transpose(0, 2, 1)[..., None]
    reading_low = reading.reshape(questions, ANS, D).astype(jnp.bfloat16)
    answer_middle = answer_hidden + project(reading_low, cross_mix)
    normed_five, scale_five = rms_forward(answer_middle, decoder_ffn_gain.astype(jnp.float32))
    normed_five = normed_five.astype(jnp.bfloat16)
    answer_before = project(normed_five, decoder_ffn_in)
    answer_active = smooth(answer_before).astype(jnp.bfloat16)
    answer_output = answer_middle + project(answer_active, decoder_ffn_out)
    upstream = decoder_cotangent.astype(jnp.float32)
    delta_active, gradient_decoder_ffn_out = project_back(
        answer_active, upstream.astype(jnp.bfloat16), decoder_ffn_out
    )
    delta_before = gelu_delta(answer_before, delta_active).astype(jnp.bfloat16)
    delta_normed, gradient_decoder_ffn_in = project_back(normed_five, delta_before, decoder_ffn_in)
    delta_middle, gradient_decoder_ffn_gain = rms_backward(
        answer_middle, scale_five, decoder_ffn_gain.astype(jnp.float32), delta_normed
    )
    delta_middle = delta_middle + upstream
    delta_reading, gradient_cross_mix = project_back(
        reading_low, delta_middle.astype(jnp.bfloat16), cross_mix
    )
    delta_reading = delta_reading.astype(jnp.bfloat16).reshape(answer_shape)
    inner = jnp.einsum("blhe,blhe->bhl", delta_reading.astype(jnp.float32), reading)[..., None]
    cross_chances = jnp.exp(cross_scores - cross_total)
    local_deltas = score_deltas(memory_value, cross_chances, delta_reading, inner)
    delta_asking = query_from_scores(local_deltas, memory_key)
    delta_asking = lax.psum(delta_asking, "blk")
    delta_memory_key, delta_memory_value = key_value_deltas(
        local_deltas, cross_chances.astype(jnp.bfloat16), asking, delta_reading
    )
    delta_normed, gradient_cross_query = project_back(
        normed_four, delta_asking.astype(jnp.bfloat16).reshape(questions, ANS, D), cross_query
    )
    delta_hidden, gradient_decoder_cross_gain = rms_backward(
        answer_hidden, scale_four, decoder_cross_gain.astype(jnp.float32), delta_normed
    )
    delta_hidden = delta_hidden + delta_middle
    delta_attended, gradient_decoder_mix = project_back(
        answer_attended, delta_hidden.astype(jnp.bfloat16), decoder_mix
    )
    (
        delta_normed,
        gradient_decoder_query,
        gradient_decoder_key,
        gradient_decoder_value,
        gradient_decoder_bias_table,
    ) = attend_backward(
        normed_three,
        answer_heads,
        answer_total,
        answer_bias,
        answer_allowed,
        delta_attended.astype(jnp.bfloat16),
        decoder_query,
        decoder_key,
        decoder_value,
        answer_onehot,
    )
    delta_rows, gradient_decoder_self_gain = rms_backward(
        answer_rows, scale_three, decoder_self_gain.astype(jnp.float32), delta_normed
    )
    gradient_decoder_input = delta_rows + delta_hidden
    delta_final_key, gradient_cross_key = project_back(
        normed_final, delta_memory_key.astype(jnp.bfloat16).reshape(flat_rows), cross_key
    )
    delta_final_value, gradient_cross_value = project_back(
        normed_final, delta_memory_value.astype(jnp.bfloat16).reshape(flat_rows), cross_value
    )
    delta_output, gradient_final_gain = rms_backward(
        passage_output,
        scale_final,
        final_gain.astype(jnp.float32),
        delta_final_key + delta_final_value,
    )
    delta_output = delta_output + encoder_cotangent.reshape(flat_rows).astype(jnp.float32)
    delta_active, gradient_encoder_ffn_out = project_back(
        passage_active, delta_output.astype(jnp.bfloat16), encoder_ffn_out
    )
    delta_before = gelu_delta(passage_before, delta_active).astype(jnp.bfloat16)
    delta_normed, gradient_encoder_ffn_in = project_back(normed_two, delta_before, encoder_ffn_in)
    delta_hidden, gradient_encoder_ffn_gain = rms_backward(
        passage_hidden, scale_two, encoder_ffn_gain.astype(jnp.float32), delta_normed
    )
    delta_hidden = delta_hidden + delta_output
    delta_attended, gradient_encoder_mix = project_back(
        passage_attended, delta_hidden.astype(jnp.bfloat16), encoder_mix
    )
    (
        delta_normed,
        gradient_encoder_query,
        gradient_encoder_key,
        gradient_encoder_value,
        gradient_encoder_bias_table,
    ) = attend_backward(
        normed_one,
        passage_heads,
        passage_total,
        passage_bias,
        passage_allowed,
        delta_attended.astype(jnp.bfloat16),
        encoder_query,
        encoder_key,
        encoder_value,
        passage_onehot,
    )
    delta_rows, gradient_encoder_attn_gain = rms_backward(
        passage_rows, scale_one, encoder_attn_gain.astype(jnp.float32), delta_normed
    )
    gradient_encoder_input = (delta_rows + delta_hidden).reshape(encoder_input.shape)
    sizes = ring.sizes

    def columns(whole):
        return [whole[:, at : at + D] for at in range(0, whole.shape[1], D)]

    def reduced(units, order):
        names = ("c", "y", "z", "x")
        return ring.scatter_all(unit_parts(units, ring), names, order)

    def gathered(mine):
        return ring.gather(ring.gather(mine, "y"), "c")

    group_memory = reduced([gradient_cross_key, gradient_cross_value], "cyxz")
    group_in = reduced(columns(gradient_encoder_ffn_in), "cxyz")
    group_attend = reduced(
        [
            gradient_encoder_mix,
            gradient_encoder_query,
            gradient_encoder_key,
            gradient_encoder_value,
        ],
        "cyxz",
    )
    out_parts = gradient_encoder_ffn_out.astype(jnp.bfloat16).reshape(
        sizes["z"], sizes["x"], sizes["c"], sizes["y"], -1, D
    )
    group_out = ring.scatter_all(out_parts, ("z", "x", "c", "y"), "cyxz")
    share_of_answers = [
        gradient_cross_query,
        gradient_cross_mix,
        gradient_decoder_mix,
        gradient_decoder_query,
    ]
    answers = [
        unit_parts(columns(gradient_decoder_ffn_in), ring),
        unit_parts(share_of_answers, ring),
        unit_parts([gradient_decoder_key, gradient_decoder_value], ring),
        gradient_decoder_ffn_out.astype(jnp.bfloat16)
        .reshape(sizes["z"], sizes["x"], sizes["c"], sizes["y"], -1, D)
        .transpose(2, 3, 0, 1, 4, 5),
    ]
    core = ring.place("c")
    row = ring.place("y")
    answers = jnp.concatenate([item[core, row] for item in answers], axis=2)
    group_answers = ring.scatter_all(answers, ("z", "x"), "xz")
    mine = jnp.concatenate([group_memory, group_in, group_attend, group_out, group_answers], axis=0)
    whole = gathered(mine)
    whole = whole.reshape((ring.blk,) + whole.shape[2:])
    quarter = 4 * (D // ring.dp) // ring.blk
    half = quarter // 2
    sections = []
    at = 0
    for width in (half, quarter, quarter, quarter, quarter, quarter, half, quarter):
        sections.append(whole[:, at : at + width])
        at += width
    gradient_cross_key, gradient_cross_value = units_back(sections[0], 2)
    gradient_encoder_ffn_in = jnp.concatenate(list(units_back(sections[1], 4)), axis=1)
    (
        gradient_encoder_mix,
        gradient_encoder_query,
        gradient_encoder_key,
        gradient_encoder_value,
    ) = units_back(sections[2], 4)
    gradient_encoder_ffn_out = sections[3].astype(jnp.float32).reshape(-1, D)
    gradient_decoder_ffn_in = jnp.concatenate(list(units_back(sections[4], 4)), axis=1)
    (
        gradient_cross_query,
        gradient_cross_mix,
        gradient_decoder_mix,
        gradient_decoder_query,
    ) = units_back(sections[5], 4)
    gradient_decoder_key, gradient_decoder_value = units_back(sections[6], 2)
    gradient_decoder_ffn_out = sections[7].astype(jnp.float32).reshape(-1, D)

    once = lax.axis_index("blk") == 0
    small = [
        gradient_encoder_attn_gain,
        gradient_encoder_ffn_gain,
        gradient_final_gain,
        gradient_encoder_bias_table,
    ] + [
        jnp.where(once, item, 0.0)
        for item in (
            gradient_decoder_self_gain,
            gradient_decoder_cross_gain,
            gradient_decoder_ffn_gain,
            gradient_decoder_bias_table,
        )
    ]
    small = jnp.concatenate([item.reshape(ring.dp, -1) for item in small], axis=1)
    small = lax.dynamic_index_in_dim(ring.total(small), lax.axis_index("dp"), 0, keepdims=False)
    gain = D // ring.dp
    table = NB * H // ring.dp
    places = [0, gain, gain, gain, table, gain, gain, gain, table]
    cuts = [sum(places[: at + 1]) for at in range(len(places))]
    (
        gradient_encoder_attn_gain,
        gradient_encoder_ffn_gain,
        gradient_final_gain,
        gradient_encoder_bias_table,
        gradient_decoder_self_gain,
        gradient_decoder_cross_gain,
        gradient_decoder_ffn_gain,
        gradient_decoder_bias_table,
    ) = [small[low:high] for low, high in zip(cuts[:-1], cuts[1:])]
    gradient_encoder_bias_table = gradient_encoder_bias_table.reshape(-1, H)
    gradient_decoder_bias_table = gradient_decoder_bias_table.reshape(-1, H)
    return (
        passage_output.reshape(encoder_input.shape).astype(jnp.bfloat16),
        answer_output.astype(jnp.bfloat16),
        gradient_encoder_input,
        gradient_decoder_input,
        gradient_encoder_attn_gain,
        gradient_encoder_query,
        gradient_encoder_key,
        gradient_encoder_value,
        gradient_encoder_mix,
        gradient_encoder_bias_table,
        gradient_encoder_ffn_gain,
        gradient_encoder_ffn_in,
        gradient_encoder_ffn_out,
        gradient_final_gain,
        gradient_cross_key,
        gradient_cross_value,
        gradient_decoder_self_gain,
        gradient_decoder_query,
        gradient_decoder_key,
        gradient_decoder_value,
        gradient_decoder_mix,
        gradient_decoder_bias_table,
        gradient_decoder_cross_gain,
        gradient_cross_query,
        gradient_cross_mix,
        gradient_decoder_ffn_gain,
        gradient_decoder_ffn_in,
        gradient_decoder_ffn_out,
    )


def solution(mesh):
    ring = Ring(mesh.shape["dp"], mesh.shape["blk"])
    return jax.shard_map(
        functools.partial(on_device, ring),
        mesh=mesh,
        in_specs=(
            P("dp", "blk", None, None),
            P("dp", None, None),
            P("dp", "blk", None, None),
            P("dp", None, None),
            P("dp", "blk", None),
            P("dp", "blk", None),
            P("dp"),
            P(),
            P(),
            P(),
            P(),
            P(),
            P(),
            P(),
            P(),
            P(),
            P(),
            P(),
            P(),
            P(),
            P(),
            P(),
            P(),
            P(),
            P(),
            P(),
            P(),
            P(),
            P(),
            P(),
            P(),
        ),
        out_specs=(
            P("dp", "blk", None, None),
            P("dp", None, None),
            P("dp", "blk", None, None),
            P("dp", None, None),
            P("dp"),
            P("dp", None),
            P("dp", None),
            P("dp", None),
            P("dp", None),
            P("dp", None),
            P("dp"),
            P("dp", None),
            P("dp", None),
            P("dp"),
            P("dp", None),
            P("dp", None),
            P("dp"),
            P("dp", None),
            P("dp", None),
            P("dp", None),
            P("dp", None),
            P("dp", None),
            P("dp"),
            P("dp", None),
            P("dp", None),
            P("dp"),
            P("dp", None),
            P("dp", None),
        ),
        check_vma=False,
    )
```

```python
import functools
import math

import jax
import jax.numpy as jnp
from jax import lax
from jax.experimental import pallas as pl
from jax.experimental.pallas import tpu as pltpu
from jax.sharding import PartitionSpec as P

D = 768
H = 12
HD = 64
NB = 32
MAXD = 128
ROW = 256
ANS = 20


EPSILON = 1e-06
NEGATIVE = -1e30


SLOT = 32
ANY = pl.ANY
LIMIT = 60 << 20


def dot(left, right):
    return jnp.dot(left, right, preferred_element_type=jnp.float32)


def dot_rows(left, right):
    return lax.dot_general(
        left, right, (((1,), (1,)), ((), ())), preferred_element_type=jnp.float32
    )


def dot_tokens(left, right):
    return lax.dot_general(
        left, right, (((0,), (0,)), ((), ())), preferred_element_type=jnp.float32
    )


def low(values):
    return values.astype(jnp.bfloat16)


def wide(values):
    return values.astype(jnp.float32)


def rms_scale(values):
    return lax.rsqrt(jnp.mean(values * values, axis=-1, keepdims=True) + EPSILON)


def head_lanes(rows, width=D):
    return lax.broadcasted_iota(jnp.int32, (rows, width), 1) // HD


def spread(rows):
    lanes = head_lanes(rows.shape[0])
    values = wide(rows)
    return low(jnp.concatenate([jnp.where(lanes == h, values, 0.0) for h in range(H)], axis=0))


def fold(full):
    rows = full.shape[0] // H
    lanes = head_lanes(rows)
    total = jnp.zeros((rows, full.shape[1]), jnp.float32)
    for h in range(H):
        total = jnp.where(lanes == h, full[h * rows : (h + 1) * rows], total)
    return total


def gelu_pair(values):
    square = values * values
    inner = values * (0.7978845608 + (0.7978845608 * 0.044715) * square)
    half = 0.5 + 0.5 * jnp.tanh(inner)
    active = values * half
    slope = 0.7978845608 + (3.0 * 0.7978845608 * 0.044715) * square
    return (active, half + 2.0 * active * (1.0 - half) * slope)


class Copies:
    def __init__(self, semaphores):
        self.semaphores = semaphores
        self.count = 0
        self.open = []

    def start(self, source, target):
        copy = pltpu.make_async_copy(source, target, self.semaphores.at[self.count])
        self.count += 1
        copy.start()
        return copy

    def out(self, source, target):
        self.open.append(self.start(source, target))

    def finish(self):
        for copy in self.open:
            copy.wait()


def kernel_call(body, operands, spaces, outs, scratch, flops, bytes_accessed):
    return pl.pallas_call(
        body,
        in_specs=[pl.BlockSpec(memory_space=space) for space in spaces],
        out_specs=[pl.BlockSpec(memory_space=space) for _, _, space in outs],
        out_shape=[jax.ShapeDtypeStruct(shape, dtype) for shape, dtype, _ in outs],
        scratch_shapes=scratch,
        compiler_params=pltpu.CompilerParams(vmem_limit_bytes=LIMIT),
        cost_estimate=pl.CostEstimate(
            flops=flops, bytes_accessed=bytes_accessed, transcendentals=0
        ),
    )(*operands)


BF = jnp.bfloat16
F32 = jnp.float32
VM = pltpu.VMEM


def answer_start_kernel(
    length_ref, input_ref, bias_ref, self_gain_ref, cross_gain_ref,
    query_hbm, key_hbm, value_hbm, mix_hbm, ask_hbm,
    normed_ref, heads_ref, chance_ref, attended_ref, hidden_ref, crossed_ref, asking_ref,
    weights, arrivals,
):
    copies = Copies(arrivals)
    waits = [
        copies.start(source, weights.at[at])
        for at, source in enumerate((query_hbm, key_hbm, value_hbm, mix_hbm, ask_hbm))
    ]
    values = wide(input_ref[...])
    normed = low(values * rms_scale(values) * wide(self_gain_ref[...]))
    normed_ref[...] = normed
    for at in range(3):
        waits[at].wait()
        heads_ref[at] = low(dot(normed, weights[at]))
    questions = values.shape[0] // SLOT
    row = lax.broadcasted_iota(jnp.int32, (H * SLOT, SLOT), 0) % SLOT
    column = lax.broadcasted_iota(jnp.int32, (H * SLOT, SLOT), 1)
    for at in range(questions):
        rows = slice(at * SLOT, (at + 1) * SLOT)
        scores = dot_rows(spread(heads_ref[0, rows]), heads_ref[1, rows]) + bias_ref[...]
        allowed = (column <= row) & (column < length_ref[at])
        scores = jnp.where(allowed, scores, NEGATIVE)
        powers = jnp.exp(scores - jnp.max(scores, axis=1, keepdims=True))
        chances = low(powers / jnp.sum(powers, axis=1, keepdims=True))
        chance_ref[at] = chances
        attended_ref[rows] = low(fold(dot(chances, heads_ref[2, rows])))
    waits[3].wait()
    hidden = values + dot(attended_ref[...], weights[3])
    hidden_ref[...] = hidden
    crossed = low(hidden * rms_scale(hidden) * wide(cross_gain_ref[...]))
    crossed_ref[...] = crossed
    waits[4].wait()
    asking_ref[...] = low(dot(crossed, weights[4]))


def answer_start(length, rows, bias, self_gain, cross_gain, weights):
    count = rows.shape[0]
    questions = count // SLOT
    return kernel_call(
        answer_start_kernel,
        (length, rows, bias, self_gain, cross_gain) + tuple(weights),
        [pltpu.SMEM] + [VM] * 4 + [ANY] * 5,
        [
            ((count, D), BF, VM),
            ((3, count, D), BF, VM),
            ((questions, H * SLOT, SLOT), BF, VM),
            ((count, D), BF, VM),
            ((count, D), F32, VM),
            ((count, D), BF, VM),
            ((count, D), BF, VM),
        ],
        [VM((5, D, D), BF), pltpu.SemaphoreType.DMA((5,))],
        10 * count * D * D,
        10 * D * D,
    )


def passage_kernel(
    input_ref, segment_row_ref, segment_column_ref, slope_ref,
    attn_gain_ref, ffn_gain_ref, final_gain_ref, asking_ref,
    query_hbm, key_hbm, value_hbm, mix_hbm, in_hbm, out_hbm, cross_key_hbm, cross_value_hbm,
    normed_hbm, heads_hbm, chance_hbm, attended_hbm, hidden_hbm, second_hbm,
    active_hbm, bend_hbm, encoded_hbm, result_hbm, final_hbm, memory_hbm, score_hbm, packed_ref,
    square, wide_in, wide_out, normed, heads, chance, attended, hidden, second,
    active, bend, encoded, result, final, memory, score, masks, arrivals,
):
    copies = Copies(arrivals)
    square_hbm = (query_hbm, key_hbm, value_hbm, mix_hbm, cross_key_hbm, cross_value_hbm)
    waits = [copies.start(source, square.at[at]) for at, source in enumerate(square_hbm[:4])]
    wait_in = copies.start(in_hbm, wide_in)
    wait_out = copies.start(out_hbm, wide_out)
    waits += [copies.start(square_hbm[at], square.at[at]) for at in (4, 5)]
    rows = input_ref.shape[0]
    blocks = rows // ROW

    values = wide(input_ref[...])
    normed[...] = low(values * rms_scale(values) * wide(attn_gain_ref[...]))
    copies.out(normed, normed_hbm)
    for at in range(3):
        waits[at].wait()
        heads[at] = low(dot(normed[...], square[at]))
    copies.out(heads, heads_hbm)

    place_row = lax.broadcasted_iota(jnp.int32, (ROW, ROW), 0)
    place_column = lax.broadcasted_iota(jnp.int32, (ROW, ROW), 1)
    for block in range(blocks):
        own = segment_column_ref[:, block : block + 1] == segment_row_ref[block : block + 1, :]
        masks[block] = jnp.where(own | (place_row == place_column), 0.0, NEGATIVE)

    second_half = lax.broadcasted_iota(jnp.int32, (ROW, 2 * HD), 1) >= HD

    @pl.loop(0, H // 2)
    def _(pair):
        lanes = pl.ds(pl.multiple_of(pair * 2 * HD, 2 * HD), 2 * HD)
        sums = []
        for which in range(2):
            head = pair * 2 + which
            slopes = jnp.broadcast_to(slope_ref[pl.ds(head, 1), :], (ROW, 2 * ROW))
            bias = pltpu.roll(slopes, ROW, 1, stride=1, stride_axis=0)[:, :ROW]
            for block in range(blocks):
                span = slice(block * ROW, (block + 1) * ROW)
                asked = heads[0, span, lanes]
                own = jnp.where(second_half == (which == 1), asked, jnp.zeros_like(asked))
                scores = dot_rows(own, heads[1, span, lanes]) + (bias + masks[block])
                powers = jnp.exp(scores - jnp.max(scores, axis=1, keepdims=True))
                chances = low(powers * (1.0 / jnp.sum(powers, axis=1, keepdims=True)))
                chance[head, block] = chances
                taken = dot(chances, heads[2, span, lanes])
                if which == 0:
                    sums.append(taken)
                else:
                    attended[span, lanes] = low(jnp.where(second_half, taken, sums[block]))

    copies.out(chance, chance_hbm)
    copies.out(attended, attended_hbm)
    waits[3].wait()
    hidden[...] = wide(input_ref[...]) + dot(attended[...], square[3])
    copies.out(hidden, hidden_hbm)
    values = hidden[...]
    second[...] = low(values * rms_scale(values) * wide(ffn_gain_ref[...]))
    copies.out(second, second_hbm)
    wait_in.wait()

    @pl.loop(0, in_hbm.shape[1] // D)
    def _(at):
        lanes = pl.ds(pl.multiple_of(at * D, D), D)
        up, slope = gelu_pair(dot(second[...], wide_in[:, lanes]))
        active[:, lanes] = low(up)
        bend[:, lanes] = low(slope)

    copies.out(active, active_hbm)
    copies.out(bend, bend_hbm)
    wait_out.wait()

    @pl.loop(0, D // ROW)
    def _(at):
        lanes = pl.ds(pl.multiple_of(at * ROW, ROW), ROW)
        encoded[:, lanes] = hidden[:, lanes] + dot(active[...], wide_out[:, lanes])

    copies.out(encoded, encoded_hbm)
    values = encoded[...]
    result[...] = low(values)
    copies.out(result, result_hbm)
    final[...] = low(values * rms_scale(values) * wide(final_gain_ref[...]))
    copies.out(final, final_hbm)
    for at in range(2):
        waits[4 + at].wait()
        memory[at] = low(dot(final[...], square[4 + at]))
    copies.out(memory, memory_hbm)

    lane = lax.broadcasted_iota(jnp.int32, (SLOT, 128), 1)
    for block in range(blocks):
        span = slice(block * ROW, (block + 1) * ROW)
        slots = slice(block * SLOT, (block + 1) * SLOT)
        scores = dot_rows(spread(asking_ref[slots]), memory[0, span])
        visible = segment_row_ref[block : block + 1, :] >= 0
        scores = jnp.where(visible, scores, NEGATIVE)
        score[block] = scores
        top = jnp.max(scores, axis=1, keepdims=True)
        powers = jnp.exp(scores - top)
        sums = jnp.sum(powers, axis=1, keepdims=True)
        reading = fold(dot(low(powers * (1.0 / sums)), memory[1, span]))
        packed_ref[slots, :D] = low(reading)
        total = top + jnp.log(sums)
        extra = jnp.zeros((SLOT, 128), F32)
        for h in range(H):
            rest = total[h * SLOT : (h + 1) * SLOT]
            for piece in range(3):
                part = wide(low(rest))
                extra = jnp.where(lane == piece * H + h, part, extra)
                rest = rest - part
        packed_ref[slots, D:] = low(extra)
    copies.out(score, score_hbm)
    copies.finish()


def passage(rows, segment_row, segment_column, slopes, gains, asking, weights):
    count = rows.shape[0]
    blocks = count // ROW
    wide_size = weights[4].shape[1]
    whole = [
        ((count, D), BF),
        ((3, count, D), BF),
        ((H, blocks, ROW, ROW), BF),
        ((count, D), BF),
        ((count, D), F32),
        ((count, D), BF),
        ((count, wide_size), BF),
        ((count, wide_size), BF),
        ((count, D), F32),
        ((count, D), BF),
        ((count, D), BF),
        ((2, count, D), BF),
        ((blocks, H * SLOT, ROW), F32),
    ]
    return kernel_call(
        passage_kernel,
        (rows, segment_row, segment_column, slopes) + tuple(gains) + (asking,) + tuple(weights),
        [VM] * 8 + [ANY] * 8,
        [(shape, dtype, ANY) for shape, dtype in whole]
        + [((blocks * SLOT, D + 128), BF, VM)],
        [VM((6, D, D), BF), VM((D, wide_size), BF), VM((wide_size, D), BF)]
        + [VM(shape, dtype) for shape, dtype in whole]
        + [VM((blocks, ROW, ROW), F32), pltpu.SemaphoreType.DMA((32,))],
        28 * count * D * D,
        80 * D * D,
    )


def rms_back(values, gain, upstream):
    scale = rms_scale(values)
    scaled = upstream * gain
    inner = jnp.mean(scaled * values, axis=-1, keepdims=True)
    delta = scaled * scale - values * (scale * scale * scale) * inner
    return (delta, jnp.sum(upstream * values * scale, axis=0, keepdims=True))


def exact_dot(left, right, rows=False):
    return lax.dot_general(
        left,
        right,
        (((1,), (1 if rows else 0,)), ((), ())),
        precision=lax.Precision.HIGHEST,
        preferred_element_type=jnp.float32,
    )


def head_columns(values):
    return jnp.concatenate([values[:, h : h + 1] for h in range(H)], axis=0)


def answer_middle_kernel(
    every_ref, asking_ref, hidden_ref, upstream_ref, gain_ref, score_hbm, memory_hbm,
    mix_hbm, in_hbm, out_hbm,
    result_ref, low_ref, wide_ref, middle_ref, gain_delta_ref, memory_delta_hbm, asking_delta_ref,
    score, memory, memory_delta, mix, wide_in, wide_out, arrivals,
):
    copies = Copies(arrivals)
    wait_mix = copies.start(mix_hbm, mix)
    wait_in = copies.start(in_hbm, wide_in)
    wait_out = copies.start(out_hbm, wide_out)
    wait_score = copies.start(score_hbm, score)
    wait_memory = copies.start(memory_hbm, memory)
    count = asking_ref.shape[0]

    from_piece = lax.broadcasted_iota(jnp.int32, (128, 128), 0)
    to_head = lax.broadcasted_iota(jnp.int32, (128, 128), 1)
    same = (from_piece % H == to_head) & (from_piece < 3 * H)
    pieces = low(jnp.where(same, 1.0, 0.0))
    lane_head = lax.broadcasted_iota(jnp.int32, (128, D), 1) // HD
    widen = jnp.where(lane_head == lax.broadcasted_iota(jnp.int32, (128, D), 0), 1.0, 0.0)

    totals = [dot(every_ref[at, :, D:], pieces) for at in range(every_ref.shape[0])]
    top = functools.reduce(jnp.maximum, totals)
    powers = [jnp.exp(total - top) for total in totals]
    sums = functools.reduce(jnp.add, powers)
    reading = jnp.zeros((count, D), F32)
    for at, power in enumerate(powers):
        reading += wide(every_ref[at, :, :D]) * exact_dot(power / sums, widen)
    whole_total = top + jnp.log(sums)
    reading_low = low(reading)
    low_ref[0] = reading_low
    wait_mix.wait()
    middle = hidden_ref[...] + dot(reading_low, mix[...])
    gain = wide(gain_ref[...])
    fifth = low(middle * rms_scale(middle) * gain)
    low_ref[1] = fifth
    upstream = upstream_ref[...]
    wait_in.wait()
    wait_out.wait()

    @pl.loop(0, wide_in.shape[1] // D)
    def _(at):
        lanes = pl.ds(pl.multiple_of(at * D, D), D)
        active, slope = gelu_pair(dot(fifth, wide_in[:, lanes]))
        wide_ref[0, :, lanes] = low(active)
        wide_ref[1, :, lanes] = low(dot_rows(upstream, wide_out[lanes, :]) * slope)

    delta, gain_delta = rms_back(middle, gain, dot_rows(wide_ref[1], wide_in[...]))
    gain_delta_ref[...] = gain_delta
    delta += wide(upstream)
    middle_ref[...] = delta
    delta_low = low(delta)
    low_ref[2] = delta_low
    taken = low(dot_rows(delta_low, mix[...]))
    inner = exact_dot(wide(taken) * reading, widen, rows=True)
    wait_score.wait()
    wait_memory.wait()
    for block in range(count // SLOT):
        slots = slice(block * SLOT, (block + 1) * SLOT)
        span = slice(block * ROW, (block + 1) * ROW)
        chances = jnp.exp(score[block] - head_columns(whole_total[slots]))
        asked = spread(asking_ref[slots])
        upward = spread(taken[slots])
        delta_chances = dot_rows(upward, memory[1, span])
        deltas = low(chances * (delta_chances - head_columns(inner[slots])))
        memory_delta[0, span] = low(dot_tokens(deltas, asked))
        memory_delta[1, span] = low(dot_tokens(low(chances), upward))
        asking_delta_ref[slots] = low(fold(dot(deltas, memory[0, span])))
    copies.out(memory_delta, memory_delta_hbm)
    answer = middle
    for at in range(0, wide_out.shape[0], D):
        answer += dot(wide_ref[0, :, at : at + D], wide_out[at : at + D, :])
    result_ref[...] = low(answer)
    copies.finish()


def answer_middle(every, asking, hidden, upstream, gain, score, memory, weights):
    count = asking.shape[0]
    wide_size = weights[1].shape[1]
    return kernel_call(
        answer_middle_kernel,
        (every, asking, hidden, upstream, gain, score, memory) + tuple(weights),
        [VM] * 5 + [ANY] * 5,
        [
            ((count, D), BF, VM),
            ((3, count, D), BF, VM),
            ((2, count, wide_size), BF, VM),
            ((count, D), F32, VM),
            ((1, D), F32, VM),
            (memory.shape, BF, ANY),
            ((count, D), BF, VM),
        ],
        [
            VM(score.shape, F32),
            VM(memory.shape, BF),
            VM(memory.shape, BF),
            VM((D, D), BF),
            VM((D, wide_size), BF),
            VM((wide_size, D), BF),
            pltpu.SemaphoreType.DMA((8,)),
        ],
        40 * count * D * D,
        24 * D * D,
    )


def memory_back_kernel(
    place_ref, gain_ref, delta_hbm, final_hbm, encoded_hbm, upstream_hbm, key_hbm, value_hbm,
    send_hbm, keep_hbm, output_hbm, output_low_hbm, gain_delta_ref,
    delta, final, encoded, upstream, weights, send, keep, output, output_low, arrivals,
):
    copies = Copies(arrivals)
    wait_delta = copies.start(delta_hbm, delta)
    wait_final = copies.start(final_hbm, final)
    waits = [copies.start(key_hbm, weights.at[0]), copies.start(value_hbm, weights.at[1])]
    waits += [copies.start(encoded_hbm, encoded), copies.start(upstream_hbm, upstream)]
    core = place_ref[0]
    wait_delta.wait()
    wait_final.wait()
    send[...] = low(dot_tokens(final[...], delta[1 - core]))
    copies.out(send, send_hbm)
    keep[...] = low(dot_tokens(final[...], delta[core]))
    copies.out(keep, keep_hbm)
    for wait in waits:
        wait.wait()
    upward = dot_rows(delta[0], weights[0]) + dot_rows(delta[1], weights[1])
    back, gain_delta = rms_back(encoded[...], wide(gain_ref[...]), upward)
    gain_delta_ref[...] = gain_delta
    back += wide(upstream[...])
    output[...] = back
    output_low[...] = low(back)
    copies.out(output, output_hbm)
    copies.out(output_low, output_low_hbm)
    copies.finish()


def memory_back(place, gain, delta, final, encoded, upstream, weights):
    count = final.shape[0]
    return kernel_call(
        memory_back_kernel,
        (place, gain, delta, final, encoded, upstream) + tuple(weights),
        [pltpu.SMEM, VM] + [ANY] * 6,
        [
            ((D, D), BF, ANY),
            ((D, D), BF, ANY),
            ((count, D), F32, ANY),
            ((count, D), BF, ANY),
            ((1, D), F32, VM),
        ],
        [
            VM((2, count, D), BF), VM((count, D), BF), VM((count, D), F32), VM((count, D), BF),
            VM((2, D, D), BF), VM((D, D), BF), VM((D, D), BF), VM((count, D), F32),
            VM((count, D), BF), pltpu.SemaphoreType.DMA((12,)),
        ],
        8 * count * D * D,
        20 * D * D,
    )


def wide_out_back_kernel(
    place_ref, output_hbm, weight_hbm, active_hbm, bend_hbm,
    send_hbm, keep_hbm, before_hbm,
    output, weight, active, bend, send, keep, before, arrivals,
):
    copies = Copies(arrivals)
    waits = [
        copies.start(source, target)
        for source, target in (
            (output_hbm, output), (active_hbm, active), (weight_hbm, weight), (bend_hbm, bend)
        )
    ]
    core = place_ref[0]
    half = D // 2
    other = pl.ds(pl.multiple_of((1 - core) * half, half), half)
    own = pl.ds(pl.multiple_of(core * half, half), half)
    steps = weight.shape[0] // D
    waits[0].wait()
    waits[1].wait()

    @pl.loop(0, steps)
    def _(at):
        part = pl.ds(pl.multiple_of(at * D, D), D)
        send[part, :] = low(dot_tokens(active[:, part], output[:, other]))

    copies.out(send, send_hbm)

    @pl.loop(0, steps)
    def _(at):
        part = pl.ds(pl.multiple_of(at * D, D), D)
        keep[part, :] = low(dot_tokens(active[:, part], output[:, own]))

    copies.out(keep, keep_hbm)
    waits[2].wait()
    waits[3].wait()

    @pl.loop(0, steps)
    def _(at):
        part = pl.ds(pl.multiple_of(at * D, D), D)
        up = dot_rows(output[...], weight[part, :])
        before[:, part] = low(up * wide(bend[:, part]))

    copies.out(before, before_hbm)
    copies.finish()


def wide_out_back(place, output, weight, active, bend):
    count = output.shape[0]
    wide_size = weight.shape[0]
    return kernel_call(
        wide_out_back_kernel,
        (place, output, weight, active, bend),
        [pltpu.SMEM] + [ANY] * 4,
        [
            ((wide_size, D // 2), BF, ANY),
            ((wide_size, D // 2), BF, ANY),
            ((count, wide_size), BF, ANY),
        ],
        [
            VM((count, D), BF), VM((wide_size, D), BF), VM((count, wide_size), BF),
            VM((count, wide_size), BF), VM((wide_size, D // 2), BF), VM((wide_size, D // 2), BF),
            VM((count, wide_size), BF), pltpu.SemaphoreType.DMA((12,)),
        ],
        16 * count * D * D,
        40 * D * D,
    )


def wide_in_back_kernel(
    place_ref, gain_ref, before_hbm, second_hbm, weight_hbm, hidden_hbm, output_hbm, mix_hbm,
    send_hbm, keep_hbm, hidden_delta_hbm, hidden_low_hbm, attended_delta_hbm, gain_delta_ref,
    before, second, weight, hidden, output, mix, send, keep, upward, hidden_delta, hidden_low,
    attended_delta, arrivals,
):
    copies = Copies(arrivals)
    waits = [
        copies.start(source, target)
        for source, target in (
            (before_hbm, before), (second_hbm, second), (weight_hbm, weight),
            (hidden_hbm, hidden), (output_hbm, output), (mix_hbm, mix),
        )
    ]
    core = place_ref[0]
    steps = weight.shape[1] // D // 2
    waits[0].wait()
    waits[1].wait()

    @pl.loop(0, steps)
    def _(at):
        part = pl.ds(pl.multiple_of(((1 - core) * steps + at) * D, D), D)
        send[at] = low(dot_tokens(second[...], before[:, part]))

    copies.out(send, send_hbm)

    @pl.loop(0, steps)
    def _(at):
        part = pl.ds(pl.multiple_of((core * steps + at) * D, D), D)
        keep[at] = low(dot_tokens(second[...], before[:, part]))

    copies.out(keep, keep_hbm)
    waits[2].wait()

    @pl.loop(0, D // ROW)
    def _(at):
        part = pl.ds(pl.multiple_of(at * ROW, ROW), ROW)
        upward[:, part] = dot_rows(before[...], weight[part, :])

    for wait in waits[3:]:
        wait.wait()
    back, gain_delta = rms_back(hidden[...], wide(gain_ref[...]), upward[...])
    gain_delta_ref[...] = gain_delta
    back += output[...]
    hidden_delta[...] = back
    copies.out(hidden_delta, hidden_delta_hbm)
    hidden_low[...] = low(back)
    copies.out(hidden_low, hidden_low_hbm)
    attended_delta[...] = low(dot_rows(hidden_low[...], mix[...]))
    copies.out(attended_delta, attended_delta_hbm)
    copies.finish()


def wide_in_back(place, gain, before, second, weight, hidden, output, mix):
    count = second.shape[0]
    wide_size = weight.shape[1]
    steps = wide_size // D // 2
    return kernel_call(
        wide_in_back_kernel,
        (place, gain, before, second, weight, hidden, output, mix),
        [pltpu.SMEM, VM] + [ANY] * 6,
        [
            ((steps, D, D), BF, ANY),
            ((steps, D, D), BF, ANY),
            ((count, D), F32, ANY),
            ((count, D), BF, ANY),
            ((count, D), BF, ANY),
            ((1, D), F32, VM),
        ],
        [
            VM((count, wide_size), BF), VM((count, D), BF), VM((D, wide_size), BF),
            VM((count, D), F32), VM((count, D), F32), VM((D, D), BF),
            VM((steps, D, D), BF), VM((steps, D, D), BF), VM((count, D), F32),
            VM((count, D), F32), VM((count, D), BF), VM((count, D), BF),
            pltpu.SemaphoreType.DMA((16,)),
        ],
        18 * count * D * D,
        40 * D * D,
    )


def attend_back_kernel(
    heads_hbm, chance_hbm, upstream_hbm,
    delta_hbm, slope_delta_ref,
    heads, chance, upstream, delta, gathered, arrivals,
):
    copies = Copies(arrivals)
    waits = [
        copies.start(source, target)
        for source, target in ((heads_hbm, heads), (upstream_hbm, upstream), (chance_hbm, chance))
    ]
    for wait in waits:
        wait.wait()
    blocks = upstream.shape[0] // ROW
    second_half = lax.broadcasted_iota(jnp.int32, (ROW, 2 * HD), 1) >= HD
    place_row = lax.broadcasted_iota(jnp.int32, (ROW, ROW), 0)
    place_column = lax.broadcasted_iota(jnp.int32, (ROW, ROW), 1)
    mirror = low(jnp.where(place_row + place_column == ROW - 1, 1.0, 0.0))

    @pl.loop(0, H // 2)
    def _(pair):
        lanes = pl.ds(pl.multiple_of(pair * 2 * HD, 2 * HD), 2 * HD)
        kept = []
        for which in range(2):
            head = pair * 2 + which
            for block in range(blocks):
                span = slice(block * ROW, (block + 1) * ROW)
                query, key, value = (heads[at, span, lanes] for at in range(3))
                upward = upstream[span, lanes]
                own = jnp.where(second_half == (which == 1), upward, jnp.zeros_like(upward))
                chances = chance[head, block]
                weight = wide(chances)
                delta_chances = dot_rows(own, value)
                inner = jnp.sum(delta_chances * weight, axis=1, keepdims=True)
                deltas = low(weight * (delta_chances - inner))
                turned = dot(mirror, deltas)
                if block == 0:
                    gathered[...] = turned
                else:
                    gathered[...] += turned
                news = [dot(deltas, key), dot_tokens(deltas, query), dot_tokens(chances, upward)]
                if which == 0:
                    kept.append(news)
                else:
                    for at in range(3):
                        both = jnp.where(second_half, news[at], kept[block][at])
                        delta[at, span, lanes] = low(both)
            padded = jnp.concatenate([gathered[...], jnp.zeros((ROW, ROW), F32)], axis=1)
            rolled = pltpu.roll(padded, 1, 1, stride=1, stride_axis=0)
            slope_delta_ref[pl.ds(head, 1), :] = jnp.sum(rolled, axis=0, keepdims=True)

    copies.out(delta, delta_hbm)
    copies.finish()


def attend_back(heads, chance, upstream):
    count = upstream.shape[0]
    return kernel_call(
        attend_back_kernel,
        (heads, chance, upstream),
        [ANY] * 3,
        [(heads.shape, BF, ANY), ((H, 2 * ROW), F32, VM)],
        [
            VM(heads.shape, BF), VM(chance.shape, BF), VM(upstream.shape, BF),
            VM(heads.shape, BF), VM((ROW, ROW), F32), pltpu.SemaphoreType.DMA((4,)),
        ],
        20 * count * ROW * D,
        20 * D * D,
    )


def heads_weight_kernel(
    place_ref, normed_hbm, attended_hbm, delta_hbm, hidden_low_hbm,
    part_hbm, inputs, deltas, part, arrivals,
):
    copies = Copies(arrivals)
    waits = [
        copies.start(normed_hbm, inputs.at[0]),
        copies.start(attended_hbm, inputs.at[1]),
        copies.start(delta_hbm, deltas.at[pl.ds(0, 3)]),
        copies.start(hidden_low_hbm, deltas.at[3]),
    ]
    for wait in waits:
        wait.wait()
    core = place_ref[0]

    @pl.loop(0, 2)
    def _(at):
        unit = core * 2 + at
        part[at] = low(dot_tokens(inputs[unit // 3], deltas[unit]))

    copies.out(part, part_hbm)
    copies.finish()


def heads_weight(core, normed, attended, delta, hidden_low):
    count = normed.shape[0]
    return kernel_call(
        heads_weight_kernel,
        (core, normed, attended, delta, hidden_low),
        [pltpu.SMEM] + [ANY] * 4,
        [((2, D, D), BF, ANY)],
        [
            VM((2, count, D), BF), VM((4, count, D), BF), VM((2, D, D), BF),
            pltpu.SemaphoreType.DMA((8,)),
        ],
        4 * count * D * D,
        16 * D * D,
    )[0]


def passage_end_kernel(
    gain_ref, input_hbm, delta_hbm, hidden_delta_hbm, query_hbm, key_hbm, value_hbm,
    gradient_hbm, gain_delta_ref,
    values, delta, hidden_delta, weights, gradient, arrivals,
):
    copies = Copies(arrivals)
    wait_delta = copies.start(delta_hbm, delta)
    waits = [
        copies.start(source, weights.at[at])
        for at, source in enumerate((query_hbm, key_hbm, value_hbm))
    ]
    wait_input = copies.start(input_hbm, values)
    wait_hidden = copies.start(hidden_delta_hbm, hidden_delta)
    wait_delta.wait()
    for wait in waits:
        wait.wait()
    upward = dot_rows(delta[0], weights[0])
    upward += dot_rows(delta[1], weights[1])
    upward += dot_rows(delta[2], weights[2])
    wait_input.wait()
    wait_hidden.wait()
    back, gain_delta = rms_back(wide(values[...]), wide(gain_ref[...]), upward)
    gain_delta_ref[...] = gain_delta
    gradient[...] = back + hidden_delta[...]
    copies.out(gradient, gradient_hbm)
    copies.finish()


def passage_end(gain, rows, delta, hidden_delta, weights):
    count = rows.shape[0]
    return kernel_call(
        passage_end_kernel,
        (gain, rows, delta, hidden_delta) + tuple(weights),
        [VM] + [ANY] * 6,
        [((count, D), F32, ANY), ((1, D), F32, VM)],
        [
            VM((count, D), BF), VM((3, count, D), BF), VM((count, D), F32), VM((3, D, D), BF),
            VM((count, D), F32), pltpu.SemaphoreType.DMA((8,)),
        ],
        6 * count * D * D,
        30 * D * D,
    )


def answer_end_kernel(
    asking_delta_ref, middle_ref, hidden_ref, input_ref, cross_gain_ref, self_gain_ref,
    heads_ref, chance_ref, ask_hbm, mix_hbm, query_hbm, key_hbm, value_hbm,
    gradient_ref, hidden_low_ref, delta_ref, cross_delta_ref, self_delta_ref, score_delta_ref,
    weights, arrivals,
):
    copies = Copies(arrivals)
    waits = [
        copies.start(source, weights.at[at])
        for at, source in enumerate((ask_hbm, mix_hbm, query_hbm, key_hbm, value_hbm))
    ]
    waits[0].wait()
    upward = dot_rows(asking_delta_ref[...], weights[0])
    back, gain_delta = rms_back(hidden_ref[...], wide(cross_gain_ref[...]), upward)
    cross_delta_ref[...] = gain_delta
    back += middle_ref[...]
    hidden_low = low(back)
    hidden_low_ref[...] = hidden_low
    waits[1].wait()
    upward = low(dot_rows(hidden_low, weights[1]))
    for block in range(upward.shape[0] // SLOT):
        slots = slice(block * SLOT, (block + 1) * SLOT)
        chances = chance_ref[block]
        taken = spread(upward[slots])
        delta_chances = dot_rows(taken, heads_ref[2, slots])
        inner = jnp.sum(delta_chances * wide(chances), axis=1, keepdims=True)
        deltas = low(wide(chances) * (delta_chances - inner))
        if block == 0:
            score_delta_ref[...] = wide(deltas)
        else:
            score_delta_ref[...] += wide(deltas)
        delta_ref[0, slots] = low(fold(dot(deltas, heads_ref[1, slots])))
        delta_ref[1, slots] = low(dot_tokens(deltas, spread(heads_ref[0, slots])))
        delta_ref[2, slots] = low(dot_tokens(chances, taken))
    for wait in waits[2:]:
        wait.wait()
    upward = dot_rows(delta_ref[0], weights[2])
    upward += dot_rows(delta_ref[1], weights[3])
    upward += dot_rows(delta_ref[2], weights[4])
    start_delta, gain_delta = rms_back(wide(input_ref[...]), wide(self_gain_ref[...]), upward)
    self_delta_ref[...] = gain_delta
    gradient_ref[...] = start_delta + back


def answer_end(asking_delta, middle, hidden, rows, cross_gain, self_gain, heads, chance, weights):
    count = rows.shape[0]
    return kernel_call(
        answer_end_kernel,
        (asking_delta, middle, hidden, rows, cross_gain, self_gain, heads, chance)
        + tuple(weights),
        [VM] * 8 + [ANY] * 5,
        [
            ((count, D), F32, VM),
            ((count, D), BF, VM),
            ((3, count, D), BF, VM),
            ((1, D), F32, VM),
            ((1, D), F32, VM),
            ((H * SLOT, SLOT), F32, VM),
        ],
        [VM((5, D, D), BF), pltpu.SemaphoreType.DMA((5,))],
        12 * count * D * D,
        12 * D * D,
    )


def answer_wide_weight_kernel(place_ref, fifth_ref, wide_ref, upstream_ref, part_ref, full):
    core = place_ref[0]
    row = place_ref[1]
    shards, width = part_ref.shape[0], part_ref.shape[1] // 2
    half = D // 2
    part = pl.ds(pl.multiple_of((core * 2 + row) * D, D), D)
    inner = low(dot_tokens(fifth_ref[...], wide_ref[1, :, part]))
    for shard in range(shards):
        part_ref[shard, :width] = inner[shard * width : (shard + 1) * width]
    columns = pl.ds(pl.multiple_of(core * half, half), half)
    upstream = upstream_ref[:, columns]

    @pl.loop(0, wide_ref.shape[2] // D)
    def _(at):
        span = pl.ds(pl.multiple_of(at * D, D), D)
        full[span, :] = low(dot_tokens(wide_ref[0, :, span], upstream))

    for shard in range(shards):
        for side in range(2):
            begin = shard * 4 * width + row * 2 * width + side * width
            rows = pl.ds(pl.multiple_of(begin, 16), width)
            part_ref[shard, width:, side * half : (side + 1) * half] = full[rows, :]


def answer_wide_weight(place, fifth, wide_pair, upstream, shards):
    wide_size = wide_pair.shape[2]
    return kernel_call(
        answer_wide_weight_kernel,
        (place, fifth, wide_pair, upstream),
        [pltpu.SMEM] + [VM] * 3,
        [((shards, 2 * D // shards, D), BF, VM)],
        [VM((wide_size, D // 2), BF)],
        6 * fifth.shape[0] * D * D,
        8 * D * D,
    )[0]


def answer_square_weight_kernel(
    place_ref, crossed_ref, low_ref, attended_ref, normed_ref, asking_delta_ref, hidden_low_ref,
    delta_ref, part_ref, inputs, deltas, full,
):
    core = place_ref[0]
    row = place_ref[1]
    shards, width = part_ref.shape[0], part_ref.shape[1] * 2 // 3
    inputs[0] = crossed_ref[...]
    inputs[1] = low_ref[0]
    inputs[2] = attended_ref[...]
    inputs[3] = normed_ref[...]
    deltas[0] = asking_delta_ref[...]
    deltas[1] = low_ref[2]
    deltas[2] = hidden_low_ref[...]
    deltas[3] = delta_ref[0]
    unit = core * 2 + row
    first = low(dot_tokens(inputs[unit], deltas[unit]))
    full[...] = low(dot_tokens(normed_ref[...], delta_ref[1 + core]))
    for shard in range(shards):
        part_ref[shard, :width] = first[shard * width : (shard + 1) * width]
        rows = pl.ds(pl.multiple_of(shard * width + row * (width // 2), 16), width // 2)
        part_ref[shard, width:] = full[rows, :]


def answer_square_weight(
    place, crossed, lows, attended, normed, asking_delta, hidden_low, delta, shards
):
    count = crossed.shape[0]
    return kernel_call(
        answer_square_weight_kernel,
        (place, crossed, lows, attended, normed, asking_delta, hidden_low, delta),
        [pltpu.SMEM] + [VM] * 7,
        [((shards, 3 * D // shards // 2, D), BF, VM)],
        [VM((4, count, D), BF), VM((4, count, D), BF), VM((D, D), BF)],
        4 * count * D * D,
        6 * D * D,
    )[0]


class Ring:
    def __init__(self, mesh):
        self.dp = mesh.shape["dp"]
        self.blk = mesh.shape["blk"]
        depth = 4 if self.dp % 4 == 0 else self.dp
        self.sizes = {"z": depth, "x": self.dp // depth, "y": self.blk // 2, "c": 2}
        self.cut = self.blk == 4 and self.dp == 8

    def place(self, name):
        across = lax.axis_index("dp")
        along = lax.axis_index("blk")
        return {
            "z": across // self.sizes["x"],
            "x": across % self.sizes["x"],
            "y": along // self.sizes["c"],
            "c": along % self.sizes["c"],
        }[name]

    def shift(self, values, *names):
        sizes = self.sizes
        moves = []
        for z in range(sizes["z"]):
            for x in range(sizes["x"]):
                for y in range(sizes["y"]):
                    for c in range(sizes["c"]):
                        here = {"z": z, "x": x, "y": y, "c": c}
                        there = dict(here)
                        for name in names:
                            there[name] = (there[name] + 1) % sizes[name]
                        moves.append((self.number(here), self.number(there)))
        return lax.ppermute(values, ("dp", "blk"), moves)

    def number(self, at):
        sizes = self.sizes
        across = at["z"] * sizes["x"] + at["x"]
        along = at["y"] * sizes["c"] + at["c"]
        return across * self.blk + along

    def scatter(self, terms, names, order):
        names = list(names)
        for name in order:
            axis = names.index(name)
            names.pop(axis)
            size = self.sizes[name]
            here = self.place(name)

            def parts(index, terms=terms, axis=axis, size=size):
                return [
                    lax.dynamic_index_in_dim(term, index % size, axis, keepdims=False)
                    for term in terms
                ]

            got = self.shift(added(parts(here + size - 1)), name)
            for step in range(2, size):
                got = self.shift(added([got] + parts(here + size - step)), name)
            terms = [got] + parts(here)
        return added(terms)

    def total(self, values):
        count = self.dp * self.blk
        bit = 1
        while bit < count:
            moves = [(index, index ^ bit) for index in range(count)]
            values = values + lax.ppermute(values, ("dp", "blk"), moves)
            bit *= 2
        return values


def added(terms):
    return low(functools.reduce(jnp.add, [wide(term) for term in terms]))


def offset_buckets(offsets, both_ways):
    if both_ways:
        buckets = NB // 2
        index = jnp.where(offsets > 0, buckets, 0)
        distance = jnp.abs(offsets)
    else:
        buckets = NB
        index = jnp.zeros_like(offsets)
        distance = jnp.maximum(-offsets, 0)
    exact = buckets // 2
    index = index + jnp.minimum(distance, exact)
    for step in range(1, buckets - exact):
        border = math.ceil(exact * (MAXD / exact) ** (step / (buckets - exact)) - 1e-09)
        index = index + jnp.where(distance >= border, 1, 0)
    matches = index[..., None] == jnp.arange(NB, dtype=jnp.int32)
    return matches.astype(jnp.float32)


def on_device(
    ring,
    encoder_input,
    decoder_input,
    encoder_cotangent,
    decoder_cotangent,
    segment_ids,
    padding_mask,
    answer_length,
    encoder_attn_gain,
    encoder_query,
    encoder_key,
    encoder_value,
    encoder_mix,
    encoder_bias_table,
    encoder_ffn_gain,
    encoder_ffn_in,
    encoder_ffn_out,
    final_gain,
    cross_key,
    cross_value,
    decoder_self_gain,
    decoder_query,
    decoder_key,
    decoder_value,
    decoder_mix,
    decoder_bias_table,
    decoder_cross_gain,
    cross_query,
    cross_mix,
    decoder_ffn_gain,
    decoder_ffn_in,
    decoder_ffn_out,
):
    sizes = ring.sizes
    questions = encoder_input.shape[0]
    batch = questions * encoder_input.shape[1]
    passage_rows = encoder_input.reshape(batch * ROW, D)
    passage_upstream = encoder_cotangent.reshape(batch * ROW, D)
    segments = segment_ids.reshape(batch, ROW)
    segment_row = jnp.where(padding_mask.reshape(batch, ROW) == 1, segments, -1)
    core = ring.place("c")
    row = ring.place("y")
    place = jnp.stack([core, row]).astype(jnp.int32)
    other = jnp.stack([1 - core, row]).astype(jnp.int32)

    def line(gain):
        return gain.reshape(1, D)

    def slots(rows):
        return jnp.pad(rows, ((0, 0), (0, SLOT - ANS), (0, 0))).reshape(questions * SLOT, D)

    def unslots(rows):
        return rows.reshape(questions, SLOT, D)[:, :ANS]

    passage_match = offset_buckets(jnp.arange(2 * ROW, dtype=jnp.int32) - ROW, True)
    places = jnp.arange(SLOT, dtype=jnp.int32)
    answer_match = offset_buckets(places[None, :] - places[:, None], False)
    passage_slopes = jnp.einsum(
        "kn,nh->hk", passage_match, wide(encoder_bias_table), precision=lax.Precision.HIGHEST
    )
    answer_bias = jnp.einsum(
        "ijn,nh->hij", answer_match, wide(decoder_bias_table), precision=lax.Precision.HIGHEST
    ).reshape(H * SLOT, SLOT)

    answer_rows = slots(decoder_input)
    answer_upstream = slots(decoder_cotangent)
    (
        answer_normed,
        answer_heads,
        answer_chances,
        answer_attended,
        answer_hidden,
        answer_crossed,
        asking,
    ) = answer_start(
        answer_length,
        answer_rows,
        answer_bias,
        line(decoder_self_gain),
        line(decoder_cross_gain),
        (decoder_query, decoder_key, decoder_value, decoder_mix, cross_query),
    )
    (
        normed,
        heads,
        chances,
        attended,
        hidden,
        second,
        active,
        bend,
        encoded,
        result,
        final,
        memory,
        scores,
        packed,
    ) = passage(
        passage_rows,
        segment_row,
        segments.T,
        passage_slopes,
        (line(encoder_attn_gain), line(encoder_ffn_gain), line(final_gain)),
        asking,
        (
            encoder_query,
            encoder_key,
            encoder_value,
            encoder_mix,
            encoder_ffn_in,
            encoder_ffn_out,
            cross_key,
            cross_value,
        ),
    )
    every = lax.all_gather(packed, "blk", axis=0)
    (
        answer_result,
        answer_lows,
        answer_wides,
        middle_delta,
        answer_ffn_gain_delta,
        memory_delta,
        asking_delta,
    ) = answer_middle(
        every,
        asking,
        answer_hidden,
        answer_upstream,
        line(decoder_ffn_gain),
        scores,
        memory,
        (cross_mix, decoder_ffn_in, decoder_ffn_out),
    )
    if ring.cut:
        asking_delta = added([asking_delta, ring.shift(asking_delta, "c")])
        asking_delta = added([asking_delta, ring.shift(asking_delta, "y")])
    else:
        asking_delta = low(lax.psum(wide(asking_delta), "blk"))
    if ring.cut:
        answer_wide_part = answer_wide_weight(
            place, answer_lows[1], answer_wides, answer_upstream, ring.dp
        )
    memory_send, memory_keep, output_delta, output_low, final_gain_delta = memory_back(
        place,
        line(final_gain),
        memory_delta,
        final,
        encoded,
        passage_upstream,
        (cross_key, cross_value),
    )
    out_send, out_keep, before = wide_out_back(place, output_low, encoder_ffn_out, active, bend)
    in_send, in_keep, hidden_delta, hidden_low, attended_delta, ffn_gain_delta = wide_in_back(
        place,
        line(encoder_ffn_gain),
        before,
        second,
        encoder_ffn_in,
        hidden,
        output_delta,
        encoder_mix,
    )
    (
        answer_gradient,
        answer_hidden_low,
        answer_heads_delta,
        cross_gain_delta,
        self_gain_delta,
        answer_score_delta,
    ) = answer_end(
        asking_delta,
        middle_delta,
        answer_hidden,
        answer_rows,
        line(decoder_cross_gain),
        line(decoder_self_gain),
        answer_heads,
        answer_chances,
        (cross_query, decoder_mix, decoder_query, decoder_key, decoder_value),
    )
    if ring.cut:
        answer_square_part = answer_square_weight(
            place,
            answer_crossed,
            answer_lows,
            answer_attended,
            answer_normed,
            asking_delta,
            answer_hidden_low,
            answer_heads_delta,
            ring.dp,
        )
    heads_delta, slope_delta = attend_back(heads, chances, attended_delta)
    heads_send = heads_weight(other, normed, attended, heads_delta, hidden_low)
    heads_keep = heads_weight(place, normed, attended, heads_delta, hidden_low)
    passage_gradient, attn_gain_delta = passage_end(
        line(encoder_attn_gain),
        passage_rows,
        heads_delta,
        hidden_delta,
        (encoder_query, encoder_key, encoder_value),
    )

    table_delta = jnp.einsum(
        "hk,kn->nh", slope_delta, passage_match, precision=lax.Precision.HIGHEST
    )
    answer_table_delta = jnp.einsum(
        "hij,ijn->nh",
        answer_score_delta.reshape(H, SLOT, SLOT),
        answer_match,
        precision=lax.Precision.HIGHEST,
    )
    once = lax.axis_index("blk") == 0
    small = [attn_gain_delta, ffn_gain_delta, final_gain_delta, table_delta] + [
        jnp.where(once, item, 0.0)
        for item in (self_gain_delta, cross_gain_delta, answer_ffn_gain_delta, answer_table_delta)
    ]
    small = jnp.concatenate([item.reshape(ring.dp, -1) for item in small], axis=1)
    small = lax.dynamic_index_in_dim(ring.total(small), lax.axis_index("dp"), 0, keepdims=False)
    gain = D // ring.dp
    table = NB * H // ring.dp
    cuts = [0]
    for width in (gain, gain, gain, table, gain, gain, gain, table):
        cuts.append(cuts[-1] + width)
    (
        gradient_encoder_attn_gain,
        gradient_encoder_ffn_gain,
        gradient_final_gain,
        gradient_encoder_bias_table,
        gradient_decoder_self_gain,
        gradient_decoder_cross_gain,
        gradient_decoder_ffn_gain,
        gradient_decoder_bias_table,
    ) = [small[begin:end] for begin, end in zip(cuts[:-1], cuts[1:])]
    gradient_encoder_bias_table = gradient_encoder_bias_table.reshape(-1, H)
    gradient_decoder_bias_table = gradient_decoder_bias_table.reshape(-1, H)

    weights = (cut_weights if ring.cut else whole_weights)(
        ring,
        core,
        (memory_send, memory_keep),
        (out_send, out_keep),
        (in_send, in_keep),
        (heads_send, heads_keep),
        (answer_wide_part, answer_square_part)
        if ring.cut
        else (
            (answer_lows[1], answer_wides[1]),
            (answer_wides[0], answer_upstream),
            (answer_crossed, asking_delta),
            (answer_lows[0], answer_lows[2]),
            (answer_attended, answer_hidden_low),
            (answer_normed, answer_heads_delta[0]),
            (answer_normed, answer_heads_delta[1]),
            (answer_normed, answer_heads_delta[2]),
        ),
    )
    (
        gradient_cross_key,
        gradient_cross_value,
        gradient_encoder_ffn_out,
        gradient_encoder_ffn_in,
        gradient_encoder_query,
        gradient_encoder_key,
        gradient_encoder_value,
        gradient_encoder_mix,
        gradient_decoder_ffn_in,
        gradient_decoder_ffn_out,
        gradient_cross_query,
        gradient_cross_mix,
        gradient_decoder_mix,
        gradient_decoder_query,
        gradient_decoder_key,
        gradient_decoder_value,
    ) = [wide(item) for item in weights]
    return (
        result.reshape(encoder_input.shape),
        unslots(answer_result),
        passage_gradient.reshape(encoder_input.shape),
        unslots(answer_gradient),
        gradient_encoder_attn_gain,
        gradient_encoder_query,
        gradient_encoder_key,
        gradient_encoder_value,
        gradient_encoder_mix,
        gradient_encoder_bias_table,
        gradient_encoder_ffn_gain,
        gradient_encoder_ffn_in,
        gradient_encoder_ffn_out,
        gradient_final_gain,
        gradient_cross_key,
        gradient_cross_value,
        gradient_decoder_self_gain,
        gradient_decoder_query,
        gradient_decoder_key,
        gradient_decoder_value,
        gradient_decoder_mix,
        gradient_decoder_bias_table,
        gradient_decoder_cross_gain,
        gradient_cross_query,
        gradient_cross_mix,
        gradient_decoder_ffn_gain,
        gradient_decoder_ffn_in,
        gradient_decoder_ffn_out,
    )


def cut_weights(ring, core, memory, out, inner, attend, answers):
    sizes = ring.sizes
    deep, across = sizes["z"], sizes["x"]
    rows = D // ring.dp
    row = ring.place("y")

    def crossed(pair, shape):
        send, keep = pair
        return [ring.shift(send, "c").reshape(shape), keep.reshape(shape)]

    def gathered(mine):
        near = ring.shift(mine, "y")
        pair = jnp.stack([jnp.where(row == 0, mine, near), jnp.where(row == 0, near, mine)])
        far = ring.shift(pair, "c")
        return jnp.stack([jnp.where(core == 0, pair, far), jnp.where(core == 0, far, pair)])

    answer_wide, answer_square = (
        ring.scatter([part.reshape(deep, across, -1, D)], "zx", "xz") for part in answers
    )
    memory = ring.scatter(crossed(memory, (deep, across, 2, rows // 2, D)), "zxy", "yxz")
    out = ring.scatter(crossed(out, (deep, across, 2, 2 * rows, D // 2)), "zxy", "xyz")
    inner = ring.scatter(crossed(inner, (2, deep, across, rows, D)), "yzx", "yxz")
    attend = ring.scatter(crossed(attend, (2, deep, across, rows, D)), "yzx", "xyz")

    first = jnp.concatenate([memory, inner, answer_wide, answer_square], axis=0)
    first = gathered(first)
    out = gathered(out)
    attend = gathered(attend)
    parts = []
    begin = 0
    for size in (rows // 2, rows, rows, rows, rows, rows // 2):
        parts.append(first[:, :, begin : begin + size])
        begin += size
    memory, inner, answer_in, answer_out, answer_units, answer_halves = parts

    def side_by_side(units):
        return jnp.concatenate([units[c, y] for c in range(2) for y in range(2)], axis=1)

    def halves(units):
        return [units[c].reshape(rows, D) for c in range(2)]

    answer_out = jnp.concatenate([answer_out[..., : D // 2], answer_out[..., D // 2 :]], axis=2)
    whole_out, whole_answer_out = (
        jnp.concatenate([part[c].reshape(4 * rows, D // 2) for c in range(2)], axis=1)
        for part in (out, answer_out)
    )
    return (
        *halves(memory),
        whole_out,
        side_by_side(inner),
        *[attend[c, y] for c in range(2) for y in range(2)],
        side_by_side(answer_in),
        whole_answer_out,
        *[answer_units[c, y] for c in range(2) for y in range(2)],
        *halves(answer_halves),
    )


def whole_weights(ring, core, memory, out, inner, attend, answers):
    def both(pair):
        send, keep = pair
        return (jnp.where(core == 0, keep, send), jnp.where(core == 0, send, keep))

    def shared(gradient):
        return lax.psum_scatter(low(gradient), "dp", scatter_dimension=0, tiled=True)

    def summed(gradient):
        return lax.psum(shared(gradient), "blk")

    passages = list(both(memory))
    passages.append(jnp.concatenate(both(out), axis=1))
    passages.append(jnp.concatenate([unit for half in both(inner) for unit in half], axis=1))
    passages += [unit for half in both(attend) for unit in half]
    return tuple(summed(item) for item in passages) + tuple(
        shared(dot_tokens(inputs, upstream)) for inputs, upstream in answers
    )


def solution(mesh):
    dims = {4: P("dp", "blk", None, None), 3: P("dp", None, None), 2: P("dp", None), 1: P("dp")}
    rows = P("dp", "blk", None)
    return jax.shard_map(
        functools.partial(on_device, Ring(mesh)),
        mesh=mesh,
        in_specs=(dims[4], dims[3], dims[4], dims[3], rows, rows, dims[1]) + (P(),) * 24,
        out_specs=(dims[4], dims[3], dims[4], dims[3])
        + tuple(dims[1 if at in (0, 6, 9, 12, 18, 21) else 2] for at in range(24)),
        check_vma=False,
    )
```

```python
import functools
import math

import jax
import jax.numpy as jnp
from jax import lax
from jax.experimental import pallas as pl
from jax.experimental.pallas import tpu as pltpu
from jax.sharding import PartitionSpec as P

D = 768
H = 12
HD = 64
NB = 32
MAXD = 128
ROW = 256
ANS = 20


EPSILON = 1e-06
NEGATIVE = -1e30


SLOT = 32
ANY = pl.ANY
VM = pltpu.VMEM
BF = jnp.bfloat16
F32 = jnp.float32
LIMIT = 60 << 20


def dot(left, right):
    return jnp.dot(left, right, preferred_element_type=jnp.float32)


def dot_rows(left, right):
    return lax.dot_general(
        left, right, (((1,), (1,)), ((), ())), preferred_element_type=jnp.float32
    )


def dot_tokens(left, right):
    return lax.dot_general(
        left, right, (((0,), (0,)), ((), ())), preferred_element_type=jnp.float32
    )


def low(values):
    return values.astype(jnp.bfloat16)


def wide(values):
    return values.astype(jnp.float32)


def slotted(ref):
    spare = jnp.zeros((SLOT - ANS, D), F32)
    return jnp.concatenate(
        [part for at in range(ref.shape[0]) for part in (wide(ref[at]), spare)], axis=0
    )


def unslotted(values, ref):
    for at in range(ref.shape[0]):
        ref[at] = values[at * SLOT : at * SLOT + ANS].astype(ref.dtype)


ATTN, FFN, FINAL, SELF, CROSS, ANSWER = range(6)


def gain_row(gains_ref, which):
    return gains_ref[which : which + 1, :]


def rms_scale(values):
    return lax.rsqrt(jnp.mean(values * values, axis=-1, keepdims=True) + EPSILON)


def head_lanes(rows, width=D):
    return lax.broadcasted_iota(jnp.int32, (rows, width), 1) // HD


def spread(rows):
    lanes = head_lanes(rows.shape[0])
    values = wide(rows)
    return low(jnp.concatenate([jnp.where(lanes == h, values, 0.0) for h in range(H)], axis=0))


def fold(full):
    rows = full.shape[0] // H
    lanes = head_lanes(rows)
    total = jnp.zeros((rows, full.shape[1]), jnp.float32)
    for h in range(H):
        total = jnp.where(lanes == h, full[h * rows : (h + 1) * rows], total)
    return total


def gelu_pair(values):
    square = values * values
    inner = values * (0.7978845608 + (0.7978845608 * 0.044715) * square)
    half = 0.5 + 0.5 * jnp.tanh(inner)
    active = values * half
    slope = 0.7978845608 + (3.0 * 0.7978845608 * 0.044715) * square
    return (active, half + 2.0 * active * (1.0 - half) * slope)


class Copies:
    def __init__(self, semaphores):
        self.semaphores = semaphores
        self.count = 0
        self.open = []

    def start(self, source, target):
        copy = pltpu.make_async_copy(source, target, self.semaphores.at[self.count])
        self.count += 1
        copy.start()
        return copy

    def out(self, source, target):
        self.open.append(self.start(source, target))

    def finish(self):
        for copy in self.open:
            copy.wait()


def kernel_call(body, operands, spaces, outs, scratch, after=()):
    if after:
        first, *_ = lax.optimization_barrier((operands[0], *after))
        operands = (first, *operands[1:])
    return pl.pallas_call(
        body,
        in_specs=[pl.BlockSpec(memory_space=space) for space in spaces],
        out_specs=[pl.BlockSpec(memory_space=space) for _, _, space in outs],
        out_shape=[jax.ShapeDtypeStruct(shape, dtype) for shape, dtype, _ in outs],
        scratch_shapes=scratch,
        compiler_params=pltpu.CompilerParams(vmem_limit_bytes=LIMIT),
        cost_estimate=pl.CostEstimate(flops=10**13, bytes_accessed=10**9, transcendentals=0),
    )(*operands)


def answer_start_kernel(
    length_ref, input_ref, bias_ref, gains_ref,
    query_hbm, key_hbm, value_hbm, mix_hbm, ask_hbm,
    normed_ref, heads_ref, chance_ref, attended_ref, hidden_ref, crossed_ref, asking_ref,
    weights, arrivals,
):
    copies = Copies(arrivals)
    waits = [
        copies.start(source, weights.at[at])
        for at, source in enumerate((query_hbm, key_hbm, value_hbm, mix_hbm, ask_hbm))
    ]
    values = slotted(input_ref)
    normed = low(values * rms_scale(values) * gain_row(gains_ref, SELF))
    normed_ref[...] = normed
    for at in range(3):
        waits[at].wait()
        heads_ref[at] = low(dot(normed, weights[at]))
    questions = values.shape[0] // SLOT
    row = lax.broadcasted_iota(jnp.int32, (H * SLOT, SLOT), 0) % SLOT
    column = lax.broadcasted_iota(jnp.int32, (H * SLOT, SLOT), 1)
    for at in range(questions):
        rows = slice(at * SLOT, (at + 1) * SLOT)
        scores = dot_rows(spread(heads_ref[0, rows]), heads_ref[1, rows]) + bias_ref[...]
        allowed = (column <= row) & (column < length_ref[at])
        scores = jnp.where(allowed, scores, NEGATIVE)
        powers = jnp.exp(scores - jnp.max(scores, axis=1, keepdims=True))
        chances = low(powers / jnp.sum(powers, axis=1, keepdims=True))
        chance_ref[at] = chances
        attended_ref[rows] = low(fold(dot(chances, heads_ref[2, rows])))
    waits[3].wait()
    hidden = values + dot(attended_ref[...], weights[3])
    hidden_ref[...] = hidden
    crossed = low(hidden * rms_scale(hidden) * gain_row(gains_ref, CROSS))
    crossed_ref[...] = crossed
    waits[4].wait()
    asking_ref[...] = low(dot(crossed, weights[4]))


def answer_start(length, rows, bias, gains, weights):
    questions = rows.shape[0]
    count = questions * SLOT
    return kernel_call(
        answer_start_kernel,
        (length, rows, bias, gains) + tuple(weights),
        [pltpu.SMEM] + [VM] * 3 + [ANY] * 5,
        [
            ((count, D), BF, VM),
            ((3, count, D), BF, VM),
            ((questions, H * SLOT, SLOT), BF, VM),
            ((count, D), BF, VM),
            ((count, D), F32, VM),
            ((count, D), BF, VM),
            ((count, D), BF, VM),
        ],
        [VM((5, D, D), BF), pltpu.SemaphoreType.DMA((5,))],
    )


def passage_kernel(
    input_ref, segment_row_ref, segment_column_ref, slope_ref,
    gains_ref, asking_ref,
    query_hbm, key_hbm, value_hbm, mix_hbm, in_hbm, out_hbm, cross_key_hbm, cross_value_hbm,
    normed_hbm, heads_hbm, chance_hbm, attended_hbm, hidden_hbm, second_hbm,
    active_hbm, bend_hbm, encoded_hbm, result_hbm, final_hbm, memory_hbm, score_hbm, packed_ref,
    square, wide_in, wide_out, normed, heads, chance, attended, hidden, second,
    active, bend, encoded, result, final, memory, score, masks, arrivals,
):
    copies = Copies(arrivals)
    square_hbm = (query_hbm, key_hbm, value_hbm, mix_hbm, cross_key_hbm, cross_value_hbm)
    waits = [copies.start(source, square.at[at]) for at, source in enumerate(square_hbm[:4])]
    wait_in = copies.start(in_hbm, wide_in)
    wait_out = copies.start(out_hbm, wide_out)
    waits += [copies.start(square_hbm[at], square.at[at]) for at in (4, 5)]
    rows = input_ref.shape[0]
    blocks = rows // ROW

    values = wide(input_ref[...])
    normed[...] = low(values * rms_scale(values) * gain_row(gains_ref, ATTN))
    copies.out(normed, normed_hbm)
    for at in range(3):
        waits[at].wait()
        heads[at] = low(dot(normed[...], square[at]))
    copies.out(heads, heads_hbm)

    place_row = lax.broadcasted_iota(jnp.int32, (ROW, ROW), 0)
    place_column = lax.broadcasted_iota(jnp.int32, (ROW, ROW), 1)
    for block in range(blocks):
        own = segment_column_ref[:, block : block + 1] == segment_row_ref[block : block + 1, :]
        masks[block] = jnp.where(own | (place_row == place_column), 0.0, NEGATIVE)

    second_half = lax.broadcasted_iota(jnp.int32, (ROW, 2 * HD), 1) >= HD

    @pl.loop(0, H // 2)
    def _(pair):
        lanes = pl.ds(pl.multiple_of(pair * 2 * HD, 2 * HD), 2 * HD)
        sums = []
        for which in range(2):
            head = pair * 2 + which
            slopes = jnp.broadcast_to(slope_ref[pl.ds(head, 1), :], (ROW, 2 * ROW))
            bias = pltpu.roll(slopes, ROW, 1, stride=1, stride_axis=0)[:, :ROW]
            for block in range(blocks):
                span = slice(block * ROW, (block + 1) * ROW)
                asked = heads[0, span, lanes]
                own = jnp.where(second_half == (which == 1), asked, jnp.zeros_like(asked))
                scores = dot_rows(own, heads[1, span, lanes]) + (bias + masks[block])
                powers = jnp.exp(scores - jnp.max(scores, axis=1, keepdims=True))
                chances = low(powers * (1.0 / jnp.sum(powers, axis=1, keepdims=True)))
                chance[head, block] = chances
                taken = dot(chances, heads[2, span, lanes])
                if which == 0:
                    sums.append(taken)
                else:
                    attended[span, lanes] = low(jnp.where(second_half, taken, sums[block]))

    copies.out(chance, chance_hbm)
    copies.out(attended, attended_hbm)
    waits[3].wait()
    hidden[...] = wide(input_ref[...]) + dot(attended[...], square[3])
    copies.out(hidden, hidden_hbm)
    values = hidden[...]
    second[...] = low(values * rms_scale(values) * gain_row(gains_ref, FFN))
    copies.out(second, second_hbm)
    wait_in.wait()

    @pl.loop(0, in_hbm.shape[1] // D)
    def _(at):
        lanes = pl.ds(pl.multiple_of(at * D, D), D)
        up, slope = gelu_pair(dot(second[...], wide_in[:, lanes]))
        active[:, lanes] = low(up)
        bend[:, lanes] = low(slope)

    copies.out(active, active_hbm)
    copies.out(bend, bend_hbm)
    wait_out.wait()

    @pl.loop(0, D // ROW)
    def _(at):
        lanes = pl.ds(pl.multiple_of(at * ROW, ROW), ROW)
        encoded[:, lanes] = hidden[:, lanes] + dot(active[...], wide_out[:, lanes])

    copies.out(encoded, encoded_hbm)
    values = encoded[...]
    result[...] = low(values)
    copies.out(result, result_hbm)
    final[...] = low(values * rms_scale(values) * gain_row(gains_ref, FINAL))
    copies.out(final, final_hbm)
    for at in range(2):
        waits[4 + at].wait()
        memory[at] = low(dot(final[...], square[4 + at]))
    copies.out(memory, memory_hbm)

    lane = lax.broadcasted_iota(jnp.int32, (SLOT, 128), 1)
    for block in range(blocks):
        span = slice(block * ROW, (block + 1) * ROW)
        slots = slice(block * SLOT, (block + 1) * SLOT)
        scores = dot_rows(spread(asking_ref[slots]), memory[0, span])
        visible = segment_row_ref[block : block + 1, :] >= 0
        scores = jnp.where(visible, scores, NEGATIVE)
        score[block] = scores
        top = jnp.max(scores, axis=1, keepdims=True)
        powers = jnp.exp(scores - top)
        sums = jnp.sum(powers, axis=1, keepdims=True)
        reading = fold(dot(low(powers * (1.0 / sums)), memory[1, span]))
        packed_ref[slots, :D] = low(reading)
        total = top + jnp.log(sums)
        extra = jnp.zeros((SLOT, 128), F32)
        for h in range(H):
            rest = total[h * SLOT : (h + 1) * SLOT]
            for piece in range(3):
                part = wide(low(rest))
                extra = jnp.where(lane == piece * H + h, part, extra)
                rest = rest - part
        packed_ref[slots, D:] = low(extra)
    copies.out(score, score_hbm)
    copies.finish()


def passage(rows, segment_row, segment_column, slopes, gains, asking, weights):
    count = rows.shape[0]
    blocks = count // ROW
    wide_size = weights[4].shape[1]
    whole = [
        ((count, D), BF),
        ((3, count, D), BF),
        ((H, blocks, ROW, ROW), BF),
        ((count, D), BF),
        ((count, D), F32),
        ((count, D), BF),
        ((count, wide_size), BF),
        ((count, wide_size), BF),
        ((count, D), F32),
        ((count, D), BF),
        ((count, D), BF),
        ((2, count, D), BF),
        ((blocks, H * SLOT, ROW), F32),
    ]
    return kernel_call(
        passage_kernel,
        (rows, segment_row, segment_column, slopes, gains, asking) + tuple(weights),
        [VM] * 6 + [ANY] * 8,
        [(shape, dtype, ANY) for shape, dtype in whole]
        + [((blocks * SLOT, D + 128), BF, VM)],
        [VM((6, D, D), BF), VM((D, wide_size), BF), VM((wide_size, D), BF)]
        + [VM(shape, dtype) for shape, dtype in whole]
        + [VM((blocks, ROW, ROW), F32), pltpu.SemaphoreType.DMA((32,))],
    )


def rms_back(values, gain, upstream):
    scale = rms_scale(values)
    scaled = upstream * gain
    inner = jnp.mean(scaled * values, axis=-1, keepdims=True)
    delta = scaled * scale - values * (scale * scale * scale) * inner
    return (delta, jnp.sum(upstream * values * scale, axis=0, keepdims=True))


def exact_dot(left, right, rows=False):
    return lax.dot_general(
        left,
        right,
        (((1,), (1 if rows else 0,)), ((), ())),
        precision=lax.Precision.HIGHEST,
        preferred_element_type=jnp.float32,
    )


def head_columns(values):
    return jnp.concatenate([values[:, h : h + 1] for h in range(H)], axis=0)


def bucket_of(offsets, both_ways):
    if both_ways:
        buckets = NB // 2
        index = jnp.where(offsets > 0, buckets, 0)
        distance = jnp.abs(offsets)
    else:
        buckets = NB
        index = jnp.zeros_like(offsets)
        distance = jnp.maximum(-offsets, 0)
    exact = buckets // 2
    index = index + jnp.minimum(distance, exact)
    for step in range(1, buckets - exact):
        border = math.ceil(exact * (MAXD / exact) ** (step / (buckets - exact)) - 1e-09)
        index = index + jnp.where(distance >= border, 1, 0)
    return index


def tree_sum(items):
    while len(items) > 1:
        items = [
            items[at] + items[at + 1] if at + 1 < len(items) else items[at]
            for at in range(0, len(items), 2)
        ]
    return items[0]


def answer_middle_kernel(
    every_refs, asking_ref, hidden_ref, upstream_ref, gains_ref, score_hbm, memory_hbm,
    mix_hbm, in_hbm, out_hbm,
    result_ref, low_ref, wide_ref, middle_ref, gain_delta_ref, memory_delta_hbm, asking_delta_ref,
    score, memory, memory_delta, mix, wide_in, wide_out, arrivals,
):
    copies = Copies(arrivals)
    wait_mix = copies.start(mix_hbm, mix)
    wait_in = copies.start(in_hbm, wide_in)
    wait_out = copies.start(out_hbm, wide_out)
    wait_score = copies.start(score_hbm, score)
    wait_memory = copies.start(memory_hbm, memory)
    count = asking_ref.shape[0]

    from_piece = lax.broadcasted_iota(jnp.int32, (128, 128), 0)
    to_head = lax.broadcasted_iota(jnp.int32, (128, 128), 1)
    same = (from_piece % H == to_head) & (from_piece < 3 * H)
    pieces = low(jnp.where(same, 1.0, 0.0))
    lane_head = lax.broadcasted_iota(jnp.int32, (128, D), 1) // HD
    widen = jnp.where(lane_head == lax.broadcasted_iota(jnp.int32, (128, D), 0), 1.0, 0.0)

    totals = [dot(ref[:, D:], pieces) for ref in every_refs]
    top = functools.reduce(jnp.maximum, totals)
    powers = [jnp.exp(total - top) for total in totals]
    sums = tree_sum(powers)
    reading = tree_sum(
        [
            wide(ref[:, :D]) * exact_dot(power / sums, widen)
            for ref, power in zip(every_refs, powers)
        ]
    )
    whole_total = top + jnp.log(sums)
    reading_low = low(reading)
    low_ref[0] = reading_low
    wait_mix.wait()
    middle = hidden_ref[...] + dot(reading_low, mix[...])
    gain = gain_row(gains_ref, ANSWER)
    fifth = low(middle * rms_scale(middle) * gain)
    low_ref[1] = fifth
    upstream_wide = slotted(upstream_ref)
    upstream = low(upstream_wide)
    wait_in.wait()
    wait_out.wait()

    @pl.loop(0, wide_in.shape[1] // D)
    def _(at):
        lanes = pl.ds(pl.multiple_of(at * D, D), D)
        active, slope = gelu_pair(dot(fifth, wide_in[:, lanes]))
        wide_ref[0, :, lanes] = low(active)
        wide_ref[1, :, lanes] = low(dot_rows(upstream, wide_out[lanes, :]) * slope)

    delta, gain_delta = rms_back(middle, gain, dot_rows(wide_ref[1], wide_in[...]))
    gain_delta_ref[...] = gain_delta
    delta += upstream_wide
    middle_ref[...] = delta
    delta_low = low(delta)
    low_ref[2] = delta_low
    taken = low(dot_rows(delta_low, mix[...]))
    inner = exact_dot(wide(taken) * reading, widen, rows=True)
    wait_score.wait()
    wait_memory.wait()
    for block in range(count // SLOT):
        slots = slice(block * SLOT, (block + 1) * SLOT)
        span = slice(block * ROW, (block + 1) * ROW)
        chances = jnp.exp(score[block] - head_columns(whole_total[slots]))
        asked = spread(asking_ref[slots])
        upward = spread(taken[slots])
        delta_chances = dot_rows(upward, memory[1, span])
        deltas = low(chances * (delta_chances - head_columns(inner[slots])))
        memory_delta[0, span] = low(dot_tokens(deltas, asked))
        memory_delta[1, span] = low(dot_tokens(low(chances), upward))
        asking_delta_ref[slots] = low(fold(dot(deltas, memory[0, span])))
    copies.out(memory_delta, memory_delta_hbm)
    answer = middle
    for at in range(0, wide_out.shape[0], D):
        answer += dot(wide_ref[0, :, at : at + D], wide_out[at : at + D, :])
    unslotted(answer, result_ref)
    copies.finish()


def answer_middle(every, asking, hidden, upstream, gains, score, memory, weights):
    count = asking.shape[0]
    wide_size = weights[1].shape[1]
    blocks = len(every)

    def body(*refs):
        answer_middle_kernel(refs[:blocks], *refs[blocks:])

    return kernel_call(
        body,
        tuple(every) + (asking, hidden, upstream, gains, score, memory) + tuple(weights),
        [VM] * (blocks + 4) + [ANY] * 5,
        [
            (upstream.shape, BF, VM),
            ((3, count, D), BF, VM),
            ((2, count, wide_size), BF, VM),
            ((count, D), F32, VM),
            ((1, D), F32, VM),
            (memory.shape, BF, ANY),
            ((count, D), BF, VM),
        ],
        [
            VM(score.shape, F32),
            VM(memory.shape, BF),
            VM(memory.shape, BF),
            VM((D, D), BF),
            VM((D, wide_size), BF),
            VM((wide_size, D), BF),
            pltpu.SemaphoreType.DMA((8,)),
        ],
    )


def memory_back_kernel(
    place_ref, gains_ref, delta_hbm, final_hbm, encoded_hbm, upstream_hbm, key_hbm, value_hbm,
    active_hbm,
    send_hbm, keep_hbm, output_hbm, output_low_hbm, gain_delta_ref,
    delta, final, encoded, upstream, weights, active, send, keep, output, output_low, arrivals,
):
    copies = Copies(arrivals)
    shards, rows = send.shape[0], send.shape[2]
    width = D // shards
    half = D // 2
    steps = active.shape[1] // D
    wait_delta = copies.start(delta_hbm, delta)
    waits = [copies.start(key_hbm, weights.at[0]), copies.start(value_hbm, weights.at[1])]
    wait_encoded = copies.start(encoded_hbm, encoded)
    wait_upstream = copies.start(upstream_hbm, upstream)
    wait_final = copies.start(final_hbm, final)
    wait_active = []
    for at in range(steps):
        part = pl.ds(at * D, D)
        wait_active.append(copies.start(active_hbm.at[:, part], active.at[:, part]))
    core = place_ref[0]
    wait_delta.wait()
    for wait in waits:
        wait.wait()
    upward = dot_rows(delta[0], weights[0]) + dot_rows(delta[1], weights[1])
    wait_encoded.wait()
    wait_upstream.wait()
    back, gain_delta = rms_back(encoded[...], gain_row(gains_ref, FINAL), upward)
    gain_delta_ref[...] = gain_delta
    back += wide(upstream[...])
    output[...] = back
    output_low[...] = low(back)
    copies.out(output, output_hbm)
    copies.out(output_low, output_low_hbm)
    wait_final.wait()
    for side, (part_ref, part_hbm) in enumerate(((send, send_hbm), (keep, keep_hbm))):
        which = core if side else 1 - core
        first = low(dot_tokens(final[...], delta[which]))
        for shard in range(shards):
            for row in range(2):
                begin = shard * width + row * (width // 2)
                part_ref[shard, row, : width // 2] = first[begin : begin + width // 2]
        columns = pl.ds(pl.multiple_of(which * half, half), half)
        for at in range(steps):
            if side == 0:
                wait_active[at].wait()
            later = low(dot_tokens(active[:, at * D : (at + 1) * D], output_low[:, columns]))
            for piece in range(D // width):
                shard, place = divmod(at * D // width + piece, 4)
                row, part = divmod(place, 2)
                part_ref[shard, row, width // 2 :, part * half : (part + 1) * half] = later[
                    piece * width : (piece + 1) * width
                ]
            done = pl.ds(at * shards // steps, shards // steps)
            copies.out(part_ref.at[done], part_hbm.at[done])
    copies.finish()


def memory_back(place, gains, delta, final, encoded, upstream, weights, active, shards, after=()):
    count = final.shape[0]
    wide_size = active.shape[1]
    shape = (shards, 2, 3 * D // shards // 2, D)
    return kernel_call(
        memory_back_kernel,
        (place, gains, delta, final, encoded, upstream) + tuple(weights) + (active,),
        [pltpu.SMEM, VM] + [ANY] * 7,
        [
            (shape, BF, ANY),
            (shape, BF, ANY),
            ((count, D), F32, ANY),
            ((count, D), BF, ANY),
            ((1, D), F32, VM),
        ],
        [
            VM((2, count, D), BF), VM((count, D), BF), VM((count, D), F32), VM((count, D), BF),
            VM((2, D, D), BF), VM((count, wide_size), BF), VM(shape, BF), VM(shape, BF),
            VM((count, D), F32), VM((count, D), BF), pltpu.SemaphoreType.DMA((24,)),
        ],
        after,
    )


def wide_out_back_kernel(
    output_hbm, weight_hbm, bend_hbm, before_hbm,
    output, weight, bend, before, arrivals,
):
    copies = Copies(arrivals)
    steps = weight.shape[0] // D
    wait = copies.start(output_hbm, output)
    waits = []
    for at in range(steps):
        part = pl.ds(at * D, D)
        waits.append(copies.start(weight_hbm.at[part], weight.at[part]))
        waits.append(copies.start(bend_hbm.at[:, part], bend.at[:, part]))
    wait.wait()
    for at in range(steps):
        part = slice(at * D, (at + 1) * D)
        waits[2 * at].wait()
        up = dot_rows(output[...], weight[part, :])
        waits[2 * at + 1].wait()
        before[:, part] = low(up * wide(bend[:, part]))
        copies.out(before.at[:, part], before_hbm.at[:, part])
    copies.finish()


def wide_out_back(output, weight, bend, after=()):
    count = output.shape[0]
    wide_size = weight.shape[0]
    return kernel_call(
        wide_out_back_kernel,
        (output, weight, bend),
        [ANY] * 3,
        [((count, wide_size), BF, ANY)],
        [
            VM((count, D), BF), VM((wide_size, D), BF), VM((count, wide_size), BF),
            VM((count, wide_size), BF), pltpu.SemaphoreType.DMA((16,)),
        ],
        after,
    )[0]


def wide_in_weight_kernel(
    place_ref, second_hbm, before_hbm, send_hbm, keep_hbm, second, before, send, keep, arrivals
):
    copies = Copies(arrivals)
    steps = before.shape[1] // D // 2
    core = place_ref[0]
    wait = copies.start(second_hbm, second)
    units = [(1 - core) * steps + at for at in range(steps)]
    units += [core * steps + at for at in range(steps)]
    waits = []
    for unit in units:
        part = pl.ds(pl.multiple_of(unit * D, D), D)
        waits.append(copies.start(before_hbm.at[:, part], before.at[:, part]))
    wait.wait()
    for at, unit in enumerate(units):
        waits[at].wait()
        part = pl.ds(pl.multiple_of(unit * D, D), D)
        target, target_hbm = (send, send_hbm) if at < steps else (keep, keep_hbm)
        target[at % steps] = low(dot_tokens(second[...], before[:, part]))
        copies.out(target.at[at % steps], target_hbm.at[at % steps])
    copies.finish()


def wide_in_weight(place, second, before, after=()):
    count, wide_size = before.shape
    shape = (wide_size // D // 2, D, D)
    return kernel_call(
        wide_in_weight_kernel,
        (place, second, before),
        [pltpu.SMEM] + [ANY] * 2,
        [(shape, BF, ANY), (shape, BF, ANY)],
        [
            VM((count, D), BF), VM((count, wide_size), BF), VM(shape, BF), VM(shape, BF),
            pltpu.SemaphoreType.DMA((16,)),
        ],
        after,
    )


def wide_in_back_kernel(
    gains_ref, before_hbm, weight_hbm, hidden_hbm, output_hbm, mix_hbm,
    hidden_delta_hbm, hidden_low_hbm, attended_delta_hbm, gain_delta_ref,
    before, weight, hidden, output, mix, upward, hidden_delta, hidden_low, attended_delta, arrivals,
):
    copies = Copies(arrivals)
    wait_before = copies.start(before_hbm, before)
    waits = []
    for at in range(D // ROW):
        part = pl.ds(at * ROW, ROW)
        waits.append(copies.start(weight_hbm.at[part], weight.at[part]))
    later = [
        copies.start(source, target)
        for source, target in ((hidden_hbm, hidden), (output_hbm, output), (mix_hbm, mix))
    ]
    wait_before.wait()
    for at in range(D // ROW):
        waits[at].wait()
        part = slice(at * ROW, (at + 1) * ROW)
        upward[:, part] = dot_rows(before[...], weight[part, :])
    for wait in later:
        wait.wait()
    back, gain_delta = rms_back(hidden[...], gain_row(gains_ref, FFN), upward[...])
    gain_delta_ref[...] = gain_delta
    back += output[...]
    hidden_delta[...] = back
    copies.out(hidden_delta, hidden_delta_hbm)
    hidden_low[...] = low(back)
    copies.out(hidden_low, hidden_low_hbm)
    attended_delta[...] = low(dot_rows(hidden_low[...], mix[...]))
    copies.out(attended_delta, attended_delta_hbm)
    copies.finish()


def wide_in_back(gains, before, weight, hidden, output, mix, after=()):
    count, wide_size = before.shape
    return kernel_call(
        wide_in_back_kernel,
        (gains, before, weight, hidden, output, mix),
        [VM] + [ANY] * 5,
        [
            ((count, D), F32, ANY),
            ((count, D), BF, ANY),
            ((count, D), BF, ANY),
            ((1, D), F32, VM),
        ],
        [
            VM((count, wide_size), BF), VM((D, wide_size), BF), VM((count, D), F32),
            VM((count, D), F32), VM((D, D), BF), VM((count, D), F32), VM((count, D), F32),
            VM((count, D), BF), VM((count, D), BF), pltpu.SemaphoreType.DMA((16,)),
        ],
        after,
    )


def attend_back_kernel(
    heads_hbm, chance_hbm, upstream_hbm,
    delta_hbm, slope_delta_ref,
    heads, chance, upstream, delta, gathered, arrivals,
):
    copies = Copies(arrivals)
    waits = [
        copies.start(source, target)
        for source, target in ((heads_hbm, heads), (upstream_hbm, upstream), (chance_hbm, chance))
    ]
    for wait in waits:
        wait.wait()
    blocks = upstream.shape[0] // ROW
    second_half = lax.broadcasted_iota(jnp.int32, (ROW, 2 * HD), 1) >= HD
    place_row = lax.broadcasted_iota(jnp.int32, (ROW, ROW), 0)
    place_column = lax.broadcasted_iota(jnp.int32, (ROW, ROW), 1)
    mirror = low(jnp.where(place_row + place_column == ROW - 1, 1.0, 0.0))

    @pl.loop(0, H // 2)
    def _(pair):
        lanes = pl.ds(pl.multiple_of(pair * 2 * HD, 2 * HD), 2 * HD)
        kept = []
        for which in range(2):
            head = pair * 2 + which
            for block in range(blocks):
                span = slice(block * ROW, (block + 1) * ROW)
                query, key, value = (heads[at, span, lanes] for at in range(3))
                upward = upstream[span, lanes]
                own = jnp.where(second_half == (which == 1), upward, jnp.zeros_like(upward))
                chances = chance[head, block]
                weight = wide(chances)
                delta_chances = dot_rows(own, value)
                inner = jnp.sum(delta_chances * weight, axis=1, keepdims=True)
                deltas = low(weight * (delta_chances - inner))
                turned = dot(mirror, deltas)
                if block == 0:
                    gathered[...] = turned
                else:
                    gathered[...] += turned
                news = [dot(deltas, key), dot_tokens(deltas, query), dot_tokens(chances, upward)]
                if which == 0:
                    kept.append(news)
                else:
                    for at in range(3):
                        both = jnp.where(second_half, news[at], kept[block][at])
                        delta[at, span, lanes] = low(both)
            padded = jnp.concatenate([gathered[...], jnp.zeros((ROW, ROW), F32)], axis=1)
            rolled = pltpu.roll(padded, 1, 1, stride=1, stride_axis=0)
            slope_delta_ref[pl.ds(head, 1), :] = jnp.sum(rolled, axis=0, keepdims=True)

    copies.out(delta, delta_hbm)
    copies.finish()


def attend_back(heads, chance, upstream, after=()):
    count = upstream.shape[0]
    return kernel_call(
        attend_back_kernel,
        (heads, chance, upstream),
        [ANY] * 3,
        [(heads.shape, BF, ANY), ((H, 2 * ROW), F32, VM)],
        [
            VM(heads.shape, BF), VM(chance.shape, BF), VM(upstream.shape, BF),
            VM(heads.shape, BF), VM((ROW, ROW), F32), pltpu.SemaphoreType.DMA((4,)),
        ],
        after,
    )


def heads_weight_kernel(
    place_ref, normed_hbm, attended_hbm, delta_hbm, hidden_low_hbm,
    part_ref, inputs, deltas, arrivals,
):
    copies = Copies(arrivals)
    waits = [
        copies.start(normed_hbm, inputs.at[0]),
        copies.start(delta_hbm, deltas.at[pl.ds(0, 3)]),
        copies.start(attended_hbm, inputs.at[1]),
        copies.start(hidden_low_hbm, deltas.at[3]),
    ]
    for wait in waits:
        wait.wait()
    for at in range(2):
        unit = place_ref[0] * 2 + at
        part_ref[at] = low(dot_tokens(inputs[unit // 3], deltas[unit]))


def heads_weight(place, normed, attended, delta, hidden_low, after=()):
    count = normed.shape[0]
    return kernel_call(
        heads_weight_kernel,
        (place, normed, attended, delta, hidden_low),
        [pltpu.SMEM] + [ANY] * 4,
        [((2, D, D), BF, VM)],
        [VM((2, count, D), BF), VM((4, count, D), BF), pltpu.SemaphoreType.DMA((4,))],
        after,
    )[0]


def passage_end_kernel(
    place_ref, gains_ref, slope_delta_ref, answer_table_ref, ffn_gain_ref, final_gain_ref,
    self_gain_ref, cross_gain_ref, answer_gain_ref,
    input_hbm, delta_hbm, hidden_delta_hbm, query_hbm, key_hbm, value_hbm,
    gradient_hbm, small_ref,
    values, delta, hidden_delta, weights, gradient, arrivals,
):
    copies = Copies(arrivals)
    wait_delta = copies.start(delta_hbm, delta)
    waits = [
        copies.start(source, weights.at[at])
        for at, source in enumerate((query_hbm, key_hbm, value_hbm))
    ]
    wait_input = copies.start(input_hbm, values)
    wait_hidden = copies.start(hidden_delta_hbm, hidden_delta)
    once = jnp.where((place_ref[0] == 0) & (place_ref[1] == 0), 1.0, 0.0)
    small_ref[...] = jnp.zeros_like(small_ref)
    small_ref[FFN : FFN + 1, :] = ffn_gain_ref[...]
    small_ref[FINAL : FINAL + 1, :] = final_gain_ref[...]
    small_ref[SELF : SELF + 1, :] = self_gain_ref[...] * once
    small_ref[CROSS : CROSS + 1, :] = cross_gain_ref[...] * once
    small_ref[ANSWER : ANSWER + 1, :] = answer_gain_ref[...] * once
    offsets = lax.broadcasted_iota(jnp.int32, (2 * ROW, 128), 0) - ROW
    matches = bucket_of(offsets, True) == lax.broadcasted_iota(jnp.int32, (2 * ROW, 128), 1)
    table = exact_dot(slope_delta_ref[...], jnp.where(matches, 1.0, 0.0))
    small_ref[8 : 8 + H, :128] = table
    small_ref[8 : 8 + H, 128:256] = answer_table_ref[:H, :] * once
    wait_delta.wait()
    for wait in waits:
        wait.wait()
    upward = dot_rows(delta[0], weights[0])
    upward += dot_rows(delta[1], weights[1])
    upward += dot_rows(delta[2], weights[2])
    wait_input.wait()
    wait_hidden.wait()
    back, gain_delta = rms_back(wide(values[...]), gain_row(gains_ref, ATTN), upward)
    small_ref[ATTN : ATTN + 1, :] = gain_delta
    gradient[...] = back + hidden_delta[...]
    copies.out(gradient, gradient_hbm)
    copies.finish()


def passage_end(place, gains, small, rows, delta, hidden_delta, weights, after=()):
    count = rows.shape[0]
    return kernel_call(
        passage_end_kernel,
        (place, gains) + tuple(small) + (rows, delta, hidden_delta) + tuple(weights),
        [pltpu.SMEM] + [VM] * 8 + [ANY] * 6,
        [((count, D), F32, ANY), ((24, D), F32, VM)],
        [
            VM((count, D), BF), VM((3, count, D), BF), VM((count, D), F32), VM((3, D, D), BF),
            VM((count, D), F32), pltpu.SemaphoreType.DMA((8,)),
        ],
        after,
    )


def answer_end_kernel(
    asking_refs, middle_ref, hidden_ref, input_ref, gains_ref,
    heads_ref, chance_ref, ask_hbm, mix_hbm, query_hbm, key_hbm, value_hbm,
    gradient_ref, asking_delta_ref, hidden_low_ref, delta_ref, cross_delta_ref, self_delta_ref,
    table_ref,
    weights, score_delta, arrivals,
):
    copies = Copies(arrivals)
    waits = [
        copies.start(source, weights.at[at])
        for at, source in enumerate((ask_hbm, mix_hbm, query_hbm, key_hbm, value_hbm))
    ]
    waits[0].wait()
    asking_delta_ref[...] = low(tree_sum([wide(ref[...]) for ref in asking_refs]))
    upward = dot_rows(asking_delta_ref[...], weights[0])
    back, gain_delta = rms_back(hidden_ref[...], gain_row(gains_ref, CROSS), upward)
    cross_delta_ref[...] = gain_delta
    back += middle_ref[...]
    hidden_low = low(back)
    hidden_low_ref[...] = hidden_low
    waits[1].wait()
    upward = low(dot_rows(hidden_low, weights[1]))
    for block in range(upward.shape[0] // SLOT):
        slots = slice(block * SLOT, (block + 1) * SLOT)
        chances = chance_ref[block]
        taken = spread(upward[slots])
        delta_chances = dot_rows(taken, heads_ref[2, slots])
        inner = jnp.sum(delta_chances * wide(chances), axis=1, keepdims=True)
        deltas = low(wide(chances) * (delta_chances - inner))
        if block == 0:
            score_delta[...] = wide(deltas)
        else:
            score_delta[...] += wide(deltas)
        delta_ref[0, slots] = low(fold(dot(deltas, heads_ref[1, slots])))
        delta_ref[1, slots] = low(dot_tokens(deltas, spread(heads_ref[0, slots])))
        delta_ref[2, slots] = low(dot_tokens(chances, taken))
    for wait in waits[2:]:
        wait.wait()
    upward = dot_rows(delta_ref[0], weights[2])
    upward += dot_rows(delta_ref[1], weights[3])
    upward += dot_rows(delta_ref[2], weights[4])
    start_delta, gain_delta = rms_back(slotted(input_ref), gain_row(gains_ref, SELF), upward)
    self_delta_ref[...] = gain_delta
    unslotted(start_delta + back, gradient_ref)
    row = lax.broadcasted_iota(jnp.int32, (H * SLOT, 128), 0) % SLOT
    lane = lax.broadcasted_iota(jnp.int32, (H * SLOT, 128), 1)
    sums = jnp.zeros((H * SLOT, 128), F32)
    for column in range(ANS):
        here = bucket_of(column - row, False) == lane
        sums += jnp.where(here, score_delta[:, column : column + 1], 0.0)
    head = lax.broadcasted_iota(jnp.int32, (16, H * SLOT), 0)
    own = lax.broadcasted_iota(jnp.int32, (16, H * SLOT), 1) // SLOT == head
    table_ref[...] = exact_dot(jnp.where(own, 1.0, 0.0), sums)


def answer_end(asking_deltas, middle, hidden, rows, gains, heads, chance, weights, after=()):
    count = hidden.shape[0]
    blocks = len(asking_deltas)

    def body(*refs):
        answer_end_kernel(refs[:blocks], *refs[blocks:])

    return kernel_call(
        body,
        tuple(asking_deltas) + (middle, hidden, rows, gains, heads, chance) + tuple(weights),
        [VM] * (blocks + 6) + [ANY] * 5,
        [
            (rows.shape, F32, VM),
            ((count, D), BF, VM),
            ((count, D), BF, VM),
            ((3, count, D), BF, VM),
            ((1, D), F32, VM),
            ((1, D), F32, VM),
            ((16, 128), F32, VM),
        ],
        [VM((5, D, D), BF), VM((H * SLOT, SLOT), F32), pltpu.SemaphoreType.DMA((5,))],
        after,
    )


def answer_wide_weight_kernel(
    place_ref, lows_ref, wide_ref, upstream_ref, send_ref, keep_ref, inner, full
):
    core = place_ref[0]
    row = place_ref[1]
    width = send_ref.shape[1] // 2
    half = D // 2
    part = pl.ds(pl.multiple_of((core * 2 + row) * D, D), D)
    inner[...] = low(dot_tokens(lows_ref[1], wide_ref[1, :, part]))
    upstream = slotted(upstream_ref)
    upstream = low(jnp.where(core == 0, upstream[:, :half], upstream[:, half:]))

    @pl.loop(0, wide_ref.shape[2] // D)
    def _(at):
        span = pl.ds(pl.multiple_of(at * D, D), D)
        full[span, :] = low(dot_tokens(wide_ref[0, :, span], upstream))

    for part_ref, sent in ((send_ref, True), (keep_ref, False)):
        for at in range(part_ref.shape[0]):
            own = place_ref[2]
            shard = at * 2 + (1 - own if sent else own)
            rows = pl.ds(pl.multiple_of(shard * width, 16), width)
            part_ref[at, :width] = inner[rows, :]
            for side in range(2):
                begin = shard * 4 * width + row * 2 * width + side * width
                rows = pl.ds(pl.multiple_of(begin, 16), width)
                part_ref[at, width:, side * half : (side + 1) * half] = full[rows, :]


def answer_wide_weight(place, lows, wide_pair, upstream, shards, after=()):
    wide_size = wide_pair.shape[2]
    shape = (shards // 2, 2 * D // shards, D)
    return kernel_call(
        answer_wide_weight_kernel,
        (place, lows, wide_pair, upstream),
        [pltpu.SMEM] + [VM] * 3,
        [(shape, BF, VM), (shape, BF, VM)],
        [VM((D, D), BF), VM((wide_size, D // 2), BF)],
        after,
    )


def answer_square_weight_kernel(
    place_ref, crossed_ref, low_ref, attended_ref, normed_ref, asking_delta_ref, hidden_low_ref,
    delta_ref, send_ref, keep_ref, inputs, deltas, first, full,
):
    core = place_ref[0]
    row = place_ref[1]
    width = send_ref.shape[1] * 2 // 3
    inputs[0] = crossed_ref[...]
    inputs[1] = low_ref[0]
    inputs[2] = attended_ref[...]
    inputs[3] = normed_ref[...]
    deltas[0] = asking_delta_ref[...]
    deltas[1] = low_ref[2]
    deltas[2] = hidden_low_ref[...]
    deltas[3] = delta_ref[0]
    unit = core * 2 + row
    first[...] = low(dot_tokens(inputs[unit], deltas[unit]))
    full[...] = low(dot_tokens(normed_ref[...], delta_ref[1 + core]))
    for part_ref, sent in ((send_ref, True), (keep_ref, False)):
        for at in range(part_ref.shape[0]):
            own = place_ref[3]
            shard = at // 2 * 4 + (1 - own if sent else own) * 2 + at % 2
            rows = pl.ds(pl.multiple_of(shard * width, 16), width)
            part_ref[at, :width] = first[rows, :]
            rows = pl.ds(pl.multiple_of(shard * width + row * (width // 2), 16), width // 2)
            part_ref[at, width:] = full[rows, :]


def answer_square_weight(
    place, crossed, lows, attended, normed, asking_delta, hidden_low, delta, shards, after=()
):
    count = crossed.shape[0]
    shape = (shards // 2, 3 * D // shards // 2, D)
    return kernel_call(
        answer_square_weight_kernel,
        (place, crossed, lows, attended, normed, asking_delta, hidden_low, delta),
        [pltpu.SMEM] + [VM] * 7,
        [(shape, BF, VM), (shape, BF, VM)],
        [VM((4, count, D), BF), VM((4, count, D), BF), VM((D, D), BF), VM((D, D), BF)],
        after,
    )


class Ring:
    def __init__(self, mesh):
        self.dp = mesh.shape["dp"]
        self.blk = mesh.shape["blk"]
        self.cut = self.blk == 4 and self.dp == 8

    def bit(self, name):
        return {"c": 1, "y": 2, "x": 4, "l": 8, "h": 16}[name]

    def number(self):
        return lax.axis_index("dp") * self.blk + lax.axis_index("blk")

    def place(self, name):
        return self.number() // self.bit(name) % 2

    def swap(self, values, *names):
        mask = sum(self.bit(name) for name in names)
        moves = [(at, at ^ mask) for at in range(self.dp * self.blk)]
        return lax.ppermute(values, ("dp", "blk"), moves)

    def total(self, values):
        count = self.dp * self.blk
        mask = 1
        while mask < count:
            moves = [(at, at ^ mask) for at in range(count)]
            values = values + lax.ppermute(values, ("dp", "blk"), moves)
            mask *= 2
        return values


def added(terms):
    return low(functools.reduce(jnp.add, [wide(term) for term in terms]))


class Flow:
    def __init__(self, ring, send, keep, name, names, rest):
        shape = (2,) * len(names) + tuple(rest)
        self.ring = ring
        self.names = list(names)
        self.sent = [send]
        self.terms = [keep.reshape(shape)]
        self.arriving = [ring.swap(send, name).reshape(shape)]

    def take(self):
        self.terms = self.arriving + self.terms
        self.arriving = []

    def send(self, name):
        self.take()
        axis = self.names.index(name)
        self.names.pop(axis)
        here = self.ring.place(name)

        def parts(index):
            return [lax.dynamic_index_in_dim(term, index, axis, False) for term in self.terms]

        self.sent = [added(parts(1 - here))]
        self.terms = parts(here)
        self.arriving = [self.ring.swap(self.sent[0], name)]
        return self

    def sum(self):
        self.take()
        return added(self.terms)


def sent(*flows):
    return [item for flow in flows for item in flow.sent]


def together(items, *flows):
    arrivals = [flow.arriving[0] for flow in flows]
    items = lax.optimization_barrier((*items, *arrivals))
    for flow, arrival in zip(flows, items[len(items) - len(flows) :]):
        flow.arriving = [arrival]
    return items[: len(items) - len(flows)]


def offset_matches(offsets, both_ways):
    matches = bucket_of(offsets, both_ways)[..., None] == jnp.arange(NB, dtype=jnp.int32)
    return matches.astype(jnp.float32)


def on_device(
    ring,
    encoder_input,
    decoder_input,
    encoder_cotangent,
    decoder_cotangent,
    segment_ids,
    padding_mask,
    answer_length,
    encoder_attn_gain,
    encoder_query,
    encoder_key,
    encoder_value,
    encoder_mix,
    encoder_bias_table,
    encoder_ffn_gain,
    encoder_ffn_in,
    encoder_ffn_out,
    final_gain,
    cross_key,
    cross_value,
    decoder_self_gain,
    decoder_query,
    decoder_key,
    decoder_value,
    decoder_mix,
    decoder_bias_table,
    decoder_cross_gain,
    cross_query,
    cross_mix,
    decoder_ffn_gain,
    decoder_ffn_in,
    decoder_ffn_out,
):
    cut = ring.cut
    shard = D // ring.dp
    questions = encoder_input.shape[0]
    batch = questions * encoder_input.shape[1]
    passage_rows = encoder_input.reshape(batch * ROW, D)
    passage_upstream = encoder_cotangent.reshape(batch * ROW, D)
    segments = segment_ids.reshape(batch, ROW)
    segment_row = jnp.where(padding_mask.reshape(batch, ROW) == 1, segments, -1)
    core = ring.place("c")
    row = lax.axis_index("blk") // 2
    place = jnp.stack([core, row, ring.place("x"), ring.place("l")]).astype(jnp.int32)
    other = 1 - place
    gains = wide(
        jnp.stack(
            [
                encoder_attn_gain,
                encoder_ffn_gain,
                final_gain,
                decoder_self_gain,
                decoder_cross_gain,
                decoder_ffn_gain,
            ]
        )
    )
    passage_slopes = jnp.einsum(
        "kn,nh->hk",
        offset_matches(jnp.arange(2 * ROW, dtype=jnp.int32) - ROW, True),
        wide(encoder_bias_table),
        precision=lax.Precision.HIGHEST,
    )
    places = jnp.arange(SLOT, dtype=jnp.int32)
    answer_bias = jnp.einsum(
        "ijn,nh->hij",
        offset_matches(places[None, :] - places[:, None], False),
        wide(decoder_bias_table),
        precision=lax.Precision.HIGHEST,
    ).reshape(H * SLOT, SLOT)

    (
        answer_normed,
        answer_heads,
        answer_chances,
        answer_attended,
        answer_hidden,
        answer_crossed,
        asking,
    ) = answer_start(
        answer_length,
        decoder_input,
        answer_bias,
        gains,
        (decoder_query, decoder_key, decoder_value, decoder_mix, cross_query),
    )
    (
        normed,
        heads,
        chances,
        attended,
        hidden,
        second,
        active,
        bend,
        encoded,
        result,
        final,
        memory,
        scores,
        packed,
    ) = passage(
        passage_rows,
        segment_row,
        segments.T,
        passage_slopes,
        gains,
        asking,
        (
            encoder_query,
            encoder_key,
            encoder_value,
            encoder_mix,
            encoder_ffn_in,
            encoder_ffn_out,
            cross_key,
            cross_value,
        ),
    )
    def neighbours(values):
        if cut:
            return [values] + [ring.swap(values, *names) for names in ("c", "y", "yc")]
        every = lax.all_gather(values, "blk", axis=0)
        return [every[at] for at in range(ring.blk)]

    (
        answer_result,
        answer_lows,
        answer_wides,
        middle_delta,
        answer_gain_delta,
        memory_delta,
        asking_delta,
    ) = answer_middle(
        neighbours(packed),
        asking,
        answer_hidden,
        decoder_cotangent,
        gains,
        scores,
        memory,
        (cross_mix, decoder_ffn_in, decoder_ffn_out),
    )

    asking_deltas = neighbours(asking_delta)
    after = []
    if cut:
        send, keep = answer_wide_weight(
            place, answer_lows, answer_wides, decoder_cotangent, ring.dp
        )
        answer_wide = Flow(ring, send, keep, "x", "hl", (2 * shard, D))
        after = sent(answer_wide)
    memory_send, memory_keep, output_delta, output_low, final_gain_delta = memory_back(
        place,
        gains,
        memory_delta,
        final,
        encoded,
        passage_upstream,
        (cross_key, cross_value),
        active,
        ring.dp,
        after=after,
    )
    if cut:
        memory_flow = Flow(ring, memory_send, memory_keep, "c", "hlxy", (3 * shard // 2, D))
        after = sent(memory_flow) + asking_deltas
    before = wide_out_back(output_low, encoder_ffn_out, bend, after=after)
    if cut:
        (before,) = together([before], memory_flow, answer_wide)
        memory_flow.send("y")
        answer_wide.send("l")
        after = sent(memory_flow, answer_wide)
    in_send, in_keep = wide_in_weight(place, second, before, after=after)
    if cut:
        in_flow = Flow(ring, in_send, in_keep, "c", "yhlx", (shard, D))
        after = sent(in_flow)
    hidden_delta, hidden_low, attended_delta, ffn_gain_delta = wide_in_back(
        gains, before, encoder_ffn_in, hidden, output_delta, encoder_mix, after=after
    )
    if cut:
        (attended_delta,) = together([attended_delta], in_flow, answer_wide)
        in_flow.send("x")
        answer_wide.send("h")
        after = sent(in_flow, answer_wide)
    heads_delta, slope_delta = attend_back(heads, chances, attended_delta, after=after)
    heads_send = heads_weight(other, normed, attended, heads_delta, hidden_low)
    if cut:
        (heads_send,) = together([heads_send], memory_flow, answer_wide)
        heads_flow = Flow(ring, heads_send, heads_send, "c", "yhlx", (shard, D))
        memory_flow.send("x")
        after = sent(heads_flow, memory_flow)
    heads_keep = heads_weight(place, normed, attended, heads_delta, hidden_low, after=after)
    if cut:
        heads_flow.terms = [heads_keep.reshape(heads_flow.terms[0].shape)]
        (heads_keep,) = together([heads_keep], heads_flow)
        heads_flow.send("y")
        after = sent(heads_flow)
    (
        answer_gradient,
        asking_delta,
        answer_hidden_low,
        answer_heads_delta,
        cross_gain_delta,
        self_gain_delta,
        answer_table_delta,
    ) = answer_end(
        asking_deltas,
        middle_delta,
        answer_hidden,
        decoder_input,
        gains,
        answer_heads,
        answer_chances,
        (cross_query, decoder_mix, decoder_query, decoder_key, decoder_value),
        after=after,
    )
    after = []
    if cut:
        send, keep = answer_square_weight(
            place,
            answer_crossed,
            answer_lows,
            answer_attended,
            answer_normed,
            asking_delta,
            answer_hidden_low,
            answer_heads_delta,
            ring.dp,
        )
        (send,) = together([send], in_flow)
        answer_square = Flow(ring, send, keep, "l", "hx", (3 * shard // 2, D))
        in_flow.send("y")
        after = sent(answer_square, in_flow)
    passage_gradient, small = passage_end(
        place,
        gains,
        (
            slope_delta,
            answer_table_delta,
            ffn_gain_delta,
            final_gain_delta,
            self_gain_delta,
            cross_gain_delta,
            answer_gain_delta,
        ),
        passage_rows,
        heads_delta,
        hidden_delta,
        (encoder_query, encoder_key, encoder_value),
        after=after,
    )

    if cut:
        (small,) = together([small], heads_flow, memory_flow, answer_square)
        heads_flow.send("x")
        memory_flow.send("l")
        answer_square.send("h")
    small = ring.total(small)
    mine = lax.axis_index("dp")
    gain_deltas = lax.dynamic_slice_in_dim(small[:6], mine * shard, shard, 1)
    tables = NB // ring.dp
    table_deltas = [
        lax.dynamic_slice_in_dim(small[8 : 8 + H, begin : begin + NB], mine * tables, tables, 1).T
        for begin in (0, 128)
    ]

    if cut:
        weights = cut_weights(
            ring, memory_flow, in_flow, heads_flow, answer_wide, answer_square, small
        )
    else:
        weights = whole_weights(
            core,
            (memory_send, memory_keep),
            (in_send, in_keep),
            (heads_send, heads_keep),
            (
                (answer_lows[1], answer_wides[1]),
                (
                    answer_wides[0],
                    low(slotted(decoder_cotangent)),
                ),
                (answer_crossed, asking_delta),
                (answer_lows[0], answer_lows[2]),
                (answer_attended, answer_hidden_low),
                (answer_normed, answer_heads_delta[0]),
                (answer_normed, answer_heads_delta[1]),
                (answer_normed, answer_heads_delta[2]),
            ),
        )
    (
        gradient_cross_key,
        gradient_cross_value,
        gradient_encoder_ffn_out,
        gradient_encoder_ffn_in,
        gradient_encoder_query,
        gradient_encoder_key,
        gradient_encoder_value,
        gradient_encoder_mix,
        gradient_decoder_ffn_in,
        gradient_decoder_ffn_out,
        gradient_cross_query,
        gradient_cross_mix,
        gradient_decoder_mix,
        gradient_decoder_query,
        gradient_decoder_key,
        gradient_decoder_value,
    ) = [wide(item) for item in weights]
    return (
        result.reshape(encoder_input.shape),
        answer_result,
        passage_gradient.reshape(encoder_input.shape),
        answer_gradient,
        gain_deltas[ATTN],
        gradient_encoder_query,
        gradient_encoder_key,
        gradient_encoder_value,
        gradient_encoder_mix,
        table_deltas[0],
        gain_deltas[FFN],
        gradient_encoder_ffn_in,
        gradient_encoder_ffn_out,
        gain_deltas[FINAL],
        gradient_cross_key,
        gradient_cross_value,
        gain_deltas[SELF],
        gradient_decoder_query,
        gradient_decoder_key,
        gradient_decoder_value,
        gradient_decoder_mix,
        table_deltas[1],
        gain_deltas[CROSS],
        gradient_cross_query,
        gradient_cross_mix,
        gain_deltas[ANSWER],
        gradient_decoder_ffn_in,
        gradient_decoder_ffn_out,
    )


def cut_weights(ring, memory, inner, heads, answer_wide, answer_square, small):
    rows = D // ring.dp
    core = ring.place("c")
    row = lax.axis_index("blk") // 2

    def gathered(mine):
        near = ring.swap(mine, "y")
        pair = jnp.stack([jnp.where(row == 0, mine, near), jnp.where(row == 0, near, mine)])
        far = ring.swap(pair, "c")
        return jnp.stack([jnp.where(core == 0, pair, far), jnp.where(core == 0, far, pair)])

    together([], inner, memory, answer_square)
    inner.send("l")
    memory.send("h")
    answer_square.send("x")
    together([], heads, inner, memory)
    heads.send("l")
    inner.send("h")
    together([], heads, inner, answer_square)
    heads.send("h")
    first = jnp.concatenate(
        [flow.sum() for flow in (memory, answer_wide, answer_square, inner)], axis=0
    )
    first = gathered(first)
    heads = gathered(heads.sum())
    parts = []
    begin = 0
    for size in (rows // 2, rows, rows, rows, rows, rows // 2, rows):
        parts.append(first[:, :, begin : begin + size])
        begin += size
    memory, out, answer_in, answer_out, answer_units, answer_halves, inner = parts

    def side_by_side(units):
        return jnp.concatenate([units[c, y] for c in range(2) for y in range(2)], axis=1)

    def stacked(units):
        return [units[c].reshape(rows, D) for c in range(2)]

    def unhalved(part):
        columns = []
        for c in range(2):
            pieces = [
                part[c, y, :, side : side + D // 2] for y in range(2) for side in (0, D // 2)
            ]
            columns.append(jnp.concatenate(pieces, axis=0))
        return jnp.concatenate(columns, axis=1)

    return (
        *stacked(memory),
        unhalved(out),
        side_by_side(inner),
        *[heads[c, y] for c in range(2) for y in range(2)],
        side_by_side(answer_in),
        unhalved(answer_out),
        *[answer_units[c, y] for c in range(2) for y in range(2)],
        *stacked(answer_halves),
    )


def whole_weights(core, memory, inner, heads, answers):
    def both(pair):
        send, keep = pair
        return (jnp.where(core == 0, keep, send), jnp.where(core == 0, send, keep))

    def shared(gradient):
        return lax.psum_scatter(low(gradient), "dp", scatter_dimension=0, tiled=True)

    def summed(gradient):
        return lax.psum(shared(gradient), "blk")

    memory = both(memory)
    shards, _, rows, _ = memory[0].shape
    cut = rows // 3
    passages = [part[:, :, :cut].reshape(D, D) for part in memory]
    out = [
        part[:, :, cut:]
        .reshape(shards, 2, 2 * cut, 2, D // 2)
        .swapaxes(2, 3)
        .reshape(8 * cut * shards, D // 2)
        for part in memory
    ]
    passages.append(jnp.concatenate(out, axis=1))
    passages.append(jnp.concatenate([unit for half in both(inner) for unit in half], axis=1))
    passages += [unit for half in both(heads) for unit in half]
    return tuple(summed(item) for item in passages) + tuple(
        shared(dot_tokens(inputs, upstream)) for inputs, upstream in answers
    )


def solution(mesh):
    dims = {4: P("dp", "blk", None, None), 3: P("dp", None, None), 2: P("dp", None), 1: P("dp")}
    rows = P("dp", "blk", None)
    return jax.shard_map(
        functools.partial(on_device, Ring(mesh)),
        mesh=mesh,
        in_specs=(dims[4], dims[3], dims[4], dims[3], rows, rows, dims[1]) + (P(),) * 24,
        out_specs=(dims[4], dims[3], dims[4], dims[3])
        + tuple(dims[1 if at in (0, 6, 9, 12, 18, 21) else 2] for at in range(24)),
        check_vma=False,
    )
```

```python
import functools
import math

import jax
import jax.numpy as jnp
from jax import lax
from jax.experimental import pallas as pl
from jax.experimental.pallas import tpu as pltpu
from jax.sharding import PartitionSpec as P

D = 768
H = 12
HD = 64
NB = 32
MAXD = 128
ROW = 256
ANS = 20


EPSILON = 1e-06
NEGATIVE = -1e30


SLOT = 32
ANY = pl.ANY
VM = pltpu.VMEM
BF = jnp.bfloat16
F32 = jnp.float32
LIMIT = 60 << 20


def dot(left, right):
    return jnp.dot(left, right, preferred_element_type=jnp.float32)


def dot_rows(left, right):
    return lax.dot_general(
        left, right, (((1,), (1,)), ((), ())), preferred_element_type=jnp.float32
    )


def dot_tokens(left, right):
    return lax.dot_general(
        left, right, (((0,), (0,)), ((), ())), preferred_element_type=jnp.float32
    )


def low(values):
    return values.astype(jnp.bfloat16)


def wide(values):
    return values.astype(jnp.float32)


def slotted(ref):
    spare = jnp.zeros((SLOT - ANS, D), F32)
    return jnp.concatenate(
        [part for at in range(ref.shape[0]) for part in (wide(ref[at]), spare)], axis=0
    )


def unslotted(values, ref):
    for at in range(ref.shape[0]):
        ref[at] = values[at * SLOT : at * SLOT + ANS].astype(ref.dtype)


ATTN, FFN, FINAL, SELF, CROSS, ANSWER = range(6)


def gain_row(gains_ref, which):
    return gains_ref[which : which + 1, :]


def rms_scale(values):
    return lax.rsqrt(jnp.mean(values * values, axis=-1, keepdims=True) + EPSILON)


def head_lanes(rows, width=D):
    return lax.broadcasted_iota(jnp.int32, (rows, width), 1) // HD


def spread(rows):
    lanes = head_lanes(rows.shape[0])
    values = wide(rows)
    return low(jnp.concatenate([jnp.where(lanes == h, values, 0.0) for h in range(H)], axis=0))


def fold(full):
    rows = full.shape[0] // H
    lanes = head_lanes(rows)
    total = jnp.zeros((rows, full.shape[1]), jnp.float32)
    for h in range(H):
        total = jnp.where(lanes == h, full[h * rows : (h + 1) * rows], total)
    return total


def gelu_pair(values):
    square = values * values
    inner = values * (0.7978845608 + (0.7978845608 * 0.044715) * square)
    half = 0.5 + 0.5 * jnp.tanh(inner)
    active = values * half
    slope = 0.7978845608 + (3.0 * 0.7978845608 * 0.044715) * square
    return (active, half + 2.0 * active * (1.0 - half) * slope)


class Copies:
    def __init__(self, semaphores):
        self.semaphores = semaphores
        self.count = 0
        self.open = []

    def start(self, source, target):
        copy = pltpu.make_async_copy(source, target, self.semaphores.at[self.count])
        self.count += 1
        copy.start()
        return copy

    def out(self, source, target):
        self.open.append(self.start(source, target))

    def finish(self):
        for copy in self.open:
            copy.wait()


def kernel_call(body, operands, spaces, outs, scratch, after=()):
    if after:
        first, *_ = lax.optimization_barrier((operands[0], *after))
        operands = (first, *operands[1:])
    return pl.pallas_call(
        body,
        in_specs=[pl.BlockSpec(memory_space=space) for space in spaces],
        out_specs=[pl.BlockSpec(memory_space=space) for _, _, space in outs],
        out_shape=[jax.ShapeDtypeStruct(shape, dtype) for shape, dtype, _ in outs],
        scratch_shapes=scratch,
        compiler_params=pltpu.CompilerParams(vmem_limit_bytes=LIMIT),
        cost_estimate=pl.CostEstimate(flops=10**13, bytes_accessed=10**9, transcendentals=0),
    )(*operands)


def bucket_of(offsets, both_ways):
    if both_ways:
        buckets = NB // 2
        index = jnp.where(offsets > 0, buckets, 0)
        distance = jnp.abs(offsets)
    else:
        buckets = NB
        index = jnp.zeros_like(offsets)
        distance = jnp.maximum(-offsets, 0)
    exact = buckets // 2
    index = index + jnp.minimum(distance, exact)
    for step in range(1, buckets - exact):
        border = math.ceil(exact * (MAXD / exact) ** (step / (buckets - exact)) - 1e-09)
        index = index + jnp.where(distance >= border, 1, 0)
    return index


def table_slopes(table, width, both_ways, turn):
    offsets = turn * (lax.broadcasted_iota(jnp.int32, (NB, width), 1) - width // 2)
    matches = bucket_of(offsets, both_ways) == lax.broadcasted_iota(jnp.int32, (NB, width), 0)
    return dot(table, low(jnp.where(matches, 1.0, 0.0)))


def slope_bias(slopes, rows):
    width = slopes.shape[1]
    spread_slopes = jnp.broadcast_to(slopes, (rows, width))
    return pltpu.roll(spread_slopes, width // 2, 1, stride=1, stride_axis=0)[:, : width // 2]


def passage_kernel(
    length_ref, answer_input_ref, input_ref, segment_ref, padding_ref, table_ref, answer_table_ref,
    gain_refs,
    answer_query_hbm, answer_key_hbm, answer_value_hbm, answer_mix_hbm, ask_hbm,
    query_hbm, key_hbm, value_hbm, mix_hbm, in_hbm, out_hbm, cross_key_hbm, cross_value_hbm,
    gains_ref, answer_normed_ref, answer_heads_ref, answer_chance_ref, answer_attended_ref,
    answer_hidden_ref, crossed_ref, asking_ref, packed_ref,
    inputs_hbm, heads_hbm, chance_hbm, hidden_hbm, second_hbm,
    active_hbm, bend_hbm, encoded_hbm, result_hbm, final_hbm, memory_hbm, score_hbm,
    answer_square, square, wide_in, wide_out, slopes, arrivals,
    inputs, heads, chance, hidden, second,
    active, bend, memory, score,
):
    copies = Copies(arrivals)
    answer_waits = [
        copies.start(source, answer_square.at[at])
        for at, source in enumerate(
            (answer_query_hbm, answer_key_hbm, answer_value_hbm, answer_mix_hbm, ask_hbm)
        )
    ]
    square_hbm = (query_hbm, key_hbm, value_hbm, mix_hbm)
    waits = [copies.start(source, square.at[at]) for at, source in enumerate(square_hbm)]
    wait_in = copies.start(in_hbm, wide_in)
    wait_out = copies.start(out_hbm, wide_out)
    rows = input_ref.shape[0]
    blocks = rows // ROW
    normed = inputs.at[0]
    attended = inputs.at[1]

    gains = [wide(ref[...]).reshape(1, D) for ref in gain_refs]
    for at, gain in enumerate(gains):
        gains_ref[at : at + 1, :] = gain
    values = wide(input_ref[...])
    normed[...] = low(values * rms_scale(values) * gains[ATTN])
    slopes[...] = table_slopes(table_ref[...], 2 * ROW, True, 1)
    place_row = lax.broadcasted_iota(jnp.int32, (ROW, ROW), 0)
    place_column = lax.broadcasted_iota(jnp.int32, (ROW, ROW), 1)
    for block in range(blocks):
        segment_row = jnp.broadcast_to(segment_ref[block], (ROW, ROW))
        padding_row = jnp.broadcast_to(padding_ref[block], (ROW, ROW))
        own = (segment_row == segment_row.T) & (padding_row == 1)
        score[block, :ROW] = jnp.where(own | (place_row == place_column), 0.0, NEGATIVE)

    answer_values = slotted(answer_input_ref)
    answer_normed = low(answer_values * rms_scale(answer_values) * gains[SELF])
    answer_normed_ref[...] = answer_normed
    for at in range(3):
        answer_waits[at].wait()
        answer_heads_ref[at] = low(dot(answer_normed, answer_square[at]))
    cross_waits = [
        copies.start(source, answer_square.at[at])
        for at, source in enumerate((cross_key_hbm, cross_value_hbm))
    ]
    answer_slopes = table_slopes(answer_table_ref[...], 128, False, 1)
    answer_bias = jnp.concatenate(
        [slope_bias(answer_slopes[h : h + 1], SLOT)[:, :SLOT] for h in range(H)], axis=0
    )
    row = lax.broadcasted_iota(jnp.int32, (H * SLOT, SLOT), 0) % SLOT
    column = lax.broadcasted_iota(jnp.int32, (H * SLOT, SLOT), 1)
    for at in range(blocks):
        slots = slice(at * SLOT, (at + 1) * SLOT)
        asked = spread(answer_heads_ref[0, slots])
        scores = dot_rows(asked, answer_heads_ref[1, slots]) + answer_bias
        allowed = (column <= row) & (column < length_ref[at])
        scores = jnp.where(allowed, scores, NEGATIVE)
        powers = jnp.exp(scores - jnp.max(scores, axis=1, keepdims=True))
        chances = low(powers / jnp.sum(powers, axis=1, keepdims=True))
        answer_chance_ref[at] = chances
        answer_attended_ref[slots] = low(fold(dot(chances, answer_heads_ref[2, slots])))
    answer_waits[3].wait()
    answer_hidden = answer_values + dot(answer_attended_ref[...], answer_square[3])
    answer_hidden_ref[...] = answer_hidden
    crossed = low(answer_hidden * rms_scale(answer_hidden) * gains[CROSS])
    crossed_ref[...] = crossed
    answer_waits[4].wait()
    asking_ref[...] = low(dot(crossed, answer_square[4]))

    for at in range(3):
        waits[at].wait()
        heads[at] = low(dot(normed[...], square[at]))
    heads_out = copies.start(heads, heads_hbm)
    second_half = lax.broadcasted_iota(jnp.int32, (ROW, 2 * HD), 1) >= HD

    for pair in range(H // 2):
        lanes = slice(pair * 2 * HD, (pair + 1) * 2 * HD)
        sums = []
        for which in range(2):
            head = pair * 2 + which
            bias = slope_bias(slopes[head : head + 1, :], ROW)
            for block in range(blocks):
                span = slice(block * ROW, (block + 1) * ROW)
                asked = heads[0, span, lanes]
                own = jnp.where(second_half == (which == 1), asked, jnp.zeros_like(asked))
                scores = dot_rows(own, heads[1, span, lanes]) + (bias + score[block, :ROW])
                powers = jnp.exp(scores - jnp.max(scores, axis=1, keepdims=True))
                chances = low(powers * (1.0 / jnp.sum(powers, axis=1, keepdims=True)))
                chance[head, block] = chances.T
                taken = dot(chances, heads[2, span, lanes])
                if which == 0:
                    sums.append(taken)
                else:
                    attended[span, lanes] = low(jnp.where(second_half, taken, sums[block]))
        part = pl.ds(pair * 2, 2)
        copies.out(chance.at[part], chance_hbm.at[part])

    copies.out(inputs, inputs_hbm)
    waits[3].wait()
    values = wide(input_ref[...]) + dot(attended[...], square[3])
    hidden[...] = values
    hidden_out = copies.start(hidden, hidden_hbm)
    second[...] = low(values * rms_scale(values) * gains[FFN])
    copies.out(second, second_hbm)
    wait_in.wait()
    for at in range(in_hbm.shape[1] // D):
        lanes = slice(at * D, (at + 1) * D)
        up, slope = gelu_pair(dot(second[...], wide_in[:, lanes]))
        active[:, lanes] = low(up)
        bend[:, lanes] = low(slope)
        copies.out(active.at[:, lanes], active_hbm.at[:, lanes])
        copies.out(bend.at[:, lanes], bend_hbm.at[:, lanes])
    wait_out.wait()
    values = hidden[...] + dot(active[...], wide_out[...])
    hidden_out.wait()
    hidden[...] = values
    copies.out(hidden, encoded_hbm)
    heads_out.wait()
    result = heads.at[0]
    final = heads.at[1]
    result[...] = low(values)
    copies.out(result, result_hbm)
    final[...] = low(values * rms_scale(values) * gains[FINAL])
    copies.out(final, final_hbm)
    for at in range(2):
        cross_waits[at].wait()
        memory[at] = low(dot(final[...], answer_square[at]))
    copies.out(memory, memory_hbm)

    lane = lax.broadcasted_iota(jnp.int32, (SLOT, 128), 1)
    for block in range(blocks):
        span = slice(block * ROW, (block + 1) * ROW)
        slots = slice(block * SLOT, (block + 1) * SLOT)
        scores = dot_rows(spread(asking_ref[slots]), memory[0, span])
        scores = jnp.where(padding_ref[block] == 1, scores, NEGATIVE)
        score[block] = scores
        top = jnp.max(scores, axis=1, keepdims=True)
        powers = jnp.exp(scores - top)
        sums = jnp.sum(powers, axis=1, keepdims=True)
        reading = fold(dot(low(powers * (1.0 / sums)), memory[1, span]))
        packed_ref[slots, :D] = low(reading)
        total = top + jnp.log(sums)
        extra = jnp.zeros((SLOT, 128), F32)
        for h in range(H):
            rest = total[h * SLOT : (h + 1) * SLOT]
            for piece in range(3):
                part = wide(low(rest))
                extra = jnp.where(lane == piece * H + h, part, extra)
                rest = rest - part
        packed_ref[slots, D:] = low(extra)
    copies.out(score, score_hbm)
    copies.finish()


def passage(
    length, answer_input, rows, segments, padding, table, answer_table, gains, answer_weights, weights
):
    count = rows.shape[0]
    blocks = count // ROW
    slots = blocks * SLOT
    wide_size = weights[4].shape[1]
    small = [
        ((len(gains), D), F32),
        ((slots, D), BF),
        ((3, slots, D), BF),
        ((blocks, H * SLOT, SLOT), BF),
        ((slots, D), BF),
        ((slots, D), F32),
        ((slots, D), BF),
        ((slots, D), BF),
        ((slots, D + 128), BF),
    ]
    whole = [
        ((2, count, D), BF),
        ((3, count, D), BF),
        ((H, blocks, ROW, ROW), BF),
        ((count, D), F32),
        ((count, D), BF),
        ((count, wide_size), BF),
        ((count, wide_size), BF),
        ((count, D), F32),
        ((count, D), BF),
        ((count, D), BF),
        ((2, count, D), BF),
        ((blocks, H * SLOT, ROW), F32),
    ]
    first = 7

    def body(*refs):
        last = first + len(gains)
        passage_kernel(*refs[:first], refs[first:last], *refs[last:])

    return kernel_call(
        body,
        (length, answer_input, rows, segments, padding, table, answer_table)
        + tuple(gains)
        + tuple(answer_weights)
        + tuple(weights),
        [pltpu.SMEM] + [VM] * (6 + len(gains)) + [ANY] * 13,
        [(shape, dtype, VM) for shape, dtype in small]
        + [(shape, dtype, ANY) for shape, dtype in whole],
        [
            VM((5, D, D), BF),
            VM((4, D, D), BF),
            VM((D, wide_size), BF),
            VM((wide_size, D), BF),
            VM((H, 2 * ROW), F32),
            pltpu.SemaphoreType.DMA((40,)),
        ]
        + [VM(shape, dtype) for at, (shape, dtype) in enumerate(whole) if at not in (7, 8, 9)],
    )


def rms_back(values, gain, upstream):
    scale = rms_scale(values)
    scaled = upstream * gain
    inner = jnp.mean(scaled * values, axis=-1, keepdims=True)
    delta = scaled * scale - values * (scale * scale * scale) * inner
    return (delta, jnp.sum(upstream * values * scale, axis=0, keepdims=True))


def exact_dot(left, right, rows=False):
    return lax.dot_general(
        left,
        right,
        (((1,), (1 if rows else 0,)), ((), ())),
        precision=lax.Precision.HIGHEST,
        preferred_element_type=jnp.float32,
    )


def head_columns(values):
    return jnp.concatenate([values[:, h : h + 1] for h in range(H)], axis=0)


def tree_sum(items):
    while len(items) > 1:
        items = [
            items[at] + items[at + 1] if at + 1 < len(items) else items[at]
            for at in range(0, len(items), 2)
        ]
    return items[0]


def answer_up_kernel(upstream_ref, out_hbm, up_ref, weight, arrivals):
    copies = Copies(arrivals)
    waits = []
    for at in range(out_hbm.shape[0] // D):
        part = pl.ds(at * D, D)
        waits.append(copies.start(out_hbm.at[part], weight.at[part]))
    upstream = low(slotted(upstream_ref))
    for at, wait in enumerate(waits):
        part = slice(at * D, (at + 1) * D)
        wait.wait()
        up_ref[:, part] = dot_rows(upstream, weight[part, :])


def answer_up(upstream, weight):
    return kernel_call(
        answer_up_kernel,
        (upstream, weight),
        [VM, ANY],
        [((upstream.shape[0] * SLOT, weight.shape[0]), F32, VM)],
        [VM(weight.shape, BF), pltpu.SemaphoreType.DMA((4,))],
    )[0]


def answer_middle_kernel(
    every_refs, asking_ref, hidden_ref, up_ref, upstream_ref, gains_ref, score_hbm, memory_hbm,
    mix_hbm, in_hbm,
    low_ref, wide_ref, middle_ref, middle_delta_ref, gain_delta_ref, memory_delta_hbm,
    asking_delta_ref,
    score, memory, memory_delta, mix, wide_in, arrivals,
):
    copies = Copies(arrivals)
    wait_mix = copies.start(mix_hbm, mix)
    wait_in = copies.start(in_hbm, wide_in)
    wait_memory = copies.start(memory_hbm, memory)
    wait_score = copies.start(score_hbm, score)
    count = asking_ref.shape[0]

    from_piece = lax.broadcasted_iota(jnp.int32, (128, 128), 0)
    to_head = lax.broadcasted_iota(jnp.int32, (128, 128), 1)
    same = (from_piece % H == to_head) & (from_piece < 3 * H)
    pieces = low(jnp.where(same, 1.0, 0.0))
    lane_head = lax.broadcasted_iota(jnp.int32, (128, D), 1) // HD
    widen = jnp.where(lane_head == lax.broadcasted_iota(jnp.int32, (128, D), 0), 1.0, 0.0)

    totals = [dot(ref[:, D:], pieces) for ref in every_refs]
    top = functools.reduce(jnp.maximum, totals)
    powers = [jnp.exp(total - top) for total in totals]
    sums = tree_sum(powers)
    reading = tree_sum(
        [
            wide(ref[:, :D]) * exact_dot(power / sums, widen)
            for ref, power in zip(every_refs, powers)
        ]
    )
    whole_total = top + jnp.log(sums)
    reading_low = low(reading)
    low_ref[0] = reading_low
    wait_mix.wait()
    middle = hidden_ref[...] + dot(reading_low, mix[...])
    middle_ref[...] = middle
    gain = gain_row(gains_ref, ANSWER)
    fifth = low(middle * rms_scale(middle) * gain)
    low_ref[1] = fifth
    wait_in.wait()
    for at in range(wide_in.shape[1] // D):
        lanes = slice(at * D, (at + 1) * D)
        active, slope = gelu_pair(dot(fifth, wide_in[:, lanes]))
        wide_ref[0, :, lanes] = low(active)
        wide_ref[1, :, lanes] = low(up_ref[:, lanes] * slope)
    delta, gain_delta = rms_back(middle, gain, dot_rows(wide_ref[1], wide_in[...]))
    gain_delta_ref[...] = gain_delta
    delta += slotted(upstream_ref)
    middle_delta_ref[...] = delta
    delta_low = low(delta)
    low_ref[2] = delta_low
    taken = low(dot_rows(delta_low, mix[...]))
    inner = exact_dot(wide(taken) * reading, widen, rows=True)
    wait_score.wait()
    wait_memory.wait()
    for block in range(count // SLOT):
        slots = slice(block * SLOT, (block + 1) * SLOT)
        span = slice(block * ROW, (block + 1) * ROW)
        chances = jnp.exp(score[block] - head_columns(whole_total[slots]))
        asked = spread(asking_ref[slots])
        upward = spread(taken[slots])
        delta_chances = dot_rows(upward, memory[1, span])
        deltas = low(chances * (delta_chances - head_columns(inner[slots])))
        memory_delta[0, span] = low(dot_tokens(deltas, asked))
        memory_delta[1, span] = low(dot_tokens(low(chances), upward))
        asking_delta_ref[slots] = low(fold(dot(deltas, memory[0, span])))
    copies.out(memory_delta, memory_delta_hbm)
    copies.finish()


def answer_middle(every, asking, hidden, up, upstream, gains, score, memory, weights):
    count = asking.shape[0]
    wide_size = weights[1].shape[1]
    blocks = len(every)

    def body(*refs):
        answer_middle_kernel(refs[:blocks], *refs[blocks:])

    return kernel_call(
        body,
        tuple(every) + (asking, hidden, up, upstream, gains, score, memory) + tuple(weights),
        [VM] * (blocks + 5) + [ANY] * 4,
        [
            ((3, count, D), BF, VM),
            ((2, count, wide_size), BF, VM),
            ((count, D), F32, VM),
            ((count, D), F32, VM),
            ((1, D), F32, VM),
            (memory.shape, BF, ANY),
            ((count, D), BF, VM),
        ],
        [
            VM(score.shape, F32),
            VM(memory.shape, BF),
            VM(memory.shape, BF),
            VM((D, D), BF),
            VM((D, wide_size), BF),
            pltpu.SemaphoreType.DMA((8,)),
        ],
    )


def memory_back_kernel(
    place_ref, gains_ref, delta_hbm, final_hbm, encoded_hbm, upstream_hbm, key_hbm, value_hbm,
    active_hbm, weight_hbm, bend_hbm,
    send_hbm, keep_hbm, output_hbm, before_hbm, gain_delta_ref,
    delta, final, encoded, upstream, weights, active, weight, bend, send, keep, output, before,
    arrivals,
):
    copies = Copies(arrivals)
    shards, rows = send.shape[0], send.shape[2]
    width = D // shards
    half = D // 2
    steps = active.shape[1] // D
    wait_delta = copies.start(delta_hbm, delta)
    waits = [copies.start(key_hbm, weights.at[0]), copies.start(value_hbm, weights.at[1])]
    wait_encoded = copies.start(encoded_hbm, encoded)
    wait_upstream = copies.start(upstream_hbm, upstream)
    wait_final = copies.start(final_hbm, final)
    wait_active = []
    for at in range(steps):
        part = pl.ds(at * D, D)
        wait_active.append(copies.start(active_hbm.at[:, part], active.at[:, part]))
    wait_back = []
    for at in range(steps):
        part = pl.ds(at * D, D)
        wait_back.append(
            [
                copies.start(weight_hbm.at[part], weight.at[part]),
                copies.start(bend_hbm.at[:, part], bend.at[:, part]),
            ]
        )
    core = place_ref[0]
    wait_delta.wait()
    for wait in waits:
        wait.wait()
    upward = dot_rows(delta[0], weights[0]) + dot_rows(delta[1], weights[1])
    wait_encoded.wait()
    wait_upstream.wait()
    back, gain_delta = rms_back(encoded[...], gain_row(gains_ref, FINAL), upward)
    gain_delta_ref[...] = gain_delta
    back += wide(upstream[...])
    output[...] = back
    copies.out(output, output_hbm)
    output_low = low(back)
    wait_final.wait()

    def halves(first, second):
        return (jnp.where(core == 0, second, first), jnp.where(core == 0, first, second))

    units = [dot_tokens(final[...], delta[at]) for at in range(2)]
    for part_ref, first in zip((send, keep), halves(*units)):
        first = low(first)
        for shard in range(shards):
            for row in range(2):
                begin = shard * width + row * (width // 2)
                part_ref[shard, row, : width // 2] = first[begin : begin + width // 2]
    for at in range(steps):
        wait_active[at].wait()
        later = dot_tokens(active[:, at * D : (at + 1) * D], output_low)
        done = pl.ds(at * shards // steps, shards // steps)
        pairs = zip((send, keep), (send_hbm, keep_hbm), halves(later[:, :half], later[:, half:]))
        for part_ref, part_hbm, columns in pairs:
            columns = low(columns)
            for piece in range(D // width):
                shard, place = divmod(at * D // width + piece, 4)
                row, part = divmod(place, 2)
                part_ref[shard, row, width // 2 :, part * half : (part + 1) * half] = columns[
                    piece * width : (piece + 1) * width
                ]
            copies.out(part_ref.at[done], part_hbm.at[done])
    for at in range(steps):
        part = slice(at * D, (at + 1) * D)
        for wait in wait_back[at]:
            wait.wait()
        before[:, part] = low(dot_rows(output_low, weight[part, :]) * wide(bend[:, part]))
        copies.out(before.at[:, part], before_hbm.at[:, part])
    copies.finish()


def memory_back(
    place, gains, delta, final, encoded, upstream, weights, active, weight, bend, shards, after=()
):
    count = final.shape[0]
    wide_size = active.shape[1]
    shape = (shards, 2, 3 * D // shards // 2, D)
    return kernel_call(
        memory_back_kernel,
        (place, gains, delta, final, encoded, upstream)
        + tuple(weights)
        + (active, weight, bend),
        [pltpu.SMEM, VM] + [ANY] * 9,
        [
            (shape, BF, ANY),
            (shape, BF, ANY),
            ((count, D), F32, ANY),
            ((count, wide_size), BF, ANY),
            ((1, D), F32, VM),
        ],
        [
            VM((2, count, D), BF), VM((count, D), BF), VM((count, D), F32), VM((count, D), BF),
            VM((2, D, D), BF), VM((count, wide_size), BF), VM((wide_size, D), BF),
            VM((count, wide_size), BF), VM(shape, BF), VM(shape, BF), VM((count, D), F32),
            VM((count, wide_size), BF), pltpu.SemaphoreType.DMA((40,)),
        ],
        after,
    )


def wide_in_back_kernel(
    place_ref, gains_ref, second_hbm, before_hbm, weight_hbm, hidden_hbm, output_hbm, mix_hbm,
    send_hbm, keep_hbm, hidden_delta_hbm, hidden_low_hbm, attended_delta_hbm, gain_delta_ref,
    second, before, weight, hidden, output, mix, send, keep, hidden_delta, hidden_low,
    attended_delta, arrivals,
):
    copies = Copies(arrivals)
    steps = before.shape[1] // D // 2
    core = place_ref[0]
    wait_second = copies.start(second_hbm, second)
    units = [(1 - core) * steps + at for at in range(steps)]
    units += [core * steps + at for at in range(steps)]
    waits = []
    for unit in units:
        part = pl.ds(pl.multiple_of(unit * D, D), D)
        waits.append(copies.start(before_hbm.at[:, part], before.at[:, part]))
    later = [
        copies.start(source, target)
        for source, target in (
            (weight_hbm, weight), (hidden_hbm, hidden), (output_hbm, output), (mix_hbm, mix)
        )
    ]
    wait_second.wait()
    for at, unit in enumerate(units):
        waits[at].wait()
        part = pl.ds(pl.multiple_of(unit * D, D), D)
        target, target_hbm = (send, send_hbm) if at < steps else (keep, keep_hbm)
        target[at % steps] = low(dot_tokens(second[...], before[:, part]))
        copies.out(target.at[at % steps], target_hbm.at[at % steps])
    for wait in later:
        wait.wait()
    upward = dot_rows(before[...], weight[...])
    back, gain_delta = rms_back(hidden[...], gain_row(gains_ref, FFN), upward)
    gain_delta_ref[...] = gain_delta
    back += output[...]
    hidden_delta[...] = back
    copies.out(hidden_delta, hidden_delta_hbm)
    hidden_low[...] = low(back)
    copies.out(hidden_low, hidden_low_hbm)
    attended_delta[...] = low(dot_rows(hidden_low[...], mix[...]))
    copies.out(attended_delta, attended_delta_hbm)
    copies.finish()


def wide_in_back(place, gains, second, before, weight, hidden, output, mix, after=()):
    count, wide_size = before.shape
    shape = (wide_size // D // 2, D, D)
    return kernel_call(
        wide_in_back_kernel,
        (place, gains, second, before, weight, hidden, output, mix),
        [pltpu.SMEM, VM] + [ANY] * 6,
        [
            (shape, BF, ANY),
            (shape, BF, ANY),
            ((count, D), F32, ANY),
            ((count, D), BF, ANY),
            ((count, D), BF, ANY),
            ((1, D), F32, VM),
        ],
        [
            VM((count, D), BF), VM((count, wide_size), BF), VM((D, wide_size), BF),
            VM((count, D), F32), VM((count, D), F32), VM((D, D), BF), VM(shape, BF),
            VM(shape, BF), VM((count, D), F32), VM((count, D), BF), VM((count, D), BF),
            pltpu.SemaphoreType.DMA((24,)),
        ],
        after,
    )


def attend_back_kernel(
    place_ref, heads_hbm, chance_hbm, upstream_hbm, inputs_hbm, hidden_low_hbm,
    delta_hbm, slope_delta_ref, send_hbm,
    heads, chance, upstream, inputs, delta, gathered, send, arrivals,
):
    copies = Copies(arrivals)
    pairs = H // 2
    waits = []
    for pair in range(pairs):
        lanes = pl.ds(pair * 2 * HD, 2 * HD)
        part = pl.ds(pair * 2, 2)
        waits.append(
            [
                copies.start(heads_hbm.at[:, :, lanes], heads.at[:, :, lanes]),
                copies.start(upstream_hbm.at[:, lanes], upstream.at[:, lanes]),
                copies.start(chance_hbm.at[part], chance.at[part]),
            ]
        )
    wait_inputs = copies.start(inputs_hbm, inputs)
    wait_hidden = copies.start(hidden_low_hbm, delta.at[3])
    blocks = upstream.shape[0] // ROW
    second_half = lax.broadcasted_iota(jnp.int32, (ROW, 2 * HD), 1) >= HD
    place_row = lax.broadcasted_iota(jnp.int32, (ROW, ROW), 0)
    place_column = lax.broadcasted_iota(jnp.int32, (ROW, ROW), 1)
    mirror = low(jnp.where(place_row + place_column == ROW - 1, 1.0, 0.0))

    for pair in range(pairs):
        lanes = slice(pair * 2 * HD, (pair + 1) * 2 * HD)
        for wait in waits[pair]:
            wait.wait()
        kept = []
        for which in range(2):
            head = pair * 2 + which
            for block in range(blocks):
                span = slice(block * ROW, (block + 1) * ROW)
                query, key, value = (heads[at, span, lanes] for at in range(3))
                upward = upstream[span, lanes]
                own = jnp.where(second_half == (which == 1), upward, jnp.zeros_like(upward))
                chances = chance[head, block]
                weight = wide(chances)
                delta_chances = dot_rows(value, own)
                inner = jnp.sum(delta_chances * weight, axis=0, keepdims=True)
                deltas = low(weight * (delta_chances - inner))
                if block == 0:
                    gathered[...] = wide(deltas)
                else:
                    gathered[...] += wide(deltas)
                own_key = key.T[which * HD : (which + 1) * HD]
                news = [low(dot(own_key, deltas)), dot(deltas, query), dot(chances, upward)]
                if which == 0:
                    kept.append(news)
                else:
                    delta[0, span, lanes] = jnp.concatenate([kept[block][0], news[0]], axis=0).T
                    for at in (1, 2):
                        both = jnp.where(second_half, news[at], kept[block][at])
                        delta[at, span, lanes] = low(both)
            whole = gathered[...]
            most = low(whole)
            turned = dot(mirror, most) + dot(mirror, low(whole - wide(most)))
            padded = jnp.concatenate([turned, jnp.zeros((ROW, ROW), F32)], axis=1)
            rolled = pltpu.roll(padded, 1, 1, stride=1, stride_axis=0)
            slope_delta_ref[head : head + 1, :] = jnp.sum(rolled, axis=0, keepdims=True)
        done = pl.ds(pair * 2 * HD, 2 * HD)
        copies.out(delta.at[pl.ds(0, 3), :, done], delta_hbm.at[pl.ds(0, 3), :, done])

    wait_hidden.wait()
    copies.out(delta.at[3], delta_hbm.at[3])
    wait_inputs.wait()
    for at in range(2):
        unit = (1 - place_ref[0]) * 2 + at
        send[at] = low(dot_tokens(inputs[unit // 3], delta[unit]))
        copies.out(send.at[at], send_hbm.at[at])
    copies.finish()


def attend_back(place, heads, chance, upstream, inputs, hidden_low, after=()):
    count = upstream.shape[0]
    return kernel_call(
        attend_back_kernel,
        (place, heads, chance, upstream, inputs, hidden_low),
        [pltpu.SMEM] + [ANY] * 5,
        [((4, count, D), BF, ANY), ((H, 2 * ROW), F32, VM), ((2, D, D), BF, ANY)],
        [
            VM(heads.shape, BF), VM(chance.shape, BF), VM(upstream.shape, BF),
            VM(inputs.shape, BF), VM((4, count, D), BF), VM((ROW, ROW), F32), VM((2, D, D), BF),
            pltpu.SemaphoreType.DMA((32,)),
        ],
        after,
    )


def heads_weight_kernel(place_ref, inputs_hbm, deltas_hbm, part_hbm, inputs, deltas, part, arrivals):
    copies = Copies(arrivals)
    units = [place_ref[0] * 2 + at for at in range(2)]
    waits = [
        (
            copies.start(inputs_hbm.at[unit // 3], inputs.at[at]),
            copies.start(deltas_hbm.at[unit], deltas.at[at]),
        )
        for at, unit in enumerate(units)
    ]
    for at in range(2):
        for wait in waits[at]:
            wait.wait()
        part[at] = low(dot_tokens(inputs[at], deltas[at]))
        copies.out(part.at[at], part_hbm.at[at])
    copies.finish()


def heads_weight(place, inputs, deltas, after=()):
    shape = (2,) + inputs.shape[1:]
    return kernel_call(
        heads_weight_kernel,
        (place, inputs, deltas),
        [pltpu.SMEM] + [ANY] * 2,
        [((2, D, D), BF, ANY)],
        [VM(shape, BF), VM(shape, BF), VM((2, D, D), BF), pltpu.SemaphoreType.DMA((8,))],
        after,
    )[0]


def passage_end_kernel(
    place_ref, gains_ref, slope_delta_ref, answer_table_ref, ffn_gain_ref, final_gain_ref,
    self_gain_ref, cross_gain_ref, answer_gain_ref,
    input_hbm, delta_hbm, hidden_delta_hbm, query_hbm, key_hbm, value_hbm,
    gradient_hbm, small_ref,
    values, delta, hidden_delta, weights, gradient, arrivals,
):
    copies = Copies(arrivals)
    wait_delta = copies.start(delta_hbm.at[pl.ds(0, 3)], delta)
    waits = [
        copies.start(source, weights.at[at])
        for at, source in enumerate((query_hbm, key_hbm, value_hbm))
    ]
    wait_input = copies.start(input_hbm, values)
    wait_hidden = copies.start(hidden_delta_hbm, hidden_delta)
    once = jnp.where((place_ref[0] == 0) & (place_ref[1] == 0), 1.0, 0.0)
    small_ref[...] = jnp.zeros_like(small_ref)
    small_ref[FFN : FFN + 1, :] = ffn_gain_ref[...]
    small_ref[FINAL : FINAL + 1, :] = final_gain_ref[...]
    small_ref[SELF : SELF + 1, :] = self_gain_ref[...] * once
    small_ref[CROSS : CROSS + 1, :] = cross_gain_ref[...] * once
    small_ref[ANSWER : ANSWER + 1, :] = answer_gain_ref[...] * once
    offsets = ROW - lax.broadcasted_iota(jnp.int32, (2 * ROW, 128), 0)
    matches = bucket_of(offsets, True) == lax.broadcasted_iota(jnp.int32, (2 * ROW, 128), 1)
    table = exact_dot(slope_delta_ref[...], jnp.where(matches, 1.0, 0.0))
    small_ref[8 : 8 + H, :128] = table
    small_ref[8 : 8 + H, 128:256] = answer_table_ref[:H, :] * once
    wait_delta.wait()
    for wait in waits:
        wait.wait()
    upward = dot_rows(delta[0], weights[0])
    upward += dot_rows(delta[1], weights[1])
    upward += dot_rows(delta[2], weights[2])
    wait_input.wait()
    wait_hidden.wait()
    back, gain_delta = rms_back(wide(values[...]), gain_row(gains_ref, ATTN), upward)
    small_ref[ATTN : ATTN + 1, :] = gain_delta
    gradient[...] = back + hidden_delta[...]
    copies.out(gradient, gradient_hbm)
    copies.finish()


def passage_end(place, gains, small, rows, delta, hidden_delta, weights, after=()):
    count = rows.shape[0]
    return kernel_call(
        passage_end_kernel,
        (place, gains) + tuple(small) + (rows, delta, hidden_delta) + tuple(weights),
        [pltpu.SMEM] + [VM] * 8 + [ANY] * 6,
        [((count, D), F32, ANY), ((24, D), F32, VM)],
        [
            VM((count, D), BF), VM((3, count, D), BF), VM((count, D), F32), VM((3, D, D), BF),
            VM((count, D), F32), pltpu.SemaphoreType.DMA((8,)),
        ],
        after,
    )


def answer_end_kernel(
    asking_refs, middle_delta_ref, middle_ref, wide_ref, hidden_ref, input_ref, gains_ref,
    heads_ref, chance_ref, ask_hbm, mix_hbm, query_hbm, key_hbm, value_hbm, out_hbm,
    result_ref, gradient_ref, asking_delta_ref, hidden_low_ref, delta_ref, cross_delta_ref,
    self_delta_ref, table_ref,
    weights, wide_out, score_delta, arrivals,
):
    copies = Copies(arrivals)
    waits = [
        copies.start(source, weights.at[at])
        for at, source in enumerate((ask_hbm, mix_hbm, query_hbm, key_hbm, value_hbm))
    ]
    wait_out = copies.start(out_hbm, wide_out)
    asking_delta_ref[...] = low(tree_sum([wide(ref[...]) for ref in asking_refs]))
    waits[0].wait()
    upward = dot_rows(asking_delta_ref[...], weights[0])
    back, gain_delta = rms_back(hidden_ref[...], gain_row(gains_ref, CROSS), upward)
    cross_delta_ref[...] = gain_delta
    back += middle_delta_ref[...]
    hidden_low = low(back)
    hidden_low_ref[...] = hidden_low
    waits[1].wait()
    upward = low(dot_rows(hidden_low, weights[1]))
    column = lax.broadcasted_iota(jnp.int32, (SLOT, 128), 0)
    lane = lax.broadcasted_iota(jnp.int32, (SLOT, 128), 1)
    mirror = low(jnp.where(column + lane == SLOT - 1, 1.0, 0.0))
    for block in range(upward.shape[0] // SLOT):
        slots = slice(block * SLOT, (block + 1) * SLOT)
        chances = chance_ref[block]
        taken = spread(upward[slots])
        delta_chances = dot_rows(taken, heads_ref[2, slots])
        inner = jnp.sum(delta_chances * wide(chances), axis=1, keepdims=True)
        deltas = low(wide(chances) * (delta_chances - inner))
        turned = dot(deltas, mirror)
        if block == 0:
            score_delta[...] = turned
        else:
            score_delta[...] += turned
        delta_ref[0, slots] = low(fold(dot(deltas, heads_ref[1, slots])))
        delta_ref[1, slots] = low(dot_tokens(deltas, spread(heads_ref[0, slots])))
        delta_ref[2, slots] = low(dot_tokens(chances, taken))
    for wait in waits[2:]:
        wait.wait()
    upward = dot_rows(delta_ref[0], weights[2])
    upward += dot_rows(delta_ref[1], weights[3])
    upward += dot_rows(delta_ref[2], weights[4])
    start_delta, gain_delta = rms_back(slotted(input_ref), gain_row(gains_ref, SELF), upward)
    self_delta_ref[...] = gain_delta
    unslotted(start_delta + back, gradient_ref)
    sums = []
    for h in range(H):
        rows = score_delta[h * SLOT : (h + 1) * SLOT]
        rolled = pltpu.roll(rows, 0, 1, stride=1, stride_axis=0)
        sums.append(jnp.sum(rolled, axis=0, keepdims=True))
    sums.append(jnp.zeros((16 - H, 128), F32))
    offsets = (SLOT - 1) - lax.broadcasted_iota(jnp.int32, (128, 128), 0)
    matches = bucket_of(offsets, False) == lax.broadcasted_iota(jnp.int32, (128, 128), 1)
    table_ref[...] = exact_dot(jnp.concatenate(sums, axis=0), jnp.where(matches, 1.0, 0.0))
    wait_out.wait()
    unslotted(middle_ref[...] + dot(wide_ref[0], wide_out[...]), result_ref)


def answer_end(
    asking_deltas, middle_delta, middle, wide_pair, hidden, rows, gains, heads, chance, weights,
    after=()
):
    count = hidden.shape[0]
    blocks = len(asking_deltas)

    def body(*refs):
        answer_end_kernel(refs[:blocks], *refs[blocks:])

    return kernel_call(
        body,
        tuple(asking_deltas)
        + (middle_delta, middle, wide_pair, hidden, rows, gains, heads, chance)
        + tuple(weights),
        [VM] * (blocks + 8) + [ANY] * 6,
        [
            (rows.shape, BF, VM),
            (rows.shape, F32, VM),
            ((count, D), BF, VM),
            ((count, D), BF, VM),
            ((3, count, D), BF, VM),
            ((1, D), F32, VM),
            ((1, D), F32, VM),
            ((16, 128), F32, VM),
        ],
        [
            VM((5, D, D), BF), VM(weights[5].shape, BF), VM((H * SLOT, 128), F32),
            pltpu.SemaphoreType.DMA((6,)),
        ],
        after,
    )


def answer_wide_weight_kernel(
    place_ref, lows_ref, wide_ref, upstream_ref, send_ref, keep_ref, inner, full
):
    core = place_ref[0]
    row = place_ref[1]
    width = send_ref.shape[1] // 2
    half = D // 2
    part = pl.ds(pl.multiple_of((core * 2 + row) * D, D), D)
    inner[...] = low(dot_tokens(lows_ref[1], wide_ref[1, :, part]))
    upstream = slotted(upstream_ref)
    upstream = low(jnp.where(core == 0, upstream[:, :half], upstream[:, half:]))

    for at in range(wide_ref.shape[2] // D):
        span = slice(at * D, (at + 1) * D)
        full[span, :] = low(dot_tokens(wide_ref[0, :, span], upstream))

    for part_ref, sent in ((send_ref, True), (keep_ref, False)):
        for at in range(part_ref.shape[0]):
            own = place_ref[2]
            shard = at * 2 + (1 - own if sent else own)
            rows = pl.ds(pl.multiple_of(shard * width, 16), width)
            part_ref[at, :width] = inner[rows, :]
            for side in range(2):
                begin = shard * 4 * width + row * 2 * width + side * width
                rows = pl.ds(pl.multiple_of(begin, 16), width)
                part_ref[at, width:, side * half : (side + 1) * half] = full[rows, :]


def answer_wide_weight(place, lows, wide_pair, upstream, shards, after=()):
    wide_size = wide_pair.shape[2]
    shape = (shards // 2, 2 * D // shards, D)
    return kernel_call(
        answer_wide_weight_kernel,
        (place, lows, wide_pair, upstream),
        [pltpu.SMEM] + [VM] * 3,
        [(shape, BF, VM), (shape, BF, VM)],
        [VM((D, D), BF), VM((wide_size, D // 2), BF)],
        after,
    )


def answer_square_weight_kernel(
    place_ref, crossed_ref, low_ref, attended_ref, normed_ref, asking_delta_ref, hidden_low_ref,
    delta_ref, send_ref, keep_ref, inputs, deltas, first, full,
):
    core = place_ref[0]
    row = place_ref[1]
    width = send_ref.shape[1] * 2 // 3
    inputs[0] = crossed_ref[...]
    inputs[1] = low_ref[0]
    inputs[2] = attended_ref[...]
    inputs[3] = normed_ref[...]
    deltas[0] = asking_delta_ref[...]
    deltas[1] = low_ref[2]
    deltas[2] = hidden_low_ref[...]
    deltas[3] = delta_ref[0]
    unit = core * 2 + row
    first[...] = low(dot_tokens(inputs[unit], deltas[unit]))
    full[...] = low(dot_tokens(normed_ref[...], delta_ref[1 + core]))
    for part_ref, sent in ((send_ref, True), (keep_ref, False)):
        for at in range(part_ref.shape[0]):
            own = place_ref[3]
            shard = at // 2 * 4 + (1 - own if sent else own) * 2 + at % 2
            rows = pl.ds(pl.multiple_of(shard * width, 16), width)
            part_ref[at, :width] = first[rows, :]
            rows = pl.ds(pl.multiple_of(shard * width + row * (width // 2), 16), width // 2)
            part_ref[at, width:] = full[rows, :]


def answer_square_weight(
    place, crossed, lows, attended, normed, asking_delta, hidden_low, delta, shards, after=()
):
    count = crossed.shape[0]
    shape = (shards // 2, 3 * D // shards // 2, D)
    return kernel_call(
        answer_square_weight_kernel,
        (place, crossed, lows, attended, normed, asking_delta, hidden_low, delta),
        [pltpu.SMEM] + [VM] * 7,
        [(shape, BF, VM), (shape, BF, VM)],
        [VM((4, count, D), BF), VM((4, count, D), BF), VM((D, D), BF), VM((D, D), BF)],
        after,
    )


class Ring:
    def __init__(self, mesh):
        self.dp = mesh.shape["dp"]
        self.blk = mesh.shape["blk"]
        self.cut = self.blk == 4 and self.dp == 8

    def bit(self, name):
        return {"c": 1, "y": 2, "x": 4, "l": 8, "h": 16}[name]

    def number(self):
        return lax.axis_index("dp") * self.blk + lax.axis_index("blk")

    def place(self, name):
        return self.number() // self.bit(name) % 2

    def swap(self, values, *names):
        mask = sum(self.bit(name) for name in names)
        moves = [(at, at ^ mask) for at in range(self.dp * self.blk)]
        return lax.ppermute(values, ("dp", "blk"), moves)


def added(terms):
    return low(functools.reduce(jnp.add, [wide(term) for term in terms]))


class Flow:
    def __init__(self, ring, send, keep, name, names, rest):
        shape = (2,) * len(names) + tuple(rest)
        self.ring = ring
        self.names = list(names)
        self.sent = [send]
        self.terms = [keep.reshape(shape)]
        self.arriving = [ring.swap(send, name).reshape(shape)]

    def take(self):
        self.terms = self.arriving + self.terms
        self.arriving = []

    def send(self, name):
        self.take()
        axis = self.names.index(name)
        self.names.pop(axis)
        here = self.ring.place(name)

        def parts(index):
            return [lax.dynamic_index_in_dim(term, index, axis, False) for term in self.terms]

        self.sent = [added(parts(1 - here))]
        self.terms = parts(here)
        self.arriving = [self.ring.swap(self.sent[0], name)]
        return self

    def sum(self):
        self.take()
        return added(self.terms)


class Total:
    def __init__(self, ring, values):
        self.ring = ring
        self.values = values
        self.arriving = []

    def send(self, name):
        self.sum()
        self.arriving = [self.ring.swap(self.values, name)]

    def sum(self):
        if self.arriving:
            self.values = self.values + self.arriving[0]
        self.arriving = []
        return self.values


class Beside:
    def __init__(self, ring, mine):
        self.ring = ring
        self.row = lax.axis_index("blk") // 2
        self.core = ring.place("c")
        self.mine = mine
        self.arriving = [ring.swap(mine, "y")]

    def paired(self, place, arrival):
        first = place == 0
        return jnp.stack(
            [jnp.where(first, self.mine, arrival), jnp.where(first, arrival, self.mine)]
        )

    def send(self):
        self.mine = self.paired(self.row, self.arriving[0])
        self.arriving = [self.ring.swap(self.mine, "c")]

    def whole(self):
        return self.paired(self.core, self.arriving[0])


def sent(*flows):
    return [item for flow in flows for item in flow.sent]


def together(items, *flows):
    arrivals = [flow.arriving[0] for flow in flows]
    items = lax.optimization_barrier((*items, *arrivals))
    for flow, arrival in zip(flows, items[len(items) - len(flows) :]):
        flow.arriving = [arrival]
    return items[: len(items) - len(flows)]


def on_device(
    ring,
    encoder_input,
    decoder_input,
    encoder_cotangent,
    decoder_cotangent,
    segment_ids,
    padding_mask,
    answer_length,
    encoder_attn_gain,
    encoder_query,
    encoder_key,
    encoder_value,
    encoder_mix,
    encoder_bias_table,
    encoder_ffn_gain,
    encoder_ffn_in,
    encoder_ffn_out,
    final_gain,
    cross_key,
    cross_value,
    decoder_self_gain,
    decoder_query,
    decoder_key,
    decoder_value,
    decoder_mix,
    decoder_bias_table,
    decoder_cross_gain,
    cross_query,
    cross_mix,
    decoder_ffn_gain,
    decoder_ffn_in,
    decoder_ffn_out,
):
    cut = ring.cut
    shard = D // ring.dp
    questions = encoder_input.shape[0]
    batch = questions * encoder_input.shape[1]
    passage_rows = encoder_input.reshape(batch * ROW, D)
    passage_upstream = encoder_cotangent.reshape(batch * ROW, D)
    core = ring.place("c")
    row = lax.axis_index("blk") // 2
    place = jnp.stack([core, row, ring.place("x"), ring.place("l")]).astype(jnp.int32)
    (
        gains,
        answer_normed,
        answer_heads,
        answer_chances,
        answer_attended,
        answer_hidden,
        answer_crossed,
        asking,
        packed,
        inputs,
        heads,
        chances,
        hidden,
        second,
        active,
        bend,
        encoded,
        result,
        final,
        memory,
        scores,
    ) = passage(
        answer_length,
        decoder_input,
        passage_rows,
        segment_ids.reshape(batch, 1, ROW),
        padding_mask.reshape(batch, 1, ROW),
        encoder_bias_table.T,
        decoder_bias_table.T,
        (
            encoder_attn_gain,
            encoder_ffn_gain,
            final_gain,
            decoder_self_gain,
            decoder_cross_gain,
            decoder_ffn_gain,
        ),
        (decoder_query, decoder_key, decoder_value, decoder_mix, cross_query),
        (
            encoder_query,
            encoder_key,
            encoder_value,
            encoder_mix,
            encoder_ffn_in,
            encoder_ffn_out,
            cross_key,
            cross_value,
        ),
    )

    def neighbours(values):
        if cut:
            return [values] + [ring.swap(values, *names) for names in ("c", "y", "yc")]
        every = lax.all_gather(values, "blk", axis=0)
        return [every[at] for at in range(ring.blk)]

    every = neighbours(packed)
    (upstream_cue, _) = lax.optimization_barrier((decoder_cotangent, packed))
    answer_upward = answer_up(upstream_cue, decoder_ffn_out)
    (
        answer_lows,
        answer_wides,
        answer_middle_rows,
        middle_delta,
        answer_gain_delta,
        memory_delta,
        asking_delta,
    ) = answer_middle(
        every,
        asking,
        answer_hidden,
        answer_upward,
        decoder_cotangent,
        gains,
        scores,
        memory,
        (cross_mix, decoder_ffn_in),
    )

    asking_deltas = neighbours(asking_delta)
    after = []
    if cut:
        send, keep = answer_wide_weight(
            place, answer_lows, answer_wides, decoder_cotangent, ring.dp
        )
        answer_wide = Flow(ring, send, keep, "x", "hl", (2 * shard, D))
        after = sent(answer_wide)
    memory_send, memory_keep, output_delta, before, final_gain_delta = memory_back(
        place,
        gains,
        memory_delta,
        final,
        encoded,
        passage_upstream,
        (cross_key, cross_value),
        active,
        encoder_ffn_out,
        bend,
        ring.dp,
        after=after,
    )
    if cut:
        (memory_send, before) = together([memory_send, before], answer_wide)
        memory_flow = Flow(ring, memory_send, memory_keep, "c", "hlxy", (3 * shard // 2, D))
        answer_wide.send("l")
        after = sent(memory_flow, answer_wide) + asking_deltas
    in_send, in_keep, hidden_delta, hidden_low, attended_delta, ffn_gain_delta = wide_in_back(
        place,
        gains,
        second,
        before,
        encoder_ffn_in,
        hidden,
        output_delta,
        encoder_mix,
        after=after,
    )
    if cut:
        (in_send, attended_delta) = together(
            [in_send, attended_delta], memory_flow, answer_wide
        )
        in_flow = Flow(ring, in_send, in_keep, "c", "yhlx", (shard, D))
        memory_flow.send("y")
        answer_wide.send("h")
        after = sent(in_flow, memory_flow, answer_wide)
    heads_delta, slope_delta, heads_send = attend_back(
        place, heads, chances, attended_delta, inputs, hidden_low, after=after
    )
    if cut:
        (heads_send,) = together([heads_send], in_flow, answer_wide)
        heads_flow = Flow(ring, heads_send, heads_send, "c", "yhlx", (shard, D))
        in_flow.send("x")
        after = sent(heads_flow, in_flow)
    heads_keep = heads_weight(place, inputs, heads_delta, after=after)
    if cut:
        heads_flow.terms = [heads_keep.reshape(heads_flow.terms[0].shape)]
        (heads_keep,) = together([heads_keep], heads_flow, memory_flow)
        heads_flow.send("y")
        memory_flow.send("x")
        after = sent(heads_flow, memory_flow)
    (
        answer_result,
        answer_gradient,
        asking_delta,
        answer_hidden_low,
        answer_heads_delta,
        cross_gain_delta,
        self_gain_delta,
        answer_table_delta,
    ) = answer_end(
        asking_deltas,
        middle_delta,
        answer_middle_rows,
        answer_wides,
        answer_hidden,
        decoder_input,
        gains,
        answer_heads,
        answer_chances,
        (
            cross_query,
            decoder_mix,
            decoder_query,
            decoder_key,
            decoder_value,
            decoder_ffn_out,
        ),
        after=after,
    )
    after = []
    if cut:
        send, keep = answer_square_weight(
            place,
            answer_crossed,
            answer_lows,
            answer_attended,
            answer_normed,
            asking_delta,
            answer_hidden_low,
            answer_heads_delta,
            ring.dp,
        )
        (send,) = together([send], in_flow)
        answer_square = Flow(ring, send, keep, "l", "hx", (3 * shard // 2, D))
        in_flow.send("y")
        after = sent(answer_square, in_flow)
    passage_gradient, small = passage_end(
        place,
        gains,
        (
            slope_delta,
            answer_table_delta,
            ffn_gain_delta,
            final_gain_delta,
            self_gain_delta,
            cross_gain_delta,
            answer_gain_delta,
        ),
        passage_rows,
        heads_delta,
        hidden_delta,
        (encoder_query, encoder_key, encoder_value),
        after=after,
    )

    if cut:
        weights, small = cut_weights(
            ring, memory_flow, in_flow, heads_flow, answer_wide, answer_square, small
        )
    else:
        small = lax.psum(small, ("dp", "blk"))
    mine = lax.axis_index("dp")
    gain_deltas = lax.dynamic_slice_in_dim(small[:6], mine * shard, shard, 1)
    tables = NB // ring.dp
    table_deltas = [
        lax.dynamic_slice_in_dim(small[8 : 8 + H, begin : begin + NB], mine * tables, tables, 1).T
        for begin in (0, 128)
    ]

    if not cut:
        weights = whole_weights(
            core,
            (memory_send, memory_keep),
            (in_send, in_keep),
            (heads_send, heads_keep),
            (
                (answer_lows[1], answer_wides[1]),
                (
                    answer_wides[0],
                    low(slotted(decoder_cotangent)),
                ),
                (answer_crossed, asking_delta),
                (answer_lows[0], answer_lows[2]),
                (answer_attended, answer_hidden_low),
                (answer_normed, answer_heads_delta[0]),
                (answer_normed, answer_heads_delta[1]),
                (answer_normed, answer_heads_delta[2]),
            ),
        )
    (
        gradient_cross_key,
        gradient_cross_value,
        gradient_encoder_ffn_out,
        gradient_encoder_ffn_in,
        gradient_encoder_query,
        gradient_encoder_key,
        gradient_encoder_value,
        gradient_encoder_mix,
        gradient_decoder_ffn_in,
        gradient_decoder_ffn_out,
        gradient_cross_query,
        gradient_cross_mix,
        gradient_decoder_mix,
        gradient_decoder_query,
        gradient_decoder_key,
        gradient_decoder_value,
    ) = [wide(item) for item in weights]
    return (
        result.reshape(encoder_input.shape),
        answer_result,
        passage_gradient.reshape(encoder_input.shape),
        answer_gradient,
        gain_deltas[ATTN],
        gradient_encoder_query,
        gradient_encoder_key,
        gradient_encoder_value,
        gradient_encoder_mix,
        table_deltas[0],
        gain_deltas[FFN],
        gradient_encoder_ffn_in,
        gradient_encoder_ffn_out,
        gain_deltas[FINAL],
        gradient_cross_key,
        gradient_cross_value,
        gain_deltas[SELF],
        gradient_decoder_query,
        gradient_decoder_key,
        gradient_decoder_value,
        gradient_decoder_mix,
        table_deltas[1],
        gain_deltas[CROSS],
        gradient_cross_query,
        gradient_cross_mix,
        gain_deltas[ANSWER],
        gradient_decoder_ffn_in,
        gradient_decoder_ffn_out,
    )


def cut_weights(ring, memory, inner, heads, answer_wide, answer_square, small):
    rows = D // ring.dp
    (small,) = together([small], memory)
    small = Total(ring, small)
    memory.send("l")
    small.send("c")
    together([], heads, answer_square, small)
    heads.send("x")
    answer_square.send("h")
    small.send("y")
    together([], inner, memory, small)
    inner.send("l")
    memory.send("h")
    small.send("x")
    together([], heads, inner, answer_square, small)
    heads.send("l")
    inner.send("h")
    answer_square.send("x")
    small.send("l")
    together([], heads, inner, memory, small)
    heads.send("h")
    first = Beside(
        ring, jnp.concatenate([memory.sum(), answer_wide.sum(), inner.sum()], axis=0)
    )
    small.send("h")
    together([], heads, answer_square, first)
    last = Beside(ring, jnp.concatenate([heads.sum(), answer_square.sum()], axis=0))
    first.send()
    together([], last, small)
    last.send()
    first = first.whole()
    last = last.whole()
    parts = []
    begin = 0
    for size in (rows // 2, rows, rows, rows, rows):
        parts.append(first[:, :, begin : begin + size])
        begin += size
    memory, out, answer_in, answer_out, inner = parts
    heads = last[:, :, :rows]
    answer_units = last[:, :, rows : 2 * rows]
    answer_halves = last[:, :, 2 * rows :]

    def side_by_side(units):
        return jnp.concatenate([units[c, y] for c in range(2) for y in range(2)], axis=1)

    def stacked(units):
        return [units[c].reshape(rows, D) for c in range(2)]

    def unhalved(part):
        columns = []
        for c in range(2):
            pieces = [
                part[c, y, :, side : side + D // 2] for y in range(2) for side in (0, D // 2)
            ]
            columns.append(jnp.concatenate(pieces, axis=0))
        return jnp.concatenate(columns, axis=1)

    return (
        *stacked(memory),
        unhalved(out),
        side_by_side(inner),
        *[heads[c, y] for c in range(2) for y in range(2)],
        side_by_side(answer_in),
        unhalved(answer_out),
        *[answer_units[c, y] for c in range(2) for y in range(2)],
        *stacked(answer_halves),
    ), small.sum()


def whole_weights(core, memory, inner, heads, answers):
    def both(pair):
        send, keep = pair
        return (jnp.where(core == 0, keep, send), jnp.where(core == 0, send, keep))

    def shared(gradient):
        return lax.psum_scatter(low(gradient), "dp", scatter_dimension=0, tiled=True)

    def summed(gradient):
        return lax.psum(shared(gradient), "blk")

    memory = both(memory)
    shards, _, rows, _ = memory[0].shape
    cut = rows // 3
    passages = [part[:, :, :cut].reshape(D, D) for part in memory]
    out = [
        part[:, :, cut:]
        .reshape(shards, 2, 2 * cut, 2, D // 2)
        .swapaxes(2, 3)
        .reshape(8 * cut * shards, D // 2)
        for part in memory
    ]
    passages.append(jnp.concatenate(out, axis=1))
    passages.append(jnp.concatenate([unit for half in both(inner) for unit in half], axis=1))
    passages += [unit for half in both(heads) for unit in half]
    return tuple(summed(item) for item in passages) + tuple(
        shared(dot_tokens(inputs, upstream)) for inputs, upstream in answers
    )


def solution(mesh):
    dims = {4: P("dp", "blk", None, None), 3: P("dp", None, None), 2: P("dp", None), 1: P("dp")}
    rows = P("dp", "blk", None)
    return jax.shard_map(
        functools.partial(on_device, Ring(mesh)),
        mesh=mesh,
        in_specs=(dims[4], dims[3], dims[4], dims[3], rows, rows, dims[1]) + (P(),) * 24,
        out_specs=(dims[4], dims[3], dims[4], dims[3])
        + tuple(dims[1 if at in (0, 6, 9, 12, 18, 21) else 2] for at in range(24)),
        check_vma=False,
    )
```

```python
import functools
import math

import jax
import jax.numpy as jnp
from jax import lax
from jax.experimental import pallas as pl
from jax.experimental.pallas import tpu as pltpu
from jax.sharding import PartitionSpec as P

D = 768
H = 12
HD = 64
NB = 32
MAXD = 128
ROW = 256
ANS = 20


EPSILON = 1e-06
NEGATIVE = -1e30


SLOT = 32
ANY = pl.ANY
VM = pltpu.VMEM
BF = jnp.bfloat16
F32 = jnp.float32
LIMIT = 60 << 20


def dot(left, right):
    return jnp.dot(left, right, preferred_element_type=jnp.float32)


def dot_rows(left, right):
    return lax.dot_general(
        left, right, (((1,), (1,)), ((), ())), preferred_element_type=jnp.float32
    )


def dot_tokens(left, right):
    return lax.dot_general(
        left, right, (((0,), (0,)), ((), ())), preferred_element_type=jnp.float32
    )


def low(values):
    return values.astype(jnp.bfloat16)


def wide(values):
    return values.astype(jnp.float32)


def slotted(ref):
    spare = jnp.zeros((SLOT - ANS, D), F32)
    return jnp.concatenate(
        [part for at in range(ref.shape[0]) for part in (wide(ref[at]), spare)], axis=0
    )


def unslotted(values, ref):
    for at in range(ref.shape[0]):
        ref[at] = values[at * SLOT : at * SLOT + ANS].astype(ref.dtype)


ATTN, FFN, FINAL, SELF, CROSS, ANSWER = range(6)


def gain_row(gains_ref, which):
    return gains_ref[which : which + 1, :]


def rms_scale(values):
    return lax.rsqrt(jnp.mean(values * values, axis=-1, keepdims=True) + EPSILON)


def head_lanes(rows, width=D):
    return lax.broadcasted_iota(jnp.int32, (rows, width), 1) // HD


def spread(rows):
    lanes = head_lanes(rows.shape[0])
    values = wide(rows)
    return low(jnp.concatenate([jnp.where(lanes == h, values, 0.0) for h in range(H)], axis=0))


def fold(full):
    rows = full.shape[0] // H
    lanes = head_lanes(rows)
    total = jnp.zeros((rows, full.shape[1]), jnp.float32)
    for h in range(H):
        total = jnp.where(lanes == h, full[h * rows : (h + 1) * rows], total)
    return total


def gelu_pair(values):
    square = values * values
    inner = values * (0.7978845608 + (0.7978845608 * 0.044715) * square)
    half = 0.5 + 0.5 * jnp.tanh(inner)
    active = values * half
    slope = 0.7978845608 + (3.0 * 0.7978845608 * 0.044715) * square
    return (active, half + 2.0 * active * (1.0 - half) * slope)


class Copies:
    def __init__(self, semaphores):
        self.semaphores = semaphores
        self.count = 0
        self.open = []

    def start(self, source, target):
        copy = pltpu.make_async_copy(source, target, self.semaphores.at[self.count])
        self.count += 1
        copy.start()
        return copy

    def out(self, source, target):
        self.open.append(self.start(source, target))

    def finish(self):
        for copy in self.open:
            copy.wait()


def kernel_call(body, operands, spaces, outs, scratch, after=()):
    if after:
        first, *_ = lax.optimization_barrier((operands[0], *after))
        operands = (first, *operands[1:])
    return pl.pallas_call(
        body,
        in_specs=[pl.BlockSpec(memory_space=space) for space in spaces],
        out_specs=[pl.BlockSpec(memory_space=space) for _, _, space in outs],
        out_shape=[jax.ShapeDtypeStruct(shape, dtype) for shape, dtype, _ in outs],
        scratch_shapes=scratch,
        compiler_params=pltpu.CompilerParams(vmem_limit_bytes=LIMIT),
        cost_estimate=pl.CostEstimate(flops=10**13, bytes_accessed=10**9, transcendentals=0),
    )(*operands)


def bucket_of(offsets, both_ways):
    if both_ways:
        buckets = NB // 2
        index = jnp.where(offsets > 0, buckets, 0)
        distance = jnp.abs(offsets)
    else:
        buckets = NB
        index = jnp.zeros_like(offsets)
        distance = jnp.maximum(-offsets, 0)
    exact = buckets // 2
    index = index + jnp.minimum(distance, exact)
    for step in range(1, buckets - exact):
        border = math.ceil(exact * (MAXD / exact) ** (step / (buckets - exact)) - 1e-09)
        index = index + jnp.where(distance >= border, 1, 0)
    return index


def table_slopes(table, width, both_ways, turn):
    offsets = turn * (lax.broadcasted_iota(jnp.int32, (NB, width), 1) - width // 2)
    matches = bucket_of(offsets, both_ways) == lax.broadcasted_iota(jnp.int32, (NB, width), 0)
    return dot(table, low(jnp.where(matches, 1.0, 0.0)))


def slope_bias(slopes, rows):
    width = slopes.shape[1]
    spread_slopes = jnp.broadcast_to(slopes, (rows, width))
    return pltpu.roll(spread_slopes, width // 2, 1, stride=1, stride_axis=0)[:, : width // 2]


def passage_kernel(
    length_ref, answer_input_ref, input_ref, segment_ref, padding_ref, table_ref, answer_table_ref,
    gain_refs,
    answer_query_hbm, answer_key_hbm, answer_value_hbm, answer_mix_hbm, ask_hbm,
    query_hbm, key_hbm, value_hbm, mix_hbm, in_hbm, out_hbm, cross_key_hbm, cross_value_hbm,
    gains_ref, answer_normed_ref, answer_heads_ref, answer_chance_ref, answer_attended_ref,
    answer_hidden_ref, crossed_ref, asking_ref, packed_ref,
    inputs_hbm, heads_hbm, chance_hbm, hidden_hbm, second_hbm,
    active_hbm, bend_hbm, encoded_hbm, result_hbm, final_hbm, memory_hbm, score_hbm,
    answer_square, square, wide_in, wide_out, slopes, arrivals,
    inputs, heads, chance, hidden, second,
    active, bend, memory, score,
):
    copies = Copies(arrivals)
    answer_waits = [
        copies.start(source, answer_square.at[at])
        for at, source in enumerate(
            (answer_query_hbm, answer_key_hbm, answer_value_hbm, answer_mix_hbm, ask_hbm)
        )
    ]
    square_hbm = (query_hbm, key_hbm, value_hbm, mix_hbm)
    waits = [copies.start(source, square.at[at]) for at, source in enumerate(square_hbm)]
    wait_in = copies.start(in_hbm, wide_in)
    wait_out = copies.start(out_hbm, wide_out)
    rows = input_ref.shape[0]
    blocks = rows // ROW
    normed = inputs.at[0]
    attended = inputs.at[1]

    gains = [wide(ref[...]).reshape(1, D) for ref in gain_refs]
    for at, gain in enumerate(gains):
        gains_ref[at : at + 1, :] = gain
    values = wide(input_ref[...])
    normed[...] = low(values * rms_scale(values) * gains[ATTN])
    slopes[...] = table_slopes(table_ref[...], 2 * ROW, True, 1)
    place_row = lax.broadcasted_iota(jnp.int32, (ROW, ROW), 0)
    place_column = lax.broadcasted_iota(jnp.int32, (ROW, ROW), 1)
    for block in range(blocks):
        segment_row = jnp.broadcast_to(segment_ref[block], (ROW, ROW))
        padding_row = jnp.broadcast_to(padding_ref[block], (ROW, ROW))
        own = (segment_row == segment_row.T) & (padding_row == 1)
        score[block, :ROW] = jnp.where(own | (place_row == place_column), 0.0, NEGATIVE)

    answer_values = slotted(answer_input_ref)
    answer_normed = low(answer_values * rms_scale(answer_values) * gains[SELF])
    answer_normed_ref[...] = answer_normed
    for at in range(3):
        answer_waits[at].wait()
        answer_heads_ref[at] = low(dot(answer_normed, answer_square[at]))
    cross_waits = [
        copies.start(source, answer_square.at[at])
        for at, source in enumerate((cross_key_hbm, cross_value_hbm))
    ]
    answer_slopes = table_slopes(answer_table_ref[...], 128, False, 1)
    answer_bias = jnp.concatenate(
        [slope_bias(answer_slopes[h : h + 1], SLOT)[:, :SLOT] for h in range(H)], axis=0
    )
    row = lax.broadcasted_iota(jnp.int32, (H * SLOT, SLOT), 0) % SLOT
    column = lax.broadcasted_iota(jnp.int32, (H * SLOT, SLOT), 1)
    for at in range(blocks):
        slots = slice(at * SLOT, (at + 1) * SLOT)
        asked = spread(answer_heads_ref[0, slots])
        scores = dot_rows(asked, answer_heads_ref[1, slots]) + answer_bias
        allowed = (column <= row) & (column < length_ref[at])
        scores = jnp.where(allowed, scores, NEGATIVE)
        powers = jnp.exp(scores - jnp.max(scores, axis=1, keepdims=True))
        chances = low(powers / jnp.sum(powers, axis=1, keepdims=True))
        answer_chance_ref[at] = chances
        answer_attended_ref[slots] = low(fold(dot(chances, answer_heads_ref[2, slots])))
    answer_waits[3].wait()
    answer_hidden = answer_values + dot(answer_attended_ref[...], answer_square[3])
    answer_hidden_ref[...] = answer_hidden
    crossed = low(answer_hidden * rms_scale(answer_hidden) * gains[CROSS])
    crossed_ref[...] = crossed
    answer_waits[4].wait()
    asking_ref[...] = low(dot(crossed, answer_square[4]))

    for at in range(3):
        waits[at].wait()
        heads[at] = low(dot(normed[...], square[at]))
    heads_out = copies.start(heads, heads_hbm)
    second_half = lax.broadcasted_iota(jnp.int32, (ROW, 2 * HD), 1) >= HD

    for pair in range(H // 2):
        lanes = slice(pair * 2 * HD, (pair + 1) * 2 * HD)
        sums = []
        for which in range(2):
            head = pair * 2 + which
            bias = slope_bias(slopes[head : head + 1, :], ROW)
            for block in range(blocks):
                span = slice(block * ROW, (block + 1) * ROW)
                asked = heads[0, span, lanes]
                own = jnp.where(second_half == (which == 1), asked, jnp.zeros_like(asked))
                scores = dot_rows(own, heads[1, span, lanes]) + (bias + score[block, :ROW])
                powers = jnp.exp(scores - jnp.max(scores, axis=1, keepdims=True))
                chances = low(powers * (1.0 / jnp.sum(powers, axis=1, keepdims=True)))
                chance[head, block] = chances.T
                taken = dot(chances, heads[2, span, lanes])
                if which == 0:
                    sums.append(taken)
                else:
                    attended[span, lanes] = low(jnp.where(second_half, taken, sums[block]))
        part = pl.ds(pair * 2, 2)
        copies.out(chance.at[part], chance_hbm.at[part])

    copies.out(inputs, inputs_hbm)
    waits[3].wait()
    values = wide(input_ref[...]) + dot(attended[...], square[3])
    hidden[...] = values
    hidden_out = copies.start(hidden, hidden_hbm)
    second[...] = low(values * rms_scale(values) * gains[FFN])
    copies.out(second, second_hbm)
    wait_in.wait()
    for at in range(in_hbm.shape[1] // D):
        lanes = slice(at * D, (at + 1) * D)
        up, slope = gelu_pair(dot(second[...], wide_in[:, lanes]))
        active[:, lanes] = low(up)
        bend[:, lanes] = low(slope)
        copies.out(active.at[:, lanes], active_hbm.at[:, lanes])
        copies.out(bend.at[:, lanes], bend_hbm.at[:, lanes])
    wait_out.wait()
    values = hidden[...] + dot(active[...], wide_out[...])
    hidden_out.wait()
    hidden[...] = values
    copies.out(hidden, encoded_hbm)
    heads_out.wait()
    result = heads.at[0]
    final = heads.at[1]
    result[...] = low(values)
    copies.out(result, result_hbm)
    final[...] = low(values * rms_scale(values) * gains[FINAL])
    copies.out(final, final_hbm)
    for at in range(2):
        cross_waits[at].wait()
        memory[at] = low(dot(final[...], answer_square[at]))
    copies.out(memory, memory_hbm)

    lane = lax.broadcasted_iota(jnp.int32, (SLOT, 128), 1)
    for block in range(blocks):
        span = slice(block * ROW, (block + 1) * ROW)
        slots = slice(block * SLOT, (block + 1) * SLOT)
        scores = dot_rows(spread(asking_ref[slots]), memory[0, span])
        scores = jnp.where(padding_ref[block] == 1, scores, NEGATIVE)
        score[block] = scores
        top = jnp.max(scores, axis=1, keepdims=True)
        powers = jnp.exp(scores - top)
        sums = jnp.sum(powers, axis=1, keepdims=True)
        reading = fold(dot(low(powers * (1.0 / sums)), memory[1, span]))
        packed_ref[slots, :D] = low(reading)
        total = top + jnp.log(sums)
        extra = jnp.zeros((SLOT, 128), F32)
        for h in range(H):
            rest = total[h * SLOT : (h + 1) * SLOT]
            for piece in range(3):
                part = wide(low(rest))
                extra = jnp.where(lane == piece * H + h, part, extra)
                rest = rest - part
        packed_ref[slots, D:] = low(extra)
    copies.out(score, score_hbm)
    copies.finish()


def passage(
    length, answer_input, rows, segments, padding, table, answer_table, gains, answer_weights, weights
):
    count = rows.shape[0]
    blocks = count // ROW
    slots = blocks * SLOT
    wide_size = weights[4].shape[1]
    small = [
        ((len(gains), D), F32),
        ((slots, D), BF),
        ((3, slots, D), BF),
        ((blocks, H * SLOT, SLOT), BF),
        ((slots, D), BF),
        ((slots, D), F32),
        ((slots, D), BF),
        ((slots, D), BF),
        ((slots, D + 128), BF),
    ]
    whole = [
        ((2, count, D), BF),
        ((3, count, D), BF),
        ((H, blocks, ROW, ROW), BF),
        ((count, D), F32),
        ((count, D), BF),
        ((count, wide_size), BF),
        ((count, wide_size), BF),
        ((count, D), F32),
        ((count, D), BF),
        ((count, D), BF),
        ((2, count, D), BF),
        ((blocks, H * SLOT, ROW), F32),
    ]
    first = 7

    def body(*refs):
        last = first + len(gains)
        passage_kernel(*refs[:first], refs[first:last], *refs[last:])

    return kernel_call(
        body,
        (length, answer_input, rows, segments, padding, table, answer_table)
        + tuple(gains)
        + tuple(answer_weights)
        + tuple(weights),
        [pltpu.SMEM] + [VM] * (6 + len(gains)) + [ANY] * 13,
        [(shape, dtype, VM) for shape, dtype in small]
        + [(shape, dtype, ANY) for shape, dtype in whole],
        [
            VM((5, D, D), BF),
            VM((4, D, D), BF),
            VM((D, wide_size), BF),
            VM((wide_size, D), BF),
            VM((H, 2 * ROW), F32),
            pltpu.SemaphoreType.DMA((40,)),
        ]
        + [VM(shape, dtype) for at, (shape, dtype) in enumerate(whole) if at not in (7, 8, 9)],
    )


def rms_back(values, gain, upstream):
    scale = rms_scale(values)
    scaled = upstream * gain
    inner = jnp.mean(scaled * values, axis=-1, keepdims=True)
    delta = scaled * scale - values * (scale * scale * scale) * inner
    return (delta, jnp.sum(upstream * values * scale, axis=0, keepdims=True))


def exact_dot(left, right, rows=False):
    return lax.dot_general(
        left,
        right,
        (((1,), (1 if rows else 0,)), ((), ())),
        precision=lax.Precision.HIGHEST,
        preferred_element_type=jnp.float32,
    )


def head_columns(values):
    return jnp.concatenate([values[:, h : h + 1] for h in range(H)], axis=0)


def tree_sum(items):
    while len(items) > 1:
        items = [
            items[at] + items[at + 1] if at + 1 < len(items) else items[at]
            for at in range(0, len(items), 2)
        ]
    return items[0]


def answer_up_kernel(upstream_ref, out_hbm, up_ref, weight, arrivals):
    copies = Copies(arrivals)
    waits = []
    for at in range(out_hbm.shape[0] // D):
        part = pl.ds(at * D, D)
        waits.append(copies.start(out_hbm.at[part], weight.at[part]))
    upstream = low(slotted(upstream_ref))
    for at, wait in enumerate(waits):
        part = slice(at * D, (at + 1) * D)
        wait.wait()
        up_ref[:, part] = dot_rows(upstream, weight[part, :])


def answer_up(upstream, weight):
    return kernel_call(
        answer_up_kernel,
        (upstream, weight),
        [VM, ANY],
        [((upstream.shape[0] * SLOT, weight.shape[0]), F32, VM)],
        [VM(weight.shape, BF), pltpu.SemaphoreType.DMA((4,))],
    )[0]


def answer_middle_kernel(
    every_refs, asking_ref, hidden_ref, up_ref, upstream_ref, gains_ref, score_hbm, memory_hbm,
    mix_hbm, in_hbm,
    low_ref, wide_ref, middle_ref, middle_delta_ref, gain_delta_ref, memory_delta_hbm,
    asking_delta_ref,
    score, memory, memory_delta, mix, wide_in, arrivals,
):
    copies = Copies(arrivals)
    wait_mix = copies.start(mix_hbm, mix)
    wait_in = copies.start(in_hbm, wide_in)
    wait_memory = copies.start(memory_hbm, memory)
    wait_score = copies.start(score_hbm, score)
    count = asking_ref.shape[0]

    from_piece = lax.broadcasted_iota(jnp.int32, (128, 128), 0)
    to_head = lax.broadcasted_iota(jnp.int32, (128, 128), 1)
    same = (from_piece % H == to_head) & (from_piece < 3 * H)
    pieces = low(jnp.where(same, 1.0, 0.0))
    lane_head = lax.broadcasted_iota(jnp.int32, (128, D), 1) // HD
    widen = jnp.where(lane_head == lax.broadcasted_iota(jnp.int32, (128, D), 0), 1.0, 0.0)

    totals = [dot(ref[:, D:], pieces) for ref in every_refs]
    top = functools.reduce(jnp.maximum, totals)
    powers = [jnp.exp(total - top) for total in totals]
    sums = tree_sum(powers)
    reading = tree_sum(
        [
            wide(ref[:, :D]) * exact_dot(power / sums, widen)
            for ref, power in zip(every_refs, powers)
        ]
    )
    whole_total = top + jnp.log(sums)
    reading_low = low(reading)
    low_ref[0] = reading_low
    wait_mix.wait()
    middle = hidden_ref[...] + dot(reading_low, mix[...])
    middle_ref[...] = middle
    gain = gain_row(gains_ref, ANSWER)
    fifth = low(middle * rms_scale(middle) * gain)
    low_ref[1] = fifth
    wait_in.wait()
    for at in range(wide_in.shape[1] // D):
        lanes = slice(at * D, (at + 1) * D)
        active, slope = gelu_pair(dot(fifth, wide_in[:, lanes]))
        wide_ref[0, :, lanes] = low(active)
        wide_ref[1, :, lanes] = low(up_ref[:, lanes] * slope)
    delta, gain_delta = rms_back(middle, gain, dot_rows(wide_ref[1], wide_in[...]))
    gain_delta_ref[...] = gain_delta
    delta += slotted(upstream_ref)
    middle_delta_ref[...] = delta
    delta_low = low(delta)
    low_ref[2] = delta_low
    taken = low(dot_rows(delta_low, mix[...]))
    inner = exact_dot(wide(taken) * reading, widen, rows=True)
    wait_score.wait()
    wait_memory.wait()
    for block in range(count // SLOT):
        slots = slice(block * SLOT, (block + 1) * SLOT)
        span = slice(block * ROW, (block + 1) * ROW)
        chances = jnp.exp(score[block] - head_columns(whole_total[slots]))
        asked = spread(asking_ref[slots])
        upward = spread(taken[slots])
        delta_chances = dot_rows(upward, memory[1, span])
        deltas = low(chances * (delta_chances - head_columns(inner[slots])))
        memory_delta[0, span] = low(dot_tokens(deltas, asked))
        memory_delta[1, span] = low(dot_tokens(low(chances), upward))
        asking_delta_ref[slots] = low(fold(dot(deltas, memory[0, span])))
    copies.out(memory_delta, memory_delta_hbm)
    copies.finish()


def answer_middle(every, asking, hidden, up, upstream, gains, score, memory, weights):
    count = asking.shape[0]
    wide_size = weights[1].shape[1]
    blocks = len(every)

    def body(*refs):
        answer_middle_kernel(refs[:blocks], *refs[blocks:])

    return kernel_call(
        body,
        tuple(every) + (asking, hidden, up, upstream, gains, score, memory) + tuple(weights),
        [VM] * (blocks + 5) + [ANY] * 4,
        [
            ((3, count, D), BF, VM),
            ((2, count, wide_size), BF, VM),
            ((count, D), F32, VM),
            ((count, D), F32, VM),
            ((1, D), F32, VM),
            (memory.shape, BF, ANY),
            ((count, D), BF, VM),
        ],
        [
            VM(score.shape, F32),
            VM(memory.shape, BF),
            VM(memory.shape, BF),
            VM((D, D), BF),
            VM((D, wide_size), BF),
            pltpu.SemaphoreType.DMA((8,)),
        ],
    )


def memory_back_kernel(
    place_ref, gains_ref, delta_hbm, final_hbm, encoded_hbm, upstream_hbm, key_hbm, value_hbm,
    active_hbm, weight_hbm, bend_hbm,
    send_hbm, keep_hbm, output_hbm, before_hbm, gain_delta_ref,
    delta, final, encoded, upstream, weights, active, weight, bend, both, output, before, arrivals,
):
    copies = Copies(arrivals)
    shards = both.shape[1]
    width = D // shards
    half = D // 2
    steps = active.shape[1] // D
    wait_delta = copies.start(delta_hbm, delta)
    waits = [copies.start(key_hbm, weights.at[0]), copies.start(value_hbm, weights.at[1])]
    wait_encoded = copies.start(encoded_hbm, encoded)
    wait_upstream = copies.start(upstream_hbm, upstream)
    wait_final = copies.start(final_hbm, final)
    wait_active = []
    for at in range(steps):
        part = pl.ds(at * D, D)
        wait_active.append(copies.start(active_hbm.at[:, part], active.at[:, part]))
    wait_back = []
    for at in range(steps):
        part = pl.ds(at * D, D)
        wait_back.append(
            [
                copies.start(weight_hbm.at[part], weight.at[part]),
                copies.start(bend_hbm.at[:, part], bend.at[:, part]),
            ]
        )
    core = place_ref[0]
    wait_delta.wait()
    for wait in waits:
        wait.wait()
    upward = dot_rows(delta[0], weights[0]) + dot_rows(delta[1], weights[1])
    wait_encoded.wait()
    wait_upstream.wait()
    back, gain_delta = rms_back(encoded[...], gain_row(gains_ref, FINAL), upward)
    gain_delta_ref[...] = gain_delta
    back += wide(upstream[...])
    output[...] = back
    copies.out(output, output_hbm)
    output_low = low(back)
    wait_final.wait()

    for side in range(2):
        first = low(dot_tokens(final[...], delta[side]))
        for shard in range(shards):
            for row in range(2):
                begin = shard * width + row * (width // 2)
                both[side, shard, row, : width // 2] = first[begin : begin + width // 2]
    for at in range(steps):
        wait_active[at].wait()
        later = low(dot_tokens(active[:, at * D : (at + 1) * D], output_low))
        for side in range(2):
            columns = slice(side * half, (side + 1) * half)
            for piece in range(D // width):
                shard, place = divmod(at * D // width + piece, 4)
                row, part = divmod(place, 2)
                rows = slice(piece * width, (piece + 1) * width)
                lanes = slice(part * half, (part + 1) * half)
                both[side, shard, row, width // 2 :, lanes] = later[rows, columns]
        done = pl.ds(at * shards // steps, shards // steps)
        copies.out(both.at[1 - core, done], send_hbm.at[done])
        copies.out(both.at[core, done], keep_hbm.at[done])
    for at in range(steps):
        part = slice(at * D, (at + 1) * D)
        for wait in wait_back[at]:
            wait.wait()
        before[:, part] = low(dot_rows(output_low, weight[part, :]) * wide(bend[:, part]))
        copies.out(before.at[:, part], before_hbm.at[:, part])
    copies.finish()


def memory_back(
    place, gains, delta, final, encoded, upstream, weights, active, weight, bend, shards, after=()
):
    count = final.shape[0]
    wide_size = active.shape[1]
    shape = (shards, 2, 3 * D // shards // 2, D)
    return kernel_call(
        memory_back_kernel,
        (place, gains, delta, final, encoded, upstream)
        + tuple(weights)
        + (active, weight, bend),
        [pltpu.SMEM, VM] + [ANY] * 9,
        [
            (shape, BF, ANY),
            (shape, BF, ANY),
            ((count, D), F32, ANY),
            ((count, wide_size), BF, ANY),
            ((1, D), F32, VM),
        ],
        [
            VM((2, count, D), BF), VM((count, D), BF), VM((count, D), F32), VM((count, D), BF),
            VM((2, D, D), BF), VM((count, wide_size), BF), VM((wide_size, D), BF),
            VM((count, wide_size), BF), VM((2,) + shape, BF), VM((count, D), F32),
            VM((count, wide_size), BF), pltpu.SemaphoreType.DMA((40,)),
        ],
        after,
    )


def wide_in_back_kernel(
    place_ref, gains_ref, second_hbm, before_hbm, weight_hbm, hidden_hbm, output_hbm, mix_hbm,
    send_hbm, keep_hbm, hidden_delta_hbm, hidden_low_hbm, attended_delta_hbm, gain_delta_ref,
    second, before, weight, hidden, output, mix, send, keep, hidden_delta, hidden_low,
    attended_delta, arrivals,
):
    copies = Copies(arrivals)
    steps = before.shape[1] // D // 2
    core = place_ref[0]
    wait_second = copies.start(second_hbm, second)
    units = [(1 - core) * steps + at for at in range(steps)]
    units += [core * steps + at for at in range(steps)]
    waits = []
    for unit in units:
        part = pl.ds(pl.multiple_of(unit * D, D), D)
        waits.append(copies.start(before_hbm.at[:, part], before.at[:, part]))
    later = [
        copies.start(source, target)
        for source, target in (
            (weight_hbm, weight), (hidden_hbm, hidden), (output_hbm, output), (mix_hbm, mix)
        )
    ]
    wait_second.wait()
    for at, unit in enumerate(units):
        waits[at].wait()
        part = pl.ds(pl.multiple_of(unit * D, D), D)
        target, target_hbm = (send, send_hbm) if at < steps else (keep, keep_hbm)
        target[at % steps] = low(dot_tokens(second[...], before[:, part]))
        copies.out(target.at[at % steps], target_hbm.at[at % steps])
    for wait in later:
        wait.wait()
    upward = dot_rows(before[...], weight[...])
    back, gain_delta = rms_back(hidden[...], gain_row(gains_ref, FFN), upward)
    gain_delta_ref[...] = gain_delta
    back += output[...]
    hidden_delta[...] = back
    copies.out(hidden_delta, hidden_delta_hbm)
    hidden_low[...] = low(back)
    copies.out(hidden_low, hidden_low_hbm)
    attended_delta[...] = low(dot_rows(hidden_low[...], mix[...]))
    copies.out(attended_delta, attended_delta_hbm)
    copies.finish()


def wide_in_back(place, gains, second, before, weight, hidden, output, mix, after=()):
    count, wide_size = before.shape
    shape = (wide_size // D // 2, D, D)
    return kernel_call(
        wide_in_back_kernel,
        (place, gains, second, before, weight, hidden, output, mix),
        [pltpu.SMEM, VM] + [ANY] * 6,
        [
            (shape, BF, ANY),
            (shape, BF, ANY),
            ((count, D), F32, ANY),
            ((count, D), BF, ANY),
            ((count, D), BF, ANY),
            ((1, D), F32, VM),
        ],
        [
            VM((count, D), BF), VM((count, wide_size), BF), VM((D, wide_size), BF),
            VM((count, D), F32), VM((count, D), F32), VM((D, D), BF), VM(shape, BF),
            VM(shape, BF), VM((count, D), F32), VM((count, D), BF), VM((count, D), BF),
            pltpu.SemaphoreType.DMA((24,)),
        ],
        after,
    )


def attend_back_kernel(
    place_ref, heads_hbm, chance_hbm, upstream_hbm, inputs_hbm, hidden_low_hbm,
    delta_hbm, slope_delta_ref, send_hbm, keep_hbm,
    heads, chance, upstream, inputs, delta, gathered, units, arrivals,
):
    copies = Copies(arrivals)
    pairs = H // 2
    waits = []
    for pair in range(pairs):
        lanes = pl.ds(pair * 2 * HD, 2 * HD)
        part = pl.ds(pair * 2, 2)
        waits.append(
            [
                copies.start(heads_hbm.at[:, :, lanes], heads.at[:, :, lanes]),
                copies.start(upstream_hbm.at[:, lanes], upstream.at[:, lanes]),
                copies.start(chance_hbm.at[part], chance.at[part]),
            ]
        )
    wait_inputs = copies.start(inputs_hbm, inputs)
    wait_hidden = copies.start(hidden_low_hbm, delta.at[3])
    blocks = upstream.shape[0] // ROW
    second_half = lax.broadcasted_iota(jnp.int32, (ROW, 2 * HD), 1) >= HD
    place_row = lax.broadcasted_iota(jnp.int32, (ROW, ROW), 0)
    place_column = lax.broadcasted_iota(jnp.int32, (ROW, ROW), 1)
    mirror = low(jnp.where(place_row + place_column == ROW - 1, 1.0, 0.0))

    for pair in range(pairs):
        lanes = slice(pair * 2 * HD, (pair + 1) * 2 * HD)
        for wait in waits[pair]:
            wait.wait()
        kept = []
        for which in range(2):
            head = pair * 2 + which
            for block in range(blocks):
                span = slice(block * ROW, (block + 1) * ROW)
                query, key, value = (heads[at, span, lanes] for at in range(3))
                upward = upstream[span, lanes]
                own = jnp.where(second_half == (which == 1), upward, jnp.zeros_like(upward))
                chances = chance[head, block]
                weight = wide(chances)
                delta_chances = dot_rows(value, own)
                inner = jnp.sum(delta_chances * weight, axis=0, keepdims=True)
                deltas = low(weight * (delta_chances - inner))
                if block == 0:
                    gathered[...] = wide(deltas)
                else:
                    gathered[...] += wide(deltas)
                own_key = key.T[which * HD : (which + 1) * HD]
                news = [low(dot(own_key, deltas)), dot(deltas, query), dot(chances, upward)]
                if which == 0:
                    kept.append(news)
                else:
                    delta[0, span, lanes] = jnp.concatenate([kept[block][0], news[0]], axis=0).T
                    for at in (1, 2):
                        both = jnp.where(second_half, news[at], kept[block][at])
                        delta[at, span, lanes] = low(both)
            whole = gathered[...]
            most = low(whole)
            turned = dot(mirror, most) + dot(mirror, low(whole - wide(most)))
            padded = jnp.concatenate([turned, jnp.zeros((ROW, ROW), F32)], axis=1)
            rolled = pltpu.roll(padded, 1, 1, stride=1, stride_axis=0)
            slope_delta_ref[head : head + 1, :] = jnp.sum(rolled, axis=0, keepdims=True)
        done = pl.ds(pair * 2 * HD, 2 * HD)
        copies.out(delta.at[pl.ds(0, 3), :, done], delta_hbm.at[:, :, done])

    wait_hidden.wait()
    wait_inputs.wait()
    for unit in range(4):
        units[unit // 2, unit % 2] = low(dot_tokens(inputs[unit // 3], delta[unit]))
    copies.out(units.at[1 - place_ref[0]], send_hbm)
    copies.out(units.at[place_ref[0]], keep_hbm)
    copies.finish()


def attend_back(place, heads, chance, upstream, inputs, hidden_low, after=()):
    count = upstream.shape[0]
    return kernel_call(
        attend_back_kernel,
        (place, heads, chance, upstream, inputs, hidden_low),
        [pltpu.SMEM] + [ANY] * 5,
        [
            ((3, count, D), BF, ANY),
            ((H, 2 * ROW), F32, VM),
            ((2, D, D), BF, ANY),
            ((2, D, D), BF, ANY),
        ],
        [
            VM(heads.shape, BF), VM(chance.shape, BF), VM(upstream.shape, BF),
            VM(inputs.shape, BF), VM((4, count, D), BF), VM((ROW, ROW), F32),
            VM((2, 2, D, D), BF), pltpu.SemaphoreType.DMA((36,)),
        ],
        after,
    )


def passage_end_kernel(
    place_ref, gains_ref, slope_delta_ref, answer_table_ref, ffn_gain_ref, final_gain_ref,
    self_gain_ref, cross_gain_ref, answer_gain_ref,
    input_hbm, delta_hbm, hidden_delta_hbm, query_hbm, key_hbm, value_hbm,
    gradient_hbm, small_low_ref,
    values, delta, hidden_delta, weights, gradient, small_ref, arrivals,
):
    copies = Copies(arrivals)
    wait_delta = copies.start(delta_hbm, delta)
    waits = [
        copies.start(source, weights.at[at])
        for at, source in enumerate((query_hbm, key_hbm, value_hbm))
    ]
    wait_input = copies.start(input_hbm, values)
    wait_hidden = copies.start(hidden_delta_hbm, hidden_delta)
    once = jnp.where((place_ref[0] == 0) & (place_ref[1] == 0), 1.0, 0.0)
    small_ref[...] = jnp.zeros_like(small_ref)
    small_ref[FFN : FFN + 1, :] = ffn_gain_ref[...]
    small_ref[FINAL : FINAL + 1, :] = final_gain_ref[...]
    small_ref[SELF : SELF + 1, :] = self_gain_ref[...] * once
    small_ref[CROSS : CROSS + 1, :] = cross_gain_ref[...] * once
    small_ref[ANSWER : ANSWER + 1, :] = answer_gain_ref[...] * once
    offsets = ROW - lax.broadcasted_iota(jnp.int32, (2 * ROW, 128), 0)
    matches = bucket_of(offsets, True) == lax.broadcasted_iota(jnp.int32, (2 * ROW, 128), 1)
    table = exact_dot(slope_delta_ref[...], jnp.where(matches, 1.0, 0.0))
    small_ref[8 : 8 + H, :128] = table
    small_ref[8 : 8 + H, 128:256] = answer_table_ref[:H, :] * once
    wait_delta.wait()
    for wait in waits:
        wait.wait()
    upward = dot_rows(delta[0], weights[0])
    upward += dot_rows(delta[1], weights[1])
    upward += dot_rows(delta[2], weights[2])
    wait_input.wait()
    wait_hidden.wait()
    back, gain_delta = rms_back(wide(values[...]), gain_row(gains_ref, ATTN), upward)
    small_ref[ATTN : ATTN + 1, :] = gain_delta
    small_low_ref[...] = low(small_ref[...])
    gradient[...] = back + hidden_delta[...]
    copies.out(gradient, gradient_hbm)
    copies.finish()


def passage_end(place, gains, small, rows, delta, hidden_delta, weights, after=()):
    count = rows.shape[0]
    return kernel_call(
        passage_end_kernel,
        (place, gains) + tuple(small) + (rows, delta, hidden_delta) + tuple(weights),
        [pltpu.SMEM] + [VM] * 8 + [ANY] * 6,
        [((count, D), F32, ANY), ((32, D), BF, VM)],
        [
            VM((count, D), BF), VM((3, count, D), BF), VM((count, D), F32), VM((3, D, D), BF),
            VM((count, D), F32), VM((32, D), F32), pltpu.SemaphoreType.DMA((8,)),
        ],
        after,
    )


def answer_end_kernel(
    asking_refs, middle_delta_ref, hidden_ref, input_ref, gains_ref,
    heads_ref, chance_ref, ask_hbm, mix_hbm, query_hbm, key_hbm, value_hbm,
    gradient_ref, asking_delta_ref, hidden_low_ref, delta_ref, cross_delta_ref,
    self_delta_ref, table_ref,
    weights, score_delta, arrivals,
):
    copies = Copies(arrivals)
    waits = [
        copies.start(source, weights.at[at])
        for at, source in enumerate((ask_hbm, mix_hbm, query_hbm, key_hbm, value_hbm))
    ]
    asking_delta_ref[...] = low(tree_sum([wide(ref[...]) for ref in asking_refs]))
    waits[0].wait()
    upward = dot_rows(asking_delta_ref[...], weights[0])
    back, gain_delta = rms_back(hidden_ref[...], gain_row(gains_ref, CROSS), upward)
    cross_delta_ref[...] = gain_delta
    back += middle_delta_ref[...]
    hidden_low = low(back)
    hidden_low_ref[...] = hidden_low
    waits[1].wait()
    upward = low(dot_rows(hidden_low, weights[1]))
    column = lax.broadcasted_iota(jnp.int32, (SLOT, 128), 0)
    lane = lax.broadcasted_iota(jnp.int32, (SLOT, 128), 1)
    mirror = low(jnp.where(column + lane == SLOT - 1, 1.0, 0.0))
    for block in range(upward.shape[0] // SLOT):
        slots = slice(block * SLOT, (block + 1) * SLOT)
        chances = chance_ref[block]
        taken = spread(upward[slots])
        delta_chances = dot_rows(taken, heads_ref[2, slots])
        inner = jnp.sum(delta_chances * wide(chances), axis=1, keepdims=True)
        deltas = low(wide(chances) * (delta_chances - inner))
        turned = dot(deltas, mirror)
        if block == 0:
            score_delta[...] = turned
        else:
            score_delta[...] += turned
        delta_ref[0, slots] = low(fold(dot(deltas, heads_ref[1, slots])))
        delta_ref[1, slots] = low(dot_tokens(deltas, spread(heads_ref[0, slots])))
        delta_ref[2, slots] = low(dot_tokens(chances, taken))
    for wait in waits[2:]:
        wait.wait()
    upward = dot_rows(delta_ref[0], weights[2])
    upward += dot_rows(delta_ref[1], weights[3])
    upward += dot_rows(delta_ref[2], weights[4])
    start_delta, gain_delta = rms_back(slotted(input_ref), gain_row(gains_ref, SELF), upward)
    self_delta_ref[...] = gain_delta
    unslotted(start_delta + back, gradient_ref)
    sums = []
    for h in range(H):
        rows = score_delta[h * SLOT : (h + 1) * SLOT]
        rolled = pltpu.roll(rows, 0, 1, stride=1, stride_axis=0)
        sums.append(jnp.sum(rolled, axis=0, keepdims=True))
    sums.append(jnp.zeros((16 - H, 128), F32))
    offsets = (SLOT - 1) - lax.broadcasted_iota(jnp.int32, (128, 128), 0)
    matches = bucket_of(offsets, False) == lax.broadcasted_iota(jnp.int32, (128, 128), 1)
    table_ref[...] = exact_dot(jnp.concatenate(sums, axis=0), jnp.where(matches, 1.0, 0.0))


def answer_out_kernel(middle_ref, wide_ref, out_hbm, result_ref, weight, arrivals):
    copies = Copies(arrivals)
    waits = []
    for at in range(out_hbm.shape[0] // D):
        part = pl.ds(at * D, D)
        waits.append(copies.start(out_hbm.at[part], weight.at[part]))
    total = middle_ref[...]
    for at, wait in enumerate(waits):
        part = slice(at * D, (at + 1) * D)
        wait.wait()
        total += dot(wide_ref[0, :, part], weight[part, :])
    unslotted(total, result_ref)


def answer_out(middle, wide_pair, weight, like, after=()):
    return kernel_call(
        answer_out_kernel,
        (middle, wide_pair, weight),
        [VM, VM, ANY],
        [(like.shape, BF, VM)],
        [VM(weight.shape, BF), pltpu.SemaphoreType.DMA((4,))],
        after,
    )[0]


def answer_end(
    asking_deltas, middle_delta, hidden, rows, gains, heads, chance, weights, after=()
):
    count = hidden.shape[0]
    blocks = len(asking_deltas)

    def body(*refs):
        answer_end_kernel(refs[:blocks], *refs[blocks:])

    return kernel_call(
        body,
        tuple(asking_deltas)
        + (middle_delta, hidden, rows, gains, heads, chance)
        + tuple(weights),
        [VM] * (blocks + 6) + [ANY] * 5,
        [
            (rows.shape, F32, VM),
            ((count, D), BF, VM),
            ((count, D), BF, VM),
            ((3, count, D), BF, VM),
            ((1, D), F32, VM),
            ((1, D), F32, VM),
            ((16, 128), F32, VM),
        ],
        [
            VM((5, D, D), BF), VM((H * SLOT, 128), F32), pltpu.SemaphoreType.DMA((5,)),
        ],
        after,
    )


def answer_wide_weight_kernel(
    place_ref, lows_ref, wide_ref, upstream_ref, send_ref, keep_ref, inner, full
):
    core = place_ref[0]
    row = place_ref[1]
    width = send_ref.shape[1] // 2
    half = D // 2
    part = pl.ds(pl.multiple_of((core * 2 + row) * D, D), D)
    inner[...] = low(dot_tokens(lows_ref[1], wide_ref[1, :, part]))
    upstream = slotted(upstream_ref)
    upstream = low(jnp.where(core == 0, upstream[:, :half], upstream[:, half:]))

    for at in range(wide_ref.shape[2] // D):
        span = slice(at * D, (at + 1) * D)
        full[span, :] = low(dot_tokens(wide_ref[0, :, span], upstream))

    for part_ref, sent in ((send_ref, True), (keep_ref, False)):
        for at in range(part_ref.shape[0]):
            own = place_ref[2]
            shard = at * 2 + (1 - own if sent else own)
            rows = pl.ds(pl.multiple_of(shard * width, 16), width)
            part_ref[at, :width] = inner[rows, :]
            for side in range(2):
                begin = shard * 4 * width + row * 2 * width + side * width
                rows = pl.ds(pl.multiple_of(begin, 16), width)
                part_ref[at, width:, side * half : (side + 1) * half] = full[rows, :]


def answer_wide_weight(place, lows, wide_pair, upstream, shards, after=()):
    wide_size = wide_pair.shape[2]
    shape = (shards // 2, 2 * D // shards, D)
    return kernel_call(
        answer_wide_weight_kernel,
        (place, lows, wide_pair, upstream),
        [pltpu.SMEM] + [VM] * 3,
        [(shape, BF, VM), (shape, BF, VM)],
        [VM((D, D), BF), VM((wide_size, D // 2), BF)],
        after,
    )


def answer_square_weight_kernel(
    place_ref, crossed_ref, low_ref, attended_ref, normed_ref, asking_delta_ref, hidden_low_ref,
    delta_ref, send_ref, keep_ref, inputs, deltas, first, full,
):
    core = place_ref[0]
    row = place_ref[1]
    width = send_ref.shape[1] * 2 // 3
    inputs[0] = crossed_ref[...]
    inputs[1] = low_ref[0]
    inputs[2] = attended_ref[...]
    inputs[3] = normed_ref[...]
    deltas[0] = asking_delta_ref[...]
    deltas[1] = low_ref[2]
    deltas[2] = hidden_low_ref[...]
    deltas[3] = delta_ref[0]
    unit = core * 2 + row
    first[...] = low(dot_tokens(inputs[unit], deltas[unit]))
    full[...] = low(dot_tokens(normed_ref[...], delta_ref[1 + core]))
    for part_ref, sent in ((send_ref, True), (keep_ref, False)):
        for at in range(part_ref.shape[0]):
            own = place_ref[3]
            shard = at // 2 * 4 + (1 - own if sent else own) * 2 + at % 2
            rows = pl.ds(pl.multiple_of(shard * width, 16), width)
            part_ref[at, :width] = first[rows, :]
            rows = pl.ds(pl.multiple_of(shard * width + row * (width // 2), 16), width // 2)
            part_ref[at, width:] = full[rows, :]


def answer_square_weight(
    place, crossed, lows, attended, normed, asking_delta, hidden_low, delta, shards, after=()
):
    count = crossed.shape[0]
    shape = (shards // 2, 3 * D // shards // 2, D)
    return kernel_call(
        answer_square_weight_kernel,
        (place, crossed, lows, attended, normed, asking_delta, hidden_low, delta),
        [pltpu.SMEM] + [VM] * 7,
        [(shape, BF, VM), (shape, BF, VM)],
        [VM((4, count, D), BF), VM((4, count, D), BF), VM((D, D), BF), VM((D, D), BF)],
        after,
    )


class Part:
    def __init__(self, rows, left, first=0):
        self.rows = rows
        self.left = list(left)
        self.first = first
        self.terms = []

    def array(self, values, names):
        values = values.reshape((2,) * len(names) + (-1, values.shape[-1]))
        self.terms.append((values, list(names), None))
        return self

    def size(self, name):
        count = len([one for one in self.left if one != name])
        return (2**count) * self.rows if name else self.rows

    def sent(self, name, values, begin):
        self.left.remove(name)


class Total(Part):
    def __init__(self, values):
        super().__init__(values.shape[0], "")
        self.terms.append((values, [], 0))

    def size(self, name):
        return self.rows

    def sent(self, name, values, begin):
        self.terms = [(values, [], begin)]


PLACES = "cyxlh"


def bus(place, jobs, after=()):
    arrays = []
    plans = []
    scratch = []
    outs = []
    for name, parts in jobs:
        begin = 0
        for part in parts:
            kept = [one for one in part.left if one != name] if name else []
            for values, names, start in part.terms:
                at = [id(one) for one in arrays]
                if id(values) not in at:
                    arrays.append(values)
                    at.append(id(values))
                inner = [one for one in names if one in kept]
                room = (2,) * len(inner) + (part.rows, D) if start is None else (
                    (2 ** len(inner)) * part.rows, D
                )
                plans.append(
                    (len(outs), begin, at.index(id(values)), names, start, inner, part, kept, name)
                )
                scratch.append(VM(room, BF))
            begin += part.size(name)
        outs.append(((begin, D), BF, VM))
    count = len(arrays)

    def body(place_ref, *refs):
        sources, targets = refs[:count], refs[count : count + len(outs)]
        rooms, semaphores = refs[count + len(outs) : -1], refs[-1]
        copies = Copies(semaphores)

        def spot(one, part, name):
            own = place_ref[PLACES.index(one)]
            return 1 - own if one == name else own

        waits = []
        for room, (_, _, source, names, start, inner, part, kept, name) in zip(rooms, plans):
            if start is None:
                index = [
                    slice(None) if one in kept else spot(one, part, name) for one in names
                ]
                origin = sources[source].at[(*index, pl.ds(part.first, part.rows))]
            else:
                row = start
                for depth, one in enumerate(names):
                    if one not in kept:
                        stride = (2 ** (len(names) - 1 - depth)) * part.rows
                        row = row + spot(one, part, name) * stride
                length = (2 ** len(inner)) * part.rows
                origin = sources[source].at[pl.ds(pl.multiple_of(row, 16), length)]
            waits.append(copies.start(origin, room))
        for wait in waits:
            wait.wait()
        sums = {}
        for room, (out, begin, _, _, start, inner, part, kept, name) in zip(rooms, plans):
            for number in range(2 ** len(kept)):
                bits = [number >> (len(kept) - 1 - depth) & 1 for depth in range(len(kept))]
                at = dict(zip(kept, bits))
                if start is None:
                    value = room[tuple(at[one] for one in inner)] if inner else room[...]
                else:
                    value = room[number * part.rows : (number + 1) * part.rows]
                sums.setdefault((out, begin + number * part.rows, part.rows), []).append(value)
        for (out, begin, rows), values in sums.items():
            total = functools.reduce(jnp.add, [wide(value) for value in values])
            targets[out][begin : begin + rows] = low(total)

    return kernel_call(
        body,
        (place, *arrays),
        [pltpu.SMEM] + [ANY] * count,
        outs,
        scratch + [pltpu.SemaphoreType.DMA((len(plans),))],
        after,
    )


def ride(ring, place, jobs, after=()):
    sends = list(bus(place, jobs, after))
    trip = []
    for (name, parts), values in zip(jobs, sends):
        begin = 0
        stops = []
        for part in parts:
            length = part.size(name)
            part.sent(name, values, begin)
            stops.append((part, begin, list(part.left)))
            begin += length
        trip.append([ring.swap(values, name), stops])
    return trip, sends


def arrive(items, *trips):
    legs = [leg for trip in trips for leg in trip]
    items = lax.optimization_barrier((*items, *[leg[0] for leg in legs]))
    count = len(items) - len(legs)
    for values, (_, stops) in zip(items[count:], legs):
        for part, begin, names in stops:
            part.terms.append((values, names, begin))
    return items[:count]


def assemble_kernel(place_ref, mine_hbm, near_hbm, far_hbm, across_hbm, *refs, lay):
    outs, whole, arrivals = refs[:-2], refs[-2], refs[-1]
    copies = Copies(arrivals)
    core, row = place_ref[0], place_ref[1]
    waits = [
        copies.start(mine_hbm, whole.at[core, row]),
        copies.start(near_hbm, whole.at[core, 1 - row]),
        copies.start(far_hbm, whole.at[1 - core, row]),
        copies.start(across_hbm, whole.at[1 - core, 1 - row]),
    ]
    for wait in waits:
        wait.wait()
    for out, rows, columns, part in lay:
        c, y, begin, lanes = part
        height, width = rows[1] - rows[0], columns[1] - columns[0]
        outs[out][rows[0] : rows[1], columns[0] : columns[1]] = wide(
            whole[c, y, begin : begin + height, lanes : lanes + width]
        )


def assemble(place, arrays, shapes, lay):
    rows = arrays[0].shape[0]
    return kernel_call(
        functools.partial(assemble_kernel, lay=lay),
        (place, *arrays),
        [pltpu.SMEM] + [ANY] * 4,
        [(shape, F32, VM) for shape in shapes],
        [VM((2, 2, rows, D), BF), pltpu.SemaphoreType.DMA((4,))],
    )


def layout(rows):
    half = D // 2
    lay = []
    shapes = []

    def stacked(begin):
        for c in range(2):
            for y in range(2):
                at = (y * rows // 2, (y + 1) * rows // 2)
                lay.append((len(shapes), at, (0, D), (c, y, begin, 0)))
            shapes.append((rows, D))

    def unhalved(begin):
        for c in range(2):
            for y in range(2):
                for side in range(2):
                    low_row = (y * 2 + side) * rows
                    lay.append(
                        (
                            len(shapes),
                            (low_row, low_row + rows),
                            (c * half, (c + 1) * half),
                            (c, y, begin, side * half),
                        )
                    )
        shapes.append((4 * rows, D))

    def side_by_side(begin):
        for c in range(2):
            for y in range(2):
                at = c * 2 + y
                lay.append((len(shapes), (0, rows), (at * D, (at + 1) * D), (c, y, begin, 0)))
        shapes.append((rows, 4 * D))

    def units(begin):
        for c in range(2):
            for y in range(2):
                lay.append((len(shapes), (0, rows), (0, D), (c, y, begin, 0)))
                shapes.append((rows, D))

    return lay, shapes, stacked, unhalved, side_by_side, units


class Ring:
    def __init__(self, mesh):
        self.dp = mesh.shape["dp"]
        self.blk = mesh.shape["blk"]
        self.cut = self.blk == 4 and self.dp == 8

    def bit(self, name):
        return {"c": 1, "y": 2, "x": 4, "l": 8, "h": 16}[name]

    def number(self):
        return lax.axis_index("dp") * self.blk + lax.axis_index("blk")

    def place(self, name):
        return self.number() // self.bit(name) % 2

    def swap(self, values, *names):
        mask = sum(self.bit(name) for name in names)
        moves = [(at, at ^ mask) for at in range(self.dp * self.blk)]
        return lax.ppermute(values, ("dp", "blk"), moves)


class Beside:
    def __init__(self, ring, mine):
        self.ring = ring
        self.mine = mine
        self.arriving = [ring.swap(mine, "y"), ring.swap(mine, "c")]

    def send(self, cues=()):
        near, far, *_ = lax.optimization_barrier((*self.arriving, *cues))
        self.arriving = [near, far, self.ring.swap(near, "c")]

    def arrays(self, cues=()):
        near, far, across, *_ = lax.optimization_barrier((*self.arriving, *cues))
        return [self.mine, near, far, across]


def on_device(
    ring,
    encoder_input,
    decoder_input,
    encoder_cotangent,
    decoder_cotangent,
    segment_ids,
    padding_mask,
    answer_length,
    encoder_attn_gain,
    encoder_query,
    encoder_key,
    encoder_value,
    encoder_mix,
    encoder_bias_table,
    encoder_ffn_gain,
    encoder_ffn_in,
    encoder_ffn_out,
    final_gain,
    cross_key,
    cross_value,
    decoder_self_gain,
    decoder_query,
    decoder_key,
    decoder_value,
    decoder_mix,
    decoder_bias_table,
    decoder_cross_gain,
    cross_query,
    cross_mix,
    decoder_ffn_gain,
    decoder_ffn_in,
    decoder_ffn_out,
):
    cut = ring.cut
    shard = D // ring.dp
    questions = encoder_input.shape[0]
    batch = questions * encoder_input.shape[1]
    passage_rows = encoder_input.reshape(batch * ROW, D)
    passage_upstream = encoder_cotangent.reshape(batch * ROW, D)
    core = ring.place("c")
    row = lax.axis_index("blk") // 2
    place = [core, row, ring.place("x"), ring.place("l"), ring.place("h")]
    place = jnp.stack(place).astype(jnp.int32)
    (
        gains,
        answer_normed,
        answer_heads,
        answer_chances,
        answer_attended,
        answer_hidden,
        answer_crossed,
        asking,
        packed,
        inputs,
        heads,
        chances,
        hidden,
        second,
        active,
        bend,
        encoded,
        result,
        final,
        memory,
        scores,
    ) = passage(
        answer_length,
        decoder_input,
        passage_rows,
        segment_ids.reshape(batch, 1, ROW),
        padding_mask.reshape(batch, 1, ROW),
        encoder_bias_table.T,
        decoder_bias_table.T,
        (
            encoder_attn_gain,
            encoder_ffn_gain,
            final_gain,
            decoder_self_gain,
            decoder_cross_gain,
            decoder_ffn_gain,
        ),
        (decoder_query, decoder_key, decoder_value, decoder_mix, cross_query),
        (
            encoder_query,
            encoder_key,
            encoder_value,
            encoder_mix,
            encoder_ffn_in,
            encoder_ffn_out,
            cross_key,
            cross_value,
        ),
    )

    def neighbours(values):
        if cut:
            return [values] + [ring.swap(values, *names) for names in ("c", "y", "yc")]
        every = lax.all_gather(values, "blk", axis=0)
        return [every[at] for at in range(ring.blk)]

    every = neighbours(packed)
    (upstream_cue, _) = lax.optimization_barrier((decoder_cotangent, packed))
    answer_upward = answer_up(upstream_cue, decoder_ffn_out)
    (
        answer_lows,
        answer_wides,
        answer_middle_rows,
        middle_delta,
        answer_gain_delta,
        memory_delta,
        asking_delta,
    ) = answer_middle(
        every,
        asking,
        answer_hidden,
        answer_upward,
        decoder_cotangent,
        gains,
        scores,
        memory,
        (cross_mix, decoder_ffn_in),
    )

    asking_deltas = neighbours(asking_delta)
    after = []
    if cut:
        half = shard // 2
        send, keep = answer_wide_weight(
            place, answer_lows, answer_wides, decoder_cotangent, ring.dp
        )
        answer_wide = Part(2 * shard, "lh").array(keep, "hl")
        wide_trip = [[ring.swap(send, "x").reshape(2, 2, 2 * shard, D), []]]
        after = [send]
    memory_send, memory_keep, output_delta, before, final_gain_delta = memory_back(
        place,
        gains,
        memory_delta,
        final,
        encoded,
        passage_upstream,
        (cross_key, cross_value),
        active,
        encoder_ffn_out,
        bend,
        ring.dp,
        after=after,
    )
    if cut:
        (memory_send, cue) = arrive([memory_send, place], wide_trip)
        answer_wide.array(wide_trip[0][0], "hl")
        memory_got = ring.swap(memory_send, "c")
        trip, sends = ride(ring, cue, [("l", [answer_wide])])
        after = sends + [memory_send] + asking_deltas
    (
        answer_gradient,
        asking_delta,
        answer_hidden_low,
        answer_heads_delta,
        cross_gain_delta,
        self_gain_delta,
        answer_table_delta,
    ) = answer_end(
        asking_deltas,
        middle_delta,
        answer_hidden,
        decoder_input,
        gains,
        answer_heads,
        answer_chances,
        (cross_query, decoder_mix, decoder_query, decoder_key, decoder_value),
        after=after,
    )
    after = []
    if cut:
        send, keep = answer_square_weight(
            place,
            answer_crossed,
            answer_lows,
            answer_attended,
            answer_normed,
            asking_delta,
            answer_hidden_low,
            answer_heads_delta,
            ring.dp,
        )
        send, memory_got, cue = arrive([send, memory_got, place], trip)
        answer_square = Part(3 * half, "hx").array(keep, "hx")
        square_got = ring.swap(send, "l")
        top = 4 * 16
        memory_first = Part(top, "yxlh").array(memory_keep, "hlxy").array(memory_got, "hlxy")
        memory_second = Part(3 * half - top, "xylh", top)
        memory_second.array(memory_keep, "hlxy").array(memory_got, "hlxy")
        trip_memory, sends = ride(
            ring, cue, [("y", [memory_first]), ("x", [memory_second]), ("h", [answer_wide])]
        )
        after = sends + [send]
    in_send, in_keep, hidden_delta, hidden_low, attended_delta, ffn_gain_delta = wide_in_back(
        place,
        gains,
        second,
        before,
        encoder_ffn_in,
        hidden,
        output_delta,
        encoder_mix,
        after=after,
    )
    after = []
    if cut:
        in_send, attended_delta = arrive([in_send, attended_delta], trip_memory)
        in_got = ring.swap(in_send, "c")
        after = [in_send]
    answer_result = answer_out(
        answer_middle_rows, answer_wides, decoder_ffn_out, decoder_input, after=after
    )
    after = []
    if cut:
        answer_result, attended_delta, in_got, square_got, cue = lax.optimization_barrier(
            (answer_result, attended_delta, in_got, square_got, place)
        )
        answer_square.array(square_got, "hx")
        in_first = Part(half, "yxlh").array(in_keep, "yhlx").array(in_got, "yhlx")
        in_second = Part(half, "xylh", half).array(in_keep, "yhlx").array(in_got, "yhlx")
        trip_in, after = ride(
            ring,
            cue,
            [
                ("y", [in_first, memory_second]),
                ("x", [in_second, memory_first]),
                ("h", [answer_square]),
            ],
        )
    heads_delta, slope_delta, heads_send, heads_keep = attend_back(
        place, heads, chances, attended_delta, inputs, hidden_low, after=after
    )
    after = []
    if cut:
        heads_send, cue = arrive([heads_send, place], trip_in)
        heads_got = ring.swap(heads_send, "c")
        trip_in, sends = ride(
            ring,
            cue,
            [
                ("x", [in_first, answer_square]),
                ("y", [in_second]),
                ("l", [memory_first, memory_second]),
            ],
        )
        heads_got, cue, *_ = lax.optimization_barrier((heads_got, place, *sends))
        heads_first = Part(half, "yxlh").array(heads_keep, "yhlx").array(heads_got, "yhlx")
        heads_second = Part(half, "xylh", half)
        heads_second.array(heads_keep, "yhlx").array(heads_got, "yhlx")
        trip_heads, after = ride(ring, cue, [("y", [heads_first]), ("x", [heads_second])])
    passage_gradient, small = passage_end(
        place,
        gains,
        (
            slope_delta,
            answer_table_delta,
            ffn_gain_delta,
            final_gain_delta,
            self_gain_delta,
            cross_gain_delta,
            answer_gain_delta,
        ),
        passage_rows,
        heads_delta,
        hidden_delta,
        (encoder_query, encoder_key, encoder_value),
        after=after,
    )
    if cut:
        small_got = ring.swap(small, "c")
        small_got, cue = arrive([small_got, place], trip_in, trip_heads)
        total = Total(small)
        total.terms.append((small_got, [], 0))
        trip, sends = ride(
            ring,
            cue,
            [
                ("x", [heads_first]),
                ("y", [heads_second, total]),
                ("l", [in_first, in_second]),
                ("h", [memory_first, memory_second]),
            ],
        )
        (cue,) = arrive([place], trip)
        trip, sends = ride(
            ring,
            cue,
            [("l", [heads_first, heads_second, total]), ("h", [in_first, in_second])],
        )
        (done,) = bus(
            place, [(None, [memory_first, memory_second, answer_wide, answer_square])], sends
        )
        done, cue = arrive([done, place], trip)
        first = Beside(ring, done)
        trip, sends = ride(ring, cue, [("h", [heads_first, heads_second, total])])
        cue, *first.arriving = arrive([place, *first.arriving], trip)
        done, small = bus(
            cue,
            [(None, [in_first, in_second, heads_first, heads_second]), (None, [total])],
        )
        last = Beside(ring, done)
        small_got = ring.swap(small, "x")
        first.send([done])
        lay, shapes, stacked, unhalved, side_by_side, units = layout(shard)
        stacked(0)
        unhalved(half)
        side_by_side(half + shard)
        unhalved(half + 2 * shard)
        units(half + 3 * shard)
        stacked(half + 4 * shard)
        weights = list(assemble(place, first.arrays(), shapes, lay))
        last.send(weights[:1])
        lay, shapes, stacked, unhalved, side_by_side, units = layout(shard)
        side_by_side(0)
        units(shard)
        weights += list(assemble(place, last.arrays(), shapes, lay))
        small = wide(small) + wide(small_got)
    else:
        small = lax.psum(wide(small), ("dp", "blk"))
    mine = lax.axis_index("dp")
    gain_deltas = lax.dynamic_slice_in_dim(small[:6], mine * shard, shard, 1)
    tables = NB // ring.dp
    table_deltas = [
        lax.dynamic_slice_in_dim(small[8 : 8 + H, begin : begin + NB], mine * tables, tables, 1).T
        for begin in (0, 128)
    ]

    if not cut:
        weights = whole_weights(
            core,
            (memory_send, memory_keep),
            (in_send, in_keep),
            (heads_send, heads_keep),
            (
                (answer_lows[1], answer_wides[1]),
                (
                    answer_wides[0],
                    low(slotted(decoder_cotangent)),
                ),
                (answer_crossed, asking_delta),
                (answer_lows[0], answer_lows[2]),
                (answer_attended, answer_hidden_low),
                (answer_normed, answer_heads_delta[0]),
                (answer_normed, answer_heads_delta[1]),
                (answer_normed, answer_heads_delta[2]),
            ),
        )
    (
        gradient_cross_key,
        gradient_cross_value,
        gradient_encoder_ffn_out,
        gradient_decoder_ffn_in,
        gradient_decoder_ffn_out,
        gradient_cross_query,
        gradient_cross_mix,
        gradient_decoder_mix,
        gradient_decoder_query,
        gradient_decoder_key,
        gradient_decoder_value,
        gradient_encoder_ffn_in,
        gradient_encoder_query,
        gradient_encoder_key,
        gradient_encoder_value,
        gradient_encoder_mix,
    ) = weights
    return (
        result.reshape(encoder_input.shape),
        answer_result,
        passage_gradient.reshape(encoder_input.shape),
        answer_gradient,
        gain_deltas[ATTN],
        gradient_encoder_query,
        gradient_encoder_key,
        gradient_encoder_value,
        gradient_encoder_mix,
        table_deltas[0],
        gain_deltas[FFN],
        gradient_encoder_ffn_in,
        gradient_encoder_ffn_out,
        gain_deltas[FINAL],
        gradient_cross_key,
        gradient_cross_value,
        gain_deltas[SELF],
        gradient_decoder_query,
        gradient_decoder_key,
        gradient_decoder_value,
        gradient_decoder_mix,
        table_deltas[1],
        gain_deltas[CROSS],
        gradient_cross_query,
        gradient_cross_mix,
        gain_deltas[ANSWER],
        gradient_decoder_ffn_in,
        gradient_decoder_ffn_out,
    )


def whole_weights(core, memory, inner, heads, answers):
    def both(pair):
        send, keep = pair
        return (jnp.where(core == 0, keep, send), jnp.where(core == 0, send, keep))

    def shared(gradient):
        return lax.psum_scatter(low(gradient), "dp", scatter_dimension=0, tiled=True)

    def summed(gradient):
        return lax.psum(shared(gradient), "blk")

    memory = both(memory)
    shards, _, rows, _ = memory[0].shape
    cut = rows // 3
    passages = [part[:, :, :cut].reshape(D, D) for part in memory]
    out = [
        part[:, :, cut:]
        .reshape(shards, 2, 2 * cut, 2, D // 2)
        .swapaxes(2, 3)
        .reshape(8 * cut * shards, D // 2)
        for part in memory
    ]
    passages.append(jnp.concatenate(out, axis=1))
    passages.append(jnp.concatenate([unit for half in both(inner) for unit in half], axis=1))
    passages += [unit for half in both(heads) for unit in half]
    passages = [wide(summed(item)) for item in passages]
    answers = [wide(shared(dot_tokens(inputs, upstream))) for inputs, upstream in answers]
    return passages[:3] + answers + passages[3:]


def solution(mesh):
    dims = {4: P("dp", "blk", None, None), 3: P("dp", None, None), 2: P("dp", None), 1: P("dp")}
    rows = P("dp", "blk", None)
    return jax.shard_map(
        functools.partial(on_device, Ring(mesh)),
        mesh=mesh,
        in_specs=(dims[4], dims[3], dims[4], dims[3], rows, rows, dims[1]) + (P(),) * 24,
        out_specs=(dims[4], dims[3], dims[4], dims[3])
        + tuple(dims[1 if at in (0, 6, 9, 12, 18, 21) else 2] for at in range(24)),
        check_vma=False,
    )
```

```python
import functools
import math

import jax
import jax.numpy as jnp
from jax import lax
from jax.experimental import pallas as pl
from jax.experimental.pallas import tpu as pltpu
from jax.sharding import PartitionSpec as P

D = 768
H = 12
HD = 64
NB = 32
MAXD = 128
ROW = 256
ANS = 20


EPSILON = 1e-06
NEGATIVE = -1e30


SLOT = 32
ANY = pl.ANY
VM = pltpu.VMEM
BF = jnp.bfloat16
F32 = jnp.float32
LIMIT = 60 << 20


def dot(left, right):
    return jnp.dot(left, right, preferred_element_type=jnp.float32)


def dot_rows(left, right):
    return lax.dot_general(
        left, right, (((1,), (1,)), ((), ())), preferred_element_type=jnp.float32
    )


def dot_tokens(left, right):
    return lax.dot_general(
        left, right, (((0,), (0,)), ((), ())), preferred_element_type=jnp.float32
    )


def low(values):
    return values.astype(jnp.bfloat16)


def wide(values):
    return values.astype(jnp.float32)


def slotted(ref):
    spare = jnp.zeros((SLOT - ANS, D), F32)
    return jnp.concatenate(
        [part for at in range(ref.shape[0]) for part in (wide(ref[at]), spare)], axis=0
    )


def unslotted(values, ref):
    for at in range(ref.shape[0]):
        ref[at] = values[at * SLOT : at * SLOT + ANS].astype(ref.dtype)


ATTN, FFN, FINAL, SELF, CROSS, ANSWER = range(6)


def gain_row(gains_ref, which):
    return gains_ref[which : which + 1, :]


def rms_scale(values):
    return lax.rsqrt(jnp.mean(values * values, axis=-1, keepdims=True) + EPSILON)


def head_lanes(rows, width=D):
    return lax.broadcasted_iota(jnp.int32, (rows, width), 1) // HD


def spread(rows):
    lanes = head_lanes(rows.shape[0])
    values = wide(rows)
    return low(jnp.concatenate([jnp.where(lanes == h, values, 0.0) for h in range(H)], axis=0))


def fold(full):
    rows = full.shape[0] // H
    lanes = head_lanes(rows)
    total = jnp.zeros((rows, full.shape[1]), jnp.float32)
    for h in range(H):
        total = jnp.where(lanes == h, full[h * rows : (h + 1) * rows], total)
    return total


def gelu_pair(values):
    square = values * values
    inner = values * (0.7978845608 + (0.7978845608 * 0.044715) * square)
    half = 0.5 + 0.5 * jnp.tanh(inner)
    active = values * half
    slope = 0.7978845608 + (3.0 * 0.7978845608 * 0.044715) * square
    return (active, half + 2.0 * active * (1.0 - half) * slope)


class Copies:
    def __init__(self, semaphores):
        self.semaphores = semaphores
        self.count = 0
        self.open = []

    def start(self, source, target):
        copy = pltpu.make_async_copy(source, target, self.semaphores.at[self.count])
        self.count += 1
        copy.start()
        return copy

    def out(self, source, target):
        self.open.append(self.start(source, target))

    def finish(self):
        for copy in self.open:
            copy.wait()


def kernel_call(body, operands, spaces, outs, scratch, after=()):
    if after:
        first, *_ = lax.optimization_barrier((operands[0], *after))
        operands = (first, *operands[1:])
    return pl.pallas_call(
        body,
        in_specs=[pl.BlockSpec(memory_space=space) for space in spaces],
        out_specs=[pl.BlockSpec(memory_space=space) for _, _, space in outs],
        out_shape=[jax.ShapeDtypeStruct(shape, dtype) for shape, dtype, _ in outs],
        scratch_shapes=scratch,
        compiler_params=pltpu.CompilerParams(vmem_limit_bytes=LIMIT),
        cost_estimate=pl.CostEstimate(flops=10**13, bytes_accessed=10**9, transcendentals=0),
    )(*operands)


def bucket_of(offsets, both_ways):
    if both_ways:
        buckets = NB // 2
        index = jnp.where(offsets > 0, buckets, 0)
        distance = jnp.abs(offsets)
    else:
        buckets = NB
        index = jnp.zeros_like(offsets)
        distance = jnp.maximum(-offsets, 0)
    exact = buckets // 2
    index = index + jnp.minimum(distance, exact)
    for step in range(1, buckets - exact):
        border = math.ceil(exact * (MAXD / exact) ** (step / (buckets - exact)) - 1e-09)
        index = index + jnp.where(distance >= border, 1, 0)
    return index


def table_slopes(table, width, both_ways, turn):
    offsets = turn * (lax.broadcasted_iota(jnp.int32, (NB, width), 1) - width // 2)
    matches = bucket_of(offsets, both_ways) == lax.broadcasted_iota(jnp.int32, (NB, width), 0)
    return dot(table, low(jnp.where(matches, 1.0, 0.0)))


def slope_bias(slopes, rows):
    width = slopes.shape[1]
    spread_slopes = jnp.broadcast_to(slopes, (rows, width))
    return pltpu.roll(spread_slopes, width // 2, 1, stride=1, stride_axis=0)[:, : width // 2]


def passage_kernel(
    length_ref, answer_input_ref, input_ref, segment_ref, padding_ref, table_ref, answer_table_ref,
    gain_refs,
    answer_query_hbm, answer_key_hbm, answer_value_hbm, answer_mix_hbm, ask_hbm,
    query_hbm, key_hbm, value_hbm, mix_hbm, in_hbm, out_hbm, cross_key_hbm, cross_value_hbm,
    gains_ref, answer_normed_ref, answer_heads_ref, answer_chance_ref, answer_attended_ref,
    answer_hidden_ref, crossed_ref, asking_ref, packed_ref,
    inputs_hbm, heads_hbm, chance_hbm, hidden_hbm, second_hbm,
    active_hbm, bend_hbm, encoded_hbm, result_hbm, final_hbm, memory_hbm, score_hbm,
    answer_square, square, wide_in, wide_out, slopes, arrivals,
    inputs, heads, chance, hidden, second,
    active, bend, memory, score,
):
    copies = Copies(arrivals)
    answer_waits = [
        copies.start(source, answer_square.at[at])
        for at, source in enumerate(
            (answer_query_hbm, answer_key_hbm, answer_value_hbm, answer_mix_hbm, ask_hbm)
        )
    ]
    square_hbm = (query_hbm, key_hbm, value_hbm, mix_hbm)
    waits = [copies.start(source, square.at[at]) for at, source in enumerate(square_hbm)]
    wait_in = copies.start(in_hbm, wide_in)
    wait_out = copies.start(out_hbm, wide_out)
    rows = input_ref.shape[0]
    blocks = rows // ROW
    normed = inputs.at[0]
    attended = inputs.at[1]

    gains = [wide(ref[...]).reshape(1, D) for ref in gain_refs]
    for at, gain in enumerate(gains):
        gains_ref[at : at + 1, :] = gain
    values = wide(input_ref[...])
    normed[...] = low(values * rms_scale(values) * gains[ATTN])
    slopes[...] = table_slopes(table_ref[...], 2 * ROW, True, 1)
    place_row = lax.broadcasted_iota(jnp.int32, (ROW, ROW), 0)
    place_column = lax.broadcasted_iota(jnp.int32, (ROW, ROW), 1)
    for block in range(blocks):
        segment_row = jnp.broadcast_to(segment_ref[block], (ROW, ROW))
        padding_row = jnp.broadcast_to(padding_ref[block], (ROW, ROW))
        own = (segment_row == segment_row.T) & (padding_row == 1)
        score[block, :ROW] = jnp.where(own | (place_row == place_column), 0.0, NEGATIVE)

    answer_values = slotted(answer_input_ref)
    answer_normed = low(answer_values * rms_scale(answer_values) * gains[SELF])
    answer_normed_ref[...] = answer_normed
    for at in range(3):
        answer_waits[at].wait()
        answer_heads_ref[at] = low(dot(answer_normed, answer_square[at]))
    cross_waits = [
        copies.start(source, answer_square.at[at])
        for at, source in enumerate((cross_key_hbm, cross_value_hbm))
    ]
    answer_slopes = table_slopes(answer_table_ref[...], 128, False, 1)
    answer_bias = jnp.concatenate(
        [slope_bias(answer_slopes[h : h + 1], SLOT)[:, :SLOT] for h in range(H)], axis=0
    )
    row = lax.broadcasted_iota(jnp.int32, (H * SLOT, SLOT), 0) % SLOT
    column = lax.broadcasted_iota(jnp.int32, (H * SLOT, SLOT), 1)
    for at in range(blocks):
        slots = slice(at * SLOT, (at + 1) * SLOT)
        asked = spread(answer_heads_ref[0, slots])
        scores = dot_rows(asked, answer_heads_ref[1, slots]) + answer_bias
        allowed = (column <= row) & (column < length_ref[at])
        scores = jnp.where(allowed, scores, NEGATIVE)
        powers = jnp.exp(scores - jnp.max(scores, axis=1, keepdims=True))
        chances = low(powers / jnp.sum(powers, axis=1, keepdims=True))
        answer_chance_ref[at] = chances
        answer_attended_ref[slots] = low(fold(dot(chances, answer_heads_ref[2, slots])))
    answer_waits[3].wait()
    answer_hidden = answer_values + dot(answer_attended_ref[...], answer_square[3])
    answer_hidden_ref[...] = answer_hidden
    crossed = low(answer_hidden * rms_scale(answer_hidden) * gains[CROSS])
    crossed_ref[...] = crossed
    answer_waits[4].wait()
    asking_ref[...] = low(dot(crossed, answer_square[4]))

    for at in range(3):
        waits[at].wait()
        heads[at] = low(dot(normed[...], square[at]))
    heads_out = copies.start(heads, heads_hbm)
    second_half = lax.broadcasted_iota(jnp.int32, (ROW, 2 * HD), 1) >= HD

    for pair in range(H // 2):
        lanes = slice(pair * 2 * HD, (pair + 1) * 2 * HD)
        sums = []
        for which in range(2):
            head = pair * 2 + which
            bias = slope_bias(slopes[head : head + 1, :], ROW)
            for block in range(blocks):
                span = slice(block * ROW, (block + 1) * ROW)
                asked = heads[0, span, lanes]
                own = jnp.where(second_half == (which == 1), asked, jnp.zeros_like(asked))
                scores = dot_rows(own, heads[1, span, lanes]) + (bias + score[block, :ROW])
                powers = jnp.exp(scores - jnp.max(scores, axis=1, keepdims=True))
                chances = low(powers * (1.0 / jnp.sum(powers, axis=1, keepdims=True)))
                chance[head, block] = chances.T
                taken = dot(chances, heads[2, span, lanes])
                if which == 0:
                    sums.append(taken)
                else:
                    attended[span, lanes] = low(jnp.where(second_half, taken, sums[block]))
        part = pl.ds(pair * 2, 2)
        copies.out(chance.at[part], chance_hbm.at[part])

    copies.out(inputs, inputs_hbm)
    waits[3].wait()
    values = wide(input_ref[...]) + dot(attended[...], square[3])
    hidden[...] = values
    hidden_out = copies.start(hidden, hidden_hbm)
    second[...] = low(values * rms_scale(values) * gains[FFN])
    copies.out(second, second_hbm)
    wait_in.wait()
    for at in range(in_hbm.shape[1] // D):
        lanes = slice(at * D, (at + 1) * D)
        up, slope = gelu_pair(dot(second[...], wide_in[:, lanes]))
        active[:, lanes] = low(up)
        bend[:, lanes] = low(slope)
        copies.out(active.at[:, lanes], active_hbm.at[:, lanes])
        copies.out(bend.at[:, lanes], bend_hbm.at[:, lanes])
    wait_out.wait()
    values = hidden[...] + dot(active[...], wide_out[...])
    hidden_out.wait()
    hidden[...] = values
    copies.out(hidden, encoded_hbm)
    heads_out.wait()
    result = heads.at[0]
    final = heads.at[1]
    result[...] = low(values)
    copies.out(result, result_hbm)
    final[...] = low(values * rms_scale(values) * gains[FINAL])
    copies.out(final, final_hbm)
    for at in range(2):
        cross_waits[at].wait()
        memory[at] = low(dot(final[...], answer_square[at]))
    copies.out(memory, memory_hbm)

    lane = lax.broadcasted_iota(jnp.int32, (SLOT, 128), 1)
    for block in range(blocks):
        span = slice(block * ROW, (block + 1) * ROW)
        slots = slice(block * SLOT, (block + 1) * SLOT)
        scores = dot_rows(spread(asking_ref[slots]), memory[0, span])
        scores = jnp.where(padding_ref[block] == 1, scores, NEGATIVE)
        score[block] = scores
        top = jnp.max(scores, axis=1, keepdims=True)
        powers = jnp.exp(scores - top)
        sums = jnp.sum(powers, axis=1, keepdims=True)
        reading = fold(dot(low(powers * (1.0 / sums)), memory[1, span]))
        packed_ref[slots, :D] = low(reading)
        total = top + jnp.log(sums)
        extra = jnp.zeros((SLOT, 128), F32)
        for h in range(H):
            rest = total[h * SLOT : (h + 1) * SLOT]
            for piece in range(3):
                part = wide(low(rest))
                extra = jnp.where(lane == piece * H + h, part, extra)
                rest = rest - part
        packed_ref[slots, D:] = low(extra)
    copies.out(score, score_hbm)
    copies.finish()


def passage(
    length, answer_input, rows, segments, padding, table, answer_table, gains, answer_weights, weights
):
    count = rows.shape[0]
    blocks = count // ROW
    slots = blocks * SLOT
    wide_size = weights[4].shape[1]
    small = [
        ((len(gains), D), F32),
        ((slots, D), BF),
        ((3, slots, D), BF),
        ((blocks, H * SLOT, SLOT), BF),
        ((slots, D), BF),
        ((slots, D), F32),
        ((slots, D), BF),
        ((slots, D), BF),
        ((slots, D + 128), BF),
    ]
    whole = [
        ((2, count, D), BF),
        ((3, count, D), BF),
        ((H, blocks, ROW, ROW), BF),
        ((count, D), F32),
        ((count, D), BF),
        ((count, wide_size), BF),
        ((count, wide_size), BF),
        ((count, D), F32),
        ((count, D), BF),
        ((count, D), BF),
        ((2, count, D), BF),
        ((blocks, H * SLOT, ROW), F32),
    ]
    first = 7

    def body(*refs):
        last = first + len(gains)
        passage_kernel(*refs[:first], refs[first:last], *refs[last:])

    return kernel_call(
        body,
        (length, answer_input, rows, segments, padding, table, answer_table)
        + tuple(gains)
        + tuple(answer_weights)
        + tuple(weights),
        [pltpu.SMEM] + [VM] * (6 + len(gains)) + [ANY] * 13,
        [(shape, dtype, VM) for shape, dtype in small]
        + [(shape, dtype, ANY) for shape, dtype in whole],
        [
            VM((5, D, D), BF),
            VM((4, D, D), BF),
            VM((D, wide_size), BF),
            VM((wide_size, D), BF),
            VM((H, 2 * ROW), F32),
            pltpu.SemaphoreType.DMA((40,)),
        ]
        + [VM(shape, dtype) for at, (shape, dtype) in enumerate(whole) if at not in (7, 8, 9)],
    )


def rms_back(values, gain, upstream):
    scale = rms_scale(values)
    scaled = upstream * gain
    inner = jnp.mean(scaled * values, axis=-1, keepdims=True)
    delta = scaled * scale - values * (scale * scale * scale) * inner
    return (delta, jnp.sum(upstream * values * scale, axis=0, keepdims=True))


def exact_dot(left, right, rows=False):
    return lax.dot_general(
        left,
        right,
        (((1,), (1 if rows else 0,)), ((), ())),
        precision=lax.Precision.HIGHEST,
        preferred_element_type=jnp.float32,
    )


def head_columns(values):
    return jnp.concatenate([values[:, h : h + 1] for h in range(H)], axis=0)


def tree_sum(items):
    while len(items) > 1:
        items = [
            items[at] + items[at + 1] if at + 1 < len(items) else items[at]
            for at in range(0, len(items), 2)
        ]
    return items[0]


def answer_up_kernel(upstream_ref, out_hbm, up_ref, weight, arrivals):
    copies = Copies(arrivals)
    waits = []
    for at in range(out_hbm.shape[0] // D):
        part = pl.ds(at * D, D)
        waits.append(copies.start(out_hbm.at[part], weight.at[part]))
    upstream = low(slotted(upstream_ref))
    for at, wait in enumerate(waits):
        part = slice(at * D, (at + 1) * D)
        wait.wait()
        up_ref[:, part] = dot_rows(upstream, weight[part, :])


def answer_up(upstream, weight):
    return kernel_call(
        answer_up_kernel,
        (upstream, weight),
        [VM, ANY],
        [((upstream.shape[0] * SLOT, weight.shape[0]), F32, VM)],
        [VM(weight.shape, BF), pltpu.SemaphoreType.DMA((4,))],
    )[0]


def answer_middle_kernel(
    every_refs, asking_ref, hidden_ref, up_ref, upstream_ref, gains_ref, score_hbm, memory_hbm,
    mix_hbm, in_hbm,
    low_ref, wide_ref, middle_ref, middle_delta_ref, gain_delta_ref, memory_delta_hbm,
    asking_delta_ref, *refs, place_ref=None,
):
    *weight_refs, score, memory, memory_delta, mix, wide_in, arrivals = refs
    copies = Copies(arrivals)
    wait_mix = copies.start(mix_hbm, mix)
    wait_in = copies.start(in_hbm, wide_in)
    wait_memory = copies.start(memory_hbm, memory)
    wait_score = copies.start(score_hbm, score)
    count = asking_ref.shape[0]

    from_piece = lax.broadcasted_iota(jnp.int32, (128, 128), 0)
    to_head = lax.broadcasted_iota(jnp.int32, (128, 128), 1)
    same = (from_piece % H == to_head) & (from_piece < 3 * H)
    pieces = low(jnp.where(same, 1.0, 0.0))
    lane_head = lax.broadcasted_iota(jnp.int32, (128, D), 1) // HD
    widen = jnp.where(lane_head == lax.broadcasted_iota(jnp.int32, (128, D), 0), 1.0, 0.0)

    totals = [dot(ref[:, D:], pieces) for ref in every_refs]
    top = functools.reduce(jnp.maximum, totals)
    powers = [jnp.exp(total - top) for total in totals]
    sums = tree_sum(powers)
    reading = tree_sum(
        [
            wide(ref[:, :D]) * exact_dot(power / sums, widen)
            for ref, power in zip(every_refs, powers)
        ]
    )
    whole_total = top + jnp.log(sums)
    reading_low = low(reading)
    low_ref[0] = reading_low
    wait_mix.wait()
    middle = hidden_ref[...] + dot(reading_low, mix[...])
    middle_ref[...] = middle
    gain = gain_row(gains_ref, ANSWER)
    fifth = low(middle * rms_scale(middle) * gain)
    low_ref[1] = fifth
    wait_in.wait()
    for at in range(wide_in.shape[1] // D):
        lanes = slice(at * D, (at + 1) * D)
        active, slope = gelu_pair(dot(fifth, wide_in[:, lanes]))
        wide_ref[0, :, lanes] = low(active)
        wide_ref[1, :, lanes] = low(up_ref[:, lanes] * slope)
    delta, gain_delta = rms_back(middle, gain, dot_rows(wide_ref[1], wide_in[...]))
    gain_delta_ref[...] = gain_delta
    delta += slotted(upstream_ref)
    middle_delta_ref[...] = delta
    delta_low = low(delta)
    low_ref[2] = delta_low
    taken = low(dot_rows(delta_low, mix[...]))
    inner = exact_dot(wide(taken) * reading, widen, rows=True)
    wait_score.wait()
    wait_memory.wait()
    for block in range(count // SLOT):
        slots = slice(block * SLOT, (block + 1) * SLOT)
        span = slice(block * ROW, (block + 1) * ROW)
        chances = jnp.exp(score[block] - head_columns(whole_total[slots]))
        asked = spread(asking_ref[slots])
        upward = spread(taken[slots])
        delta_chances = dot_rows(upward, memory[1, span])
        deltas = low(chances * (delta_chances - head_columns(inner[slots])))
        memory_delta[0, span] = low(dot_tokens(deltas, asked))
        memory_delta[1, span] = low(dot_tokens(low(chances), upward))
        asking_delta_ref[slots] = low(fold(dot(deltas, memory[0, span])))
    copies.out(memory_delta, memory_delta_hbm)
    if weight_refs:
        answer_wide_weight(place_ref, low_ref, wide_ref, upstream_ref, *weight_refs)
    copies.finish()


def answer_middle(
    place, every, asking, hidden, up, upstream, gains, score, memory, weights, shards
):
    count = asking.shape[0]
    wide_size = weights[1].shape[1]
    blocks = len(every)
    outs, scratch = [], []
    if shards:
        outs = [((shards // 2, D // shards, D), BF, VM)] * 4
        scratch = [VM((D, D), BF), VM((wide_size, D // 2), BF)]

    def body(place_ref, *refs):
        answer_middle_kernel(refs[:blocks], *refs[blocks:], place_ref=place_ref)

    return kernel_call(
        body,
        (place, *every, asking, hidden, up, upstream, gains, score, memory, *weights),
        [pltpu.SMEM] + [VM] * (blocks + 5) + [ANY] * 4,
        [
            ((3, count, D), BF, VM),
            ((2, count, wide_size), BF, VM),
            ((count, D), F32, VM),
            ((count, D), F32, VM),
            ((1, D), F32, VM),
            (memory.shape, BF, ANY),
            ((count, D), BF, VM),
        ]
        + outs,
        scratch
        + [
            VM(score.shape, F32),
            VM(memory.shape, BF),
            VM(memory.shape, BF),
            VM((D, D), BF),
            VM((D, wide_size), BF),
            pltpu.SemaphoreType.DMA((8,)),
        ],
    )


def memory_back_kernel(
    place_ref, gains_ref, delta_hbm, final_hbm, encoded_hbm, upstream_hbm, key_hbm, value_hbm,
    active_hbm, weight_hbm, bend_hbm,
    send_hbm, keep_hbm, output_hbm, before_hbm, gain_delta_ref,
    delta, final, encoded, upstream, weights, active, weight, bend, both, output, before, arrivals,
):
    copies = Copies(arrivals)
    shards = both.shape[1]
    width = D // shards
    half = D // 2
    steps = active.shape[1] // D
    wait_delta = copies.start(delta_hbm, delta)
    waits = [copies.start(key_hbm, weights.at[0]), copies.start(value_hbm, weights.at[1])]
    wait_encoded = copies.start(encoded_hbm, encoded)
    wait_upstream = copies.start(upstream_hbm, upstream)
    wait_final = copies.start(final_hbm, final)
    wait_active = []
    for at in range(steps):
        part = pl.ds(at * D, D)
        wait_active.append(copies.start(active_hbm.at[:, part], active.at[:, part]))
    wait_back = []
    for at in range(steps):
        part = pl.ds(at * D, D)
        wait_back.append(
            [
                copies.start(weight_hbm.at[part], weight.at[part]),
                copies.start(bend_hbm.at[:, part], bend.at[:, part]),
            ]
        )
    core = place_ref[0]
    wait_delta.wait()
    for wait in waits:
        wait.wait()
    upward = dot_rows(delta[0], weights[0]) + dot_rows(delta[1], weights[1])
    wait_encoded.wait()
    wait_upstream.wait()
    back, gain_delta = rms_back(encoded[...], gain_row(gains_ref, FINAL), upward)
    gain_delta_ref[...] = gain_delta
    back += wide(upstream[...])
    output[...] = back
    copies.out(output, output_hbm)
    output_low = low(back)
    wait_final.wait()

    for side in range(2):
        first = low(dot_tokens(final[...], delta[side]))
        for shard in range(shards):
            for row in range(2):
                begin = shard * width + row * (width // 2)
                both[side, shard, row, : width // 2] = first[begin : begin + width // 2]
    for at in range(steps):
        wait_active[at].wait()
        later = low(dot_tokens(active[:, at * D : (at + 1) * D], output_low))
        for side in range(2):
            columns = slice(side * half, (side + 1) * half)
            for piece in range(D // width):
                shard, place = divmod(at * D // width + piece, 4)
                row, part = divmod(place, 2)
                rows = slice(piece * width, (piece + 1) * width)
                lanes = slice(part * half, (part + 1) * half)
                both[side, shard, row, width // 2 :, lanes] = later[rows, columns]
        done = pl.ds(at * shards // steps, shards // steps)
        copies.out(both.at[1 - core, done], send_hbm.at[done])
        copies.out(both.at[core, done], keep_hbm.at[done])
    for at in range(steps):
        part = slice(at * D, (at + 1) * D)
        for wait in wait_back[at]:
            wait.wait()
        before[:, part] = low(dot_rows(output_low, weight[part, :]) * wide(bend[:, part]))
        copies.out(before.at[:, part], before_hbm.at[:, part])
    copies.finish()


def memory_back(
    place, gains, delta, final, encoded, upstream, weights, active, weight, bend, shards, after=()
):
    count = final.shape[0]
    wide_size = active.shape[1]
    shape = (shards, 2, 3 * D // shards // 2, D)
    return kernel_call(
        memory_back_kernel,
        (place, gains, delta, final, encoded, upstream)
        + tuple(weights)
        + (active, weight, bend),
        [pltpu.SMEM, VM] + [ANY] * 9,
        [
            (shape, BF, ANY),
            (shape, BF, ANY),
            ((count, D), F32, ANY),
            ((count, wide_size), BF, ANY),
            ((1, D), F32, VM),
        ],
        [
            VM((2, count, D), BF), VM((count, D), BF), VM((count, D), F32), VM((count, D), BF),
            VM((2, D, D), BF), VM((count, wide_size), BF), VM((wide_size, D), BF),
            VM((count, wide_size), BF), VM((2,) + shape, BF), VM((count, D), F32),
            VM((count, wide_size), BF), pltpu.SemaphoreType.DMA((40,)),
        ],
        after,
    )


def wide_in_back_kernel(
    place_ref, gains_ref, second_hbm, before_hbm, weight_hbm, hidden_hbm, output_hbm, mix_hbm,
    send_hbm, keep_hbm, hidden_delta_hbm, hidden_low_hbm, attended_delta_hbm, gain_delta_ref,
    second, before, weight, hidden, output, mix, send, keep, hidden_delta, hidden_low,
    attended_delta, arrivals,
):
    copies = Copies(arrivals)
    steps = before.shape[1] // D // 2
    core = place_ref[0]
    wait_second = copies.start(second_hbm, second)
    units = [(1 - core) * steps + at for at in range(steps)]
    units += [core * steps + at for at in range(steps)]
    waits = []
    for unit in units:
        part = pl.ds(pl.multiple_of(unit * D, D), D)
        waits.append(copies.start(before_hbm.at[:, part], before.at[:, part]))
    later = [
        copies.start(source, target)
        for source, target in (
            (weight_hbm, weight), (hidden_hbm, hidden), (output_hbm, output), (mix_hbm, mix)
        )
    ]
    wait_second.wait()
    for at, unit in enumerate(units):
        waits[at].wait()
        part = pl.ds(pl.multiple_of(unit * D, D), D)
        target, target_hbm = (send, send_hbm) if at < steps else (keep, keep_hbm)
        target[at % steps] = low(dot_tokens(second[...], before[:, part]))
        copies.out(target.at[at % steps], target_hbm.at[at % steps])
    for wait in later:
        wait.wait()
    upward = dot_rows(before[...], weight[...])
    back, gain_delta = rms_back(hidden[...], gain_row(gains_ref, FFN), upward)
    gain_delta_ref[...] = gain_delta
    back += output[...]
    hidden_delta[...] = back
    copies.out(hidden_delta, hidden_delta_hbm)
    hidden_low[...] = low(back)
    copies.out(hidden_low, hidden_low_hbm)
    attended_delta[...] = low(dot_rows(hidden_low[...], mix[...]))
    copies.out(attended_delta, attended_delta_hbm)
    copies.finish()


def wide_in_back(place, gains, second, before, weight, hidden, output, mix, after=()):
    count, wide_size = before.shape
    shape = (wide_size // D // 2, D, D)
    return kernel_call(
        wide_in_back_kernel,
        (place, gains, second, before, weight, hidden, output, mix),
        [pltpu.SMEM, VM] + [ANY] * 6,
        [
            (shape, BF, ANY),
            (shape, BF, ANY),
            ((count, D), F32, ANY),
            ((count, D), BF, ANY),
            ((count, D), BF, ANY),
            ((1, D), F32, VM),
        ],
        [
            VM((count, D), BF), VM((count, wide_size), BF), VM((D, wide_size), BF),
            VM((count, D), F32), VM((count, D), F32), VM((D, D), BF), VM(shape, BF),
            VM(shape, BF), VM((count, D), F32), VM((count, D), BF), VM((count, D), BF),
            pltpu.SemaphoreType.DMA((24,)),
        ],
        after,
    )


def attend_back_kernel(
    place_ref, heads_hbm, chance_hbm, upstream_hbm, inputs_hbm, hidden_low_hbm,
    delta_hbm, slope_delta_ref, send_hbm, keep_hbm,
    heads, chance, upstream, inputs, delta, gathered, units, arrivals,
):
    copies = Copies(arrivals)
    pairs = H // 2
    waits = []
    for pair in range(pairs):
        lanes = pl.ds(pair * 2 * HD, 2 * HD)
        part = pl.ds(pair * 2, 2)
        waits.append(
            [
                copies.start(heads_hbm.at[:, :, lanes], heads.at[:, :, lanes]),
                copies.start(upstream_hbm.at[:, lanes], upstream.at[:, lanes]),
                copies.start(chance_hbm.at[part], chance.at[part]),
            ]
        )
    wait_inputs = copies.start(inputs_hbm, inputs)
    wait_hidden = copies.start(hidden_low_hbm, delta.at[3])
    blocks = upstream.shape[0] // ROW
    second_half = lax.broadcasted_iota(jnp.int32, (ROW, 2 * HD), 1) >= HD
    place_row = lax.broadcasted_iota(jnp.int32, (ROW, ROW), 0)
    place_column = lax.broadcasted_iota(jnp.int32, (ROW, ROW), 1)
    mirror = low(jnp.where(place_row + place_column == ROW - 1, 1.0, 0.0))

    for pair in range(pairs):
        lanes = slice(pair * 2 * HD, (pair + 1) * 2 * HD)
        for wait in waits[pair]:
            wait.wait()
        kept = []
        for which in range(2):
            head = pair * 2 + which
            for block in range(blocks):
                span = slice(block * ROW, (block + 1) * ROW)
                query, key, value = (heads[at, span, lanes] for at in range(3))
                upward = upstream[span, lanes]
                own = jnp.where(second_half == (which == 1), upward, jnp.zeros_like(upward))
                chances = chance[head, block]
                weight = wide(chances)
                delta_chances = dot_rows(value, own)
                inner = jnp.sum(delta_chances * weight, axis=0, keepdims=True)
                deltas = low(weight * (delta_chances - inner))
                if block == 0:
                    gathered[...] = wide(deltas)
                else:
                    gathered[...] += wide(deltas)
                own_key = key.T[which * HD : (which + 1) * HD]
                news = [low(dot(own_key, deltas)), dot(deltas, query), dot(chances, upward)]
                if which == 0:
                    kept.append(news)
                else:
                    delta[0, span, lanes] = jnp.concatenate([kept[block][0], news[0]], axis=0).T
                    for at in (1, 2):
                        both = jnp.where(second_half, news[at], kept[block][at])
                        delta[at, span, lanes] = low(both)
            whole = gathered[...]
            most = low(whole)
            turned = dot(mirror, most) + dot(mirror, low(whole - wide(most)))
            padded = jnp.concatenate([turned, jnp.zeros((ROW, ROW), F32)], axis=1)
            rolled = pltpu.roll(padded, 1, 1, stride=1, stride_axis=0)
            slope_delta_ref[head : head + 1, :] = jnp.sum(rolled, axis=0, keepdims=True)
        done = pl.ds(pair * 2 * HD, 2 * HD)
        copies.out(delta.at[pl.ds(0, 3), :, done], delta_hbm.at[:, :, done])

    wait_hidden.wait()
    wait_inputs.wait()
    for unit in range(4):
        units[unit // 2, unit % 2] = low(dot_tokens(inputs[unit // 3], delta[unit]))
    copies.out(units.at[1 - place_ref[0]], send_hbm)
    copies.out(units.at[place_ref[0]], keep_hbm)
    copies.finish()


def attend_back(place, heads, chance, upstream, inputs, hidden_low, after=()):
    count = upstream.shape[0]
    return kernel_call(
        attend_back_kernel,
        (place, heads, chance, upstream, inputs, hidden_low),
        [pltpu.SMEM] + [ANY] * 5,
        [
            ((3, count, D), BF, ANY),
            ((H, 2 * ROW), F32, VM),
            ((2, D, D), BF, ANY),
            ((2, D, D), BF, ANY),
        ],
        [
            VM(heads.shape, BF), VM(chance.shape, BF), VM(upstream.shape, BF),
            VM(inputs.shape, BF), VM((4, count, D), BF), VM((ROW, ROW), F32),
            VM((2, 2, D, D), BF), pltpu.SemaphoreType.DMA((36,)),
        ],
        after,
    )


def passage_end_kernel(
    place_ref, gains_ref, slope_delta_ref, answer_table_ref, ffn_gain_ref, final_gain_ref,
    self_gain_ref, cross_gain_ref, answer_gain_ref,
    input_hbm, delta_hbm, hidden_delta_hbm, query_hbm, key_hbm, value_hbm,
    gradient_hbm, small_low_ref,
    values, delta, hidden_delta, weights, gradient, small_ref, arrivals,
):
    copies = Copies(arrivals)
    wait_delta = copies.start(delta_hbm, delta)
    waits = [
        copies.start(source, weights.at[at])
        for at, source in enumerate((query_hbm, key_hbm, value_hbm))
    ]
    wait_input = copies.start(input_hbm, values)
    wait_hidden = copies.start(hidden_delta_hbm, hidden_delta)
    once = jnp.where((place_ref[0] == 0) & (place_ref[1] == 0), 1.0, 0.0)
    small_ref[...] = jnp.zeros_like(small_ref)
    small_ref[FFN : FFN + 1, :] = ffn_gain_ref[...]
    small_ref[FINAL : FINAL + 1, :] = final_gain_ref[...]
    small_ref[SELF : SELF + 1, :] = self_gain_ref[...] * once
    small_ref[CROSS : CROSS + 1, :] = cross_gain_ref[...] * once
    small_ref[ANSWER : ANSWER + 1, :] = answer_gain_ref[...] * once
    offsets = ROW - lax.broadcasted_iota(jnp.int32, (2 * ROW, 128), 0)
    matches = bucket_of(offsets, True) == lax.broadcasted_iota(jnp.int32, (2 * ROW, 128), 1)
    table = exact_dot(slope_delta_ref[...], jnp.where(matches, 1.0, 0.0))
    small_ref[8 : 8 + H, :128] = table
    small_ref[8 : 8 + H, 128:256] = answer_table_ref[:H, :] * once
    wait_delta.wait()
    for wait in waits:
        wait.wait()
    upward = dot_rows(delta[0], weights[0])
    upward += dot_rows(delta[1], weights[1])
    upward += dot_rows(delta[2], weights[2])
    wait_input.wait()
    wait_hidden.wait()
    back, gain_delta = rms_back(wide(values[...]), gain_row(gains_ref, ATTN), upward)
    small_ref[ATTN : ATTN + 1, :] = gain_delta
    small_low_ref[...] = low(small_ref[...])
    gradient[...] = back + hidden_delta[...]
    copies.out(gradient, gradient_hbm)
    copies.finish()


def passage_end(place, gains, small, rows, delta, hidden_delta, weights, after=()):
    count = rows.shape[0]
    return kernel_call(
        passage_end_kernel,
        (place, gains) + tuple(small) + (rows, delta, hidden_delta) + tuple(weights),
        [pltpu.SMEM] + [VM] * 8 + [ANY] * 6,
        [((count, D), F32, ANY), ((32, D), BF, VM)],
        [
            VM((count, D), BF), VM((3, count, D), BF), VM((count, D), F32), VM((3, D, D), BF),
            VM((count, D), F32), VM((32, D), F32), pltpu.SemaphoreType.DMA((8,)),
        ],
        after,
    )


def answer_end_kernel(
    asking_refs, middle_delta_ref, hidden_ref, input_ref, gains_ref,
    heads_ref, chance_ref, ask_hbm, mix_hbm, query_hbm, key_hbm, value_hbm,
    gradient_ref, asking_delta_ref, hidden_low_ref, delta_ref, cross_delta_ref,
    self_delta_ref, table_ref,
    weights, score_delta, arrivals,
):
    copies = Copies(arrivals)
    waits = [
        copies.start(source, weights.at[at])
        for at, source in enumerate((ask_hbm, mix_hbm, query_hbm, key_hbm, value_hbm))
    ]
    asking_delta_ref[...] = low(tree_sum([wide(ref[...]) for ref in asking_refs]))
    waits[0].wait()
    upward = dot_rows(asking_delta_ref[...], weights[0])
    back, gain_delta = rms_back(hidden_ref[...], gain_row(gains_ref, CROSS), upward)
    cross_delta_ref[...] = gain_delta
    back += middle_delta_ref[...]
    hidden_low = low(back)
    hidden_low_ref[...] = hidden_low
    waits[1].wait()
    upward = low(dot_rows(hidden_low, weights[1]))
    column = lax.broadcasted_iota(jnp.int32, (SLOT, 128), 0)
    lane = lax.broadcasted_iota(jnp.int32, (SLOT, 128), 1)
    mirror = low(jnp.where(column + lane == SLOT - 1, 1.0, 0.0))
    for block in range(upward.shape[0] // SLOT):
        slots = slice(block * SLOT, (block + 1) * SLOT)
        chances = chance_ref[block]
        taken = spread(upward[slots])
        delta_chances = dot_rows(taken, heads_ref[2, slots])
        inner = jnp.sum(delta_chances * wide(chances), axis=1, keepdims=True)
        deltas = low(wide(chances) * (delta_chances - inner))
        turned = dot(deltas, mirror)
        if block == 0:
            score_delta[...] = turned
        else:
            score_delta[...] += turned
        delta_ref[0, slots] = low(fold(dot(deltas, heads_ref[1, slots])))
        delta_ref[1, slots] = low(dot_tokens(deltas, spread(heads_ref[0, slots])))
        delta_ref[2, slots] = low(dot_tokens(chances, taken))
    for wait in waits[2:]:
        wait.wait()
    upward = dot_rows(delta_ref[0], weights[2])
    upward += dot_rows(delta_ref[1], weights[3])
    upward += dot_rows(delta_ref[2], weights[4])
    start_delta, gain_delta = rms_back(slotted(input_ref), gain_row(gains_ref, SELF), upward)
    self_delta_ref[...] = gain_delta
    unslotted(start_delta + back, gradient_ref)
    sums = []
    for h in range(H):
        rows = score_delta[h * SLOT : (h + 1) * SLOT]
        rolled = pltpu.roll(rows, 0, 1, stride=1, stride_axis=0)
        sums.append(jnp.sum(rolled, axis=0, keepdims=True))
    sums.append(jnp.zeros((16 - H, 128), F32))
    offsets = (SLOT - 1) - lax.broadcasted_iota(jnp.int32, (128, 128), 0)
    matches = bucket_of(offsets, False) == lax.broadcasted_iota(jnp.int32, (128, 128), 1)
    table_ref[...] = exact_dot(jnp.concatenate(sums, axis=0), jnp.where(matches, 1.0, 0.0))


def answer_out_kernel(middle_ref, wide_ref, out_hbm, result_ref, weight, arrivals):
    copies = Copies(arrivals)
    waits = []
    for at in range(out_hbm.shape[0] // D):
        part = pl.ds(at * D, D)
        waits.append(copies.start(out_hbm.at[part], weight.at[part]))
    total = middle_ref[...]
    for at, wait in enumerate(waits):
        part = slice(at * D, (at + 1) * D)
        wait.wait()
        total += dot(wide_ref[0, :, part], weight[part, :])
    unslotted(total, result_ref)


def answer_out(middle, wide_pair, weight, like, after=()):
    return kernel_call(
        answer_out_kernel,
        (middle, wide_pair, weight),
        [VM, VM, ANY],
        [(like.shape, BF, VM)],
        [VM(weight.shape, BF), pltpu.SemaphoreType.DMA((4,))],
        after,
    )[0]


def answer_end(
    place, asking_deltas, middle_delta, hidden, rows, gains, heads, chance, inputs, weights, shards,
    after=()
):
    count = hidden.shape[0]
    blocks = len(asking_deltas)
    outs, scratch = [], []
    if shards:
        outs = [((shards // 2, 3 * D // shards // 2, D), BF, VM)] * 2
        scratch = [VM((4, count, D), BF), VM((4, count, D), BF), VM((D, D), BF), VM((D, D), BF)]

    def body(place_ref, *refs):
        asking_refs, refs = refs[:blocks], refs[blocks:]
        input_refs, refs = refs[:4], refs[4:]
        first, last = refs[:18], refs[18:]
        share, own = last[: 6 if shards else 0], last[6 if shards else 0 :]
        answer_end_kernel(asking_refs, *first, *own)
        if shards:
            answer_square_weight(place_ref, *input_refs, first[12], first[13], first[14], *share)

    return kernel_call(
        body,
        (place, *asking_deltas, *inputs, middle_delta, hidden, rows, gains, heads, chance, *weights),
        [pltpu.SMEM] + [VM] * (blocks + 10) + [ANY] * 5,
        [
            (rows.shape, F32, VM),
            ((count, D), BF, VM),
            ((count, D), BF, VM),
            ((3, count, D), BF, VM),
            ((1, D), F32, VM),
            ((1, D), F32, VM),
            ((16, 128), F32, VM),
        ]
        + outs,
        scratch
        + [
            VM((5, D, D), BF), VM((H * SLOT, 128), F32), pltpu.SemaphoreType.DMA((5,)),
        ],
        after,
    )


def answer_wide_weight(
    place_ref, lows_ref, wide_ref, upstream_ref, in_send_ref, in_keep_ref, out_send_ref,
    out_keep_ref, inner, full
):
    core = place_ref[0]
    row = place_ref[1]
    width = in_send_ref.shape[1]
    half = D // 2
    part = pl.ds(pl.multiple_of((core * 2 + row) * D, D), D)
    inner[...] = low(dot_tokens(lows_ref[1], wide_ref[1, :, part]))
    upstream = slotted(upstream_ref)
    upstream = low(jnp.where(core == 0, upstream[:, :half], upstream[:, half:]))
    for at in range(wide_ref.shape[2] // D):
        span = slice(at * D, (at + 1) * D)
        full[span, :] = low(dot_tokens(wide_ref[0, :, span], upstream))
    for part_ref, sent in ((in_send_ref, True), (in_keep_ref, False)):
        for at in range(part_ref.shape[0]):
            own = place_ref[2]
            shard = at * 2 + (1 - own if sent else own)
            rows = pl.ds(pl.multiple_of(shard * width, 16), width)
            part_ref[at] = inner[rows, :]
    for part_ref, sent in ((out_send_ref, True), (out_keep_ref, False)):
        for at in range(part_ref.shape[0]):
            own = place_ref[3]
            shard = at // 2 * 4 + (1 - own if sent else own) * 2 + at % 2
            for side in range(2):
                begin = shard * 4 * width + row * 2 * width + side * width
                rows = pl.ds(pl.multiple_of(begin, 16), width)
                part_ref[at, :, side * half : (side + 1) * half] = full[rows, :]


def answer_square_weight(
    place_ref, crossed_ref, low_ref, attended_ref, normed_ref, asking_delta_ref, hidden_low_ref,
    delta_ref, send_ref, keep_ref, inputs, deltas, first, full,
):
    core = place_ref[0]
    row = place_ref[1]
    width = send_ref.shape[1] * 2 // 3
    inputs[0] = crossed_ref[...]
    inputs[1] = low_ref[0]
    inputs[2] = attended_ref[...]
    inputs[3] = normed_ref[...]
    deltas[0] = asking_delta_ref[...]
    deltas[1] = low_ref[2]
    deltas[2] = hidden_low_ref[...]
    deltas[3] = delta_ref[0]
    unit = core * 2 + row
    first[...] = low(dot_tokens(inputs[unit], deltas[unit]))
    full[...] = low(dot_tokens(normed_ref[...], delta_ref[1 + core]))
    for part_ref, sent in ((send_ref, True), (keep_ref, False)):
        for at in range(part_ref.shape[0]):
            own = place_ref[3]
            shard = at // 2 * 4 + (1 - own if sent else own) * 2 + at % 2
            rows = pl.ds(pl.multiple_of(shard * width, 16), width)
            part_ref[at, :width] = first[rows, :]
            rows = pl.ds(pl.multiple_of(shard * width + row * (width // 2), 16), width // 2)
            part_ref[at, width:] = full[rows, :]


class Part:
    def __init__(self, rows, left, first=0):
        self.rows = rows
        self.left = list(left)
        self.first = first
        self.terms = []

    def array(self, values, names):
        values = values.reshape((2,) * len(names) + (-1, values.shape[-1]))
        self.terms.append((values, list(names), None))
        return self

    def size(self, name):
        count = len([one for one in self.left if one != name])
        return (2**count) * self.rows if name else self.rows

    def sent(self, name, values, begin):
        self.left.remove(name)


class Total(Part):
    def __init__(self, values):
        super().__init__(values.shape[0], "")
        self.terms.append((values, [], 0))

    def size(self, name):
        return self.rows

    def sent(self, name, values, begin):
        self.terms = [(values, [], begin)]


PLACES = "cyxlh"


def bus(place, jobs, after=()):
    arrays = []
    plans = []
    scratch = []
    outs = []
    for name, parts in jobs:
        begin = 0
        for part in parts:
            kept = [one for one in part.left if one != name] if name else []
            for values, names, start in part.terms:
                at = [id(one) for one in arrays]
                if id(values) not in at:
                    arrays.append(values)
                    at.append(id(values))
                inner = [one for one in names if one in kept]
                room = (2,) * len(inner) + (part.rows, D) if start is None else (
                    (2 ** len(inner)) * part.rows, D
                )
                plans.append(
                    (len(outs), begin, at.index(id(values)), names, start, inner, part, kept, name)
                )
                scratch.append(VM(room, BF))
            begin += part.size(name)
        outs.append(((begin, D), BF, VM))
    count = len(arrays)

    def body(place_ref, *refs):
        sources, targets = refs[:count], refs[count : count + len(outs)]
        rooms, semaphores = refs[count + len(outs) : -1], refs[-1]
        copies = Copies(semaphores)

        def spot(one, part, name):
            own = place_ref[PLACES.index(one)]
            return 1 - own if one == name else own

        waits = []
        for room, (_, _, source, names, start, inner, part, kept, name) in zip(rooms, plans):
            if start is None:
                index = [
                    slice(None) if one in kept else spot(one, part, name) for one in names
                ]
                origin = sources[source].at[(*index, pl.ds(part.first, part.rows))]
            else:
                row = start
                for depth, one in enumerate(names):
                    if one not in kept:
                        stride = (2 ** (len(names) - 1 - depth)) * part.rows
                        row = row + spot(one, part, name) * stride
                length = (2 ** len(inner)) * part.rows
                origin = sources[source].at[pl.ds(pl.multiple_of(row, 16), length)]
            waits.append(copies.start(origin, room))
        for wait in waits:
            wait.wait()
        sums = {}
        for room, (out, begin, _, _, start, inner, part, kept, name) in zip(rooms, plans):
            for number in range(2 ** len(kept)):
                bits = [number >> (len(kept) - 1 - depth) & 1 for depth in range(len(kept))]
                at = dict(zip(kept, bits))
                if start is None:
                    value = room[tuple(at[one] for one in inner)] if inner else room[...]
                else:
                    value = room[number * part.rows : (number + 1) * part.rows]
                sums.setdefault((out, begin + number * part.rows, part.rows), []).append(value)
        for (out, begin, rows), values in sums.items():
            total = functools.reduce(jnp.add, [wide(value) for value in values])
            targets[out][begin : begin + rows] = low(total)

    return kernel_call(
        body,
        (place, *arrays),
        [pltpu.SMEM] + [ANY] * count,
        outs,
        scratch + [pltpu.SemaphoreType.DMA((len(plans),))],
        after,
    )


def ride(ring, place, jobs, after=()):
    sends = list(bus(place, jobs, after))
    trip = []
    for (name, parts), values in zip(jobs, sends):
        begin = 0
        stops = []
        for part in parts:
            length = part.size(name)
            part.sent(name, values, begin)
            stops.append((part, begin, list(part.left)))
            begin += length
        trip.append([ring.swap(values, name), stops])
    return trip, sends


def arrive(items, *trips):
    legs = [leg for trip in trips for leg in trip]
    items = lax.optimization_barrier((*items, *[leg[0] for leg in legs]))
    count = len(items) - len(legs)
    for values, (_, stops) in zip(items[count:], legs):
        for part, begin, names in stops:
            part.terms.append((values, names, begin))
    return items[:count]


def assemble_kernel(place_ref, mine_hbm, near_hbm, far_hbm, across_hbm, *refs, lay):
    outs, whole, arrivals = refs[:-2], refs[-2], refs[-1]
    copies = Copies(arrivals)
    core, row = place_ref[0], place_ref[1]
    waits = [
        copies.start(mine_hbm, whole.at[core, row]),
        copies.start(near_hbm, whole.at[core, 1 - row]),
        copies.start(far_hbm, whole.at[1 - core, row]),
        copies.start(across_hbm, whole.at[1 - core, 1 - row]),
    ]
    for wait in waits:
        wait.wait()
    for out, rows, columns, part in lay:
        c, y, begin, lanes = part
        height, width = rows[1] - rows[0], columns[1] - columns[0]
        outs[out][rows[0] : rows[1], columns[0] : columns[1]] = wide(
            whole[c, y, begin : begin + height, lanes : lanes + width]
        )


def assemble(place, arrays, shapes, lay):
    rows = arrays[0].shape[0]
    return kernel_call(
        functools.partial(assemble_kernel, lay=lay),
        (place, *arrays),
        [pltpu.SMEM] + [ANY] * 4,
        [(shape, F32, VM) for shape in shapes],
        [VM((2, 2, rows, D), BF), pltpu.SemaphoreType.DMA((4,))],
    )


def layout(rows):
    half = D // 2
    lay = []
    shapes = []

    def stacked(begin):
        for c in range(2):
            for y in range(2):
                at = (y * rows // 2, (y + 1) * rows // 2)
                lay.append((len(shapes), at, (0, D), (c, y, begin, 0)))
            shapes.append((rows, D))

    def unhalved(begin):
        for c in range(2):
            for y in range(2):
                for side in range(2):
                    low_row = (y * 2 + side) * rows
                    lay.append(
                        (
                            len(shapes),
                            (low_row, low_row + rows),
                            (c * half, (c + 1) * half),
                            (c, y, begin, side * half),
                        )
                    )
        shapes.append((4 * rows, D))

    def side_by_side(begin):
        for c in range(2):
            for y in range(2):
                at = c * 2 + y
                lay.append((len(shapes), (0, rows), (at * D, (at + 1) * D), (c, y, begin, 0)))
        shapes.append((rows, 4 * D))

    def units(begin):
        for c in range(2):
            for y in range(2):
                lay.append((len(shapes), (0, rows), (0, D), (c, y, begin, 0)))
                shapes.append((rows, D))

    return lay, shapes, stacked, unhalved, side_by_side, units


class Ring:
    def __init__(self, mesh):
        self.dp = mesh.shape["dp"]
        self.blk = mesh.shape["blk"]
        self.cut = self.blk == 4 and self.dp == 8

    def bit(self, name):
        return {"c": 1, "y": 2, "x": 4, "l": 8, "h": 16}[name]

    def number(self):
        return lax.axis_index("dp") * self.blk + lax.axis_index("blk")

    def place(self, name):
        return self.number() // self.bit(name) % 2

    def swap(self, values, *names):
        mask = sum(self.bit(name) for name in names)
        moves = [(at, at ^ mask) for at in range(self.dp * self.blk)]
        return lax.ppermute(values, ("dp", "blk"), moves)


class Beside:
    def __init__(self, ring, mine):
        self.ring = ring
        self.mine = mine
        self.arriving = [ring.swap(mine, "y"), ring.swap(mine, "c")]

    def send(self, cues=()):
        near, far, *_ = lax.optimization_barrier((*self.arriving, *cues))
        self.arriving = [near, far, self.ring.swap(near, "c")]

    def arrays(self, cues=()):
        near, far, across, *_ = lax.optimization_barrier((*self.arriving, *cues))
        return [self.mine, near, far, across]


def on_device(
    ring,
    encoder_input,
    decoder_input,
    encoder_cotangent,
    decoder_cotangent,
    segment_ids,
    padding_mask,
    answer_length,
    encoder_attn_gain,
    encoder_query,
    encoder_key,
    encoder_value,
    encoder_mix,
    encoder_bias_table,
    encoder_ffn_gain,
    encoder_ffn_in,
    encoder_ffn_out,
    final_gain,
    cross_key,
    cross_value,
    decoder_self_gain,
    decoder_query,
    decoder_key,
    decoder_value,
    decoder_mix,
    decoder_bias_table,
    decoder_cross_gain,
    cross_query,
    cross_mix,
    decoder_ffn_gain,
    decoder_ffn_in,
    decoder_ffn_out,
):
    cut = ring.cut
    shard = D // ring.dp
    questions = encoder_input.shape[0]
    batch = questions * encoder_input.shape[1]
    passage_rows = encoder_input.reshape(batch * ROW, D)
    passage_upstream = encoder_cotangent.reshape(batch * ROW, D)
    core = ring.place("c")
    row = lax.axis_index("blk") // 2
    place = [core, row, ring.place("x"), ring.place("l"), ring.place("h")]
    place = jnp.stack(place).astype(jnp.int32)
    (
        gains,
        answer_normed,
        answer_heads,
        answer_chances,
        answer_attended,
        answer_hidden,
        answer_crossed,
        asking,
        packed,
        inputs,
        heads,
        chances,
        hidden,
        second,
        active,
        bend,
        encoded,
        result,
        final,
        memory,
        scores,
    ) = passage(
        answer_length,
        decoder_input,
        passage_rows,
        segment_ids.reshape(batch, 1, ROW),
        padding_mask.reshape(batch, 1, ROW),
        encoder_bias_table.T,
        decoder_bias_table.T,
        (
            encoder_attn_gain,
            encoder_ffn_gain,
            final_gain,
            decoder_self_gain,
            decoder_cross_gain,
            decoder_ffn_gain,
        ),
        (decoder_query, decoder_key, decoder_value, decoder_mix, cross_query),
        (
            encoder_query,
            encoder_key,
            encoder_value,
            encoder_mix,
            encoder_ffn_in,
            encoder_ffn_out,
            cross_key,
            cross_value,
        ),
    )

    def neighbours(values):
        if cut:
            return [values] + [ring.swap(values, *names) for names in ("c", "y", "yc")]
        every = lax.all_gather(values, "blk", axis=0)
        return [every[at] for at in range(ring.blk)]

    every = neighbours(packed)
    (upstream_cue, _) = lax.optimization_barrier((decoder_cotangent, packed))
    answer_upward = answer_up(upstream_cue, decoder_ffn_out)
    (
        answer_lows,
        answer_wides,
        answer_middle_rows,
        middle_delta,
        answer_gain_delta,
        memory_delta,
        asking_delta,
        *wide_halves,
    ) = answer_middle(
        place,
        every,
        asking,
        answer_hidden,
        answer_upward,
        decoder_cotangent,
        gains,
        scores,
        memory,
        (cross_mix, decoder_ffn_in),
        ring.dp if cut else None,
    )

    asking_deltas = neighbours(asking_delta)
    after = []
    if cut:
        half = shard // 2
        in_half, in_kept, out_half, out_kept = wide_halves
        wide_first = Part(shard, "lh").array(in_kept, "hl")
        wide_second = Part(shard, "xh").array(out_kept, "hx")
        wide_got = [ring.swap(in_half, "x"), ring.swap(out_half, "l")]
        after = [in_half]
    memory_send, memory_keep, output_delta, before, final_gain_delta = memory_back(
        place,
        gains,
        memory_delta,
        final,
        encoded,
        passage_upstream,
        (cross_key, cross_value),
        active,
        encoder_ffn_out,
        bend,
        ring.dp,
        after=after,
    )
    if cut:
        memory_send, cue, *wide_got = arrive([memory_send, place, *wide_got])
        wide_first.array(wide_got[0], "hl")
        wide_second.array(wide_got[1], "hx")
        memory_got = ring.swap(memory_send, "c")
        trip, sends = ride(ring, cue, [("l", [wide_first]), ("x", [wide_second])])
        after = sends + [memory_send] + asking_deltas
    (
        answer_gradient,
        asking_delta,
        answer_hidden_low,
        answer_heads_delta,
        cross_gain_delta,
        self_gain_delta,
        answer_table_delta,
        *square_halves,
    ) = answer_end(
        place,
        asking_deltas,
        middle_delta,
        answer_hidden,
        decoder_input,
        gains,
        answer_heads,
        answer_chances,
        (answer_crossed, answer_lows, answer_attended, answer_normed),
        (cross_query, decoder_mix, decoder_query, decoder_key, decoder_value),
        ring.dp if cut else None,
        after=after,
    )
    after = []
    if cut:
        send, keep = square_halves
        send, memory_got, cue = arrive([send, memory_got, place], trip)
        answer_square = Part(3 * half, "hx").array(keep, "hx")
        square_got = ring.swap(send, "l")
        top = 5 * 16
        memory_first = Part(top, "yxlh").array(memory_keep, "hlxy").array(memory_got, "hlxy")
        memory_second = Part(3 * half - top, "xylh", top)
        memory_second.array(memory_keep, "hlxy").array(memory_got, "hlxy")
        trip_memory, sends = ride(
            ring, cue, [("y", [memory_first]), ("x", [memory_second]), ("h", [wide_first, wide_second])]
        )
        after = sends + [send]
    in_send, in_keep, hidden_delta, hidden_low, attended_delta, ffn_gain_delta = wide_in_back(
        place,
        gains,
        second,
        before,
        encoder_ffn_in,
        hidden,
        output_delta,
        encoder_mix,
        after=after,
    )
    after = []
    if cut:
        in_send, attended_delta = arrive([in_send, attended_delta], trip_memory)
        in_got = ring.swap(in_send, "c")
        after = [in_send]
    answer_result = answer_out(
        answer_middle_rows, answer_wides, decoder_ffn_out, decoder_input, after=after
    )
    after = []
    if cut:
        answer_result, attended_delta, in_got, square_got, cue = lax.optimization_barrier(
            (answer_result, attended_delta, in_got, square_got, place)
        )
        answer_square.array(square_got, "hx")
        in_first = Part(half, "yxlh").array(in_keep, "yhlx").array(in_got, "yhlx")
        in_second = Part(half, "xylh", half).array(in_keep, "yhlx").array(in_got, "yhlx")
        trip_in, after = ride(
            ring,
            cue,
            [
                ("y", [in_first, memory_second]),
                ("x", [in_second, memory_first]),
                ("h", [answer_square]),
            ],
        )
    heads_delta, slope_delta, heads_send, heads_keep = attend_back(
        place, heads, chances, attended_delta, inputs, hidden_low, after=after
    )
    after = []
    if cut:
        heads_send, cue = arrive([heads_send, place], trip_in)
        heads_got = ring.swap(heads_send, "c")
        trip_in, sends = ride(
            ring,
            cue,
            [
                ("x", [in_first]),
                ("y", [in_second]),
                ("l", [memory_first, memory_second]),
            ],
        )
        heads_got, cue, *_ = lax.optimization_barrier((heads_got, place, *sends))
        heads_first = Part(half, "yxlh").array(heads_keep, "yhlx").array(heads_got, "yhlx")
        heads_second = Part(half, "xylh", half)
        heads_second.array(heads_keep, "yhlx").array(heads_got, "yhlx")
        trip_heads, after = ride(ring, cue, [("y", [heads_first]), ("x", [heads_second])])
    passage_gradient, small = passage_end(
        place,
        gains,
        (
            slope_delta,
            answer_table_delta,
            ffn_gain_delta,
            final_gain_delta,
            self_gain_delta,
            cross_gain_delta,
            answer_gain_delta,
        ),
        passage_rows,
        heads_delta,
        hidden_delta,
        (encoder_query, encoder_key, encoder_value),
        after=after,
    )
    if cut:
        small_got = ring.swap(small, "c")
        small_got, cue = arrive([small_got, place], trip_in, trip_heads)
        total = Total(small)
        total.terms.append((small_got, [], 0))
        trip, sends = ride(
            ring,
            cue,
            [
                ("x", [heads_first, answer_square]),
                ("y", [heads_second, total]),
                ("l", [in_first, in_second]),
                ("h", [memory_first, memory_second]),
            ],
        )
        (cue,) = arrive([place], trip)
        trip, sends = ride(
            ring,
            cue,
            [("l", [heads_first, heads_second, total]), ("h", [in_first, in_second])],
        )
        (done,) = bus(
            place,
            [(None, [memory_first, memory_second, wide_first, wide_second, answer_square])],
            sends,
        )
        first = Beside(ring, done)
        cue, _ = arrive([place, done], trip)
        trip, sends = ride(ring, cue, [("h", [heads_first, heads_second, total])])
        cue, *first.arriving = arrive([place, *first.arriving], trip)
        done, small = bus(
            cue,
            [(None, [in_first, in_second, heads_first, heads_second]), (None, [total])],
        )
        last = Beside(ring, done)
        small_got = ring.swap(small, "x")
        first.send([done])
        lay, shapes, stacked, unhalved, side_by_side, units = layout(shard)
        stacked(0)
        unhalved(half)
        side_by_side(half + shard)
        unhalved(half + 2 * shard)
        units(half + 3 * shard)
        stacked(half + 4 * shard)
        weights = list(assemble(place, first.arrays(), shapes, lay))
        last.send(weights[:1])
        lay, shapes, stacked, unhalved, side_by_side, units = layout(shard)
        side_by_side(0)
        units(shard)
        weights += list(assemble(place, last.arrays(), shapes, lay))
        small = wide(small) + wide(small_got)
    else:
        small = lax.psum(wide(small), ("dp", "blk"))
    mine = lax.axis_index("dp")
    gain_deltas = lax.dynamic_slice_in_dim(small[:6], mine * shard, shard, 1)
    tables = NB // ring.dp
    table_deltas = [
        lax.dynamic_slice_in_dim(small[8 : 8 + H, begin : begin + NB], mine * tables, tables, 1).T
        for begin in (0, 128)
    ]

    if not cut:
        weights = whole_weights(
            core,
            (memory_send, memory_keep),
            (in_send, in_keep),
            (heads_send, heads_keep),
            (
                (answer_lows[1], answer_wides[1]),
                (
                    answer_wides[0],
                    low(slotted(decoder_cotangent)),
                ),
                (answer_crossed, asking_delta),
                (answer_lows[0], answer_lows[2]),
                (answer_attended, answer_hidden_low),
                (answer_normed, answer_heads_delta[0]),
                (answer_normed, answer_heads_delta[1]),
                (answer_normed, answer_heads_delta[2]),
            ),
        )
    (
        gradient_cross_key,
        gradient_cross_value,
        gradient_encoder_ffn_out,
        gradient_decoder_ffn_in,
        gradient_decoder_ffn_out,
        gradient_cross_query,
        gradient_cross_mix,
        gradient_decoder_mix,
        gradient_decoder_query,
        gradient_decoder_key,
        gradient_decoder_value,
        gradient_encoder_ffn_in,
        gradient_encoder_query,
        gradient_encoder_key,
        gradient_encoder_value,
        gradient_encoder_mix,
    ) = weights
    return (
        result.reshape(encoder_input.shape),
        answer_result,
        passage_gradient.reshape(encoder_input.shape),
        answer_gradient,
        gain_deltas[ATTN],
        gradient_encoder_query,
        gradient_encoder_key,
        gradient_encoder_value,
        gradient_encoder_mix,
        table_deltas[0],
        gain_deltas[FFN],
        gradient_encoder_ffn_in,
        gradient_encoder_ffn_out,
        gain_deltas[FINAL],
        gradient_cross_key,
        gradient_cross_value,
        gain_deltas[SELF],
        gradient_decoder_query,
        gradient_decoder_key,
        gradient_decoder_value,
        gradient_decoder_mix,
        table_deltas[1],
        gain_deltas[CROSS],
        gradient_cross_query,
        gradient_cross_mix,
        gain_deltas[ANSWER],
        gradient_decoder_ffn_in,
        gradient_decoder_ffn_out,
    )


def whole_weights(core, memory, inner, heads, answers):
    def both(pair):
        send, keep = pair
        return (jnp.where(core == 0, keep, send), jnp.where(core == 0, send, keep))

    def shared(gradient):
        return lax.psum_scatter(low(gradient), "dp", scatter_dimension=0, tiled=True)

    def summed(gradient):
        return lax.psum(shared(gradient), "blk")

    memory = both(memory)
    shards, _, rows, _ = memory[0].shape
    cut = rows // 3
    passages = [part[:, :, :cut].reshape(D, D) for part in memory]
    out = [
        part[:, :, cut:]
        .reshape(shards, 2, 2 * cut, 2, D // 2)
        .swapaxes(2, 3)
        .reshape(8 * cut * shards, D // 2)
        for part in memory
    ]
    passages.append(jnp.concatenate(out, axis=1))
    passages.append(jnp.concatenate([unit for half in both(inner) for unit in half], axis=1))
    passages += [unit for half in both(heads) for unit in half]
    passages = [wide(summed(item)) for item in passages]
    answers = [wide(shared(dot_tokens(inputs, upstream))) for inputs, upstream in answers]
    return passages[:3] + answers + passages[3:]


def solution(mesh):
    dims = {4: P("dp", "blk", None, None), 3: P("dp", None, None), 2: P("dp", None), 1: P("dp")}
    rows = P("dp", "blk", None)
    return jax.shard_map(
        functools.partial(on_device, Ring(mesh)),
        mesh=mesh,
        in_specs=(dims[4], dims[3], dims[4], dims[3], rows, rows, dims[1]) + (P(),) * 24,
        out_specs=(dims[4], dims[3], dims[4], dims[3])
        + tuple(dims[1 if at in (0, 6, 9, 12, 18, 21) else 2] for at in range(24)),
        check_vma=False,
    )
```

```python
import functools
import math

import jax
import jax.numpy as jnp
from jax import lax
from jax.experimental import pallas as pl
from jax.experimental.pallas import tpu as pltpu
from jax.sharding import PartitionSpec as P

D = 768
H = 12
HD = 64
NB = 32
MAXD = 128
ROW = 256
ANS = 20


EPSILON = 1e-06
NEGATIVE = -1e30


SLOT = 32
ANY = pl.ANY
VM = pltpu.VMEM
BF = jnp.bfloat16
F32 = jnp.float32
LIMIT = 60 << 20


def dot(left, right):
    return jnp.dot(left, right, preferred_element_type=jnp.float32)


def dot_rows(left, right):
    return lax.dot_general(
        left, right, (((1,), (1,)), ((), ())), preferred_element_type=jnp.float32
    )


def dot_tokens(left, right):
    return lax.dot_general(
        left, right, (((0,), (0,)), ((), ())), preferred_element_type=jnp.float32
    )


def low(values):
    return values.astype(jnp.bfloat16)


def wide(values):
    return values.astype(jnp.float32)


def slotted(ref):
    spare = jnp.zeros((SLOT - ANS, D), F32)
    return jnp.concatenate(
        [part for at in range(ref.shape[0]) for part in (wide(ref[at]), spare)], axis=0
    )


def unslotted(values, ref):
    for at in range(ref.shape[0]):
        ref[at] = values[at * SLOT : at * SLOT + ANS].astype(ref.dtype)


ATTN, FFN, FINAL, SELF, CROSS, ANSWER = range(6)


def gain_row(gains_ref, which):
    return gains_ref[which : which + 1, :]


def rms_scale(values):
    return lax.rsqrt(jnp.mean(values * values, axis=-1, keepdims=True) + EPSILON)


def head_lanes(rows, width=D):
    return lax.broadcasted_iota(jnp.int32, (rows, width), 1) // HD


def spread(rows):
    lanes = head_lanes(rows.shape[0])
    values = wide(rows)
    return low(jnp.concatenate([jnp.where(lanes == h, values, 0.0) for h in range(H)], axis=0))


def fold(full):
    rows = full.shape[0] // H
    lanes = head_lanes(rows)
    total = jnp.zeros((rows, full.shape[1]), jnp.float32)
    for h in range(H):
        total = jnp.where(lanes == h, full[h * rows : (h + 1) * rows], total)
    return total


def gelu_pair(values):
    square = values * values
    inner = values * (0.7978845608 + (0.7978845608 * 0.044715) * square)
    half = 0.5 + 0.5 * jnp.tanh(inner)
    active = values * half
    slope = 0.7978845608 + (3.0 * 0.7978845608 * 0.044715) * square
    return (active, half + 2.0 * active * (1.0 - half) * slope)


class Copies:
    def __init__(self, semaphores):
        self.semaphores = semaphores
        self.count = 0
        self.open = []

    def start(self, source, target):
        copy = pltpu.make_async_copy(source, target, self.semaphores.at[self.count])
        self.count += 1
        copy.start()
        return copy

    def out(self, source, target):
        self.open.append(self.start(source, target))

    def finish(self):
        for copy in self.open:
            copy.wait()


def kernel_call(body, operands, spaces, outs, scratch, after=()):
    if after:
        first, *_ = lax.optimization_barrier((operands[0], *after))
        operands = (first, *operands[1:])
    return pl.pallas_call(
        body,
        in_specs=[pl.BlockSpec(memory_space=space) for space in spaces],
        out_specs=[pl.BlockSpec(memory_space=space) for _, _, space in outs],
        out_shape=[jax.ShapeDtypeStruct(shape, dtype) for shape, dtype, _ in outs],
        scratch_shapes=scratch,
        compiler_params=pltpu.CompilerParams(vmem_limit_bytes=LIMIT),
        cost_estimate=pl.CostEstimate(flops=10**13, bytes_accessed=10**9, transcendentals=0),
    )(*operands)


def bucket_of(offsets, both_ways):
    if both_ways:
        buckets = NB // 2
        index = jnp.where(offsets > 0, buckets, 0)
        distance = jnp.abs(offsets)
    else:
        buckets = NB
        index = jnp.zeros_like(offsets)
        distance = jnp.maximum(-offsets, 0)
    exact = buckets // 2
    index = index + jnp.minimum(distance, exact)
    for step in range(1, buckets - exact):
        border = math.ceil(exact * (MAXD / exact) ** (step / (buckets - exact)) - 1e-09)
        index = index + jnp.where(distance >= border, 1, 0)
    return index


def table_slopes(table, width, both_ways, turn):
    offsets = turn * (lax.broadcasted_iota(jnp.int32, (NB, width), 1) - width // 2)
    matches = bucket_of(offsets, both_ways) == lax.broadcasted_iota(jnp.int32, (NB, width), 0)
    return dot(table, low(jnp.where(matches, 1.0, 0.0)))


def slope_bias(slopes, rows):
    width = slopes.shape[1]
    spread_slopes = jnp.broadcast_to(slopes, (rows, width))
    return pltpu.roll(spread_slopes, width // 2, 1, stride=1, stride_axis=0)[:, : width // 2]


def passage_kernel(
    length_ref, answer_input_ref, input_ref, segment_ref, padding_ref, table_ref, answer_table_ref,
    gain_refs,
    answer_query_hbm, answer_key_hbm, answer_value_hbm, answer_mix_hbm, ask_hbm,
    query_hbm, key_hbm, value_hbm, mix_hbm, in_hbm, out_hbm, cross_key_hbm, cross_value_hbm,
    gains_ref, answer_normed_ref, answer_heads_ref, answer_chance_ref, answer_attended_ref,
    answer_hidden_ref, crossed_ref, asking_ref, packed_ref,
    inputs_hbm, heads_hbm, chance_hbm, hidden_hbm, second_hbm,
    active_hbm, bend_hbm, encoded_hbm, result_hbm, final_hbm, memory_hbm, score_hbm,
    answer_square, square, wide_in, wide_out, slopes, arrivals,
    inputs, heads, chance, hidden, second,
    active, bend, memory, score,
):
    copies = Copies(arrivals)
    answer_waits = [
        copies.start(source, answer_square.at[at])
        for at, source in enumerate(
            (answer_query_hbm, answer_key_hbm, answer_value_hbm, answer_mix_hbm, ask_hbm)
        )
    ]
    square_hbm = (query_hbm, key_hbm, value_hbm, mix_hbm)
    rows = input_ref.shape[0]
    blocks = rows // ROW
    normed = inputs.at[0]
    attended = inputs.at[1]

    gains = [wide(ref[...]).reshape(1, D) for ref in gain_refs]
    for at, gain in enumerate(gains):
        gains_ref[at : at + 1, :] = gain
    values = wide(input_ref[...])
    normed[...] = low(values * rms_scale(values) * gains[ATTN])
    waits = [copies.start(source, square.at[at]) for at, source in enumerate(square_hbm)]
    slopes[...] = table_slopes(table_ref[...], 2 * ROW, True, 1)
    place_row = lax.broadcasted_iota(jnp.int32, (ROW, ROW), 0)
    place_column = lax.broadcasted_iota(jnp.int32, (ROW, ROW), 1)
    for block in range(blocks):
        segment_row = jnp.broadcast_to(segment_ref[block], (ROW, ROW))
        padding_row = jnp.broadcast_to(padding_ref[block], (ROW, ROW))
        own = (segment_row == segment_row.T) & (padding_row == 1)
        score[block, :ROW] = jnp.where(own | (place_row == place_column), 0.0, NEGATIVE)

    answer_values = slotted(answer_input_ref)
    answer_normed = low(answer_values * rms_scale(answer_values) * gains[SELF])
    answer_normed_ref[...] = answer_normed
    for at in range(3):
        answer_waits[at].wait()
        answer_heads_ref[at] = low(dot(answer_normed, answer_square[at]))
    wait_in = copies.start(in_hbm, wide_in)
    wait_out = copies.start(out_hbm, wide_out)
    cross_waits = [
        copies.start(source, answer_square.at[at])
        for at, source in enumerate((cross_key_hbm, cross_value_hbm))
    ]
    answer_slopes = table_slopes(answer_table_ref[...], 128, False, 1)
    answer_bias = jnp.concatenate(
        [slope_bias(answer_slopes[h : h + 1], SLOT)[:, :SLOT] for h in range(H)], axis=0
    )
    row = lax.broadcasted_iota(jnp.int32, (H * SLOT, SLOT), 0) % SLOT
    column = lax.broadcasted_iota(jnp.int32, (H * SLOT, SLOT), 1)
    for at in range(blocks):
        slots = slice(at * SLOT, (at + 1) * SLOT)
        asked = spread(answer_heads_ref[0, slots])
        scores = dot_rows(asked, answer_heads_ref[1, slots]) + answer_bias
        allowed = (column <= row) & (column < length_ref[at])
        scores = jnp.where(allowed, scores, NEGATIVE)
        powers = jnp.exp(scores - jnp.max(scores, axis=1, keepdims=True))
        chances = low(powers / jnp.sum(powers, axis=1, keepdims=True))
        answer_chance_ref[at] = chances
        answer_attended_ref[slots] = low(fold(dot(chances, answer_heads_ref[2, slots])))
    answer_waits[3].wait()
    answer_hidden = answer_values + dot(answer_attended_ref[...], answer_square[3])
    answer_hidden_ref[...] = answer_hidden
    crossed = low(answer_hidden * rms_scale(answer_hidden) * gains[CROSS])
    crossed_ref[...] = crossed
    answer_waits[4].wait()
    asking_ref[...] = low(dot(crossed, answer_square[4]))

    for at in range(3):
        waits[at].wait()
        heads[at] = low(dot(normed[...], square[at]))
    heads_out = copies.start(heads, heads_hbm)
    second_half = lax.broadcasted_iota(jnp.int32, (ROW, 2 * HD), 1) >= HD

    for pair in range(H // 2):
        lanes = slice(pair * 2 * HD, (pair + 1) * 2 * HD)
        sums = []
        for which in range(2):
            head = pair * 2 + which
            bias = slope_bias(slopes[head : head + 1, :], ROW)
            for block in range(blocks):
                span = slice(block * ROW, (block + 1) * ROW)
                asked = heads[0, span, lanes]
                own = jnp.where(second_half == (which == 1), asked, jnp.zeros_like(asked))
                scores = dot_rows(own, heads[1, span, lanes]) + (bias + score[block, :ROW])
                powers = jnp.exp(scores - jnp.max(scores, axis=1, keepdims=True))
                chances = low(powers * (1.0 / jnp.sum(powers, axis=1, keepdims=True)))
                chance[head, block] = chances.T
                taken = dot(chances, heads[2, span, lanes])
                if which == 0:
                    sums.append(taken)
                else:
                    attended[span, lanes] = low(jnp.where(second_half, taken, sums[block]))
        part = pl.ds(pair * 2, 2)
        copies.out(chance.at[part], chance_hbm.at[part])

    copies.out(inputs, inputs_hbm)
    waits[3].wait()
    values = wide(input_ref[...]) + dot(attended[...], square[3])
    hidden[...] = values
    hidden_out = copies.start(hidden, hidden_hbm)
    second[...] = low(values * rms_scale(values) * gains[FFN])
    copies.out(second, second_hbm)
    wait_in.wait()
    for at in range(in_hbm.shape[1] // D):
        lanes = slice(at * D, (at + 1) * D)
        up, slope = gelu_pair(dot(second[...], wide_in[:, lanes]))
        active[:, lanes] = low(up)
        bend[:, lanes] = low(slope)
        copies.out(active.at[:, lanes], active_hbm.at[:, lanes])
        copies.out(bend.at[:, lanes], bend_hbm.at[:, lanes])
    wait_out.wait()
    values = hidden[...] + dot(active[...], wide_out[...])
    hidden_out.wait()
    hidden[...] = values
    copies.out(hidden, encoded_hbm)
    heads_out.wait()
    result = heads.at[0]
    final = heads.at[1]
    result[...] = low(values)
    copies.out(result, result_hbm)
    final[...] = low(values * rms_scale(values) * gains[FINAL])
    copies.out(final, final_hbm)
    for at in range(2):
        cross_waits[at].wait()
        memory[at] = low(dot(final[...], answer_square[at]))
    copies.out(memory, memory_hbm)

    lane = lax.broadcasted_iota(jnp.int32, (SLOT, 128), 1)
    for block in range(blocks):
        span = slice(block * ROW, (block + 1) * ROW)
        slots = slice(block * SLOT, (block + 1) * SLOT)
        scores = dot_rows(spread(asking_ref[slots]), memory[0, span])
        scores = jnp.where(padding_ref[block] == 1, scores, NEGATIVE)
        score[block] = scores
        top = jnp.max(scores, axis=1, keepdims=True)
        powers = jnp.exp(scores - top)
        sums = jnp.sum(powers, axis=1, keepdims=True)
        reading = fold(dot(low(powers * (1.0 / sums)), memory[1, span]))
        packed_ref[slots, :D] = low(reading)
        total = top + jnp.log(sums)
        extra = jnp.zeros((SLOT, 128), F32)
        for h in range(H):
            rest = total[h * SLOT : (h + 1) * SLOT]
            for piece in range(3):
                part = wide(low(rest))
                extra = jnp.where(lane == piece * H + h, part, extra)
                rest = rest - part
        packed_ref[slots, D:] = low(extra)
    copies.out(score, score_hbm)
    copies.finish()


def passage(
    length, answer_input, rows, segments, padding, table, answer_table, gains, answer_weights, weights
):
    count = rows.shape[0]
    blocks = count // ROW
    slots = blocks * SLOT
    wide_size = weights[4].shape[1]
    small = [
        ((len(gains), D), F32),
        ((slots, D), BF),
        ((3, slots, D), BF),
        ((blocks, H * SLOT, SLOT), BF),
        ((slots, D), BF),
        ((slots, D), F32),
        ((slots, D), BF),
        ((slots, D), BF),
        ((slots, D + 128), BF),
    ]
    whole = [
        ((2, count, D), BF),
        ((3, count, D), BF),
        ((H, blocks, ROW, ROW), BF),
        ((count, D), F32),
        ((count, D), BF),
        ((count, wide_size), BF),
        ((count, wide_size), BF),
        ((count, D), F32),
        ((count, D), BF),
        ((count, D), BF),
        ((2, count, D), BF),
        ((blocks, H * SLOT, ROW), F32),
    ]
    first = 7

    def body(*refs):
        last = first + len(gains)
        passage_kernel(*refs[:first], refs[first:last], *refs[last:])

    return kernel_call(
        body,
        (length, answer_input, rows, segments, padding, table, answer_table)
        + tuple(gains)
        + tuple(answer_weights)
        + tuple(weights),
        [pltpu.SMEM] + [VM] * (6 + len(gains)) + [ANY] * 13,
        [(shape, dtype, VM) for shape, dtype in small]
        + [(shape, dtype, ANY) for shape, dtype in whole],
        [
            VM((5, D, D), BF),
            VM((4, D, D), BF),
            VM((D, wide_size), BF),
            VM((wide_size, D), BF),
            VM((H, 2 * ROW), F32),
            pltpu.SemaphoreType.DMA((40,)),
        ]
        + [VM(shape, dtype) for at, (shape, dtype) in enumerate(whole) if at not in (7, 8, 9)],
    )


def rms_back(values, gain, upstream):
    scale = rms_scale(values)
    scaled = upstream * gain
    inner = jnp.mean(scaled * values, axis=-1, keepdims=True)
    delta = scaled * scale - values * (scale * scale * scale) * inner
    return (delta, jnp.sum(upstream * values * scale, axis=0, keepdims=True))


def exact_dot(left, right, rows=False):
    return lax.dot_general(
        left,
        right,
        (((1,), (1 if rows else 0,)), ((), ())),
        precision=lax.Precision.HIGHEST,
        preferred_element_type=jnp.float32,
    )


def head_columns(values):
    return jnp.concatenate([values[:, h : h + 1] for h in range(H)], axis=0)


def tree_sum(items):
    while len(items) > 1:
        items = [
            items[at] + items[at + 1] if at + 1 < len(items) else items[at]
            for at in range(0, len(items), 2)
        ]
    return items[0]


def answer_up_kernel(upstream_ref, out_hbm, up_ref, weight, arrivals):
    copies = Copies(arrivals)
    waits = []
    for at in range(out_hbm.shape[0] // D):
        part = pl.ds(at * D, D)
        waits.append(copies.start(out_hbm.at[part], weight.at[part]))
    upstream = low(slotted(upstream_ref))
    for at, wait in enumerate(waits):
        part = slice(at * D, (at + 1) * D)
        wait.wait()
        up_ref[:, part] = dot_rows(upstream, weight[part, :])


def answer_up(upstream, weight):
    return kernel_call(
        answer_up_kernel,
        (upstream, weight),
        [VM, ANY],
        [((upstream.shape[0] * SLOT, weight.shape[0]), F32, VM)],
        [VM(weight.shape, BF), pltpu.SemaphoreType.DMA((4,))],
    )[0]


def answer_middle_kernel(
    every_refs, asking_ref, hidden_ref, up_ref, upstream_ref, gains_ref, score_hbm, memory_hbm,
    mix_hbm, in_hbm,
    low_ref, wide_ref, middle_ref, middle_delta_ref, gain_delta_ref, memory_delta_hbm,
    asking_delta_ref, *refs, place_ref=None,
):
    *weight_refs, score, memory, memory_delta, mix, wide_in, arrivals = refs
    copies = Copies(arrivals)
    wait_mix = copies.start(mix_hbm, mix)
    wait_in = copies.start(in_hbm, wide_in)
    wait_memory = copies.start(memory_hbm, memory)
    wait_score = copies.start(score_hbm, score)
    count = asking_ref.shape[0]

    from_piece = lax.broadcasted_iota(jnp.int32, (128, 128), 0)
    to_head = lax.broadcasted_iota(jnp.int32, (128, 128), 1)
    same = (from_piece % H == to_head) & (from_piece < 3 * H)
    pieces = low(jnp.where(same, 1.0, 0.0))
    lane_head = lax.broadcasted_iota(jnp.int32, (128, D), 1) // HD
    widen = jnp.where(lane_head == lax.broadcasted_iota(jnp.int32, (128, D), 0), 1.0, 0.0)

    totals = [dot(ref[:, D:], pieces) for ref in every_refs]
    top = functools.reduce(jnp.maximum, totals)
    powers = [jnp.exp(total - top) for total in totals]
    sums = tree_sum(powers)
    reading = tree_sum(
        [
            wide(ref[:, :D]) * exact_dot(power / sums, widen)
            for ref, power in zip(every_refs, powers)
        ]
    )
    whole_total = top + jnp.log(sums)
    reading_low = low(reading)
    low_ref[0] = reading_low
    wait_mix.wait()
    middle = hidden_ref[...] + dot(reading_low, mix[...])
    middle_ref[...] = middle
    gain = gain_row(gains_ref, ANSWER)
    fifth = low(middle * rms_scale(middle) * gain)
    low_ref[1] = fifth
    wait_in.wait()
    for at in range(wide_in.shape[1] // D):
        lanes = slice(at * D, (at + 1) * D)
        active, slope = gelu_pair(dot(fifth, wide_in[:, lanes]))
        wide_ref[0, :, lanes] = low(active)
        wide_ref[1, :, lanes] = low(up_ref[:, lanes] * slope)
    delta, gain_delta = rms_back(middle, gain, dot_rows(wide_ref[1], wide_in[...]))
    gain_delta_ref[...] = gain_delta
    delta += slotted(upstream_ref)
    middle_delta_ref[...] = delta
    delta_low = low(delta)
    low_ref[2] = delta_low
    taken = low(dot_rows(delta_low, mix[...]))
    inner = exact_dot(wide(taken) * reading, widen, rows=True)
    wait_score.wait()
    wait_memory.wait()
    for block in range(count // SLOT):
        slots = slice(block * SLOT, (block + 1) * SLOT)
        span = slice(block * ROW, (block + 1) * ROW)
        chances = jnp.exp(score[block] - head_columns(whole_total[slots]))
        asked = spread(asking_ref[slots])
        upward = spread(taken[slots])
        delta_chances = dot_rows(upward, memory[1, span])
        deltas = low(chances * (delta_chances - head_columns(inner[slots])))
        memory_delta[0, span] = low(dot_tokens(deltas, asked))
        memory_delta[1, span] = low(dot_tokens(low(chances), upward))
        asking_delta_ref[slots] = low(fold(dot(deltas, memory[0, span])))
    copies.out(memory_delta, memory_delta_hbm)
    if weight_refs:
        answer_wide_weight(place_ref, low_ref, wide_ref, upstream_ref, *weight_refs)
    copies.finish()


def answer_middle(
    place, every, asking, hidden, up, upstream, gains, score, memory, weights, shards
):
    count = asking.shape[0]
    wide_size = weights[1].shape[1]
    blocks = len(every)
    outs, scratch = [], []
    if shards:
        outs = [((shards // 2, D // shards, D), BF, VM)] * 4
        scratch = [VM((D, D), BF), VM((wide_size, D // 2), BF)]

    def body(place_ref, *refs):
        answer_middle_kernel(refs[:blocks], *refs[blocks:], place_ref=place_ref)

    return kernel_call(
        body,
        (place, *every, asking, hidden, up, upstream, gains, score, memory, *weights),
        [pltpu.SMEM] + [VM] * (blocks + 5) + [ANY] * 4,
        [
            ((3, count, D), BF, VM),
            ((2, count, wide_size), BF, VM),
            ((count, D), F32, VM),
            ((count, D), F32, VM),
            ((1, D), F32, VM),
            (memory.shape, BF, ANY),
            ((count, D), BF, VM),
        ]
        + outs,
        scratch
        + [
            VM(score.shape, F32),
            VM(memory.shape, BF),
            VM(memory.shape, BF),
            VM((D, D), BF),
            VM((D, wide_size), BF),
            pltpu.SemaphoreType.DMA((8,)),
        ],
    )


def memory_back_kernel(
    place_ref, gains_ref, delta_hbm, final_hbm, encoded_hbm, upstream_hbm, key_hbm, value_hbm,
    active_hbm, weight_hbm, bend_hbm,
    send_hbm, keep_hbm, output_hbm, before_hbm, gain_delta_ref,
    delta, final, encoded, upstream, weights, active, weight, bend, both, output, before, arrivals,
):
    copies = Copies(arrivals)
    shards = both.shape[1]
    width = D // shards
    half = D // 2
    steps = active.shape[1] // D
    wait_delta = copies.start(delta_hbm, delta)
    waits = [copies.start(key_hbm, weights.at[0]), copies.start(value_hbm, weights.at[1])]
    wait_encoded = copies.start(encoded_hbm, encoded)
    wait_upstream = copies.start(upstream_hbm, upstream)
    wait_final = copies.start(final_hbm, final)
    wait_active = []
    for at in range(steps):
        part = pl.ds(at * D, D)
        wait_active.append(copies.start(active_hbm.at[:, part], active.at[:, part]))
    wait_back = []
    for at in range(steps):
        part = pl.ds(at * D, D)
        wait_back.append(
            [
                copies.start(weight_hbm.at[part], weight.at[part]),
                copies.start(bend_hbm.at[:, part], bend.at[:, part]),
            ]
        )
    core = place_ref[0]
    wait_delta.wait()
    for wait in waits:
        wait.wait()
    upward = dot_rows(delta[0], weights[0]) + dot_rows(delta[1], weights[1])
    wait_encoded.wait()
    wait_upstream.wait()
    back, gain_delta = rms_back(encoded[...], gain_row(gains_ref, FINAL), upward)
    gain_delta_ref[...] = gain_delta
    back += wide(upstream[...])
    output[...] = back
    copies.out(output, output_hbm)
    output_low = low(back)
    wait_final.wait()

    for side in range(2):
        first = low(dot_tokens(final[...], delta[side]))
        for shard in range(shards):
            for row in range(2):
                begin = shard * width + row * (width // 2)
                both[side, shard, row, : width // 2] = first[begin : begin + width // 2]
    for at in range(steps):
        wait_active[at].wait()
        later = low(dot_tokens(active[:, at * D : (at + 1) * D], output_low))
        for side in range(2):
            columns = slice(side * half, (side + 1) * half)
            for piece in range(D // width):
                shard, place = divmod(at * D // width + piece, 4)
                row, part = divmod(place, 2)
                rows = slice(piece * width, (piece + 1) * width)
                lanes = slice(part * half, (part + 1) * half)
                both[side, shard, row, width // 2 :, lanes] = later[rows, columns]
        done = pl.ds(at * shards // steps, shards // steps)
        copies.out(both.at[1 - core, done], send_hbm.at[done])
        copies.out(both.at[core, done], keep_hbm.at[done])
    for at in range(steps):
        part = slice(at * D, (at + 1) * D)
        for wait in wait_back[at]:
            wait.wait()
        before[:, part] = low(dot_rows(output_low, weight[part, :]) * wide(bend[:, part]))
        copies.out(before.at[:, part], before_hbm.at[:, part])
    copies.finish()


def memory_back(
    place, gains, delta, final, encoded, upstream, weights, active, weight, bend, shards, after=()
):
    count = final.shape[0]
    wide_size = active.shape[1]
    shape = (shards, 2, 3 * D // shards // 2, D)
    return kernel_call(
        memory_back_kernel,
        (place, gains, delta, final, encoded, upstream)
        + tuple(weights)
        + (active, weight, bend),
        [pltpu.SMEM, VM] + [ANY] * 9,
        [
            (shape, BF, ANY),
            (shape, BF, ANY),
            ((count, D), F32, ANY),
            ((count, wide_size), BF, ANY),
            ((1, D), F32, VM),
        ],
        [
            VM((2, count, D), BF), VM((count, D), BF), VM((count, D), F32), VM((count, D), BF),
            VM((2, D, D), BF), VM((count, wide_size), BF), VM((wide_size, D), BF),
            VM((count, wide_size), BF), VM((2,) + shape, BF), VM((count, D), F32),
            VM((count, wide_size), BF), pltpu.SemaphoreType.DMA((40,)),
        ],
        after,
    )


def wide_in_back_kernel(
    place_ref, gains_ref, second_hbm, before_hbm, weight_hbm, hidden_hbm, output_hbm, mix_hbm,
    send_hbm, keep_hbm, hidden_delta_hbm, hidden_low_hbm, attended_delta_hbm, gain_delta_ref,
    second, before, weight, hidden, output, mix, send, keep, hidden_delta, hidden_low,
    attended_delta, arrivals,
):
    copies = Copies(arrivals)
    steps = before.shape[1] // D // 2
    core = place_ref[0]
    wait_second = copies.start(second_hbm, second)
    units = [(1 - core) * steps + at for at in range(steps)]
    units += [core * steps + at for at in range(steps)]
    waits = []
    for unit in units:
        part = pl.ds(pl.multiple_of(unit * D, D), D)
        waits.append(copies.start(before_hbm.at[:, part], before.at[:, part]))
    later = [
        copies.start(source, target)
        for source, target in (
            (weight_hbm, weight), (hidden_hbm, hidden), (output_hbm, output), (mix_hbm, mix)
        )
    ]
    wait_second.wait()
    for at, unit in enumerate(units):
        waits[at].wait()
        part = pl.ds(pl.multiple_of(unit * D, D), D)
        target, target_hbm = (send, send_hbm) if at < steps else (keep, keep_hbm)
        target[at % steps] = low(dot_tokens(second[...], before[:, part]))
        copies.out(target.at[at % steps], target_hbm.at[at % steps])
    for wait in later:
        wait.wait()
    upward = dot_rows(before[...], weight[...])
    back, gain_delta = rms_back(hidden[...], gain_row(gains_ref, FFN), upward)
    gain_delta_ref[...] = gain_delta
    back += output[...]
    hidden_delta[...] = back
    copies.out(hidden_delta, hidden_delta_hbm)
    hidden_low[...] = low(back)
    copies.out(hidden_low, hidden_low_hbm)
    attended_delta[...] = low(dot_rows(hidden_low[...], mix[...]))
    copies.out(attended_delta, attended_delta_hbm)
    copies.finish()


def wide_in_back(place, gains, second, before, weight, hidden, output, mix, after=()):
    count, wide_size = before.shape
    shape = (wide_size // D // 2, D, D)
    return kernel_call(
        wide_in_back_kernel,
        (place, gains, second, before, weight, hidden, output, mix),
        [pltpu.SMEM, VM] + [ANY] * 6,
        [
            (shape, BF, ANY),
            (shape, BF, ANY),
            ((count, D), F32, ANY),
            ((count, D), BF, ANY),
            ((count, D), BF, ANY),
            ((1, D), F32, VM),
        ],
        [
            VM((count, D), BF), VM((count, wide_size), BF), VM((D, wide_size), BF),
            VM((count, D), F32), VM((count, D), F32), VM((D, D), BF), VM(shape, BF),
            VM(shape, BF), VM((count, D), F32), VM((count, D), BF), VM((count, D), BF),
            pltpu.SemaphoreType.DMA((24,)),
        ],
        after,
    )


def attend_back_kernel(
    place_ref, heads_hbm, chance_hbm, upstream_hbm, inputs_hbm, hidden_low_hbm,
    delta_hbm, slope_delta_ref, send_hbm, keep_hbm,
    heads, chance, upstream, inputs, delta, gathered, units, arrivals,
):
    copies = Copies(arrivals)
    pairs = H // 2
    waits = []
    for pair in range(pairs):
        lanes = pl.ds(pair * 2 * HD, 2 * HD)
        part = pl.ds(pair * 2, 2)
        waits.append(
            [
                copies.start(heads_hbm.at[:, :, lanes], heads.at[:, :, lanes]),
                copies.start(upstream_hbm.at[:, lanes], upstream.at[:, lanes]),
                copies.start(chance_hbm.at[part], chance.at[part]),
            ]
        )
    wait_inputs = copies.start(inputs_hbm, inputs)
    wait_hidden = copies.start(hidden_low_hbm, delta.at[3])
    blocks = upstream.shape[0] // ROW
    second_half = lax.broadcasted_iota(jnp.int32, (ROW, 2 * HD), 1) >= HD
    place_row = lax.broadcasted_iota(jnp.int32, (ROW, ROW), 0)
    place_column = lax.broadcasted_iota(jnp.int32, (ROW, ROW), 1)
    mirror = low(jnp.where(place_row + place_column == ROW - 1, 1.0, 0.0))

    for pair in range(pairs):
        lanes = slice(pair * 2 * HD, (pair + 1) * 2 * HD)
        for wait in waits[pair]:
            wait.wait()
        kept = []
        for which in range(2):
            head = pair * 2 + which
            for block in range(blocks):
                span = slice(block * ROW, (block + 1) * ROW)
                query, key, value = (heads[at, span, lanes] for at in range(3))
                upward = upstream[span, lanes]
                own = jnp.where(second_half == (which == 1), upward, jnp.zeros_like(upward))
                chances = chance[head, block]
                weight = wide(chances)
                delta_chances = dot_rows(value, own)
                inner = jnp.sum(delta_chances * weight, axis=0, keepdims=True)
                deltas = low(weight * (delta_chances - inner))
                if block == 0:
                    gathered[...] = wide(deltas)
                else:
                    gathered[...] += wide(deltas)
                own_key = key.T[which * HD : (which + 1) * HD]
                news = [low(dot(own_key, deltas)), dot(deltas, query), dot(chances, upward)]
                if which == 0:
                    kept.append(news)
                else:
                    delta[0, span, lanes] = jnp.concatenate([kept[block][0], news[0]], axis=0).T
                    for at in (1, 2):
                        both = jnp.where(second_half, news[at], kept[block][at])
                        delta[at, span, lanes] = low(both)
            whole = gathered[...]
            most = low(whole)
            turned = dot(mirror, most) + dot(mirror, low(whole - wide(most)))
            padded = jnp.concatenate([turned, jnp.zeros((ROW, ROW), F32)], axis=1)
            rolled = pltpu.roll(padded, 1, 1, stride=1, stride_axis=0)
            slope_delta_ref[head : head + 1, :] = jnp.sum(rolled, axis=0, keepdims=True)
        done = pl.ds(pair * 2 * HD, 2 * HD)
        copies.out(delta.at[pl.ds(0, 3), :, done], delta_hbm.at[:, :, done])

    wait_hidden.wait()
    wait_inputs.wait()
    for unit in range(4):
        units[unit // 2, unit % 2] = low(dot_tokens(inputs[unit // 3], delta[unit]))
    copies.out(units.at[1 - place_ref[0]], send_hbm)
    copies.out(units.at[place_ref[0]], keep_hbm)
    copies.finish()


def attend_back(place, heads, chance, upstream, inputs, hidden_low, after=()):
    count = upstream.shape[0]
    return kernel_call(
        attend_back_kernel,
        (place, heads, chance, upstream, inputs, hidden_low),
        [pltpu.SMEM] + [ANY] * 5,
        [
            ((3, count, D), BF, ANY),
            ((H, 2 * ROW), F32, VM),
            ((2, D, D), BF, ANY),
            ((2, D, D), BF, ANY),
        ],
        [
            VM(heads.shape, BF), VM(chance.shape, BF), VM(upstream.shape, BF),
            VM(inputs.shape, BF), VM((4, count, D), BF), VM((ROW, ROW), F32),
            VM((2, 2, D, D), BF), pltpu.SemaphoreType.DMA((36,)),
        ],
        after,
    )


def passage_end_kernel(
    place_ref, gains_ref, slope_delta_ref, answer_table_ref, ffn_gain_ref, final_gain_ref,
    self_gain_ref, cross_gain_ref, answer_gain_ref,
    input_hbm, delta_hbm, hidden_delta_hbm, query_hbm, key_hbm, value_hbm,
    gradient_hbm, small_low_ref,
    values, delta, hidden_delta, weights, gradient, small_ref, arrivals,
):
    copies = Copies(arrivals)
    wait_delta = copies.start(delta_hbm, delta)
    waits = [
        copies.start(source, weights.at[at])
        for at, source in enumerate((query_hbm, key_hbm, value_hbm))
    ]
    wait_input = copies.start(input_hbm, values)
    wait_hidden = copies.start(hidden_delta_hbm, hidden_delta)
    once = jnp.where((place_ref[0] == 0) & (place_ref[1] == 0), 1.0, 0.0)
    small_ref[...] = jnp.zeros_like(small_ref)
    small_ref[FFN : FFN + 1, :] = ffn_gain_ref[...]
    small_ref[FINAL : FINAL + 1, :] = final_gain_ref[...]
    small_ref[SELF : SELF + 1, :] = self_gain_ref[...] * once
    small_ref[CROSS : CROSS + 1, :] = cross_gain_ref[...] * once
    small_ref[ANSWER : ANSWER + 1, :] = answer_gain_ref[...] * once
    offsets = ROW - lax.broadcasted_iota(jnp.int32, (2 * ROW, 128), 0)
    matches = bucket_of(offsets, True) == lax.broadcasted_iota(jnp.int32, (2 * ROW, 128), 1)
    table = exact_dot(slope_delta_ref[...], jnp.where(matches, 1.0, 0.0))
    small_ref[8 : 8 + H, :128] = table
    small_ref[8 : 8 + H, 128:256] = answer_table_ref[:H, :] * once
    wait_delta.wait()
    for wait in waits:
        wait.wait()
    upward = dot_rows(delta[0], weights[0])
    upward += dot_rows(delta[1], weights[1])
    upward += dot_rows(delta[2], weights[2])
    wait_input.wait()
    wait_hidden.wait()
    back, gain_delta = rms_back(wide(values[...]), gain_row(gains_ref, ATTN), upward)
    small_ref[ATTN : ATTN + 1, :] = gain_delta
    small_low_ref[...] = low(small_ref[...])
    gradient[...] = back + hidden_delta[...]
    copies.out(gradient, gradient_hbm)
    copies.finish()


def passage_end(place, gains, small, rows, delta, hidden_delta, weights, after=()):
    count = rows.shape[0]
    return kernel_call(
        passage_end_kernel,
        (place, gains) + tuple(small) + (rows, delta, hidden_delta) + tuple(weights),
        [pltpu.SMEM] + [VM] * 8 + [ANY] * 6,
        [((count, D), F32, ANY), ((32, D), BF, VM)],
        [
            VM((count, D), BF), VM((3, count, D), BF), VM((count, D), F32), VM((3, D, D), BF),
            VM((count, D), F32), VM((32, D), F32), pltpu.SemaphoreType.DMA((8,)),
        ],
        after,
    )


def answer_end_kernel(
    asking_refs, middle_delta_ref, hidden_ref, input_ref, gains_ref,
    heads_ref, chance_ref, ask_hbm, mix_hbm, query_hbm, key_hbm, value_hbm,
    gradient_ref, asking_delta_ref, hidden_low_ref, delta_ref, cross_delta_ref,
    self_delta_ref, table_ref,
    weights, score_delta, arrivals,
):
    copies = Copies(arrivals)
    waits = [
        copies.start(source, weights.at[at])
        for at, source in enumerate((ask_hbm, mix_hbm, query_hbm, key_hbm, value_hbm))
    ]
    asking_delta_ref[...] = low(tree_sum([wide(ref[...]) for ref in asking_refs]))
    waits[0].wait()
    upward = dot_rows(asking_delta_ref[...], weights[0])
    back, gain_delta = rms_back(hidden_ref[...], gain_row(gains_ref, CROSS), upward)
    cross_delta_ref[...] = gain_delta
    back += middle_delta_ref[...]
    hidden_low = low(back)
    hidden_low_ref[...] = hidden_low
    waits[1].wait()
    upward = low(dot_rows(hidden_low, weights[1]))
    column = lax.broadcasted_iota(jnp.int32, (SLOT, 128), 0)
    lane = lax.broadcasted_iota(jnp.int32, (SLOT, 128), 1)
    mirror = low(jnp.where(column + lane == SLOT - 1, 1.0, 0.0))
    for block in range(upward.shape[0] // SLOT):
        slots = slice(block * SLOT, (block + 1) * SLOT)
        chances = chance_ref[block]
        taken = spread(upward[slots])
        delta_chances = dot_rows(taken, heads_ref[2, slots])
        inner = jnp.sum(delta_chances * wide(chances), axis=1, keepdims=True)
        deltas = low(wide(chances) * (delta_chances - inner))
        turned = dot(deltas, mirror)
        if block == 0:
            score_delta[...] = turned
        else:
            score_delta[...] += turned
        delta_ref[0, slots] = low(fold(dot(deltas, heads_ref[1, slots])))
        delta_ref[1, slots] = low(dot_tokens(deltas, spread(heads_ref[0, slots])))
        delta_ref[2, slots] = low(dot_tokens(chances, taken))
    for wait in waits[2:]:
        wait.wait()
    upward = dot_rows(delta_ref[0], weights[2])
    upward += dot_rows(delta_ref[1], weights[3])
    upward += dot_rows(delta_ref[2], weights[4])
    start_delta, gain_delta = rms_back(slotted(input_ref), gain_row(gains_ref, SELF), upward)
    self_delta_ref[...] = gain_delta
    unslotted(start_delta + back, gradient_ref)
    sums = []
    for h in range(H):
        rows = score_delta[h * SLOT : (h + 1) * SLOT]
        rolled = pltpu.roll(rows, 0, 1, stride=1, stride_axis=0)
        sums.append(jnp.sum(rolled, axis=0, keepdims=True))
    sums.append(jnp.zeros((16 - H, 128), F32))
    offsets = (SLOT - 1) - lax.broadcasted_iota(jnp.int32, (128, 128), 0)
    matches = bucket_of(offsets, False) == lax.broadcasted_iota(jnp.int32, (128, 128), 1)
    table_ref[...] = exact_dot(jnp.concatenate(sums, axis=0), jnp.where(matches, 1.0, 0.0))


def answer_out_kernel(middle_ref, wide_ref, out_hbm, result_ref, weight, arrivals):
    copies = Copies(arrivals)
    waits = []
    for at in range(out_hbm.shape[0] // D):
        part = pl.ds(at * D, D)
        waits.append(copies.start(out_hbm.at[part], weight.at[part]))
    total = middle_ref[...]
    for at, wait in enumerate(waits):
        part = slice(at * D, (at + 1) * D)
        wait.wait()
        total += dot(wide_ref[0, :, part], weight[part, :])
    unslotted(total, result_ref)


def answer_out(middle, wide_pair, weight, like, after=()):
    return kernel_call(
        answer_out_kernel,
        (middle, wide_pair, weight),
        [VM, VM, ANY],
        [(like.shape, BF, VM)],
        [VM(weight.shape, BF), pltpu.SemaphoreType.DMA((4,))],
        after,
    )[0]


def answer_end(
    place, asking_deltas, middle_delta, hidden, rows, gains, heads, chance, inputs, weights, shards,
    after=()
):
    count = hidden.shape[0]
    blocks = len(asking_deltas)
    outs, scratch = [], []
    if shards:
        outs = [((shards // 2, 3 * D // shards // 2, D), BF, VM)] * 2
        scratch = [VM((4, count, D), BF), VM((4, count, D), BF), VM((D, D), BF), VM((D, D), BF)]

    def body(place_ref, *refs):
        asking_refs, refs = refs[:blocks], refs[blocks:]
        input_refs, refs = refs[:4], refs[4:]
        first, last = refs[:18], refs[18:]
        share, own = last[: 6 if shards else 0], last[6 if shards else 0 :]
        answer_end_kernel(asking_refs, *first, *own)
        if shards:
            answer_square_weight(place_ref, *input_refs, first[12], first[13], first[14], *share)

    return kernel_call(
        body,
        (place, *asking_deltas, *inputs, middle_delta, hidden, rows, gains, heads, chance, *weights),
        [pltpu.SMEM] + [VM] * (blocks + 10) + [ANY] * 5,
        [
            (rows.shape, F32, VM),
            ((count, D), BF, VM),
            ((count, D), BF, VM),
            ((3, count, D), BF, VM),
            ((1, D), F32, VM),
            ((1, D), F32, VM),
            ((16, 128), F32, VM),
        ]
        + outs,
        scratch
        + [
            VM((5, D, D), BF), VM((H * SLOT, 128), F32), pltpu.SemaphoreType.DMA((5,)),
        ],
        after,
    )


def answer_wide_weight(
    place_ref, lows_ref, wide_ref, upstream_ref, in_send_ref, in_keep_ref, out_send_ref,
    out_keep_ref, inner, full
):
    core = place_ref[0]
    row = place_ref[1]
    width = in_send_ref.shape[1]
    half = D // 2
    part = pl.ds(pl.multiple_of((core * 2 + row) * D, D), D)
    inner[...] = low(dot_tokens(lows_ref[1], wide_ref[1, :, part]))
    upstream = slotted(upstream_ref)
    upstream = low(jnp.where(core == 0, upstream[:, :half], upstream[:, half:]))
    for at in range(wide_ref.shape[2] // D):
        span = slice(at * D, (at + 1) * D)
        full[span, :] = low(dot_tokens(wide_ref[0, :, span], upstream))
    for part_ref, sent in ((in_send_ref, True), (in_keep_ref, False)):
        for at in range(part_ref.shape[0]):
            own = place_ref[2]
            shard = at * 2 + (1 - own if sent else own)
            rows = pl.ds(pl.multiple_of(shard * width, 16), width)
            part_ref[at] = inner[rows, :]
    for part_ref, sent in ((out_send_ref, True), (out_keep_ref, False)):
        for at in range(part_ref.shape[0]):
            own = place_ref[3]
            shard = at // 2 * 4 + (1 - own if sent else own) * 2 + at % 2
            for side in range(2):
                begin = shard * 4 * width + row * 2 * width + side * width
                rows = pl.ds(pl.multiple_of(begin, 16), width)
                part_ref[at, :, side * half : (side + 1) * half] = full[rows, :]


def answer_square_weight(
    place_ref, crossed_ref, low_ref, attended_ref, normed_ref, asking_delta_ref, hidden_low_ref,
    delta_ref, send_ref, keep_ref, inputs, deltas, first, full,
):
    core = place_ref[0]
    row = place_ref[1]
    width = send_ref.shape[1] * 2 // 3
    inputs[0] = crossed_ref[...]
    inputs[1] = low_ref[0]
    inputs[2] = attended_ref[...]
    inputs[3] = normed_ref[...]
    deltas[0] = asking_delta_ref[...]
    deltas[1] = low_ref[2]
    deltas[2] = hidden_low_ref[...]
    deltas[3] = delta_ref[0]
    unit = core * 2 + row
    first[...] = low(dot_tokens(inputs[unit], deltas[unit]))
    full[...] = low(dot_tokens(normed_ref[...], delta_ref[1 + core]))
    for part_ref, sent in ((send_ref, True), (keep_ref, False)):
        for at in range(part_ref.shape[0]):
            own = place_ref[3]
            shard = at // 2 * 4 + (1 - own if sent else own) * 2 + at % 2
            rows = pl.ds(pl.multiple_of(shard * width, 16), width)
            part_ref[at, :width] = first[rows, :]
            rows = pl.ds(pl.multiple_of(shard * width + row * (width // 2), 16), width // 2)
            part_ref[at, width:] = full[rows, :]


class Part:
    def __init__(self, rows, left, first=0):
        self.rows = rows
        self.left = list(left)
        self.first = first
        self.terms = []

    def array(self, values, names):
        values = values.reshape((2,) * len(names) + (-1, values.shape[-1]))
        self.terms.append((values, list(names), None))
        return self

    def size(self, name):
        count = len([one for one in self.left if one != name])
        return (2**count) * self.rows if name else self.rows

    def sent(self, name, values, begin):
        self.left.remove(name)


class Total(Part):
    def __init__(self, values):
        super().__init__(values.shape[0], "")
        self.terms.append((values, [], 0))

    def size(self, name):
        return self.rows

    def sent(self, name, values, begin):
        self.terms = [(values, [], begin)]


PLACES = "cyxlh"


def bus(place, jobs, after=()):
    arrays = []
    plans = []
    scratch = []
    outs = []
    for name, parts in jobs:
        begin = 0
        for part in parts:
            kept = [one for one in part.left if one != name] if name else []
            for values, names, start in part.terms:
                at = [id(one) for one in arrays]
                if id(values) not in at:
                    arrays.append(values)
                    at.append(id(values))
                inner = [one for one in names if one in kept]
                room = (2,) * len(inner) + (part.rows, D) if start is None else (
                    (2 ** len(inner)) * part.rows, D
                )
                plans.append(
                    (len(outs), begin, at.index(id(values)), names, start, inner, part, kept, name)
                )
                scratch.append(VM(room, BF))
            begin += part.size(name)
        outs.append(((begin, D), BF, VM))
    count = len(arrays)

    def body(place_ref, *refs):
        sources, targets = refs[:count], refs[count : count + len(outs)]
        rooms, semaphores = refs[count + len(outs) : -1], refs[-1]
        copies = Copies(semaphores)

        def spot(one, part, name):
            own = place_ref[PLACES.index(one)]
            return 1 - own if one == name else own

        waits = []
        for room, (_, _, source, names, start, inner, part, kept, name) in zip(rooms, plans):
            if start is None:
                index = [
                    slice(None) if one in kept else spot(one, part, name) for one in names
                ]
                origin = sources[source].at[(*index, pl.ds(part.first, part.rows))]
            else:
                row = start
                for depth, one in enumerate(names):
                    if one not in kept:
                        stride = (2 ** (len(names) - 1 - depth)) * part.rows
                        row = row + spot(one, part, name) * stride
                length = (2 ** len(inner)) * part.rows
                origin = sources[source].at[pl.ds(pl.multiple_of(row, 16), length)]
            waits.append(copies.start(origin, room))
        for wait in waits:
            wait.wait()
        sums = {}
        for room, (out, begin, _, _, start, inner, part, kept, name) in zip(rooms, plans):
            for number in range(2 ** len(kept)):
                bits = [number >> (len(kept) - 1 - depth) & 1 for depth in range(len(kept))]
                at = dict(zip(kept, bits))
                if start is None:
                    value = room[tuple(at[one] for one in inner)] if inner else room[...]
                else:
                    value = room[number * part.rows : (number + 1) * part.rows]
                sums.setdefault((out, begin + number * part.rows, part.rows), []).append(value)
        for (out, begin, rows), values in sums.items():
            total = functools.reduce(jnp.add, [wide(value) for value in values])
            targets[out][begin : begin + rows] = low(total)

    return kernel_call(
        body,
        (place, *arrays),
        [pltpu.SMEM] + [ANY] * count,
        outs,
        scratch + [pltpu.SemaphoreType.DMA((len(plans),))],
        after,
    )


def ride(ring, place, jobs, after=()):
    sends = list(bus(place, jobs, after))
    trip = []
    for (name, parts), values in zip(jobs, sends):
        begin = 0
        stops = []
        for part in parts:
            length = part.size(name)
            part.sent(name, values, begin)
            stops.append((part, begin, list(part.left)))
            begin += length
        trip.append([ring.swap(values, name), stops])
    return trip, sends


def arrive(items, *trips):
    legs = [leg for trip in trips for leg in trip]
    items = lax.optimization_barrier((*items, *[leg[0] for leg in legs]))
    count = len(items) - len(legs)
    for values, (_, stops) in zip(items[count:], legs):
        for part, begin, names in stops:
            part.terms.append((values, names, begin))
    return items[:count]


def assemble_kernel(place_ref, mine_hbm, near_hbm, far_hbm, across_hbm, *refs, lay):
    outs, whole, arrivals = refs[:-2], refs[-2], refs[-1]
    copies = Copies(arrivals)
    core, row = place_ref[0], place_ref[1]
    waits = [
        copies.start(mine_hbm, whole.at[core, row]),
        copies.start(near_hbm, whole.at[core, 1 - row]),
        copies.start(far_hbm, whole.at[1 - core, row]),
        copies.start(across_hbm, whole.at[1 - core, 1 - row]),
    ]
    for wait in waits:
        wait.wait()
    for out, rows, columns, part in lay:
        c, y, begin, lanes = part
        height, width = rows[1] - rows[0], columns[1] - columns[0]
        outs[out][rows[0] : rows[1], columns[0] : columns[1]] = wide(
            whole[c, y, begin : begin + height, lanes : lanes + width]
        )


def assemble(place, arrays, shapes, lay):
    rows = arrays[0].shape[0]
    return kernel_call(
        functools.partial(assemble_kernel, lay=lay),
        (place, *arrays),
        [pltpu.SMEM] + [ANY] * 4,
        [(shape, F32, VM) for shape in shapes],
        [VM((2, 2, rows, D), BF), pltpu.SemaphoreType.DMA((4,))],
    )


def layout(rows):
    half = D // 2
    lay = []
    shapes = []

    def stacked(begin):
        for c in range(2):
            for y in range(2):
                at = (y * rows // 2, (y + 1) * rows // 2)
                lay.append((len(shapes), at, (0, D), (c, y, begin, 0)))
            shapes.append((rows, D))

    def unhalved(begin):
        for c in range(2):
            for y in range(2):
                for side in range(2):
                    low_row = (y * 2 + side) * rows
                    lay.append(
                        (
                            len(shapes),
                            (low_row, low_row + rows),
                            (c * half, (c + 1) * half),
                            (c, y, begin, side * half),
                        )
                    )
        shapes.append((4 * rows, D))

    def side_by_side(begin):
        for c in range(2):
            for y in range(2):
                at = c * 2 + y
                lay.append((len(shapes), (0, rows), (at * D, (at + 1) * D), (c, y, begin, 0)))
        shapes.append((rows, 4 * D))

    def units(begin):
        for c in range(2):
            for y in range(2):
                lay.append((len(shapes), (0, rows), (0, D), (c, y, begin, 0)))
                shapes.append((rows, D))

    return lay, shapes, stacked, unhalved, side_by_side, units


class Ring:
    def __init__(self, mesh):
        self.dp = mesh.shape["dp"]
        self.blk = mesh.shape["blk"]
        self.cut = self.blk == 4 and self.dp == 8

    def bit(self, name):
        return {"c": 1, "y": 2, "x": 4, "l": 8, "h": 16}[name]

    def number(self):
        return lax.axis_index("dp") * self.blk + lax.axis_index("blk")

    def place(self, name):
        return self.number() // self.bit(name) % 2

    def swap(self, values, *names):
        mask = sum(self.bit(name) for name in names)
        moves = [(at, at ^ mask) for at in range(self.dp * self.blk)]
        return lax.ppermute(values, ("dp", "blk"), moves)


class Beside:
    def __init__(self, ring, mine):
        self.ring = ring
        self.mine = mine
        self.arriving = [ring.swap(mine, "y"), ring.swap(mine, "c")]

    def send(self, cues=()):
        near, far, *_ = lax.optimization_barrier((*self.arriving, *cues))
        self.arriving = [near, far, self.ring.swap(near, "c")]

    def arrays(self, cues=()):
        near, far, across, *_ = lax.optimization_barrier((*self.arriving, *cues))
        return [self.mine, near, far, across]


def on_device(
    ring,
    encoder_input,
    decoder_input,
    encoder_cotangent,
    decoder_cotangent,
    segment_ids,
    padding_mask,
    answer_length,
    encoder_attn_gain,
    encoder_query,
    encoder_key,
    encoder_value,
    encoder_mix,
    encoder_bias_table,
    encoder_ffn_gain,
    encoder_ffn_in,
    encoder_ffn_out,
    final_gain,
    cross_key,
    cross_value,
    decoder_self_gain,
    decoder_query,
    decoder_key,
    decoder_value,
    decoder_mix,
    decoder_bias_table,
    decoder_cross_gain,
    cross_query,
    cross_mix,
    decoder_ffn_gain,
    decoder_ffn_in,
    decoder_ffn_out,
):
    cut = ring.cut
    shard = D // ring.dp
    questions = encoder_input.shape[0]
    batch = questions * encoder_input.shape[1]
    passage_rows = encoder_input.reshape(batch * ROW, D)
    passage_upstream = encoder_cotangent.reshape(batch * ROW, D)
    core = ring.place("c")
    row = lax.axis_index("blk") // 2
    place = [core, row, ring.place("x"), ring.place("l"), ring.place("h")]
    place = jnp.stack(place).astype(jnp.int32)
    (
        gains,
        answer_normed,
        answer_heads,
        answer_chances,
        answer_attended,
        answer_hidden,
        answer_crossed,
        asking,
        packed,
        inputs,
        heads,
        chances,
        hidden,
        second,
        active,
        bend,
        encoded,
        result,
        final,
        memory,
        scores,
    ) = passage(
        answer_length,
        decoder_input,
        passage_rows,
        segment_ids.reshape(batch, 1, ROW),
        padding_mask.reshape(batch, 1, ROW),
        encoder_bias_table.T,
        decoder_bias_table.T,
        (
            encoder_attn_gain,
            encoder_ffn_gain,
            final_gain,
            decoder_self_gain,
            decoder_cross_gain,
            decoder_ffn_gain,
        ),
        (decoder_query, decoder_key, decoder_value, decoder_mix, cross_query),
        (
            encoder_query,
            encoder_key,
            encoder_value,
            encoder_mix,
            encoder_ffn_in,
            encoder_ffn_out,
            cross_key,
            cross_value,
        ),
    )

    def neighbours(values):
        if cut:
            return [values] + [ring.swap(values, *names) for names in ("c", "y", "yc")]
        every = lax.all_gather(values, "blk", axis=0)
        return [every[at] for at in range(ring.blk)]

    every = neighbours(packed)
    (upstream_cue, _) = lax.optimization_barrier((decoder_cotangent, packed))
    answer_upward = answer_up(upstream_cue, decoder_ffn_out)
    (
        answer_lows,
        answer_wides,
        answer_middle_rows,
        middle_delta,
        answer_gain_delta,
        memory_delta,
        asking_delta,
        *wide_halves,
    ) = answer_middle(
        place,
        every,
        asking,
        answer_hidden,
        answer_upward,
        decoder_cotangent,
        gains,
        scores,
        memory,
        (cross_mix, decoder_ffn_in),
        ring.dp if cut else None,
    )

    asking_deltas = neighbours(asking_delta)
    after = []
    if cut:
        half = shard // 2
        in_half, in_kept, out_half, out_kept = wide_halves
        wide_first = Part(shard, "lh").array(in_kept, "hl")
        wide_second = Part(shard, "xh").array(out_kept, "hx")
        wide_got = [ring.swap(in_half, "x"), ring.swap(out_half, "l")]
        after = [in_half]
    memory_send, memory_keep, output_delta, before, final_gain_delta = memory_back(
        place,
        gains,
        memory_delta,
        final,
        encoded,
        passage_upstream,
        (cross_key, cross_value),
        active,
        encoder_ffn_out,
        bend,
        ring.dp,
        after=after,
    )
    if cut:
        memory_send, cue, *wide_got = arrive([memory_send, place, *wide_got])
        wide_first.array(wide_got[0], "hl")
        wide_second.array(wide_got[1], "hx")
        memory_got = ring.swap(memory_send, "c")
        trip, sends = ride(ring, cue, [("l", [wide_first]), ("x", [wide_second])])
        after = sends + [memory_send] + asking_deltas
    (
        answer_gradient,
        asking_delta,
        answer_hidden_low,
        answer_heads_delta,
        cross_gain_delta,
        self_gain_delta,
        answer_table_delta,
        *square_halves,
    ) = answer_end(
        place,
        asking_deltas,
        middle_delta,
        answer_hidden,
        decoder_input,
        gains,
        answer_heads,
        answer_chances,
        (answer_crossed, answer_lows, answer_attended, answer_normed),
        (cross_query, decoder_mix, decoder_query, decoder_key, decoder_value),
        ring.dp if cut else None,
        after=after,
    )
    after = []
    if cut:
        send, keep = square_halves
        send, memory_got, cue = arrive([send, memory_got, place], trip)
        answer_square = Part(3 * half, "hx").array(keep, "hx")
        square_got = ring.swap(send, "l")
        top = 5 * 16
        memory_first = Part(top, "yxlh").array(memory_keep, "hlxy").array(memory_got, "hlxy")
        memory_second = Part(3 * half - top, "xylh", top)
        memory_second.array(memory_keep, "hlxy").array(memory_got, "hlxy")
        trip_memory, sends = ride(
            ring, cue, [("y", [memory_first]), ("x", [memory_second]), ("h", [wide_first, wide_second])]
        )
        after = sends + [send]
    in_send, in_keep, hidden_delta, hidden_low, attended_delta, ffn_gain_delta = wide_in_back(
        place,
        gains,
        second,
        before,
        encoder_ffn_in,
        hidden,
        output_delta,
        encoder_mix,
        after=after,
    )
    after = []
    if cut:
        in_got = ring.swap(in_send, "c")
        after = [in_send]
    answer_result = answer_out(
        answer_middle_rows, answer_wides, decoder_ffn_out, decoder_input, after=after
    )
    after = []
    if cut:
        answer_result, attended_delta, in_got, square_got, cue = arrive(
            [answer_result, attended_delta, in_got, square_got, place], trip_memory
        )
        answer_square.array(square_got, "hx")
        in_first = Part(half, "yxlh").array(in_keep, "yhlx").array(in_got, "yhlx")
        in_second = Part(half, "xylh", half).array(in_keep, "yhlx").array(in_got, "yhlx")
        trip_in, after = ride(
            ring,
            cue,
            [
                ("y", [in_first, memory_second]),
                ("x", [in_second, memory_first]),
                ("h", [answer_square]),
            ],
        )
    heads_delta, slope_delta, heads_send, heads_keep = attend_back(
        place, heads, chances, attended_delta, inputs, hidden_low, after=after
    )
    after = []
    if cut:
        heads_send, cue = arrive([heads_send, place], trip_in)
        heads_got = ring.swap(heads_send, "c")
        trip_in, sends = ride(
            ring,
            cue,
            [
                ("x", [in_first]),
                ("y", [in_second]),
                ("l", [memory_first, memory_second]),
            ],
        )
        heads_got, cue, *_ = lax.optimization_barrier((heads_got, place, *sends))
        heads_first = Part(half, "yxlh").array(heads_keep, "yhlx").array(heads_got, "yhlx")
        heads_second = Part(half, "xylh", half)
        heads_second.array(heads_keep, "yhlx").array(heads_got, "yhlx")
        trip_heads, after = ride(ring, cue, [("y", [heads_first]), ("x", [heads_second])])
    passage_gradient, small = passage_end(
        place,
        gains,
        (
            slope_delta,
            answer_table_delta,
            ffn_gain_delta,
            final_gain_delta,
            self_gain_delta,
            cross_gain_delta,
            answer_gain_delta,
        ),
        passage_rows,
        heads_delta,
        hidden_delta,
        (encoder_query, encoder_key, encoder_value),
        after=after,
    )
    if cut:
        small_got = ring.swap(small, "c")
        small_got, cue = arrive([small_got, place], trip_in, trip_heads)
        total = Total(small)
        total.terms.append((small_got, [], 0))
        trip, sends = ride(
            ring,
            cue,
            [
                ("x", [heads_first, answer_square]),
                ("y", [heads_second, total]),
                ("l", [in_first, in_second]),
                ("h", [memory_first, memory_second]),
            ],
        )
        (cue,) = arrive([place], trip)
        trip, sends = ride(
            ring,
            cue,
            [("l", [heads_first, heads_second, total]), ("h", [in_first, in_second])],
        )
        (done,) = bus(
            place,
            [(None, [memory_first, memory_second, wide_first, wide_second, answer_square])],
            sends,
        )
        first = Beside(ring, done)
        cue, _ = arrive([place, done], trip)
        trip, sends = ride(ring, cue, [("h", [heads_first, heads_second, total])])
        cue, *first.arriving = arrive([place, *first.arriving], trip)
        done, small = bus(
            cue,
            [(None, [in_first, in_second, heads_first, heads_second]), (None, [total])],
        )
        last = Beside(ring, done)
        small_got = ring.swap(small, "x")
        first.send([done])
        lay, shapes, stacked, unhalved, side_by_side, units = layout(shard)
        stacked(0)
        unhalved(half)
        side_by_side(half + shard)
        unhalved(half + 2 * shard)
        units(half + 3 * shard)
        stacked(half + 4 * shard)
        weights = list(assemble(place, first.arrays(), shapes, lay))
        last.send(weights[:1])
        small_got, *_ = lax.optimization_barrier((small_got, weights[0]))
        lay, shapes, stacked, unhalved, side_by_side, units = layout(shard)
        side_by_side(0)
        units(shard)
        weights += list(assemble(place, last.arrays(), shapes, lay))
        small = wide(small) + wide(small_got)
    else:
        small = lax.psum(wide(small), ("dp", "blk"))
    mine = lax.axis_index("dp")
    gain_deltas = lax.dynamic_slice_in_dim(small[:6], mine * shard, shard, 1)
    tables = NB // ring.dp
    table_deltas = [
        lax.dynamic_slice_in_dim(small[8 : 8 + H, begin : begin + NB], mine * tables, tables, 1).T
        for begin in (0, 128)
    ]

    if not cut:
        weights = whole_weights(
            core,
            (memory_send, memory_keep),
            (in_send, in_keep),
            (heads_send, heads_keep),
            (
                (answer_lows[1], answer_wides[1]),
                (
                    answer_wides[0],
                    low(slotted(decoder_cotangent)),
                ),
                (answer_crossed, asking_delta),
                (answer_lows[0], answer_lows[2]),
                (answer_attended, answer_hidden_low),
                (answer_normed, answer_heads_delta[0]),
                (answer_normed, answer_heads_delta[1]),
                (answer_normed, answer_heads_delta[2]),
            ),
        )
    (
        gradient_cross_key,
        gradient_cross_value,
        gradient_encoder_ffn_out,
        gradient_decoder_ffn_in,
        gradient_decoder_ffn_out,
        gradient_cross_query,
        gradient_cross_mix,
        gradient_decoder_mix,
        gradient_decoder_query,
        gradient_decoder_key,
        gradient_decoder_value,
        gradient_encoder_ffn_in,
        gradient_encoder_query,
        gradient_encoder_key,
        gradient_encoder_value,
        gradient_encoder_mix,
    ) = weights
    return (
        result.reshape(encoder_input.shape),
        answer_result,
        passage_gradient.reshape(encoder_input.shape),
        answer_gradient,
        gain_deltas[ATTN],
        gradient_encoder_query,
        gradient_encoder_key,
        gradient_encoder_value,
        gradient_encoder_mix,
        table_deltas[0],
        gain_deltas[FFN],
        gradient_encoder_ffn_in,
        gradient_encoder_ffn_out,
        gain_deltas[FINAL],
        gradient_cross_key,
        gradient_cross_value,
        gain_deltas[SELF],
        gradient_decoder_query,
        gradient_decoder_key,
        gradient_decoder_value,
        gradient_decoder_mix,
        table_deltas[1],
        gain_deltas[CROSS],
        gradient_cross_query,
        gradient_cross_mix,
        gain_deltas[ANSWER],
        gradient_decoder_ffn_in,
        gradient_decoder_ffn_out,
    )


def whole_weights(core, memory, inner, heads, answers):
    def both(pair):
        send, keep = pair
        return (jnp.where(core == 0, keep, send), jnp.where(core == 0, send, keep))

    def shared(gradient):
        return lax.psum_scatter(low(gradient), "dp", scatter_dimension=0, tiled=True)

    def summed(gradient):
        return lax.psum(shared(gradient), "blk")

    memory = both(memory)
    shards, _, rows, _ = memory[0].shape
    cut = rows // 3
    passages = [part[:, :, :cut].reshape(D, D) for part in memory]
    out = [
        part[:, :, cut:]
        .reshape(shards, 2, 2 * cut, 2, D // 2)
        .swapaxes(2, 3)
        .reshape(8 * cut * shards, D // 2)
        for part in memory
    ]
    passages.append(jnp.concatenate(out, axis=1))
    passages.append(jnp.concatenate([unit for half in both(inner) for unit in half], axis=1))
    passages += [unit for half in both(heads) for unit in half]
    passages = [wide(summed(item)) for item in passages]
    answers = [wide(shared(dot_tokens(inputs, upstream))) for inputs, upstream in answers]
    return passages[:3] + answers + passages[3:]


def solution(mesh):
    dims = {4: P("dp", "blk", None, None), 3: P("dp", None, None), 2: P("dp", None), 1: P("dp")}
    rows = P("dp", "blk", None)
    return jax.shard_map(
        functools.partial(on_device, Ring(mesh)),
        mesh=mesh,
        in_specs=(dims[4], dims[3], dims[4], dims[3], rows, rows, dims[1]) + (P(),) * 24,
        out_specs=(dims[4], dims[3], dims[4], dims[3])
        + tuple(dims[1 if at in (0, 6, 9, 12, 18, 21) else 2] for at in range(24)),
        check_vma=False,
    )
```

```python
import functools
import math

import jax
import jax.numpy as jnp
from jax import lax
from jax.experimental import pallas as pl
from jax.experimental.pallas import tpu as pltpu
from jax.sharding import PartitionSpec as P

D = 768
H = 12
HD = 64
NB = 32
MAXD = 128
ROW = 256
ANS = 20


EPSILON = 1e-06
NEGATIVE = -1e30


SLOT = 32
ANY = pl.ANY
VM = pltpu.VMEM
BF = jnp.bfloat16
F32 = jnp.float32
LIMIT = 60 << 20


def dot(left, right):
    return jnp.dot(left, right, preferred_element_type=jnp.float32)


def dot_rows(left, right):
    return lax.dot_general(
        left, right, (((1,), (1,)), ((), ())), preferred_element_type=jnp.float32
    )


def dot_tokens(left, right):
    return lax.dot_general(
        left, right, (((0,), (0,)), ((), ())), preferred_element_type=jnp.float32
    )


def low(values):
    return values.astype(jnp.bfloat16)


def wide(values):
    return values.astype(jnp.float32)


def slotted(ref):
    spare = jnp.zeros((SLOT - ANS, D), F32)
    return jnp.concatenate(
        [part for at in range(ref.shape[0]) for part in (wide(ref[at]), spare)], axis=0
    )


def unslotted(values, ref):
    for at in range(ref.shape[0]):
        ref[at] = values[at * SLOT : at * SLOT + ANS].astype(ref.dtype)


ATTN, FFN, FINAL, SELF, CROSS, ANSWER = range(6)


def gain_row(gains_ref, which):
    return gains_ref[which : which + 1, :]


def rms_scale(values):
    return lax.rsqrt(jnp.mean(values * values, axis=-1, keepdims=True) + EPSILON)


def head_lanes(rows, width=D):
    return lax.broadcasted_iota(jnp.int32, (rows, width), 1) // HD


def spread(rows):
    lanes = head_lanes(rows.shape[0])
    values = wide(rows)
    return low(jnp.concatenate([jnp.where(lanes == h, values, 0.0) for h in range(H)], axis=0))


def fold(full):
    rows = full.shape[0] // H
    lanes = head_lanes(rows)
    total = jnp.zeros((rows, full.shape[1]), jnp.float32)
    for h in range(H):
        total = jnp.where(lanes == h, full[h * rows : (h + 1) * rows], total)
    return total


def gelu_pair(values):
    square = values * values
    inner = values * (0.7978845608 + (0.7978845608 * 0.044715) * square)
    half = 0.5 + 0.5 * jnp.tanh(inner)
    active = values * half
    slope = 0.7978845608 + (3.0 * 0.7978845608 * 0.044715) * square
    return (active, half + 2.0 * active * (1.0 - half) * slope)


class Copies:
    def __init__(self, semaphores):
        self.semaphores = semaphores
        self.count = 0
        self.open = []

    def start(self, source, target):
        copy = pltpu.make_async_copy(source, target, self.semaphores.at[self.count])
        self.count += 1
        copy.start()
        return copy

    def out(self, source, target):
        self.open.append(self.start(source, target))

    def finish(self):
        for copy in self.open:
            copy.wait()


def kernel_call(body, operands, spaces, outs, scratch, after=()):
    if after:
        first, *_ = lax.optimization_barrier((operands[0], *after))
        operands = (first, *operands[1:])
    return pl.pallas_call(
        body,
        in_specs=[pl.BlockSpec(memory_space=space) for space in spaces],
        out_specs=[pl.BlockSpec(memory_space=space) for _, _, space in outs],
        out_shape=[jax.ShapeDtypeStruct(shape, dtype) for shape, dtype, _ in outs],
        scratch_shapes=scratch,
        compiler_params=pltpu.CompilerParams(vmem_limit_bytes=LIMIT),
        cost_estimate=pl.CostEstimate(flops=10**13, bytes_accessed=10**9, transcendentals=0),
    )(*operands)


def bucket_of(offsets, both_ways):
    if both_ways:
        buckets = NB // 2
        index = jnp.where(offsets > 0, buckets, 0)
        distance = jnp.abs(offsets)
    else:
        buckets = NB
        index = jnp.zeros_like(offsets)
        distance = jnp.maximum(-offsets, 0)
    exact = buckets // 2
    index = index + jnp.minimum(distance, exact)
    for step in range(1, buckets - exact):
        border = math.ceil(exact * (MAXD / exact) ** (step / (buckets - exact)) - 1e-09)
        index = index + jnp.where(distance >= border, 1, 0)
    return index


def table_slopes(table, width, both_ways, turn):
    offsets = turn * (lax.broadcasted_iota(jnp.int32, (NB, width), 1) - width // 2)
    matches = bucket_of(offsets, both_ways) == lax.broadcasted_iota(jnp.int32, (NB, width), 0)
    return dot(table, low(jnp.where(matches, 1.0, 0.0)))


def slope_bias(slopes, rows):
    width = slopes.shape[1]
    spread_slopes = jnp.broadcast_to(slopes, (rows, width))
    return pltpu.roll(spread_slopes, width // 2, 1, stride=1, stride_axis=0)[:, : width // 2]


def passage_kernel(
    length_ref, answer_input_ref, input_ref, segment_ref, padding_ref, table_ref, answer_table_ref,
    gain_refs,
    answer_query_hbm, answer_key_hbm, answer_value_hbm, answer_mix_hbm, ask_hbm,
    query_hbm, key_hbm, value_hbm, mix_hbm, in_hbm, out_hbm, cross_key_hbm, cross_value_hbm,
    gains_ref, answer_normed_ref, answer_heads_ref, answer_chance_ref, answer_attended_ref,
    answer_hidden_ref, crossed_ref, asking_ref, packed_ref,
    inputs_hbm, heads_hbm, chance_hbm, hidden_hbm, second_hbm,
    active_hbm, bend_hbm, encoded_hbm, result_hbm, final_hbm, memory_hbm, score_hbm,
    answer_square, square, wide_in, wide_out, slopes, arrivals,
    inputs, heads, chance, hidden, second,
    active, bend, memory, score,
):
    copies = Copies(arrivals)
    answer_waits = [
        copies.start(source, answer_square.at[at])
        for at, source in enumerate(
            (answer_query_hbm, answer_key_hbm, answer_value_hbm, answer_mix_hbm, ask_hbm)
        )
    ]
    square_hbm = (query_hbm, key_hbm, value_hbm, mix_hbm)
    rows = input_ref.shape[0]
    blocks = rows // ROW
    normed = inputs.at[0]
    attended = inputs.at[1]

    gains = [wide(ref[...]).reshape(1, D) for ref in gain_refs]
    for at, gain in enumerate(gains):
        gains_ref[at : at + 1, :] = gain
    values = wide(input_ref[...])
    normed[...] = low(values * rms_scale(values) * gains[ATTN])
    waits = [copies.start(source, square.at[at]) for at, source in enumerate(square_hbm)]
    slopes[...] = table_slopes(table_ref[...], 2 * ROW, True, 1)
    place_row = lax.broadcasted_iota(jnp.int32, (ROW, ROW), 0)
    place_column = lax.broadcasted_iota(jnp.int32, (ROW, ROW), 1)
    for block in range(blocks):
        segment_row = jnp.broadcast_to(segment_ref[block], (ROW, ROW))
        padding_row = jnp.broadcast_to(padding_ref[block], (ROW, ROW))
        own = (segment_row == segment_row.T) & (padding_row == 1)
        score[block, :ROW] = jnp.where(own | (place_row == place_column), 0.0, NEGATIVE)

    answer_values = slotted(answer_input_ref)
    answer_normed = low(answer_values * rms_scale(answer_values) * gains[SELF])
    answer_normed_ref[...] = answer_normed
    for at in range(3):
        answer_waits[at].wait()
        answer_heads_ref[at] = low(dot(answer_normed, answer_square[at]))
    wait_in = copies.start(in_hbm, wide_in)
    wait_out = copies.start(out_hbm, wide_out)
    cross_waits = [
        copies.start(source, answer_square.at[at])
        for at, source in enumerate((cross_key_hbm, cross_value_hbm))
    ]
    answer_slopes = table_slopes(answer_table_ref[...], 128, False, 1)
    answer_bias = jnp.concatenate(
        [slope_bias(answer_slopes[h : h + 1], SLOT)[:, :SLOT] for h in range(H)], axis=0
    )
    row = lax.broadcasted_iota(jnp.int32, (H * SLOT, SLOT), 0) % SLOT
    column = lax.broadcasted_iota(jnp.int32, (H * SLOT, SLOT), 1)
    for at in range(blocks):
        slots = slice(at * SLOT, (at + 1) * SLOT)
        asked = spread(answer_heads_ref[0, slots])
        scores = dot_rows(asked, answer_heads_ref[1, slots]) + answer_bias
        allowed = (column <= row) & (column < length_ref[at])
        scores = jnp.where(allowed, scores, NEGATIVE)
        powers = jnp.exp(scores - jnp.max(scores, axis=1, keepdims=True))
        chances = low(powers / jnp.sum(powers, axis=1, keepdims=True))
        answer_chance_ref[at] = chances
        answer_attended_ref[slots] = low(fold(dot(chances, answer_heads_ref[2, slots])))
    answer_waits[3].wait()
    answer_hidden = answer_values + dot(answer_attended_ref[...], answer_square[3])
    answer_hidden_ref[...] = answer_hidden
    crossed = low(answer_hidden * rms_scale(answer_hidden) * gains[CROSS])
    crossed_ref[...] = crossed
    answer_waits[4].wait()
    asking_ref[...] = low(dot(crossed, answer_square[4]))

    for at in range(3):
        waits[at].wait()
        heads[at] = low(dot(normed[...], square[at]))
    heads_out = copies.start(heads, heads_hbm)
    second_half = lax.broadcasted_iota(jnp.int32, (ROW, 2 * HD), 1) >= HD

    for pair in range(H // 2):
        lanes = slice(pair * 2 * HD, (pair + 1) * 2 * HD)
        sums = []
        for which in range(2):
            head = pair * 2 + which
            bias = slope_bias(slopes[head : head + 1, :], ROW)
            for block in range(blocks):
                span = slice(block * ROW, (block + 1) * ROW)
                asked = heads[0, span, lanes]
                own = jnp.where(second_half == (which == 1), asked, jnp.zeros_like(asked))
                scores = dot_rows(own, heads[1, span, lanes]) + (bias + score[block, :ROW])
                powers = jnp.exp(scores - jnp.max(scores, axis=1, keepdims=True))
                chances = low(powers * (1.0 / jnp.sum(powers, axis=1, keepdims=True)))
                chance[head, block] = chances.T
                taken = dot(chances, heads[2, span, lanes])
                if which == 0:
                    sums.append(taken)
                else:
                    attended[span, lanes] = low(jnp.where(second_half, taken, sums[block]))
        part = pl.ds(pair * 2, 2)
        copies.out(chance.at[part], chance_hbm.at[part])

    copies.out(inputs, inputs_hbm)
    waits[3].wait()
    values = wide(input_ref[...]) + dot(attended[...], square[3])
    hidden[...] = values
    hidden_out = copies.start(hidden, hidden_hbm)
    second[...] = low(values * rms_scale(values) * gains[FFN])
    copies.out(second, second_hbm)
    wait_in.wait()
    for at in range(in_hbm.shape[1] // D):
        lanes = slice(at * D, (at + 1) * D)
        up, slope = gelu_pair(dot(second[...], wide_in[:, lanes]))
        active[:, lanes] = low(up)
        bend[:, lanes] = low(slope)
        copies.out(active.at[:, lanes], active_hbm.at[:, lanes])
        copies.out(bend.at[:, lanes], bend_hbm.at[:, lanes])
    wait_out.wait()
    values = hidden[...] + dot(active[...], wide_out[...])
    hidden_out.wait()
    hidden[...] = values
    copies.out(hidden, encoded_hbm)
    heads_out.wait()
    result = heads.at[0]
    final = heads.at[1]
    result[...] = low(values)
    copies.out(result, result_hbm)
    final[...] = low(values * rms_scale(values) * gains[FINAL])
    copies.out(final, final_hbm)
    for at in range(2):
        cross_waits[at].wait()
        memory[at] = low(dot(final[...], answer_square[at]))
    copies.out(memory, memory_hbm)

    lane = lax.broadcasted_iota(jnp.int32, (SLOT, 128), 1)
    for block in range(blocks):
        span = slice(block * ROW, (block + 1) * ROW)
        slots = slice(block * SLOT, (block + 1) * SLOT)
        scores = dot_rows(spread(asking_ref[slots]), memory[0, span])
        scores = jnp.where(padding_ref[block] == 1, scores, NEGATIVE)
        score[block] = scores
        top = jnp.max(scores, axis=1, keepdims=True)
        powers = jnp.exp(scores - top)
        sums = jnp.sum(powers, axis=1, keepdims=True)
        reading = fold(dot(low(powers * (1.0 / sums)), memory[1, span]))
        packed_ref[slots, :D] = low(reading)
        total = top + jnp.log(sums)
        extra = jnp.zeros((SLOT, 128), F32)
        for h in range(H):
            rest = total[h * SLOT : (h + 1) * SLOT]
            for piece in range(3):
                part = wide(low(rest))
                extra = jnp.where(lane == piece * H + h, part, extra)
                rest = rest - part
        packed_ref[slots, D:] = low(extra)
    copies.out(score, score_hbm)
    copies.finish()


def passage(
    length, answer_input, rows, segments, padding, table, answer_table, gains, answer_weights, weights
):
    count = rows.shape[0]
    blocks = count // ROW
    slots = blocks * SLOT
    wide_size = weights[4].shape[1]
    small = [
        ((len(gains), D), F32),
        ((slots, D), BF),
        ((3, slots, D), BF),
        ((blocks, H * SLOT, SLOT), BF),
        ((slots, D), BF),
        ((slots, D), F32),
        ((slots, D), BF),
        ((slots, D), BF),
        ((slots, D + 128), BF),
    ]
    whole = [
        ((2, count, D), BF),
        ((3, count, D), BF),
        ((H, blocks, ROW, ROW), BF),
        ((count, D), F32),
        ((count, D), BF),
        ((count, wide_size), BF),
        ((count, wide_size), BF),
        ((count, D), F32),
        ((count, D), BF),
        ((count, D), BF),
        ((2, count, D), BF),
        ((blocks, H * SLOT, ROW), F32),
    ]
    first = 7

    def body(*refs):
        last = first + len(gains)
        passage_kernel(*refs[:first], refs[first:last], *refs[last:])

    return kernel_call(
        body,
        (length, answer_input, rows, segments, padding, table, answer_table)
        + tuple(gains)
        + tuple(answer_weights)
        + tuple(weights),
        [pltpu.SMEM] + [VM] * (6 + len(gains)) + [ANY] * 13,
        [(shape, dtype, VM) for shape, dtype in small]
        + [(shape, dtype, ANY) for shape, dtype in whole],
        [
            VM((5, D, D), BF),
            VM((4, D, D), BF),
            VM((D, wide_size), BF),
            VM((wide_size, D), BF),
            VM((H, 2 * ROW), F32),
            pltpu.SemaphoreType.DMA((40,)),
        ]
        + [VM(shape, dtype) for at, (shape, dtype) in enumerate(whole) if at not in (7, 8, 9)],
    )


def rms_back(values, gain, upstream):
    scale = rms_scale(values)
    scaled = upstream * gain
    inner = jnp.mean(scaled * values, axis=-1, keepdims=True)
    delta = scaled * scale - values * (scale * scale * scale) * inner
    return (delta, jnp.sum(upstream * values * scale, axis=0, keepdims=True))


def exact_dot(left, right, rows=False):
    return lax.dot_general(
        left,
        right,
        (((1,), (1 if rows else 0,)), ((), ())),
        precision=lax.Precision.HIGHEST,
        preferred_element_type=jnp.float32,
    )


def head_columns(values):
    return jnp.concatenate([values[:, h : h + 1] for h in range(H)], axis=0)


def tree_sum(items):
    while len(items) > 1:
        items = [
            items[at] + items[at + 1] if at + 1 < len(items) else items[at]
            for at in range(0, len(items), 2)
        ]
    return items[0]


def answer_up_kernel(upstream_ref, out_hbm, up_ref, weight, arrivals):
    copies = Copies(arrivals)
    waits = []
    for at in range(out_hbm.shape[0] // D):
        part = pl.ds(at * D, D)
        waits.append(copies.start(out_hbm.at[part], weight.at[part]))
    upstream = low(slotted(upstream_ref))
    for at, wait in enumerate(waits):
        part = slice(at * D, (at + 1) * D)
        wait.wait()
        up_ref[:, part] = dot_rows(upstream, weight[part, :])


def answer_up(upstream, weight):
    return kernel_call(
        answer_up_kernel,
        (upstream, weight),
        [VM, ANY],
        [((upstream.shape[0] * SLOT, weight.shape[0]), F32, VM)],
        [VM(weight.shape, BF), pltpu.SemaphoreType.DMA((4,))],
    )[0]


def answer_middle_kernel(
    every_refs, asking_ref, hidden_ref, up_ref, upstream_ref, gains_ref, score_hbm, memory_hbm,
    mix_hbm, in_hbm,
    low_ref, wide_ref, middle_ref, middle_delta_ref, gain_delta_ref, memory_delta_hbm,
    asking_delta_ref, *refs, place_ref=None,
):
    *weight_refs, score, memory, memory_delta, mix, wide_in, arrivals = refs
    copies = Copies(arrivals)
    wait_mix = copies.start(mix_hbm, mix)
    wait_in = copies.start(in_hbm, wide_in)
    wait_memory = copies.start(memory_hbm, memory)
    wait_score = copies.start(score_hbm, score)
    count = asking_ref.shape[0]

    from_piece = lax.broadcasted_iota(jnp.int32, (128, 128), 0)
    to_head = lax.broadcasted_iota(jnp.int32, (128, 128), 1)
    same = (from_piece % H == to_head) & (from_piece < 3 * H)
    pieces = low(jnp.where(same, 1.0, 0.0))
    lane_head = lax.broadcasted_iota(jnp.int32, (128, D), 1) // HD
    widen = jnp.where(lane_head == lax.broadcasted_iota(jnp.int32, (128, D), 0), 1.0, 0.0)

    totals = [dot(ref[:, D:], pieces) for ref in every_refs]
    top = functools.reduce(jnp.maximum, totals)
    powers = [jnp.exp(total - top) for total in totals]
    sums = tree_sum(powers)
    reading = tree_sum(
        [
            wide(ref[:, :D]) * exact_dot(power / sums, widen)
            for ref, power in zip(every_refs, powers)
        ]
    )
    whole_total = top + jnp.log(sums)
    reading_low = low(reading)
    low_ref[0] = reading_low
    wait_mix.wait()
    middle = hidden_ref[...] + dot(reading_low, mix[...])
    middle_ref[...] = middle
    gain = gain_row(gains_ref, ANSWER)
    fifth = low(middle * rms_scale(middle) * gain)
    low_ref[1] = fifth
    wait_in.wait()
    for at in range(wide_in.shape[1] // D):
        lanes = slice(at * D, (at + 1) * D)
        active, slope = gelu_pair(dot(fifth, wide_in[:, lanes]))
        wide_ref[0, :, lanes] = low(active)
        wide_ref[1, :, lanes] = low(up_ref[:, lanes] * slope)
    delta, gain_delta = rms_back(middle, gain, dot_rows(wide_ref[1], wide_in[...]))
    gain_delta_ref[...] = gain_delta
    delta += slotted(upstream_ref)
    middle_delta_ref[...] = delta
    delta_low = low(delta)
    low_ref[2] = delta_low
    taken = low(dot_rows(delta_low, mix[...]))
    inner = exact_dot(wide(taken) * reading, widen, rows=True)
    wait_score.wait()
    wait_memory.wait()
    for block in range(count // SLOT):
        slots = slice(block * SLOT, (block + 1) * SLOT)
        span = slice(block * ROW, (block + 1) * ROW)
        chances = jnp.exp(score[block] - head_columns(whole_total[slots]))
        asked = spread(asking_ref[slots])
        upward = spread(taken[slots])
        delta_chances = dot_rows(upward, memory[1, span])
        deltas = low(chances * (delta_chances - head_columns(inner[slots])))
        memory_delta[0, span] = low(dot_tokens(deltas, asked))
        memory_delta[1, span] = low(dot_tokens(low(chances), upward))
        asking_delta_ref[slots] = low(fold(dot(deltas, memory[0, span])))
    copies.out(memory_delta, memory_delta_hbm)
    if weight_refs:
        answer_wide_weight(place_ref, low_ref, wide_ref, upstream_ref, *weight_refs)
    copies.finish()


def answer_middle(
    place, every, asking, hidden, up, upstream, gains, score, memory, weights, shards
):
    count = asking.shape[0]
    wide_size = weights[1].shape[1]
    blocks = len(every)
    outs, scratch = [], []
    if shards:
        outs = [((shards // 2, D // shards, D), BF, VM)] * 4
        scratch = [VM((D, D), BF), VM((wide_size, D // 2), BF)]

    def body(place_ref, *refs):
        answer_middle_kernel(refs[:blocks], *refs[blocks:], place_ref=place_ref)

    return kernel_call(
        body,
        (place, *every, asking, hidden, up, upstream, gains, score, memory, *weights),
        [pltpu.SMEM] + [VM] * (blocks + 5) + [ANY] * 4,
        [
            ((3, count, D), BF, VM),
            ((2, count, wide_size), BF, VM),
            ((count, D), F32, VM),
            ((count, D), F32, VM),
            ((1, D), F32, VM),
            (memory.shape, BF, ANY),
            ((count, D), BF, VM),
        ]
        + outs,
        scratch
        + [
            VM(score.shape, F32),
            VM(memory.shape, BF),
            VM(memory.shape, BF),
            VM((D, D), BF),
            VM((D, wide_size), BF),
            pltpu.SemaphoreType.DMA((8,)),
        ],
    )


def memory_back_kernel(
    place_ref, gains_ref, delta_hbm, final_hbm, encoded_hbm, upstream_hbm, key_hbm, value_hbm,
    active_hbm, weight_hbm, bend_hbm,
    send_hbm, keep_hbm, output_hbm, before_hbm, gain_delta_ref,
    delta, final, encoded, upstream, weights, active, weight, bend, both, output, before, arrivals,
):
    copies = Copies(arrivals)
    shards = both.shape[1]
    width = D // shards
    half = D // 2
    steps = active.shape[1] // D
    wait_delta = copies.start(delta_hbm, delta)
    waits = [copies.start(key_hbm, weights.at[0]), copies.start(value_hbm, weights.at[1])]
    wait_encoded = copies.start(encoded_hbm, encoded)
    wait_upstream = copies.start(upstream_hbm, upstream)
    wait_final = copies.start(final_hbm, final)
    wait_active = []
    for at in range(steps):
        part = pl.ds(at * D, D)
        wait_active.append(copies.start(active_hbm.at[:, part], active.at[:, part]))
    wait_back = []
    for at in range(steps):
        part = pl.ds(at * D, D)
        wait_back.append(
            [
                copies.start(weight_hbm.at[part], weight.at[part]),
                copies.start(bend_hbm.at[:, part], bend.at[:, part]),
            ]
        )
    core = place_ref[0]
    wait_delta.wait()
    for wait in waits:
        wait.wait()
    upward = dot_rows(delta[0], weights[0]) + dot_rows(delta[1], weights[1])
    wait_encoded.wait()
    wait_upstream.wait()
    back, gain_delta = rms_back(encoded[...], gain_row(gains_ref, FINAL), upward)
    gain_delta_ref[...] = gain_delta
    back += wide(upstream[...])
    output[...] = back
    copies.out(output, output_hbm)
    output_low = low(back)
    wait_final.wait()

    for side in range(2):
        first = low(dot_tokens(final[...], delta[side]))
        for shard in range(shards):
            for row in range(2):
                begin = shard * width + row * (width // 2)
                both[side, shard, row, : width // 2] = first[begin : begin + width // 2]
    for at in range(steps):
        wait_active[at].wait()
        later = low(dot_tokens(active[:, at * D : (at + 1) * D], output_low))
        for side in range(2):
            columns = slice(side * half, (side + 1) * half)
            for piece in range(D // width):
                shard, place = divmod(at * D // width + piece, 4)
                row, part = divmod(place, 2)
                rows = slice(piece * width, (piece + 1) * width)
                lanes = slice(part * half, (part + 1) * half)
                both[side, shard, row, width // 2 :, lanes] = later[rows, columns]
        done = pl.ds(at * shards // steps, shards // steps)
        copies.out(both.at[1 - core, done], send_hbm.at[done])
        copies.out(both.at[core, done], keep_hbm.at[done])
    for at in range(steps):
        part = slice(at * D, (at + 1) * D)
        for wait in wait_back[at]:
            wait.wait()
        before[:, part] = low(dot_rows(output_low, weight[part, :]) * wide(bend[:, part]))
        copies.out(before.at[:, part], before_hbm.at[:, part])
    copies.finish()


def memory_back(
    place, gains, delta, final, encoded, upstream, weights, active, weight, bend, shards, after=()
):
    count = final.shape[0]
    wide_size = active.shape[1]
    shape = (shards, 2, 3 * D // shards // 2, D)
    return kernel_call(
        memory_back_kernel,
        (place, gains, delta, final, encoded, upstream)
        + tuple(weights)
        + (active, weight, bend),
        [pltpu.SMEM, VM] + [ANY] * 9,
        [
            (shape, BF, ANY),
            (shape, BF, ANY),
            ((count, D), F32, ANY),
            ((count, wide_size), BF, ANY),
            ((1, D), F32, VM),
        ],
        [
            VM((2, count, D), BF), VM((count, D), BF), VM((count, D), F32), VM((count, D), BF),
            VM((2, D, D), BF), VM((count, wide_size), BF), VM((wide_size, D), BF),
            VM((count, wide_size), BF), VM((2,) + shape, BF), VM((count, D), F32),
            VM((count, wide_size), BF), pltpu.SemaphoreType.DMA((40,)),
        ],
        after,
    )


def wide_in_back_kernel(
    place_ref, gains_ref, second_hbm, before_hbm, weight_hbm, hidden_hbm, output_hbm, mix_hbm,
    send_hbm, keep_hbm, hidden_delta_hbm, hidden_low_hbm, attended_delta_hbm, gain_delta_ref,
    second, before, weight, hidden, output, mix, send, keep, hidden_delta, hidden_low,
    attended_delta, arrivals,
):
    copies = Copies(arrivals)
    steps = before.shape[1] // D // 2
    core = place_ref[0]
    wait_second = copies.start(second_hbm, second)
    units = [(1 - core) * steps + at for at in range(steps)]
    units += [core * steps + at for at in range(steps)]
    waits = []
    for unit in units:
        part = pl.ds(pl.multiple_of(unit * D, D), D)
        waits.append(copies.start(before_hbm.at[:, part], before.at[:, part]))
    later = [
        copies.start(source, target)
        for source, target in (
            (weight_hbm, weight), (hidden_hbm, hidden), (output_hbm, output), (mix_hbm, mix)
        )
    ]
    wait_second.wait()
    for at, unit in enumerate(units):
        waits[at].wait()
        part = pl.ds(pl.multiple_of(unit * D, D), D)
        target, target_hbm = (send, send_hbm) if at < steps else (keep, keep_hbm)
        target[at % steps] = low(dot_tokens(second[...], before[:, part]))
        copies.out(target.at[at % steps], target_hbm.at[at % steps])
    for wait in later:
        wait.wait()
    upward = dot_rows(before[...], weight[...])
    back, gain_delta = rms_back(hidden[...], gain_row(gains_ref, FFN), upward)
    gain_delta_ref[...] = gain_delta
    back += output[...]
    hidden_delta[...] = back
    copies.out(hidden_delta, hidden_delta_hbm)
    hidden_low[...] = low(back)
    copies.out(hidden_low, hidden_low_hbm)
    attended_delta[...] = low(dot_rows(hidden_low[...], mix[...]))
    copies.out(attended_delta, attended_delta_hbm)
    copies.finish()


def wide_in_back(place, gains, second, before, weight, hidden, output, mix, after=()):
    count, wide_size = before.shape
    shape = (wide_size // D // 2, D, D)
    return kernel_call(
        wide_in_back_kernel,
        (place, gains, second, before, weight, hidden, output, mix),
        [pltpu.SMEM, VM] + [ANY] * 6,
        [
            (shape, BF, ANY),
            (shape, BF, ANY),
            ((count, D), F32, ANY),
            ((count, D), BF, ANY),
            ((count, D), BF, ANY),
            ((1, D), F32, VM),
        ],
        [
            VM((count, D), BF), VM((count, wide_size), BF), VM((D, wide_size), BF),
            VM((count, D), F32), VM((count, D), F32), VM((D, D), BF), VM(shape, BF),
            VM(shape, BF), VM((count, D), F32), VM((count, D), BF), VM((count, D), BF),
            pltpu.SemaphoreType.DMA((24,)),
        ],
        after,
    )


def attend_back_kernel(
    place_ref, heads_hbm, chance_hbm, upstream_hbm, inputs_hbm, hidden_low_hbm,
    delta_hbm, slope_delta_ref, send_hbm, keep_hbm,
    heads, chance, upstream, inputs, delta, gathered, units, arrivals,
):
    copies = Copies(arrivals)
    pairs = H // 2
    waits = []
    for pair in range(pairs):
        lanes = pl.ds(pair * 2 * HD, 2 * HD)
        part = pl.ds(pair * 2, 2)
        waits.append(
            [
                copies.start(heads_hbm.at[:, :, lanes], heads.at[:, :, lanes]),
                copies.start(upstream_hbm.at[:, lanes], upstream.at[:, lanes]),
                copies.start(chance_hbm.at[part], chance.at[part]),
            ]
        )
    wait_inputs = copies.start(inputs_hbm, inputs)
    wait_hidden = copies.start(hidden_low_hbm, delta.at[3])
    blocks = upstream.shape[0] // ROW
    second_half = lax.broadcasted_iota(jnp.int32, (ROW, 2 * HD), 1) >= HD
    place_row = lax.broadcasted_iota(jnp.int32, (ROW, ROW), 0)
    place_column = lax.broadcasted_iota(jnp.int32, (ROW, ROW), 1)
    mirror = low(jnp.where(place_row + place_column == ROW - 1, 1.0, 0.0))

    for pair in range(pairs):
        lanes = slice(pair * 2 * HD, (pair + 1) * 2 * HD)
        for wait in waits[pair]:
            wait.wait()
        kept = []
        for which in range(2):
            head = pair * 2 + which
            for block in range(blocks):
                span = slice(block * ROW, (block + 1) * ROW)
                query, key, value = (heads[at, span, lanes] for at in range(3))
                upward = upstream[span, lanes]
                own = jnp.where(second_half == (which == 1), upward, jnp.zeros_like(upward))
                chances = chance[head, block]
                weight = wide(chances)
                delta_chances = dot_rows(value, own)
                inner = jnp.sum(delta_chances * weight, axis=0, keepdims=True)
                deltas = low(weight * (delta_chances - inner))
                if block == 0:
                    gathered[...] = wide(deltas)
                else:
                    gathered[...] += wide(deltas)
                own_key = key.T[which * HD : (which + 1) * HD]
                news = [low(dot(own_key, deltas)), dot(deltas, query), dot(chances, upward)]
                if which == 0:
                    kept.append(news)
                else:
                    delta[0, span, lanes] = jnp.concatenate([kept[block][0], news[0]], axis=0).T
                    for at in (1, 2):
                        both = jnp.where(second_half, news[at], kept[block][at])
                        delta[at, span, lanes] = low(both)
            whole = gathered[...]
            most = low(whole)
            turned = dot(mirror, most) + dot(mirror, low(whole - wide(most)))
            padded = jnp.concatenate([turned, jnp.zeros((ROW, ROW), F32)], axis=1)
            rolled = pltpu.roll(padded, 1, 1, stride=1, stride_axis=0)
            slope_delta_ref[head : head + 1, :] = jnp.sum(rolled, axis=0, keepdims=True)
        done = pl.ds(pair * 2 * HD, 2 * HD)
        copies.out(delta.at[pl.ds(0, 3), :, done], delta_hbm.at[:, :, done])

    wait_hidden.wait()
    wait_inputs.wait()
    for unit in range(4):
        units[unit // 2, unit % 2] = low(dot_tokens(inputs[unit // 3], delta[unit]))
    copies.out(units.at[1 - place_ref[0]], send_hbm)
    copies.out(units.at[place_ref[0]], keep_hbm)
    copies.finish()


def attend_back(place, heads, chance, upstream, inputs, hidden_low, after=()):
    count = upstream.shape[0]
    return kernel_call(
        attend_back_kernel,
        (place, heads, chance, upstream, inputs, hidden_low),
        [pltpu.SMEM] + [ANY] * 5,
        [
            ((3, count, D), BF, ANY),
            ((H, 2 * ROW), F32, VM),
            ((2, D, D), BF, ANY),
            ((2, D, D), BF, ANY),
        ],
        [
            VM(heads.shape, BF), VM(chance.shape, BF), VM(upstream.shape, BF),
            VM(inputs.shape, BF), VM((4, count, D), BF), VM((ROW, ROW), F32),
            VM((2, 2, D, D), BF), pltpu.SemaphoreType.DMA((36,)),
        ],
        after,
    )


def passage_end_kernel(
    place_ref, gains_ref, slope_delta_ref, answer_table_ref, ffn_gain_ref, final_gain_ref,
    self_gain_ref, cross_gain_ref, answer_gain_ref,
    input_hbm, delta_hbm, hidden_delta_hbm, query_hbm, key_hbm, value_hbm,
    gradient_hbm, small_low_ref,
    values, delta, hidden_delta, weights, gradient, small_ref, arrivals,
):
    copies = Copies(arrivals)
    wait_delta = copies.start(delta_hbm, delta)
    waits = [
        copies.start(source, weights.at[at])
        for at, source in enumerate((query_hbm, key_hbm, value_hbm))
    ]
    wait_input = copies.start(input_hbm, values)
    wait_hidden = copies.start(hidden_delta_hbm, hidden_delta)
    once = jnp.where((place_ref[0] == 0) & (place_ref[1] == 0), 1.0, 0.0)
    small_ref[...] = jnp.zeros_like(small_ref)
    small_ref[FFN : FFN + 1, :] = ffn_gain_ref[...]
    small_ref[FINAL : FINAL + 1, :] = final_gain_ref[...]
    small_ref[SELF : SELF + 1, :] = self_gain_ref[...] * once
    small_ref[CROSS : CROSS + 1, :] = cross_gain_ref[...] * once
    small_ref[ANSWER : ANSWER + 1, :] = answer_gain_ref[...] * once
    offsets = ROW - lax.broadcasted_iota(jnp.int32, (2 * ROW, 128), 0)
    matches = bucket_of(offsets, True) == lax.broadcasted_iota(jnp.int32, (2 * ROW, 128), 1)
    table = exact_dot(slope_delta_ref[...], jnp.where(matches, 1.0, 0.0))
    small_ref[8 : 8 + H, :128] = table
    small_ref[8 : 8 + H, 128:256] = answer_table_ref[:H, :] * once
    wait_delta.wait()
    for wait in waits:
        wait.wait()
    upward = dot_rows(delta[0], weights[0])
    upward += dot_rows(delta[1], weights[1])
    upward += dot_rows(delta[2], weights[2])
    wait_input.wait()
    wait_hidden.wait()
    back, gain_delta = rms_back(wide(values[...]), gain_row(gains_ref, ATTN), upward)
    small_ref[ATTN : ATTN + 1, :] = gain_delta
    small_low_ref[...] = low(small_ref[...])
    gradient[...] = back + hidden_delta[...]
    copies.out(gradient, gradient_hbm)
    copies.finish()


def passage_end(place, gains, small, rows, delta, hidden_delta, weights, after=()):
    count = rows.shape[0]
    return kernel_call(
        passage_end_kernel,
        (place, gains) + tuple(small) + (rows, delta, hidden_delta) + tuple(weights),
        [pltpu.SMEM] + [VM] * 8 + [ANY] * 6,
        [((count, D), F32, ANY), ((32, D), BF, VM)],
        [
            VM((count, D), BF), VM((3, count, D), BF), VM((count, D), F32), VM((3, D, D), BF),
            VM((count, D), F32), VM((32, D), F32), pltpu.SemaphoreType.DMA((8,)),
        ],
        after,
    )


def answer_end_kernel(
    asking_refs, middle_delta_ref, hidden_ref, input_ref, gains_ref,
    heads_ref, chance_ref, ask_hbm, mix_hbm, query_hbm, key_hbm, value_hbm,
    gradient_ref, asking_delta_ref, hidden_low_ref, delta_ref, cross_delta_ref,
    self_delta_ref, table_ref,
    weights, score_delta, arrivals,
):
    copies = Copies(arrivals)
    waits = [
        copies.start(source, weights.at[at])
        for at, source in enumerate((ask_hbm, mix_hbm, query_hbm, key_hbm, value_hbm))
    ]
    asking_delta_ref[...] = low(tree_sum([wide(ref[...]) for ref in asking_refs]))
    waits[0].wait()
    upward = dot_rows(asking_delta_ref[...], weights[0])
    back, gain_delta = rms_back(hidden_ref[...], gain_row(gains_ref, CROSS), upward)
    cross_delta_ref[...] = gain_delta
    back += middle_delta_ref[...]
    hidden_low = low(back)
    hidden_low_ref[...] = hidden_low
    waits[1].wait()
    upward = low(dot_rows(hidden_low, weights[1]))
    column = lax.broadcasted_iota(jnp.int32, (SLOT, 128), 0)
    lane = lax.broadcasted_iota(jnp.int32, (SLOT, 128), 1)
    mirror = low(jnp.where(column + lane == SLOT - 1, 1.0, 0.0))
    for block in range(upward.shape[0] // SLOT):
        slots = slice(block * SLOT, (block + 1) * SLOT)
        chances = chance_ref[block]
        taken = spread(upward[slots])
        delta_chances = dot_rows(taken, heads_ref[2, slots])
        inner = jnp.sum(delta_chances * wide(chances), axis=1, keepdims=True)
        deltas = low(wide(chances) * (delta_chances - inner))
        turned = dot(deltas, mirror)
        if block == 0:
            score_delta[...] = turned
        else:
            score_delta[...] += turned
        delta_ref[0, slots] = low(fold(dot(deltas, heads_ref[1, slots])))
        delta_ref[1, slots] = low(dot_tokens(deltas, spread(heads_ref[0, slots])))
        delta_ref[2, slots] = low(dot_tokens(chances, taken))
    for wait in waits[2:]:
        wait.wait()
    upward = dot_rows(delta_ref[0], weights[2])
    upward += dot_rows(delta_ref[1], weights[3])
    upward += dot_rows(delta_ref[2], weights[4])
    start_delta, gain_delta = rms_back(slotted(input_ref), gain_row(gains_ref, SELF), upward)
    self_delta_ref[...] = gain_delta
    unslotted(start_delta + back, gradient_ref)
    sums = []
    for h in range(H):
        rows = score_delta[h * SLOT : (h + 1) * SLOT]
        rolled = pltpu.roll(rows, 0, 1, stride=1, stride_axis=0)
        sums.append(jnp.sum(rolled, axis=0, keepdims=True))
    sums.append(jnp.zeros((16 - H, 128), F32))
    offsets = (SLOT - 1) - lax.broadcasted_iota(jnp.int32, (128, 128), 0)
    matches = bucket_of(offsets, False) == lax.broadcasted_iota(jnp.int32, (128, 128), 1)
    table_ref[...] = exact_dot(jnp.concatenate(sums, axis=0), jnp.where(matches, 1.0, 0.0))


def answer_out_kernel(middle_ref, wide_ref, out_hbm, result_ref, weight, arrivals):
    copies = Copies(arrivals)
    waits = []
    for at in range(out_hbm.shape[0] // D):
        part = pl.ds(at * D, D)
        waits.append(copies.start(out_hbm.at[part], weight.at[part]))
    total = middle_ref[...]
    for at, wait in enumerate(waits):
        part = slice(at * D, (at + 1) * D)
        wait.wait()
        total += dot(wide_ref[0, :, part], weight[part, :])
    unslotted(total, result_ref)


def answer_out(middle, wide_pair, weight, like, after=()):
    return kernel_call(
        answer_out_kernel,
        (middle, wide_pair, weight),
        [VM, VM, ANY],
        [(like.shape, BF, VM)],
        [VM(weight.shape, BF), pltpu.SemaphoreType.DMA((4,))],
        after,
    )[0]


def answer_end(
    place, asking_deltas, middle_delta, hidden, rows, gains, heads, chance, inputs, weights, shards,
    after=()
):
    count = hidden.shape[0]
    blocks = len(asking_deltas)
    outs, scratch = [], []
    if shards:
        outs = [((shards // 2, 3 * D // shards // 2, D), BF, VM)] * 2
        scratch = [VM((4, count, D), BF), VM((4, count, D), BF), VM((D, D), BF), VM((D, D), BF)]

    def body(place_ref, *refs):
        asking_refs, refs = refs[:blocks], refs[blocks:]
        input_refs, refs = refs[:4], refs[4:]
        first, last = refs[:18], refs[18:]
        share, own = last[: 6 if shards else 0], last[6 if shards else 0 :]
        answer_end_kernel(asking_refs, *first, *own)
        if shards:
            answer_square_weight(place_ref, *input_refs, first[12], first[13], first[14], *share)

    return kernel_call(
        body,
        (place, *asking_deltas, *inputs, middle_delta, hidden, rows, gains, heads, chance, *weights),
        [pltpu.SMEM] + [VM] * (blocks + 10) + [ANY] * 5,
        [
            (rows.shape, F32, VM),
            ((count, D), BF, VM),
            ((count, D), BF, VM),
            ((3, count, D), BF, VM),
            ((1, D), F32, VM),
            ((1, D), F32, VM),
            ((16, 128), F32, VM),
        ]
        + outs,
        scratch
        + [
            VM((5, D, D), BF), VM((H * SLOT, 128), F32), pltpu.SemaphoreType.DMA((5,)),
        ],
        after,
    )


def answer_wide_weight(
    place_ref, lows_ref, wide_ref, upstream_ref, in_send_ref, in_keep_ref, out_send_ref,
    out_keep_ref, inner, full
):
    core = place_ref[0]
    row = place_ref[1]
    width = in_send_ref.shape[1]
    half = D // 2
    part = pl.ds(pl.multiple_of((core * 2 + row) * D, D), D)
    inner[...] = low(dot_tokens(lows_ref[1], wide_ref[1, :, part]))
    upstream = slotted(upstream_ref)
    upstream = low(jnp.where(core == 0, upstream[:, :half], upstream[:, half:]))
    for at in range(wide_ref.shape[2] // D):
        span = slice(at * D, (at + 1) * D)
        full[span, :] = low(dot_tokens(wide_ref[0, :, span], upstream))
    for part_ref, sent in ((in_send_ref, True), (in_keep_ref, False)):
        for at in range(part_ref.shape[0]):
            own = place_ref[2]
            shard = at * 2 + (1 - own if sent else own)
            rows = pl.ds(pl.multiple_of(shard * width, 16), width)
            part_ref[at] = inner[rows, :]
    for part_ref, sent in ((out_send_ref, True), (out_keep_ref, False)):
        for at in range(part_ref.shape[0]):
            own = place_ref[3]
            shard = at // 2 * 4 + (1 - own if sent else own) * 2 + at % 2
            for side in range(2):
                begin = shard * 4 * width + row * 2 * width + side * width
                rows = pl.ds(pl.multiple_of(begin, 16), width)
                part_ref[at, :, side * half : (side + 1) * half] = full[rows, :]


def answer_square_weight(
    place_ref, crossed_ref, low_ref, attended_ref, normed_ref, asking_delta_ref, hidden_low_ref,
    delta_ref, send_ref, keep_ref, inputs, deltas, first, full,
):
    core = place_ref[0]
    row = place_ref[1]
    width = send_ref.shape[1] * 2 // 3
    inputs[0] = crossed_ref[...]
    inputs[1] = low_ref[0]
    inputs[2] = attended_ref[...]
    inputs[3] = normed_ref[...]
    deltas[0] = asking_delta_ref[...]
    deltas[1] = low_ref[2]
    deltas[2] = hidden_low_ref[...]
    deltas[3] = delta_ref[0]
    unit = core * 2 + row
    first[...] = low(dot_tokens(inputs[unit], deltas[unit]))
    full[...] = low(dot_tokens(normed_ref[...], delta_ref[1 + core]))
    for part_ref, sent in ((send_ref, True), (keep_ref, False)):
        for at in range(part_ref.shape[0]):
            own = place_ref[3]
            shard = at // 2 * 4 + (1 - own if sent else own) * 2 + at % 2
            rows = pl.ds(pl.multiple_of(shard * width, 16), width)
            part_ref[at, :width] = first[rows, :]
            rows = pl.ds(pl.multiple_of(shard * width + row * (width // 2), 16), width // 2)
            part_ref[at, width:] = full[rows, :]


class Part:
    def __init__(self, rows, left, first=0):
        self.rows = rows
        self.left = list(left)
        self.first = first
        self.terms = []

    def array(self, values, names):
        values = values.reshape((2,) * len(names) + (-1, values.shape[-1]))
        self.terms.append((values, list(names), None))
        return self

    def size(self, name):
        count = len([one for one in self.left if one != name])
        return (2**count) * self.rows if name else self.rows

    def sent(self, name, values, begin):
        self.left.remove(name)


class Total(Part):
    def __init__(self, values):
        super().__init__(values.shape[0], "")
        self.terms.append((values, [], 0))

    def size(self, name):
        return self.rows

    def sent(self, name, values, begin):
        self.terms = [(values, [], begin)]


PLACES = "cyxlh"


def bus(place, jobs, after=()):
    arrays = []
    plans = []
    scratch = []
    outs = []
    for name, parts in jobs:
        begin = 0
        for part in parts:
            kept = [one for one in part.left if one != name] if name else []
            for values, names, start in part.terms:
                at = [id(one) for one in arrays]
                if id(values) not in at:
                    arrays.append(values)
                    at.append(id(values))
                inner = [one for one in names if one in kept]
                room = (2,) * len(inner) + (part.rows, D) if start is None else (
                    (2 ** len(inner)) * part.rows, D
                )
                plans.append(
                    (len(outs), begin, at.index(id(values)), names, start, inner, part, kept, name)
                )
                scratch.append(VM(room, BF))
            begin += part.size(name)
        outs.append(((begin, D), BF, VM))
    count = len(arrays)

    def body(place_ref, *refs):
        sources, targets = refs[:count], refs[count : count + len(outs)]
        rooms, semaphores = refs[count + len(outs) : -1], refs[-1]
        copies = Copies(semaphores)

        def spot(one, part, name):
            own = place_ref[PLACES.index(one)]
            return 1 - own if one == name else own

        waits = []
        for room, (_, _, source, names, start, inner, part, kept, name) in zip(rooms, plans):
            if start is None:
                index = [
                    slice(None) if one in kept else spot(one, part, name) for one in names
                ]
                origin = sources[source].at[(*index, pl.ds(part.first, part.rows))]
            else:
                row = start
                for depth, one in enumerate(names):
                    if one not in kept:
                        stride = (2 ** (len(names) - 1 - depth)) * part.rows
                        row = row + spot(one, part, name) * stride
                length = (2 ** len(inner)) * part.rows
                origin = sources[source].at[pl.ds(pl.multiple_of(row, 16), length)]
            waits.append(copies.start(origin, room))
        for wait in waits:
            wait.wait()
        sums = {}
        for room, (out, begin, _, _, start, inner, part, kept, name) in zip(rooms, plans):
            for number in range(2 ** len(kept)):
                bits = [number >> (len(kept) - 1 - depth) & 1 for depth in range(len(kept))]
                at = dict(zip(kept, bits))
                if start is None:
                    value = room[tuple(at[one] for one in inner)] if inner else room[...]
                else:
                    value = room[number * part.rows : (number + 1) * part.rows]
                sums.setdefault((out, begin + number * part.rows, part.rows), []).append(value)
        for (out, begin, rows), values in sums.items():
            total = functools.reduce(jnp.add, [wide(value) for value in values])
            targets[out][begin : begin + rows] = low(total)

    return kernel_call(
        body,
        (place, *arrays),
        [pltpu.SMEM] + [ANY] * count,
        outs,
        scratch + [pltpu.SemaphoreType.DMA((len(plans),))],
        after,
    )


def ride(ring, place, jobs, after=()):
    sends = list(bus(place, jobs, after))
    trip = []
    for (name, parts), values in zip(jobs, sends):
        begin = 0
        stops = []
        for part in parts:
            length = part.size(name)
            part.sent(name, values, begin)
            stops.append((part, begin, list(part.left)))
            begin += length
        trip.append([ring.swap(values, name), stops])
    return trip, sends


def arrive(items, *trips):
    legs = [leg for trip in trips for leg in trip]
    items = lax.optimization_barrier((*items, *[leg[0] for leg in legs]))
    count = len(items) - len(legs)
    for values, (_, stops) in zip(items[count:], legs):
        for part, begin, names in stops:
            part.terms.append((values, names, begin))
    return items[:count]


def assemble_kernel(place_ref, mine_hbm, near_hbm, far_hbm, across_hbm, *refs, lay):
    outs, whole, arrivals = refs[:-2], refs[-2], refs[-1]
    copies = Copies(arrivals)
    core, row = place_ref[0], place_ref[1]
    waits = [
        copies.start(mine_hbm, whole.at[core, row]),
        copies.start(near_hbm, whole.at[core, 1 - row]),
        copies.start(far_hbm, whole.at[1 - core, row]),
        copies.start(across_hbm, whole.at[1 - core, 1 - row]),
    ]
    for wait in waits:
        wait.wait()
    for out, rows, columns, part in lay:
        c, y, begin, lanes = part
        height, width = rows[1] - rows[0], columns[1] - columns[0]
        outs[out][rows[0] : rows[1], columns[0] : columns[1]] = wide(
            whole[c, y, begin : begin + height, lanes : lanes + width]
        )


def assemble(place, arrays, shapes, lay):
    rows = arrays[0].shape[0]
    return kernel_call(
        functools.partial(assemble_kernel, lay=lay),
        (place, *arrays),
        [pltpu.SMEM] + [ANY] * 4,
        [(shape, F32, VM) for shape in shapes],
        [VM((2, 2, rows, D), BF), pltpu.SemaphoreType.DMA((4,))],
    )


def layout(rows):
    half = D // 2
    lay = []
    shapes = []

    def stacked(begin):
        for c in range(2):
            for y in range(2):
                at = (y * rows // 2, (y + 1) * rows // 2)
                lay.append((len(shapes), at, (0, D), (c, y, begin, 0)))
            shapes.append((rows, D))

    def unhalved(begin):
        for c in range(2):
            for y in range(2):
                for side in range(2):
                    low_row = (y * 2 + side) * rows
                    lay.append(
                        (
                            len(shapes),
                            (low_row, low_row + rows),
                            (c * half, (c + 1) * half),
                            (c, y, begin, side * half),
                        )
                    )
        shapes.append((4 * rows, D))

    def side_by_side(begin):
        for c in range(2):
            for y in range(2):
                at = c * 2 + y
                lay.append((len(shapes), (0, rows), (at * D, (at + 1) * D), (c, y, begin, 0)))
        shapes.append((rows, 4 * D))

    def units(begin):
        for c in range(2):
            for y in range(2):
                lay.append((len(shapes), (0, rows), (0, D), (c, y, begin, 0)))
                shapes.append((rows, D))

    return lay, shapes, stacked, unhalved, side_by_side, units


class Ring:
    def __init__(self, mesh):
        self.dp = mesh.shape["dp"]
        self.blk = mesh.shape["blk"]
        self.cut = self.blk == 4 and self.dp == 8

    def bit(self, name):
        return {"c": 1, "y": 2, "x": 4, "l": 8, "h": 16}[name]

    def number(self):
        return lax.axis_index("dp") * self.blk + lax.axis_index("blk")

    def place(self, name):
        return self.number() // self.bit(name) % 2

    def swap(self, values, *names):
        mask = sum(self.bit(name) for name in names)
        moves = [(at, at ^ mask) for at in range(self.dp * self.blk)]
        return lax.ppermute(values, ("dp", "blk"), moves)


class Beside:
    def __init__(self, ring, mine):
        self.ring = ring
        self.mine = mine
        self.arriving = [ring.swap(mine, "y"), ring.swap(mine, "c")]

    def send(self, cues=()):
        near, far, *_ = lax.optimization_barrier((*self.arriving, *cues))
        self.arriving = [near, far, self.ring.swap(near, "c")]

    def arrays(self, cues=()):
        near, far, across, *_ = lax.optimization_barrier((*self.arriving, *cues))
        return [self.mine, near, far, across]


def on_device(
    ring,
    encoder_input,
    decoder_input,
    encoder_cotangent,
    decoder_cotangent,
    segment_ids,
    padding_mask,
    answer_length,
    encoder_attn_gain,
    encoder_query,
    encoder_key,
    encoder_value,
    encoder_mix,
    encoder_bias_table,
    encoder_ffn_gain,
    encoder_ffn_in,
    encoder_ffn_out,
    final_gain,
    cross_key,
    cross_value,
    decoder_self_gain,
    decoder_query,
    decoder_key,
    decoder_value,
    decoder_mix,
    decoder_bias_table,
    decoder_cross_gain,
    cross_query,
    cross_mix,
    decoder_ffn_gain,
    decoder_ffn_in,
    decoder_ffn_out,
):
    cut = ring.cut
    shard = D // ring.dp
    questions = encoder_input.shape[0]
    batch = questions * encoder_input.shape[1]
    passage_rows = encoder_input.reshape(batch * ROW, D)
    passage_upstream = encoder_cotangent.reshape(batch * ROW, D)
    core = ring.place("c")
    row = lax.axis_index("blk") // 2
    place = [core, row, ring.place("x"), ring.place("l"), ring.place("h")]
    place = jnp.stack(place).astype(jnp.int32)
    (
        gains,
        answer_normed,
        answer_heads,
        answer_chances,
        answer_attended,
        answer_hidden,
        answer_crossed,
        asking,
        packed,
        inputs,
        heads,
        chances,
        hidden,
        second,
        active,
        bend,
        encoded,
        result,
        final,
        memory,
        scores,
    ) = passage(
        answer_length,
        decoder_input,
        passage_rows,
        segment_ids.reshape(batch, 1, ROW),
        padding_mask.reshape(batch, 1, ROW),
        encoder_bias_table.T,
        decoder_bias_table.T,
        (
            encoder_attn_gain,
            encoder_ffn_gain,
            final_gain,
            decoder_self_gain,
            decoder_cross_gain,
            decoder_ffn_gain,
        ),
        (decoder_query, decoder_key, decoder_value, decoder_mix, cross_query),
        (
            encoder_query,
            encoder_key,
            encoder_value,
            encoder_mix,
            encoder_ffn_in,
            encoder_ffn_out,
            cross_key,
            cross_value,
        ),
    )

    def neighbours(values):
        if cut:
            return [values] + [ring.swap(values, *names) for names in ("c", "y", "yc")]
        every = lax.all_gather(values, "blk", axis=0)
        return [every[at] for at in range(ring.blk)]

    every = neighbours(packed)
    (upstream_cue, _) = lax.optimization_barrier((decoder_cotangent, packed))
    answer_upward = answer_up(upstream_cue, decoder_ffn_out)
    (
        answer_lows,
        answer_wides,
        answer_middle_rows,
        middle_delta,
        answer_gain_delta,
        memory_delta,
        asking_delta,
        *wide_halves,
    ) = answer_middle(
        place,
        every,
        asking,
        answer_hidden,
        answer_upward,
        decoder_cotangent,
        gains,
        scores,
        memory,
        (cross_mix, decoder_ffn_in),
        ring.dp if cut else None,
    )

    asking_deltas = neighbours(asking_delta)
    after = []
    if cut:
        half = shard // 2
        in_half, in_kept, out_half, out_kept = wide_halves
        wide_first = Part(shard, "lh").array(in_kept, "hl")
        wide_second = Part(shard, "xh").array(out_kept, "hx")
        wide_got = [ring.swap(in_half, "x"), ring.swap(out_half, "l")]
        after = [in_half]
    memory_send, memory_keep, output_delta, before, final_gain_delta = memory_back(
        place,
        gains,
        memory_delta,
        final,
        encoded,
        passage_upstream,
        (cross_key, cross_value),
        active,
        encoder_ffn_out,
        bend,
        ring.dp,
        after=after,
    )
    if cut:
        memory_send, cue, *wide_got = arrive([memory_send, place, *wide_got])
        wide_first.array(wide_got[0], "hl")
        wide_second.array(wide_got[1], "hx")
        memory_got = ring.swap(memory_send, "c")
        trip, sends = ride(ring, cue, [("l", [wide_first]), ("x", [wide_second])])
        after = sends + [memory_send] + asking_deltas
    (
        answer_gradient,
        asking_delta,
        answer_hidden_low,
        answer_heads_delta,
        cross_gain_delta,
        self_gain_delta,
        answer_table_delta,
        *square_halves,
    ) = answer_end(
        place,
        asking_deltas,
        middle_delta,
        answer_hidden,
        decoder_input,
        gains,
        answer_heads,
        answer_chances,
        (answer_crossed, answer_lows, answer_attended, answer_normed),
        (cross_query, decoder_mix, decoder_query, decoder_key, decoder_value),
        ring.dp if cut else None,
        after=after,
    )
    after = []
    if cut:
        send, keep = square_halves
        send, memory_got, cue = arrive([send, memory_got, place], trip)
        answer_square = Part(3 * half, "hx").array(keep, "hx")
        square_got = ring.swap(send, "l")
        top = 5 * 16
        memory_first = Part(top, "yxlh").array(memory_keep, "hlxy").array(memory_got, "hlxy")
        memory_second = Part(3 * half - top, "xylh", top)
        memory_second.array(memory_keep, "hlxy").array(memory_got, "hlxy")
        trip_memory, sends = ride(
            ring, cue, [("y", [memory_first]), ("x", [memory_second]), ("h", [wide_first, wide_second])]
        )
        after = sends + [send]
    in_send, in_keep, hidden_delta, hidden_low, attended_delta, ffn_gain_delta = wide_in_back(
        place,
        gains,
        second,
        before,
        encoder_ffn_in,
        hidden,
        output_delta,
        encoder_mix,
        after=after,
    )
    after = []
    if cut:
        in_got = ring.swap(in_send, "c")
        after = [in_send]
    answer_result = answer_out(
        answer_middle_rows, answer_wides, decoder_ffn_out, decoder_input, after=after
    )
    after = []
    if cut:
        answer_result, attended_delta, in_got, square_got, cue = arrive(
            [answer_result, attended_delta, in_got, square_got, place], trip_memory
        )
        answer_square.array(square_got, "hx")
        in_first = Part(half, "yxlh").array(in_keep, "yhlx").array(in_got, "yhlx")
        in_second = Part(half, "xylh", half).array(in_keep, "yhlx").array(in_got, "yhlx")
        trip_in, after = ride(
            ring,
            cue,
            [
                ("y", [in_first, memory_second]),
                ("x", [in_second, memory_first]),
                ("h", [answer_square]),
            ],
        )
    heads_delta, slope_delta, heads_send, heads_keep = attend_back(
        place, heads, chances, attended_delta, inputs, hidden_low, after=after
    )
    after = []
    if cut:
        heads_send, cue = arrive([heads_send, place], trip_in)
        heads_got = ring.swap(heads_send, "c")
        trip_in, sends = ride(
            ring,
            cue,
            [
                ("x", [in_first]),
                ("y", [in_second]),
                ("l", [memory_first, memory_second]),
            ],
        )
        heads_got, cue, *_ = lax.optimization_barrier((heads_got, place, *sends))
        heads_first = Part(half, "yxlh").array(heads_keep, "yhlx").array(heads_got, "yhlx")
        heads_second = Part(half, "xylh", half)
        heads_second.array(heads_keep, "yhlx").array(heads_got, "yhlx")
        trip_heads, after = ride(ring, cue, [("y", [heads_first]), ("x", [heads_second])])
    passage_gradient, small = passage_end(
        place,
        gains,
        (
            slope_delta,
            answer_table_delta,
            ffn_gain_delta,
            final_gain_delta,
            self_gain_delta,
            cross_gain_delta,
            answer_gain_delta,
        ),
        passage_rows,
        heads_delta,
        hidden_delta,
        (encoder_query, encoder_key, encoder_value),
        after=after,
    )
    if cut:
        small_got = ring.swap(small, "c")
        small_got, cue = arrive([small_got, place], trip_in, trip_heads)
        total = Total(small)
        total.terms.append((small_got, [], 0))
        trip, sends = ride(
            ring,
            cue,
            [
                ("h", [memory_first, memory_second]),
                ("x", [heads_first, answer_square]),
                ("y", [heads_second, total]),
                ("l", [in_first, in_second]),
            ],
        )
        (cue,) = arrive([place], trip)
        trip, sends = ride(
            ring,
            cue,
            [("l", [heads_first, heads_second, total]), ("h", [in_first, in_second])],
        )
        (done,) = bus(
            place,
            [(None, [memory_first, memory_second, wide_first, wide_second, answer_square])],
            sends,
        )
        first = Beside(ring, done)
        cue, _ = arrive([place, done], trip)
        trip, sends = ride(ring, cue, [("h", [heads_first, heads_second, total])])
        cue, *first.arriving = arrive([place, *first.arriving], trip)
        done, small = bus(
            cue,
            [(None, [in_first, in_second, heads_first, heads_second]), (None, [total])],
        )
        last = Beside(ring, done)
        small_got = ring.swap(small, "x")
        first.send([done])
        lay, shapes, stacked, unhalved, side_by_side, units = layout(shard)
        stacked(0)
        unhalved(half)
        side_by_side(half + shard)
        unhalved(half + 2 * shard)
        units(half + 3 * shard)
        stacked(half + 4 * shard)
        weights = list(assemble(place, first.arrays(), shapes, lay))
        last.send(weights[:1])
        small_got, *_ = lax.optimization_barrier((small_got, weights[0]))
        lay, shapes, stacked, unhalved, side_by_side, units = layout(shard)
        side_by_side(0)
        units(shard)
        weights += list(assemble(place, last.arrays(), shapes, lay))
        small = wide(small) + wide(small_got)
    else:
        small = lax.psum(wide(small), ("dp", "blk"))
    mine = lax.axis_index("dp")
    gain_deltas = lax.dynamic_slice_in_dim(small[:6], mine * shard, shard, 1)
    tables = NB // ring.dp
    table_deltas = [
        lax.dynamic_slice_in_dim(small[8 : 8 + H, begin : begin + NB], mine * tables, tables, 1).T
        for begin in (0, 128)
    ]

    if not cut:
        weights = whole_weights(
            core,
            (memory_send, memory_keep),
            (in_send, in_keep),
            (heads_send, heads_keep),
            (
                (answer_lows[1], answer_wides[1]),
                (
                    answer_wides[0],
                    low(slotted(decoder_cotangent)),
                ),
                (answer_crossed, asking_delta),
                (answer_lows[0], answer_lows[2]),
                (answer_attended, answer_hidden_low),
                (answer_normed, answer_heads_delta[0]),
                (answer_normed, answer_heads_delta[1]),
                (answer_normed, answer_heads_delta[2]),
            ),
        )
    (
        gradient_cross_key,
        gradient_cross_value,
        gradient_encoder_ffn_out,
        gradient_decoder_ffn_in,
        gradient_decoder_ffn_out,
        gradient_cross_query,
        gradient_cross_mix,
        gradient_decoder_mix,
        gradient_decoder_query,
        gradient_decoder_key,
        gradient_decoder_value,
        gradient_encoder_ffn_in,
        gradient_encoder_query,
        gradient_encoder_key,
        gradient_encoder_value,
        gradient_encoder_mix,
    ) = weights
    return (
        result.reshape(encoder_input.shape),
        answer_result,
        passage_gradient.reshape(encoder_input.shape),
        answer_gradient,
        gain_deltas[ATTN],
        gradient_encoder_query,
        gradient_encoder_key,
        gradient_encoder_value,
        gradient_encoder_mix,
        table_deltas[0],
        gain_deltas[FFN],
        gradient_encoder_ffn_in,
        gradient_encoder_ffn_out,
        gain_deltas[FINAL],
        gradient_cross_key,
        gradient_cross_value,
        gain_deltas[SELF],
        gradient_decoder_query,
        gradient_decoder_key,
        gradient_decoder_value,
        gradient_decoder_mix,
        table_deltas[1],
        gain_deltas[CROSS],
        gradient_cross_query,
        gradient_cross_mix,
        gain_deltas[ANSWER],
        gradient_decoder_ffn_in,
        gradient_decoder_ffn_out,
    )


def whole_weights(core, memory, inner, heads, answers):
    def both(pair):
        send, keep = pair
        return (jnp.where(core == 0, keep, send), jnp.where(core == 0, send, keep))

    def shared(gradient):
        return lax.psum_scatter(low(gradient), "dp", scatter_dimension=0, tiled=True)

    def summed(gradient):
        return lax.psum(shared(gradient), "blk")

    memory = both(memory)
    shards, _, rows, _ = memory[0].shape
    cut = rows // 3
    passages = [part[:, :, :cut].reshape(D, D) for part in memory]
    out = [
        part[:, :, cut:]
        .reshape(shards, 2, 2 * cut, 2, D // 2)
        .swapaxes(2, 3)
        .reshape(8 * cut * shards, D // 2)
        for part in memory
    ]
    passages.append(jnp.concatenate(out, axis=1))
    passages.append(jnp.concatenate([unit for half in both(inner) for unit in half], axis=1))
    passages += [unit for half in both(heads) for unit in half]
    passages = [wide(summed(item)) for item in passages]
    answers = [wide(shared(dot_tokens(inputs, upstream))) for inputs, upstream in answers]
    return passages[:3] + answers + passages[3:]


def solution(mesh):
    dims = {4: P("dp", "blk", None, None), 3: P("dp", None, None), 2: P("dp", None), 1: P("dp")}
    rows = P("dp", "blk", None)
    return jax.shard_map(
        functools.partial(on_device, Ring(mesh)),
        mesh=mesh,
        in_specs=(dims[4], dims[3], dims[4], dims[3], rows, rows, dims[1]) + (P(),) * 24,
        out_specs=(dims[4], dims[3], dims[4], dims[3])
        + tuple(dims[1 if at in (0, 6, 9, 12, 18, 21) else 2] for at in range(24)),
        check_vma=False,
    )
```
